32 devices in a mesh: groups: 2 (over y), adapter: 4 (over z), tensor: 2 (over x), dp: 2 (over core).
Axes of the slice: x: 2, y: 2, z: 4, core: 2. Of those that a mesh axis runs over, the one named last changes fastest.
Arguments:
- tokens: bfloat16 [16384, 8192], P(('groups', 'adapter', 'dp'), 'tensor'), parts along dimension 0, may hold values from -6 to 6
- value_weight: bfloat16 [8192, 1024], P('tensor'), may hold values from -0.0625 to 0.0625
- adapter_down_weight: bfloat16 [16, 8192, 64], P(('groups', 'adapter'), 'tensor'), parts along dimension 0, may hold values from -0.0625 to 0.0625
- adapter_up_weight: bfloat16 [16, 64, 1024], P(('groups', 'adapter')), parts along dimension 0, may hold values from -0.75 to 0.75
- row_adapter_index: int32 [16384], P(('groups', 'adapter', 'dp')), parts along dimension 0, may hold values from 0 to 7, as said below
- adapter_slot_of: int32 [16], P('groups'), parts along dimension 0, may hold values from 0 to 7, as said below
Outputs:
- value: bfloat16 [16384, 1024], P(('groups', 'adapter', 'dp'), 'tensor'), parts along dimension 0
The draws below stay inside these ranges and needn't reach their ends.
There are 2 independent parts, one for each index of `groups`. The reference program is written for one: setup_inputs(seed, part) draws one part's arguments, and reference() takes and returns one part's arrays. A program takes and returns all parts, laid end to end along the dimension named above; an argument that names none is the same for every part. Nothing has to cross between parts.
Inputs may be any that keep to these rules, and one draw needn't show every extreme that they name: `row_adapter_index`: all 128 rows of each aligned segment name one adapter. Call the owner of a row the index along the mesh axis `adapter` of the device that stores its slot, slot // 2. Among the 8 segments of one device's rows, at most 2 have one owner, and one owner receives exactly 2 segments from every device. `adapter_slot_of`: A permutation of the slots.
All inputs are finite; a program needn't handle non-finite values.
Results may differ from the reference program's by a relative error of at most 0.001.
Values may be sent and summed in bfloat16 or wider, within the bound.
No kernel may reach another device: no remote copies, remote signals or barrier semaphores. Data moves between devices by JAX's collectives and lax.ppermute only.
A program may use at most 128 MiB of HBM per device.

```python
import jax
import jax.numpy as jnp
from jax import lax

MODEL_WIDTH = 8192
VALUE_FEATURES = 1024
ADAPTER_RANK = 64
SEGMENT_ROWS = 128
SEG_DEV = 8
ADAPT_DEV = 2
CAP = 2
ADAPTER_TOTAL = 8
ROWS = 8192
N_ADAPTER = 4
N_DP = 2


def shared_plan(key):
    key_home, key_hot, key_other, key_order, key_local = jax.random.split(key, 5)
    home = jax.random.permutation(key_home, ADAPTER_TOTAL).astype(jnp.int32)
    hot = jax.random.randint(key_hot, (), 0, N_ADAPTER).astype(jnp.int32)
    blocks = N_ADAPTER * N_DP
    others = jax.vmap(lambda k: jax.random.permutation(k, N_ADAPTER - 1))(jax.random.split(key_other, blocks)).astype(jnp.int32)
    others = jnp.tile(others, (1, CAP))[:, :SEG_DEV - CAP]
    others = others + (others >= hot).astype(jnp.int32)
    owners = jnp.concatenate([jnp.zeros((blocks, CAP), jnp.int32) + hot, others], axis=1)
    orders = jax.vmap(lambda k: jax.random.permutation(k, SEG_DEV))(jax.random.split(key_order, blocks)).astype(jnp.int32)
    owners = jnp.take_along_axis(owners, orders, axis=1)
    local = jax.random.randint(key_local, (blocks, SEG_DEV), 0, ADAPT_DEV).astype(jnp.int32)
    slot_indices = owners * ADAPT_DEV + local
    inverse = jnp.argsort(home, stable=True).astype(jnp.int32)
    seg_ids = jnp.take(inverse, slot_indices)
    row_ids = jnp.repeat(seg_ids, SEGMENT_ROWS, axis=1).reshape(blocks * SEG_DEV * SEGMENT_ROWS)
    return (row_ids.astype(jnp.int32), home)


def draw_row_adapter_index(key, part):
    row_ids, home = shared_plan(key)
    return row_ids


def draw_adapter_slot_of(key, part):
    row_ids, home = shared_plan(key)
    return home


def block_scale(stream_key, shape, shards, smallest, high):
    def one(position, parts):
        heights = jax.random.uniform(jax.random.fold_in(jax.random.fold_in(stream_key, 6), position), (parts,), jnp.float32, smallest / len(shards), high / len(shards))
        return jnp.repeat(jnp.exp(heights), shape[position] // parts).reshape((-1,) + (1,) * (len(shape) - position - 1))

    level = one(*shards[0])
    for cut in shards[1:]:
        level = level * one(*cut)
    return level


def gaussian(key, extent, spread, bound, cuts=(), kind=jnp.bfloat16):
    array = jax.random.normal(key, extent, jnp.float32) * spread
    if len(cuts) > 0:
        array = block_scale(key, extent, cuts, -0.22, 0.18) * array
    return jnp.clip(array, min=-bound, max=bound).astype(kind)


def setup_inputs(seed: int = 0, part: int = 0) -> dict:
    keys = jax.random.split(jax.random.key(seed), 7)
    part_keys = jax.random.split(jax.random.fold_in(keys[6], part), 7)
    return {
        "tokens": gaussian(part_keys[0], (ROWS, MODEL_WIDTH), 1.0, 6.0, ((0, 8), (1, 2))),
        "value_weight": gaussian(keys[1], (MODEL_WIDTH, VALUE_FEATURES), MODEL_WIDTH ** -0.5, 0.0625, ((0, 2),)),
        "adapter_down_weight": gaussian(part_keys[2], (ADAPTER_TOTAL, MODEL_WIDTH, ADAPTER_RANK), MODEL_WIDTH ** -0.5, 0.0625, ((0, 4), (1, 2))),
        "adapter_up_weight": gaussian(part_keys[3], (ADAPTER_TOTAL, ADAPTER_RANK, VALUE_FEATURES), ADAPTER_RANK ** -0.5, 0.75, ((0, 4),)),
        "row_adapter_index": draw_row_adapter_index(jax.random.fold_in(jax.random.fold_in(keys[6], part), 71), part),
        "adapter_slot_of": draw_adapter_slot_of(jax.random.fold_in(jax.random.fold_in(keys[6], part), 71), part),
    }


adapter_scale = 0.5


def reference(tokens, value_weight, adapter_down_weight, adapter_up_weight, row_adapter_index, adapter_slot_of):
    base_output = jnp.dot(tokens, value_weight, preferred_element_type=jnp.float32)
    row_count = tokens.shape[0] // SEGMENT_ROWS
    seg_ids = row_adapter_index.reshape(row_count, SEGMENT_ROWS)[:, 0]
    slot_indices = jnp.take(adapter_slot_of, seg_ids).astype(jnp.int32)

    def single_segment(item):
        rows_seg, slot_index = item
        down_output = lax.dynamic_index_in_dim(adapter_down_weight, slot_index, 0, keepdims=False)
        upper_limit = lax.dynamic_index_in_dim(adapter_up_weight, slot_index, 0, keepdims=False).astype(jnp.float32)
        shrink = jnp.dot(rows_seg, down_output, preferred_element_type=jnp.float32)
        return jnp.dot(shrink, upper_limit, precision=lax.Precision.HIGHEST)

    adapter_output = lax.map(single_segment, (tokens.reshape(row_count, SEGMENT_ROWS, MODEL_WIDTH), slot_indices)).reshape(row_count * SEGMENT_ROWS, VALUE_FEATURES)
    return (base_output + adapter_scale * adapter_output).astype(jnp.bfloat16)
```

```python
import jax
import jax.numpy as jnp
from jax import lax
from jax.sharding import PartitionSpec as P

SEGMENT_ROWS = 128
adapter_scale = 0.5


def on_device(
    tokens, value_weight, adapter_down_weight, adapter_up_weight, row_adapter_index, adapter_slot_of
):
    input_rows, width = tokens.shape
    seg_dev = input_rows // SEGMENT_ROWS
    per_device, _, rank = adapter_down_weight.shape
    n_adapter = lax.axis_size("adapter")
    n_tensor = lax.axis_size("tensor")
    n_dp = lax.axis_size("dp")
    me_t = lax.axis_index("tensor")
    me_dp = lax.axis_index("dp")
    columns = value_weight.shape[1] // n_tensor
    part = rank // n_dp

    down = jnp.swapaxes(adapter_down_weight, 1, 2)
    down_part = lax.dynamic_slice_in_dim(down, me_dp * part, part, 1)
    up_part = lax.dynamic_slice(
        adapter_up_weight, (0, me_dp * part, me_t * columns), (per_device, part, columns)
    )
    all_down = lax.all_gather(down_part, ("adapter", "dp"))
    all_up = lax.all_gather(up_part, ("adapter", "dp"))

    base = jnp.dot(tokens, value_weight, preferred_element_type=jnp.float32)
    value = lax.dynamic_slice_in_dim(base, me_t * columns, columns, 1)
    for step in range(1, n_tensor):
        target = (me_t + step) % n_tensor
        sent = lax.dynamic_slice_in_dim(base, target * columns, columns, 1)
        pairs = [(i, (i + step) % n_tensor) for i in range(n_tensor)]
        value = value + lax.ppermute(sent, "tensor", pairs)

    seg_ids = row_adapter_index.reshape(seg_dev, SEGMENT_ROWS)[:, 0]
    total = n_adapter * per_device
    match = seg_ids[:, None] == jnp.arange(total, dtype=jnp.int32)[None, :]
    slot = jnp.sum(jnp.where(match, adapter_slot_of[None, :], 0), axis=1)
    chosen = slot[:, None] == jnp.arange(total, dtype=jnp.int32)[None, :]
    chosen = chosen.reshape(seg_dev, 1, n_adapter, 1, per_device, 1)

    wide = lax.dot_general(
        tokens,
        all_down.reshape(n_adapter * n_dp * per_device * part, width),
        (((1,), (1,)), ((), ())),
        preferred_element_type=jnp.float32,
    ).reshape(seg_dev, SEGMENT_ROWS, n_adapter, n_dp, per_device, part)
    shrink = jnp.sum(jnp.where(chosen, wide, 0.0), axis=(2, 4)).reshape(input_rows, rank)
    mine = shrink
    for step in range(1, n_tensor):
        pairs = [(i, (i + step) % n_tensor) for i in range(n_tensor)]
        shrink = shrink + lax.ppermute(mine, "tensor", pairs)
    picked = jnp.sum(
        jnp.where(
            chosen.reshape(seg_dev, n_adapter, 1, per_device, 1, 1),
            all_up.reshape(1, n_adapter, n_dp, per_device, part, columns).astype(jnp.float32),
            0.0,
        ),
        axis=(1, 3),
    ).reshape(seg_dev, rank, columns)
    lora = jnp.einsum(
        "sru,suv->srv",
        shrink.reshape(seg_dev, SEGMENT_ROWS, rank),
        picked,
        precision=lax.Precision.HIGHEST,
    )
    return (value + adapter_scale * lora.reshape(input_rows, columns)).astype(jnp.bfloat16)


def solution(mesh):
    return jax.shard_map(
        on_device,
        mesh=mesh,
        in_specs=(
            P(("groups", "adapter", "dp"), "tensor"),
            P("tensor", None),
            P(("groups", "adapter"), "tensor", None),
            P(("groups", "adapter"), None, None),
            P(("groups", "adapter", "dp")),
            P("groups"),
        ),
        out_specs=P(("groups", "adapter", "dp"), "tensor"),
        check_vma=False,
    )
```

```python
import functools

import jax
import jax.numpy as jnp
from jax import lax
from jax.experimental import pallas as pl
from jax.experimental.pallas import tpu as pltpu
from jax.sharding import PartitionSpec as P

SEGMENT_ROWS = 128
adapter_scale = 0.5
VMEM_BYTES = 40 * 2**20
MOST = 2


def cost(flops, moved):
    return pl.CostEstimate(flops=int(flops), bytes_accessed=int(moved), transcendentals=0)


def params():
    return pltpu.CompilerParams(vmem_limit_bytes=VMEM_BYTES)


def segment_slot(ids, slots, s):
    return slots[ids[s * SEGMENT_ROWS]]


def find_segment(ids, slots, per_device, seg_dev, owner, rank):
    found, within, count = jnp.int32(-1), jnp.int32(0), jnp.int32(0)
    for s in range(seg_dev):
        slot = segment_slot(ids, slots, s)
        hit = lax.div(slot, jnp.int32(per_device)) == owner
        take = hit & (count == rank)
        found = jnp.where(take, s, found)
        within = jnp.where(take, lax.rem(slot, jnp.int32(per_device)), within)
        count = count + hit.astype(jnp.int32)
    return found, within


def base_kernel(column, x_ref, w_ref, o_ref):
    del column
    o_ref[...] = jnp.dot(x_ref[...], w_ref[...], preferred_element_type=jnp.float32)


def base_product(tokens, weight, column, columns):
    rows, width = tokens.shape
    block = min(256, rows)
    return pl.pallas_call(
        base_kernel,
        grid_spec=pltpu.PrefetchScalarGridSpec(
            num_scalar_prefetch=1,
            grid=(rows // block,),
            in_specs=[
                pl.BlockSpec((block, width), lambda i, c: (i, 0)),
                pl.BlockSpec((width, columns), lambda i, c: (0, c[0])),
            ],
            out_specs=pl.BlockSpec((block, columns), lambda i, c: (i, 0)),
        ),
        out_shape=jax.ShapeDtypeStruct((rows, columns), jnp.float32),
        compiler_params=params(),
        cost_estimate=cost(
            2 * rows * width * columns, 2 * rows * width + 2 * width * columns + 4 * rows * columns
        ),
    )(column.reshape(1), tokens, weight)


def shrink_kernel(n_bufs, per_device, rank, seg_dev, ids, slots, owners, *refs):
    x_refs, d_refs, o_ref = refs[:MOST], refs[MOST : MOST + n_bufs], refs[-1]
    width = x_refs[0].shape[1]
    step = pl.program_id(0)
    owner = owners[step]
    for buf in range(n_bufs):
        for j in range(MOST):
            seg, within = find_segment(ids, slots, per_device, seg_dev, owner, j)

            @pl.when((step == buf) & (seg >= 0))
            def _(buf=buf, j=j, within=within):
                down = d_refs[buf][pl.ds(pl.multiple_of(within * rank, rank), rank), :width]
                o_ref[0, :, j * rank : (j + 1) * rank] = lax.dot_general(
                    x_refs[j][...], down, (((1,), (1,)), ((), ())), preferred_element_type=jnp.float32
                )

            @pl.when((step == buf) & (seg < 0))
            def _(j=j):
                o_ref[0, :, j * rank : (j + 1) * rank] = jnp.zeros((SEGMENT_ROWS, rank), jnp.float32)


def shrink_product(tokens, ids, slots, owners, buffers, per_device, rank):
    rows, width = tokens.shape
    seg_dev = rows // SEGMENT_ROWS
    n_bufs = len(buffers)

    def segment_block(j):
        def index(i, ids, slots, owners):
            seg, _ = find_segment(ids, slots, per_device, seg_dev, owners[i], j)
            return jnp.maximum(seg, 0), 0

        return pl.BlockSpec((SEGMENT_ROWS, width), index)

    whole = [pl.BlockSpec(b.shape, lambda i, *_: (0, 0)) for b in buffers]
    return pl.pallas_call(
        functools.partial(shrink_kernel, n_bufs, per_device, rank, seg_dev),
        grid_spec=pltpu.PrefetchScalarGridSpec(
            num_scalar_prefetch=3,
            grid=(n_bufs,),
            in_specs=[segment_block(j) for j in range(MOST)] + whole,
            out_specs=pl.BlockSpec((1, SEGMENT_ROWS, MOST * rank), lambda i, *_: (i, 0, 0)),
        ),
        out_shape=jax.ShapeDtypeStruct((n_bufs, SEGMENT_ROWS, MOST * rank), jnp.float32),
        compiler_params=params(),
        cost_estimate=cost(
            n_bufs * MOST * 2 * SEGMENT_ROWS * width * 256,
            n_bufs * 2 * (MOST * SEGMENT_ROWS + per_device * rank) * width,
        ),
    )(ids, slots, owners, *([tokens] * MOST), *buffers)


def combine_kernel(n_bufs, n_base, n_shrink, per_device, rank, seg_dev, ids, slots, owners, *refs):
    base_refs, refs = refs[:n_base], refs[n_base:]
    up_refs, refs = refs[:n_bufs], refs[n_bufs:]
    shrink_refs, refs = refs[: n_bufs * n_shrink], refs[n_bufs * n_shrink :]
    o_ref, up, mid = refs
    s = pl.program_id(0)
    slot = segment_slot(ids, slots, s)
    owner = lax.div(slot, jnp.int32(per_device))
    within = lax.rem(slot, jnp.int32(per_device))
    j = jnp.int32(0)
    for other in range(seg_dev):
        same = lax.div(segment_slot(ids, slots, other), jnp.int32(per_device)) == owner
        j = j + ((other < s) & same).astype(jnp.int32)
    for b in range(n_bufs):

        @pl.when(owners[b] == owner)
        def _(b=b):
            up[...] = up_refs[b][pl.ds(pl.multiple_of(within * rank, rank), rank), :]
            total = shrink_refs[b * n_shrink][0]
            for r in shrink_refs[b * n_shrink + 1 : (b + 1) * n_shrink]:
                total = total + r[0]
            mid[...] = total

    total = jnp.where(j == 0, mid[:, :rank], mid[:, rank : 2 * rank])
    high = total.astype(jnp.bfloat16)
    left = total - high.astype(jnp.float32)
    middle = left.astype(jnp.bfloat16)
    low = (left - middle.astype(jnp.float32)).astype(jnp.bfloat16)
    lora = jnp.dot(low, up[...], preferred_element_type=jnp.float32)
    lora = lora + jnp.dot(middle, up[...], preferred_element_type=jnp.float32)
    lora = lora + jnp.dot(high, up[...], preferred_element_type=jnp.float32)
    value = base_refs[0][...]
    for r in base_refs[1:]:
        value = value + r[...]
    o_ref[...] = (value + adapter_scale * lora).astype(jnp.bfloat16)


def combine(ids, slots, owners, bases, buffers, shrinks, per_device, rank):
    rows, columns = bases[0].shape
    seg_dev = rows // SEGMENT_ROWS
    n_bufs, n_shrink = len(buffers), len(shrinks[0])
    last = buffers[0].shape[1] // columns - 1
    return pl.pallas_call(
        functools.partial(combine_kernel, n_bufs, len(bases), n_shrink, per_device, rank, seg_dev),
        grid_spec=pltpu.PrefetchScalarGridSpec(
            num_scalar_prefetch=3,
            grid=(seg_dev,),
            in_specs=[pl.BlockSpec((SEGMENT_ROWS, columns), lambda i, *_: (i, 0)) for _ in bases]
            + [pl.BlockSpec((b.shape[0], columns), lambda i, *_: (0, last)) for b in buffers]
            + [
                pl.BlockSpec((1, SEGMENT_ROWS, MOST * rank), lambda i, *_, place=place: (place, 0, 0))
                for group in shrinks
                for _, place in group
            ],
            out_specs=pl.BlockSpec((SEGMENT_ROWS, columns), lambda i, *_: (i, 0)),
            scratch_shapes=[
                pltpu.VMEM((rank, columns), jnp.bfloat16),
                pltpu.VMEM((SEGMENT_ROWS, MOST * rank), jnp.float32),
            ],
        ),
        out_shape=jax.ShapeDtypeStruct((rows, columns), jnp.bfloat16),
        compiler_params=params(),
        cost_estimate=cost(6 * rows * rank * columns, (4 * len(bases) + 2) * rows * columns),
    )(ids, slots, owners, *bases, *buffers, *[array for group in shrinks for array, _ in group])


def on_device(
    tokens, value_weight, adapter_down_weight, adapter_up_weight, row_adapter_index, adapter_slot_of
):
    width = tokens.shape[1]
    per_device, _, rank = adapter_down_weight.shape
    n_adapter = lax.axis_size("adapter")
    n_tensor = lax.axis_size("tensor")
    me_a = lax.axis_index("adapter")
    me_t = lax.axis_index("tensor")
    core = lax.axis_index("dp")
    columns = value_weight.shape[1] // n_tensor
    ids, slots = row_adapter_index, adapter_slot_of

    def swap_tensor(array, step):
        pairs = [(i, (i + step) % n_tensor) for i in range(n_tensor)]
        return lax.ppermute(array, "tensor", pairs)

    def along_line(array, stage):
        up = [(2 * i, 2 * (i + 1)) for i in range(stage - 1, n_adapter - 1)]
        down = [(2 * i + 1, 2 * (i - 1) + 1) for i in range(1, n_adapter - stage + 1)]
        return lax.ppermute(array, ("adapter", "dp"), up + down)

    def swap_cores(array):
        return lax.ppermute(array, "dp", [(0, 1), (1, 0)])

    down = jnp.swapaxes(adapter_down_weight, 1, 2).reshape(per_device * rank, width)
    up = lax.dynamic_slice_in_dim(adapter_up_weight, me_t * columns, columns, 2)
    message = jnp.concatenate([down, up.reshape(per_device * rank, columns)], axis=1)

    buffers, owners = [message], [me_a]
    held = message
    stages = []
    for stage in range(1, n_adapter):
        held = along_line(held, stage)
        stages.append((held, swap_cores(held)))
        toward = jnp.where(core == 0, -stage, stage)
        owners += [me_a + toward, me_a - toward]
        buffers += [held, stages[-1][1]]

    parts = [
        swap_tensor(base_product(tokens, value_weight, (me_t + step) % n_tensor, columns), step)
        for step in range(1, n_tensor)
    ]
    bases = [base_product(tokens, value_weight, me_t, columns)] + parts

    shrinks = []
    for stage in range(n_adapter):
        if stage == 0:
            mine = [message]
            whose = jnp.stack([me_a])
        else:
            mine = list(stages[stage - 1])
            whose = jnp.stack(owners[2 * stage - 1 : 2 * stage + 1])
        shrink = shrink_product(tokens, ids, slots, whose, mine, per_device, rank)
        copies = [shrink] + [swap_tensor(shrink, step) for step in range(1, n_tensor)]
        shrinks += [[(c, place) for c in copies] for place in range(len(mine))]

    return combine(ids, slots, jnp.stack(owners), bases, buffers, shrinks, per_device, rank)


def solution(mesh):
    return jax.shard_map(
        on_device,
        mesh=mesh,
        in_specs=(
            P(("groups", "adapter", "dp"), "tensor"),
            P("tensor", None),
            P(("groups", "adapter"), "tensor", None),
            P(("groups", "adapter"), None, None),
            P(("groups", "adapter", "dp")),
            P("groups"),
        ),
        out_specs=P(("groups", "adapter", "dp"), "tensor"),
        check_vma=False,
    )
```

```python
import functools

import jax
import jax.numpy as jnp
from jax import lax
from jax.experimental import pallas as pl
from jax.experimental.pallas import tpu as pltpu
from jax.sharding import PartitionSpec as P

SEGMENT_ROWS = 128
adapter_scale = 0.5
VMEM_BYTES = 56 * 2**20
MOST = 2
CHUNKS = ((256, 3), (384, 0), (384, 1))
DEPTH = 1024
LIMIT = 2.0**23 - 1


def cost(flops, moved):
    return pl.CostEstimate(flops=int(flops), bytes_accessed=int(moved), transcendentals=0)


def params():
    return pltpu.CompilerParams(vmem_limit_bytes=VMEM_BYTES)


ANY = pl.BlockSpec(memory_space=pl.ANY)
SMEM = pl.BlockSpec(memory_space=pltpu.SMEM)


def segment_slot(ids, slots, s):
    return slots[ids[s * SEGMENT_ROWS]]


def find_segment(ids, slots, per_device, seg_dev, owner, number):
    found, within, count = jnp.int32(-1), jnp.int32(0), jnp.int32(0)
    for s in range(seg_dev):
        slot = segment_slot(ids, slots, s)
        hit = lax.div(slot, jnp.int32(per_device)) == owner
        take = hit & (count == number)
        found = jnp.where(take, s, found)
        within = jnp.where(take, lax.rem(slot, jnp.int32(per_device)), within)
        count = count + hit.astype(jnp.int32)
    return found, within


def arrival_order(me, n_adapter):
    order = [me] + [jnp.int32(-1)] * (n_adapter - 1)
    count = jnp.int32(1)
    for distance in range(1, n_adapter):
        for other in (me - distance, me + distance):
            valid = (other >= 0) & (other < n_adapter)
            order = [jnp.where(valid & (count == k), other, o) for k, o in enumerate(order)]
            count = count + valid.astype(jnp.int32)
    return order


def buffer_owners(me, core, stages):
    owners = {0: [me]}
    for stage in stages:
        if stage > 0:
            toward = jnp.where(core == 0, -stage, stage)
            owners[stage] = [me + toward, me - toward]
    return [o for stage in stages for o in owners[stage]]


def pack_kernel(place, down_ref, up_ref, o_ref, sems):
    width = down_ref.shape[1]
    columns = o_ref.shape[1] - width
    start = pl.multiple_of(place[0] * columns, columns)
    copies = [
        pltpu.make_async_copy(down_ref, o_ref.at[:, pl.ds(0, width)], sems.at[0]),
        pltpu.make_async_copy(
            up_ref.at[:, pl.ds(start, columns)], o_ref.at[:, pl.ds(width, columns)], sems.at[1]
        ),
    ]
    for copy in copies:
        copy.start()
    for copy in copies:
        copy.wait()


def pack_message(down, up, place, columns):
    rows, width = down.shape
    return pl.pallas_call(
        pack_kernel,
        in_specs=[SMEM, ANY, ANY],
        out_specs=ANY,
        out_shape=jax.ShapeDtypeStruct((rows, width + columns), jnp.bfloat16),
        scratch_shapes=[pltpu.SemaphoreType.DMA((2,))],
        compiler_params=params(),
        cost_estimate=cost(0, 4 * rows * (width + columns)),
    )(place.reshape(1), down, up)


def diagonal():
    shape = (SEGMENT_ROWS, SEGMENT_ROWS)
    return lax.broadcasted_iota(jnp.int32, shape, 0) == lax.broadcasted_iota(jnp.int32, shape, 1)


def coded_rows(rows):
    return rows * 3 // 4 + 8


def encode(values, o_ref):
    rows = values.shape[0]
    quarter = rows // 4
    largest = jnp.maximum(jnp.max(jnp.abs(values), axis=1, keepdims=True), 2.0**-100)
    power = jnp.floor(jnp.log2(largest))
    scaled = jnp.clip(jnp.round(values * jnp.exp2(22.0 - power)), -LIMIT, LIMIT)
    whole = scaled.astype(jnp.int32)
    q = [whole[i * quarter : (i + 1) * quarter] for i in range(4)]
    for i in range(3):
        o_ref[i * quarter : (i + 1) * quarter, :] = (q[i] & 0xFFFFFF) | ((q[3] >> (8 * i)) << 24)
    o_ref[3 * quarter :, :] = jnp.zeros((8, values.shape[1]), jnp.int32)
    for h in range(rows // SEGMENT_ROWS):
        column = power[h * SEGMENT_ROWS : (h + 1) * SEGMENT_ROWS]
        row = jnp.sum(jnp.where(diagonal(), column, 0.0), axis=0, keepdims=True)
        o_ref[3 * quarter + h : 3 * quarter + h + 1, :SEGMENT_ROWS] = row.astype(jnp.int32)


def decode(words, rows):
    quarter = rows // 4
    w = [words[i * quarter : (i + 1) * quarter] for i in range(3)]
    q = [(x << 8) >> 8 for x in w]
    q.append(((w[0] >> 24) & 0xFF) | (((w[1] >> 24) & 0xFF) << 8) | ((w[2] >> 24) << 16))
    powers = []
    for h in range(rows // SEGMENT_ROWS):
        row = words[3 * quarter + h : 3 * quarter + h + 1, :SEGMENT_ROWS].astype(jnp.float32)
        powers.append(jnp.sum(jnp.where(diagonal(), row, 0.0), axis=1, keepdims=True))
    scale = jnp.exp2(jnp.concatenate(powers, axis=0) - 22.0)
    return jnp.concatenate(q, axis=0).astype(jnp.float32) * scale


def base_kernel(coded, column, x_ref, w_ref, o_ref, total):
    del column
    step = pl.program_id(0)
    product = jnp.dot(x_ref[...], w_ref[...], preferred_element_type=jnp.float32)

    @pl.when(step == 0)
    def _():
        total[...] = product

    @pl.when(step > 0)
    def _():
        total[...] += product

    @pl.when(step == pl.num_programs(0) - 1)
    def _():
        if coded:
            encode(total[...], o_ref)
        else:
            o_ref[...] = total[...]


def base_product(tokens, weight, column, columns, rows, place, coded):
    width = tokens.shape[1]
    depth = min(DEPTH, width)
    out_rows = coded_rows(rows) if coded else rows
    return pl.pallas_call(
        functools.partial(base_kernel, coded),
        grid_spec=pltpu.PrefetchScalarGridSpec(
            num_scalar_prefetch=1,
            grid=(width // depth,),
            in_specs=[
                pl.BlockSpec((rows, depth), lambda i, c: (place, i)),
                pl.BlockSpec((depth, columns), lambda i, c: (i, c[0])),
            ],
            out_specs=pl.BlockSpec((out_rows, columns), lambda i, c: (0, 0)),
            scratch_shapes=[pltpu.VMEM((rows, columns), jnp.float32)],
        ),
        out_shape=jax.ShapeDtypeStruct((out_rows, columns), jnp.int32 if coded else jnp.float32),
        compiler_params=params(),
        cost_estimate=cost(
            2 * rows * width * columns, 2 * rows * width + 2 * width * columns + 4 * rows * columns
        ),
    )(column.reshape(1), tokens, weight)


def shrink_kernel(ks, stages, n_adapter, per_device, rank, ids, slots, here, x_ref, *refs):
    buffers, (o_ref, x, d, sems) = refs[:-4], refs[-4:]
    rows, width = x_ref.shape
    seg_dev = rows // SEGMENT_ROWS
    order = arrival_order(here[0], n_adapter)
    owners = buffer_owners(here[0], here[1], stages)
    work = []
    for i, k in enumerate(ks):
        for buffer, whose in zip(buffers, owners):
            down = pltpu.make_async_copy(buffer.at[:, pl.ds(0, width)], d.at[i], sems.at[i, MOST])
            pl.when(whose == order[k])(down.start)
        for j in range(MOST):
            seg, within = find_segment(ids, slots, per_device, seg_dev, order[k], j)
            start = pl.multiple_of(jnp.maximum(seg, 0) * SEGMENT_ROWS, SEGMENT_ROWS)
            load = pltpu.make_async_copy(
                x_ref.at[pl.ds(start, SEGMENT_ROWS), :], x.at[i, j], sems.at[i, j]
            )
            load.start()
            work.append((i, j, within, load, down))
    for i, j, within, load, down in work:
        if j == 0:
            down.wait()
        load.wait()
        factor = d[i, pl.ds(pl.multiple_of(within * rank, rank), rank), :]
        o_ref[i, :, j * rank : (j + 1) * rank] = lax.dot_general(
            x[i, j], factor, (((1,), (1,)), ((), ())), preferred_element_type=jnp.float32
        )


def shrink_product(ks, stages, n_adapter, tokens, ids, slots, here, buffers, per_device, rank):
    width = tokens.shape[1]
    n = len(ks)
    return pl.pallas_call(
        functools.partial(shrink_kernel, ks, stages, n_adapter, per_device, rank),
        in_specs=[SMEM, SMEM, SMEM, ANY] + [ANY] * len(buffers),
        out_specs=pl.BlockSpec(memory_space=pltpu.VMEM),
        out_shape=jax.ShapeDtypeStruct((n, SEGMENT_ROWS, MOST * rank), jnp.float32),
        scratch_shapes=[
            pltpu.VMEM((n, MOST, SEGMENT_ROWS, width), jnp.bfloat16),
            pltpu.VMEM((n, per_device * rank, width), jnp.bfloat16),
            pltpu.SemaphoreType.DMA((n, MOST + 1)),
        ],
        compiler_params=params(),
        cost_estimate=cost(
            n * MOST * 2 * SEGMENT_ROWS * width * 256,
            n * 2 * (MOST * SEGMENT_ROWS + per_device * rank) * width,
        ),
    )(ids, slots, here, tokens, *buffers)


def up_product(shrink, factor):
    high = shrink.astype(jnp.bfloat16)
    left = shrink - high.astype(jnp.float32)
    middle = left.astype(jnp.bfloat16)
    low = (left - middle.astype(jnp.float32)).astype(jnp.bfloat16)
    result = jnp.dot(low, factor, preferred_element_type=jnp.float32)
    result = result + jnp.dot(middle, factor, preferred_element_type=jnp.float32)
    return result + jnp.dot(high, factor, preferred_element_type=jnp.float32)


def fetch_up(buffers, owners, owner, target, sem):
    columns = target.shape[1]
    for buffer, whose in zip(buffers, owners):
        copy = pltpu.make_async_copy(
            buffer.at[:, pl.ds(buffer.shape[1] - columns, columns)], target, sem
        )
        pl.when(whose == owner)(copy.start)
    return copy


def early_kernel(n_adapter, n_tensor, n_calls, per_device, rank, ids, slots, here, *refs):
    n_chunks = len(CHUNKS)
    base_ref, coded_refs, refs = refs[0], refs[1 : 1 + n_chunks * (n_tensor - 1)], refs[1 + n_chunks * (n_tensor - 1) :]
    shrinks, refs = refs[: n_calls * n_tensor], refs[n_calls * n_tensor :]
    buffers, (o_ref, rest_ref, up, total, sems) = refs[:-5], refs[-5:]
    seg_dev = base_ref.shape[0] // SEGMENT_ROWS
    order = arrival_order(here[0], n_adapter)
    owners = buffer_owners(here[0], here[1], range(n_adapter - 1))
    waits = [
        fetch_up(buffers, owners, order[k], up.at[k], sems.at[k]) for k in range(n_adapter - 1)
    ]
    shares = []
    for call in range(n_calls):
        share = shrinks[call * n_tensor][...]
        for i in range(1, n_tensor):
            share = share + shrinks[call * n_tensor + i][...]
        shares += [share[i] for i in range(share.shape[0])]
    for chunk, (rows, place) in enumerate(CHUNKS):
        here_rows = pl.ds(place * rows, rows)
        value = base_ref[here_rows, :]
        for i in range(n_tensor - 1):
            value = value + decode(coded_refs[chunk * (n_tensor - 1) + i][...], rows)
        total[here_rows, :] = value
    for copy in waits:
        copy.wait()
    for k in range(n_adapter):
        for j in range(MOST):
            seg, within = find_segment(ids, slots, per_device, seg_dev, order[k], j)
            start = pl.multiple_of(jnp.maximum(seg, 0) * SEGMENT_ROWS, SEGMENT_ROWS)
            value = total[pl.ds(start, SEGMENT_ROWS), :]
            if k == n_adapter - 1:
                rest_ref[j] = value
                continue
            factor = up[k, pl.ds(pl.multiple_of(within * rank, rank), rank), :]
            lora = up_product(shares[k][:, j * rank : (j + 1) * rank], factor)

            @pl.when(seg >= 0)
            def _(start=start, value=value, lora=lora):
                o_ref[pl.ds(start, SEGMENT_ROWS), :] = (value + adapter_scale * lora).astype(
                    jnp.bfloat16
                )


def early(n_adapter, n_tensor, ids, slots, here, base, coded, shrinks, buffers, per_device, rank):
    rows, columns = base.shape
    vmem = pl.BlockSpec(memory_space=pltpu.VMEM)
    return pl.pallas_call(
        functools.partial(
            early_kernel, n_adapter, n_tensor, len(shrinks) // n_tensor, per_device, rank
        ),
        in_specs=[SMEM] * 3 + [vmem] * (1 + len(coded) + len(shrinks)) + [ANY] * len(buffers),
        out_specs=[vmem, vmem],
        out_shape=[
            jax.ShapeDtypeStruct((rows, columns), jnp.bfloat16),
            jax.ShapeDtypeStruct((MOST, SEGMENT_ROWS, columns), jnp.float32),
        ],
        scratch_shapes=[
            pltpu.VMEM((n_adapter - 1, per_device * rank, columns), jnp.bfloat16),
            pltpu.VMEM((rows, columns), jnp.float32),
            pltpu.SemaphoreType.DMA((n_adapter - 1,)),
        ],
        compiler_params=params(),
        cost_estimate=cost(6 * rows * rank * columns, (4 * n_tensor + 2) * rows * columns),
    )(ids, slots, here, base, *coded, *shrinks, *buffers)


def late_kernel(n_adapter, n_tensor, stages, per_device, rank, ids, slots, here, *refs):
    rest_ref, shrinks, refs = refs[0], refs[1 : 1 + n_tensor], refs[1 + n_tensor :]
    buffers, (_, o_ref, up, out, sems) = refs[:-5], refs[-5:]
    seg_dev = o_ref.shape[0] // SEGMENT_ROWS
    owner = arrival_order(here[0], n_adapter)[-1]
    owners = buffer_owners(here[0], here[1], stages)
    wait = fetch_up(buffers, owners, owner, up, sems.at[MOST])
    share = shrinks[0][0]
    for r in shrinks[1:]:
        share = share + r[0]
    wait.wait()
    stores = []
    for j in range(MOST):
        seg, within = find_segment(ids, slots, per_device, seg_dev, owner, j)
        start = pl.multiple_of(jnp.maximum(seg, 0) * SEGMENT_ROWS, SEGMENT_ROWS)
        factor = up[pl.ds(pl.multiple_of(within * rank, rank), rank), :]
        lora = up_product(share[:, j * rank : (j + 1) * rank], factor)
        out[j] = (rest_ref[j] + adapter_scale * lora).astype(jnp.bfloat16)
        store = pltpu.make_async_copy(out.at[j], o_ref.at[pl.ds(start, SEGMENT_ROWS), :], sems.at[j])
        pl.when(seg >= 0)(store.start)
        stores.append((seg, store))
    for seg, store in stores:
        pl.when(seg >= 0)(store.wait)


def late(n_adapter, n_tensor, stages, ids, slots, here, rest, shrinks, buffers, value, per_device, rank):
    rows, columns = value.shape
    vmem = pl.BlockSpec(memory_space=pltpu.VMEM)
    return pl.pallas_call(
        functools.partial(late_kernel, n_adapter, n_tensor, stages, per_device, rank),
        in_specs=[SMEM] * 3 + [vmem] * (1 + len(shrinks)) + [ANY] * (len(buffers) + 1),
        out_specs=ANY,
        out_shape=jax.ShapeDtypeStruct((rows, columns), jnp.bfloat16),
        scratch_shapes=[
            pltpu.VMEM((per_device * rank, columns), jnp.bfloat16),
            pltpu.VMEM((MOST, SEGMENT_ROWS, columns), jnp.bfloat16),
            pltpu.SemaphoreType.DMA((MOST + 1,)),
        ],
        input_output_aliases={4 + len(shrinks) + len(buffers): 0},
        compiler_params=params(),
        cost_estimate=cost(
            6 * MOST * SEGMENT_ROWS * rank * columns, 8 * MOST * SEGMENT_ROWS * columns
        ),
    )(ids, slots, here, rest, *shrinks, *buffers, value)


def after(array, *others):
    return lax.optimization_barrier((array, *others))[0]


def on_device(
    tokens, value_weight, adapter_down_weight, adapter_up_weight, row_adapter_index, adapter_slot_of
):
    rows, width = tokens.shape
    per_device, _, rank = adapter_down_weight.shape
    n_adapter = lax.axis_size("adapter")
    n_tensor = lax.axis_size("tensor")
    me_t = lax.axis_index("tensor")
    here = jnp.stack([lax.axis_index("adapter"), lax.axis_index("dp")])
    columns = value_weight.shape[1] // n_tensor
    ids, slots = row_adapter_index, adapter_slot_of

    def swap_tensor(array, step):
        pairs = [(i, (i + step) % n_tensor) for i in range(n_tensor)]
        return lax.ppermute(array, "tensor", pairs)

    def along_line(array, stage):
        up = [(2 * i, 2 * (i + 1)) for i in range(stage - 1, n_adapter - 1)]
        down = [(2 * i + 1, 2 * (i - 1) + 1) for i in range(1, n_adapter - stage + 1)]
        return lax.ppermute(array, ("adapter", "dp"), up + down)

    def swap_cores(array):
        return lax.ppermute(array, "dp", [(0, 1), (1, 0)])

    down = jnp.swapaxes(adapter_down_weight, 1, 2).reshape(per_device * rank, width)
    up = adapter_up_weight.reshape(per_device * rank, value_weight.shape[1])
    message = pack_message(down, up, me_t, columns)

    buffers, shrinks = [[message]], []

    def stage_buffers(stages):
        return [b for stage in stages for b in buffers[stage]]

    def shrink(ks, stages):
        mine = shrink_product(
            ks, stages, n_adapter, tokens, ids, slots, here, stage_buffers(stages), per_device, rank
        )
        shrinks.extend([mine] + [swap_tensor(mine, step) for step in range(1, n_tensor)])
        return shrinks[-n_tensor:]

    held = along_line(message, 1)
    parts = [
        [
            base_product(tokens, value_weight, (me_t + step) % n_tensor, columns, size, place, True)
            for step in range(1, n_tensor)
        ]
        for size, place in CHUNKS
    ]
    sent = [[swap_tensor(p, step + 1) for step, p in enumerate(parts[0])]]
    done = [p for group in parts for p in group] + sent[0]
    for stage in range(1, n_adapter):
        if stage < len(CHUNKS):
            sent.append([swap_tensor(after(p, held), step + 1) for step, p in enumerate(parts[stage])])
        if stage == n_adapter - 1:
            value, rest = early(
                n_adapter,
                n_tensor,
                ids,
                slots,
                here,
                base,
                [c for group in sent for c in group],
                shrinks,
                stage_buffers(range(n_adapter - 1)),
                per_device,
                rank,
            )
            done = [value]
        held = after(held, *done)
        done = sent[stage] if stage < len(CHUNKS) else []
        came = held
        if stage < n_adapter - 1:
            held = along_line(came, stage + 1)
        buffers.append([came, swap_cores(came)])
        if stage == 1:
            base = base_product(tokens, value_weight, me_t, columns, rows, 0, False)
            done = done + [base, shrink([0, 1], [0, 1])[0]]
        else:
            stages = list(range((stage + 1) // 2, stage + 1))
            done = done + [shrink([stage], stages)[0]]

    return late(
        n_adapter,
        n_tensor,
        stages,
        ids,
        slots,
        here,
        rest,
        shrinks[-n_tensor:],
        stage_buffers(stages),
        value,
        per_device,
        rank,
    )


def solution(mesh):
    return jax.shard_map(
        on_device,
        mesh=mesh,
        in_specs=(
            P(("groups", "adapter", "dp"), "tensor"),
            P("tensor", None),
            P(("groups", "adapter"), "tensor", None),
            P(("groups", "adapter"), None, None),
            P(("groups", "adapter", "dp")),
            P("groups"),
        ),
        out_specs=P(("groups", "adapter", "dp"), "tensor"),
        check_vma=False,
    )
```

```python
import functools

import jax
import jax.numpy as jnp
from jax import lax
from jax.experimental import pallas as pl
from jax.experimental.pallas import tpu as pltpu
from jax.sharding import PartitionSpec as P

SEGMENT_ROWS = 128
adapter_scale = 0.5
MOST = 2
BLOCK = 256
PIECES = 4
CHUNKS = ((6, 2), (0, 3), (3, 3))
ENTRIES = 8
MIDDLE = 1.5 * 2.0**23


def cost(flops, moved):
    return pl.CostEstimate(flops=int(flops), bytes_accessed=int(moved), transcendentals=0)


def params(mib):
    return pltpu.CompilerParams(vmem_limit_bytes=mib * 2**20)


ANY = pl.BlockSpec(memory_space=pl.ANY)
HBM = pl.BlockSpec(memory_space=pltpu.HBM)
SMEM = pl.BlockSpec(memory_space=pltpu.SMEM)
VMEM = pl.BlockSpec(memory_space=pltpu.VMEM)


def arrival_order(me, n_adapter):
    order = [me] + [jnp.int32(-1)] * (n_adapter - 1)
    count = jnp.int32(1)
    for distance in range(1, n_adapter):
        for other in (me - distance, me + distance):
            valid = (other >= 0) & (other < n_adapter)
            order = [jnp.where(valid & (count == k), other, o) for k, o in enumerate(order)]
            count = count + valid.astype(jnp.int32)
    return order


def buffer_owners(here, stages):
    owners = []
    for stage in stages:
        toward = jnp.where(here[1] == 0, -stage, stage)
        owners += [here[0] + toward, here[0] - toward] if stage > 0 else [here[0]]
    return owners


def segment_of(table, k, j):
    seg = table[k * ENTRIES + 1 + 2 * j]
    start = pl.multiple_of(jnp.maximum(seg, 0) * SEGMENT_ROWS, SEGMENT_ROWS)
    return start, seg >= 0, table[k * ENTRIES + 2 + 2 * j]


def open_kernel(n_adapter, per_device, here, ids, slots, down_ref, up_ref, o_ref, table, sems):
    width = down_ref.shape[1]
    columns = o_ref.shape[1] - width
    start = pl.multiple_of(here[2] * columns, columns)
    copies = [
        pltpu.make_async_copy(down_ref, o_ref.at[:, pl.ds(0, width)], sems.at[0]),
        pltpu.make_async_copy(
            up_ref.at[:, pl.ds(start, columns)], o_ref.at[:, pl.ds(width, columns)], sems.at[1]
        ),
    ]
    for copy in copies:
        copy.start()
    seg_dev = ids.shape[0] // SEGMENT_ROWS
    used = [slots[ids[s * SEGMENT_ROWS]] for s in range(seg_dev)]
    for k, owner in enumerate(arrival_order(here[0], n_adapter)):
        table[k * ENTRIES] = owner
        found, place = [jnp.int32(-1)] * MOST, [jnp.int32(0)] * MOST
        count = jnp.int32(0)
        for s, slot in enumerate(used):
            within = slot - owner * per_device
            hit = (within >= 0) & (within < per_device)
            for j in range(MOST):
                take = hit & (count == j)
                found[j] = jnp.where(take, s, found[j])
                place[j] = jnp.where(take, within, place[j])
            count = count + hit.astype(jnp.int32)
        for j in range(MOST):
            table[k * ENTRIES + 1 + 2 * j] = found[j]
            table[k * ENTRIES + 2 + 2 * j] = place[j]
    for copy in copies:
        copy.wait()


def open_call(here, ids, slots, down, up, n_adapter, per_device, columns):
    rows, width = down.shape
    return pl.pallas_call(
        functools.partial(open_kernel, n_adapter, per_device),
        in_specs=[SMEM, SMEM, SMEM, HBM, HBM],
        out_specs=[VMEM, SMEM],
        out_shape=[
            jax.ShapeDtypeStruct((rows, width + columns), jnp.bfloat16),
            jax.ShapeDtypeStruct((n_adapter * ENTRIES,), jnp.int32),
        ],
        scratch_shapes=[pltpu.SemaphoreType.DMA((2,))],
        compiler_params=params(8),
        cost_estimate=cost(0, 4 * rows * (width + columns)),
    )(here, ids, slots, down, up)


def diagonal():
    shape = (SEGMENT_ROWS, SEGMENT_ROWS)
    return lax.broadcasted_iota(jnp.int32, shape, 0) == lax.broadcasted_iota(jnp.int32, shape, 1)


WORDS = SEGMENT_ROWS * 3 // 4
QUARTER = SEGMENT_ROWS // 4


def coded_rows(segments):
    return segments * WORDS + 8


def encode(values, o_ref, unit, units):
    largest = jnp.maximum(jnp.max(jnp.abs(values), axis=1, keepdims=True), 2.0**-100)
    power = jnp.floor(jnp.log2(largest))
    whole = (values * jnp.exp2(21.0 - power) + MIDDLE).astype(jnp.int32) - int(MIDDLE)
    q = [whole[i * QUARTER : (i + 1) * QUARTER] for i in range(4)]
    for i in range(3):
        o_ref[unit * WORDS + i * QUARTER : unit * WORDS + (i + 1) * QUARTER, :] = (
            q[i] & 0xFFFFFF
        ) | ((q[3] >> (8 * i)) << 24)
    row = jnp.sum(jnp.where(diagonal(), power, 0.0), axis=0, keepdims=True)
    o_ref[units * WORDS + unit : units * WORDS + unit + 1, :SEGMENT_ROWS] = row.astype(jnp.int32)


def decode(ref, unit, units):
    w = [ref[unit * WORDS + i * QUARTER : unit * WORDS + (i + 1) * QUARTER, :] for i in range(3)]
    q = [(x << 8) >> 8 for x in w]
    q.append(((w[0] >> 24) & 0xFF) | (((w[1] >> 24) & 0xFF) << 8) | ((w[2] >> 24) << 16))
    row = ref[units * WORDS + unit : units * WORDS + unit + 1, :SEGMENT_ROWS].astype(jnp.float32)
    power = jnp.sum(jnp.where(diagonal(), row, 0.0), axis=1, keepdims=True)
    return jnp.concatenate(q, axis=0).astype(jnp.float32) * jnp.exp2(power - 21.0)


def base_kernel(first, sizes, coded, column, x_ref, w_ref, *refs):
    outs, (x, w, sems) = refs[: len(sizes)], refs[len(sizes) :]
    width, columns = w.shape
    rows = sum(sizes) * SEGMENT_ROWS
    start = pl.multiple_of(column[0] * columns, columns)
    depth = width // PIECES
    blocks = [(r, min(BLOCK, rows - r)) for r in range(0, rows, BLOCK)]

    def x_copy(at, size, features, sem):
        return pltpu.make_async_copy(
            x_ref.at[pl.ds(first * SEGMENT_ROWS + at, size), features],
            x.at[pl.ds(at, size), features],
            sem,
        )

    pieces = []
    for p in range(PIECES):
        features = pl.ds(p * depth, depth)
        pieces.append(
            (
                pltpu.make_async_copy(
                    w_ref.at[features, pl.ds(start, columns)], w.at[features, :], sems.at[0, p]
                ),
                x_copy(0, blocks[0][1], features, sems.at[1, p]),
            )
        )
    later = [x_copy(at, size, slice(None), sems.at[2, i]) for i, (at, size) in enumerate(blocks[1:])]
    for copy in [c for pair in pieces for c in pair] + later:
        copy.start()
    owner = [(out, unit) for out, size in enumerate(sizes) for unit in range(size)]
    if coded:
        for out, size in zip(outs, sizes):
            out[size * WORDS :, :] = jnp.zeros((8, columns), jnp.int32)
    for i, (at, size) in enumerate(blocks):
        if i == 0:
            product = None
            for p, pair in enumerate(pieces):
                for copy in pair:
                    copy.wait()
                term = jnp.dot(
                    x[at : at + size, p * depth : (p + 1) * depth],
                    w[p * depth : (p + 1) * depth, :],
                    preferred_element_type=jnp.float32,
                )
                product = term if product is None else product + term
        else:
            later[i - 1].wait()
            product = jnp.dot(x[at : at + size, :], w[...], preferred_element_type=jnp.float32)
        if not coded:
            outs[0][at : at + size, :] = product
            continue
        for r in range(0, size, SEGMENT_ROWS):
            out, unit = owner[(at + r) // SEGMENT_ROWS]
            encode(product[r : r + SEGMENT_ROWS], outs[out], unit, sizes[out])


def base_product(tokens, weight, column, columns, first, sizes, coded):
    width = tokens.shape[1]
    rows = sum(sizes) * SEGMENT_ROWS
    kind = jnp.int32 if coded else jnp.float32
    shapes = [coded_rows(n) if coded else n * SEGMENT_ROWS for n in sizes]
    return pl.pallas_call(
        functools.partial(base_kernel, first, sizes, coded),
        in_specs=[SMEM, HBM, HBM],
        out_specs=[VMEM] * len(sizes),
        out_shape=[jax.ShapeDtypeStruct((n, columns), kind) for n in shapes],
        scratch_shapes=[
            pltpu.VMEM((rows, width), jnp.bfloat16),
            pltpu.VMEM((width, columns), jnp.bfloat16),
            pltpu.SemaphoreType.DMA((3, max(PIECES, rows // BLOCK))),
        ],
        compiler_params=params(24),
        cost_estimate=cost(
            2 * rows * width * columns, 2 * rows * width + 2 * width * columns + 4 * rows * columns
        ),
    )(column.reshape(1), tokens, weight)


def shrink_kernel(ks, stages, rank, table, here, x_ref, *refs):
    buffers, (o_ref, x, d, sems) = refs[:-4], refs[-4:]
    width = x_ref.shape[1]
    owners = buffer_owners(here, stages)
    work = []
    for i, k in enumerate(ks):
        for buffer, whose in zip(buffers, owners):
            down = pltpu.make_async_copy(buffer.at[:, pl.ds(0, width)], d.at[i], sems.at[i, MOST])
            pl.when(whose == table[k * ENTRIES])(down.start)
        for j in range(MOST):
            start, _, within = segment_of(table, k, j)
            load = pltpu.make_async_copy(
                x_ref.at[pl.ds(start, SEGMENT_ROWS), :], x.at[i, j], sems.at[i, j]
            )
            load.start()
            work.append((i, j, within, load, down))
    for i, j, within, load, down in work:
        if j == 0:
            down.wait()
        load.wait()
        factor = d[i, pl.ds(pl.multiple_of(within * rank, rank), rank), :]
        o_ref[i, :, j * rank : (j + 1) * rank] = lax.dot_general(
            x[i, j], factor, (((1,), (1,)), ((), ())), preferred_element_type=jnp.float32
        )


def shrink_product(ks, stages, table, here, tokens, buffers, per_device, rank):
    width = tokens.shape[1]
    n = len(ks)
    return pl.pallas_call(
        functools.partial(shrink_kernel, ks, stages, rank),
        in_specs=[SMEM, SMEM, HBM] + [ANY] * len(buffers),
        out_specs=VMEM,
        out_shape=jax.ShapeDtypeStruct((n, SEGMENT_ROWS, MOST * rank), jnp.float32),
        scratch_shapes=[
            pltpu.VMEM((n, MOST, SEGMENT_ROWS, width), jnp.bfloat16),
            pltpu.VMEM((n, per_device * rank, width), jnp.bfloat16),
            pltpu.SemaphoreType.DMA((n, MOST + 1)),
        ],
        compiler_params=params(16),
        cost_estimate=cost(
            n * MOST * 2 * SEGMENT_ROWS * width * 256,
            n * 2 * (MOST * SEGMENT_ROWS + per_device * rank) * width,
        ),
    )(table, here, tokens, *buffers)


def up_product(shrink, factor):
    high = shrink.astype(jnp.bfloat16)
    left = shrink - high.astype(jnp.float32)
    middle = left.astype(jnp.bfloat16)
    low = (left - middle.astype(jnp.float32)).astype(jnp.bfloat16)
    result = jnp.dot(low, factor, preferred_element_type=jnp.float32)
    result = result + jnp.dot(middle, factor, preferred_element_type=jnp.float32)
    return result + jnp.dot(high, factor, preferred_element_type=jnp.float32)


def fetch_up(buffers, owners, owner, target, sem):
    columns = target.shape[1]
    for buffer, whose in zip(buffers, owners):
        copy = pltpu.make_async_copy(
            buffer.at[:, pl.ds(buffer.shape[1] - columns, columns)], target, sem
        )
        pl.when(whose == owner)(copy.start)
    return copy


def early_kernel(n_adapter, n_tensor, n_calls, rank, table, here, *refs):
    n_coded = len(CHUNKS) * (n_tensor - 1)
    base_ref, coded_refs, refs = refs[0], refs[1 : 1 + n_coded], refs[1 + n_coded :]
    shrinks, refs = refs[: n_calls * n_tensor], refs[n_calls * n_tensor :]
    buffers, (o_ref, rest_ref, up, total, sems) = refs[:-5], refs[-5:]
    owners = buffer_owners(here, range(n_adapter - 1))
    waits = [
        fetch_up(buffers, owners, table[k * ENTRIES], up.at[k], sems.at[k])
        for k in range(n_adapter - 1)
    ]
    shares = []
    for call in range(n_calls):
        share = shrinks[call * n_tensor][...]
        for i in range(1, n_tensor):
            share = share + shrinks[call * n_tensor + i][...]
        shares += [share[i] for i in range(share.shape[0])]
    for chunk, (first, number) in enumerate(CHUNKS):
        for unit in range(number):
            here_rows = pl.ds((first + unit) * SEGMENT_ROWS, SEGMENT_ROWS)
            value = base_ref[here_rows, :]
            for i in range(n_tensor - 1):
                value = value + decode(coded_refs[chunk * (n_tensor - 1) + i], unit, number)
            total[here_rows, :] = value
    for copy in waits:
        copy.wait()
    for k in range(n_adapter):
        for j in range(MOST):
            start, used, within = segment_of(table, k, j)
            value = total[pl.ds(start, SEGMENT_ROWS), :]
            if k == n_adapter - 1:
                rest_ref[j] = value
                continue
            factor = up[k, pl.ds(pl.multiple_of(within * rank, rank), rank), :]
            lora = up_product(shares[k][:, j * rank : (j + 1) * rank], factor)

            @pl.when(used)
            def _(start=start, value=value, lora=lora):
                o_ref[pl.ds(start, SEGMENT_ROWS), :] = (value + adapter_scale * lora).astype(
                    jnp.bfloat16
                )


def early(n_adapter, n_tensor, table, here, base, coded, shrinks, buffers, per_device, rank):
    rows, columns = base.shape
    return pl.pallas_call(
        functools.partial(early_kernel, n_adapter, n_tensor, len(shrinks) // n_tensor, rank),
        in_specs=[SMEM] * 2 + [VMEM] * (1 + len(coded) + len(shrinks)) + [ANY] * len(buffers),
        out_specs=[VMEM, VMEM],
        out_shape=[
            jax.ShapeDtypeStruct((rows, columns), jnp.bfloat16),
            jax.ShapeDtypeStruct((MOST, SEGMENT_ROWS, columns), jnp.float32),
        ],
        scratch_shapes=[
            pltpu.VMEM((n_adapter - 1, per_device * rank, columns), jnp.bfloat16),
            pltpu.VMEM((rows, columns), jnp.float32),
            pltpu.SemaphoreType.DMA((n_adapter - 1,)),
        ],
        compiler_params=params(16),
        cost_estimate=cost(6 * rows * rank * columns, (4 * n_tensor + 2) * rows * columns),
    )(table, here, base, *coded, *shrinks, *buffers)


def late_kernel(k, n_tensor, stages, rank, table, here, *refs):
    rest_ref, shrinks, refs = refs[0], refs[1 : 1 + n_tensor], refs[1 + n_tensor :]
    buffers, (_, o_ref, up, out, sems) = refs[:-5], refs[-5:]
    owners = buffer_owners(here, stages)
    wait = fetch_up(buffers, owners, table[k * ENTRIES], up, sems.at[MOST])
    share = shrinks[0][0]
    for r in shrinks[1:]:
        share = share + r[0]
    wait.wait()
    stores = []
    for j in range(MOST):
        start, used, within = segment_of(table, k, j)
        factor = up[pl.ds(pl.multiple_of(within * rank, rank), rank), :]
        lora = up_product(share[:, j * rank : (j + 1) * rank], factor)
        out[j] = (rest_ref[j] + adapter_scale * lora).astype(jnp.bfloat16)
        store = pltpu.make_async_copy(out.at[j], o_ref.at[pl.ds(start, SEGMENT_ROWS), :], sems.at[j])
        pl.when(used)(store.start)
        stores.append((used, store))
    for used, store in stores:
        pl.when(used)(store.wait)


def late(k, n_tensor, stages, table, here, rest, shrinks, buffers, value, per_device, rank):
    rows, columns = value.shape
    return pl.pallas_call(
        functools.partial(late_kernel, k, n_tensor, stages, rank),
        in_specs=[SMEM] * 2 + [VMEM] * (1 + len(shrinks)) + [ANY] * (len(buffers) + 1),
        out_specs=ANY,
        out_shape=jax.ShapeDtypeStruct((rows, columns), jnp.bfloat16),
        scratch_shapes=[
            pltpu.VMEM((per_device * rank, columns), jnp.bfloat16),
            pltpu.VMEM((MOST, SEGMENT_ROWS, columns), jnp.bfloat16),
            pltpu.SemaphoreType.DMA((MOST + 1,)),
        ],
        input_output_aliases={3 + len(shrinks) + len(buffers): 0},
        compiler_params=params(8),
        cost_estimate=cost(
            6 * MOST * SEGMENT_ROWS * rank * columns, 8 * MOST * SEGMENT_ROWS * columns
        ),
    )(table, here, rest, *shrinks, *buffers, value)


def after(array, *others):
    return lax.optimization_barrier((array, *others))[0]


def on_device(
    tokens, value_weight, adapter_down_weight, adapter_up_weight, row_adapter_index, adapter_slot_of
):
    rows, width = tokens.shape
    per_device, _, rank = adapter_down_weight.shape
    n_adapter = lax.axis_size("adapter")
    n_tensor = lax.axis_size("tensor")
    me_t = lax.axis_index("tensor")
    here = jnp.stack([lax.axis_index("adapter"), lax.axis_index("dp"), me_t])
    columns = value_weight.shape[1] // n_tensor

    def swap_tensor(array, step):
        pairs = [(i, (i + step) % n_tensor) for i in range(n_tensor)]
        return lax.ppermute(array, "tensor", pairs)

    def along_line(array, stage):
        up = [(2 * i, 2 * (i + 1)) for i in range(stage - 1, n_adapter - 1)]
        down = [(2 * i + 1, 2 * (i - 1) + 1) for i in range(1, n_adapter - stage + 1)]
        return lax.ppermute(array, ("adapter", "dp"), up + down)

    def swap_cores(array):
        return lax.ppermute(array, "dp", [(0, 1), (1, 0)])

    down = jnp.swapaxes(adapter_down_weight, 1, 2).reshape(per_device * rank, width)
    up = adapter_up_weight.reshape(per_device * rank, value_weight.shape[1])
    tokens, value_weight, down, up = (
        pltpu.with_memory_space_constraint(a, pltpu.HBM) for a in (tokens, value_weight, down, up)
    )
    message, table = open_call(
        here, row_adapter_index, adapter_slot_of, down, up, n_adapter, per_device, columns
    )

    buffers, shrinks = [[message]], []

    def stage_buffers(stages):
        return [b for stage in stages for b in buffers[stage]]

    def shrink(ks, stages):
        mine = shrink_product(
            ks, stages, table, here, tokens, stage_buffers(stages), per_device, rank
        )
        shrinks.extend([mine] + [swap_tensor(mine, step) for step in range(1, n_tensor)])
        return mine

    def base_for(step, chunks):
        return base_product(
            tokens,
            value_weight,
            (me_t + step) % n_tensor,
            columns,
            chunks[0][0],
            [number for _, number in chunks],
            step > 0,
        )

    held = along_line(message, 1)
    others = range(1, n_tensor)
    parts = [[base_for(step, CHUNKS[:1])[0] for step in others]]
    sent = [[swap_tensor(p, step) for step, p in zip(others, parts[0])]]
    rest_parts = [base_for(step, CHUNKS[1:]) for step in others]
    parts += [[p[i] for p in rest_parts] for i in range(len(CHUNKS) - 1)]
    done = [p for group in parts for p in group] + sent[0]
    for stage in range(1, n_adapter):
        if stage < len(CHUNKS):
            sent.append([swap_tensor(after(p, held), step) for step, p in zip(others, parts[stage])])
        came = after(held, *done)
        done = sent[stage] if stage < len(CHUNKS) else []
        if stage < n_adapter - 1:
            held = along_line(came, stage + 1)
        buffers.append([came, swap_cores(came)])
        if stage == 1:
            base = base_for(0, ((0, rows // SEGMENT_ROWS),))[0]
            done = done + [base, shrink([0, 1], [0, 1])]
            continue
        stages = list(range((stage + 1) // 2, stage + 1))
        done = [shrink([stage], stages)] + (done if stage < n_adapter - 2 else [])

    value, remaining = early(
        n_adapter,
        n_tensor,
        table,
        here,
        base,
        [c for group in sent for c in group],
        shrinks[:-n_tensor],
        stage_buffers(range(n_adapter - 1)),
        per_device,
        rank,
    )
    return late(
        n_adapter - 1,
        n_tensor,
        stages,
        table,
        here,
        remaining,
        shrinks[-n_tensor:],
        stage_buffers(stages),
        value,
        per_device,
        rank,
    )


def solution(mesh):
    return jax.shard_map(
        on_device,
        mesh=mesh,
        in_specs=(
            P(("groups", "adapter", "dp"), "tensor"),
            P("tensor", None),
            P(("groups", "adapter"), "tensor", None),
            P(("groups", "adapter"), None, None),
            P(("groups", "adapter", "dp")),
            P("groups"),
        ),
        out_specs=P(("groups", "adapter", "dp"), "tensor"),
        check_vma=False,
    )
```

```python
import functools

import jax
import jax.numpy as jnp
from jax import lax
from jax.experimental import pallas as pl
from jax.experimental.pallas import tpu as pltpu
from jax.sharding import PartitionSpec as P

SEGMENT_ROWS = 128
adapter_scale = 0.5
MOST = 2
BLOCK = 256
PIECES = 4
CHUNKS = ((6, 2), (0, 3), (3, 3))
ENTRIES = 8
MIDDLE = 1.5 * 2.0**23


def cost(flops, moved):
    return pl.CostEstimate(flops=int(flops), bytes_accessed=int(moved), transcendentals=0)


def params(mib):
    return pltpu.CompilerParams(vmem_limit_bytes=mib * 2**20)


ANY = pl.BlockSpec(memory_space=pl.ANY)
HBM = pl.BlockSpec(memory_space=pltpu.HBM)
SMEM = pl.BlockSpec(memory_space=pltpu.SMEM)
VMEM = pl.BlockSpec(memory_space=pltpu.VMEM)


def arrival_order(me, n_adapter):
    order = [me] + [jnp.int32(-1)] * (n_adapter - 1)
    count = jnp.int32(1)
    for distance in range(1, n_adapter):
        for other in (me - distance, me + distance):
            valid = (other >= 0) & (other < n_adapter)
            order = [jnp.where(valid & (count == k), other, o) for k, o in enumerate(order)]
            count = count + valid.astype(jnp.int32)
    return order


def buffer_owners(here, stages):
    owners = []
    for stage in stages:
        toward = jnp.where(here[1] == 0, -stage, stage)
        owners += [here[0] + toward, here[0] - toward] if stage > 0 else [here[0]]
    return owners


def segment_of(table, k, j):
    seg = table[k * ENTRIES + 1 + 2 * j]
    start = pl.multiple_of(jnp.maximum(seg, 0) * SEGMENT_ROWS, SEGMENT_ROWS)
    return start, seg >= 0, table[k * ENTRIES + 2 + 2 * j]


def message_kernel(here, down_ref, up_ref, o_ref, sems):
    width = down_ref.shape[1]
    columns = o_ref.shape[1] - width
    start = pl.multiple_of(here[2] * columns, columns)
    copies = [
        pltpu.make_async_copy(down_ref, o_ref.at[:, pl.ds(0, width)], sems.at[0]),
        pltpu.make_async_copy(
            up_ref.at[:, pl.ds(start, columns)], o_ref.at[:, pl.ds(width, columns)], sems.at[1]
        ),
    ]
    for copy in copies:
        copy.start()
    for copy in copies:
        copy.wait()


def message_call(here, down, up, columns):
    rows, width = down.shape
    return pl.pallas_call(
        message_kernel,
        in_specs=[SMEM, HBM, HBM],
        out_specs=VMEM,
        out_shape=jax.ShapeDtypeStruct((rows, width + columns), jnp.bfloat16),
        scratch_shapes=[pltpu.SemaphoreType.DMA((2,))],
        compiler_params=params(8),
        cost_estimate=cost(0, 4 * rows * (width + columns)),
    )(here, down, up)


def table_kernel(n_adapter, per_device, here, ids, slots, table):
    seg_dev = ids.shape[0] // SEGMENT_ROWS
    used = [slots[ids[s * SEGMENT_ROWS]] for s in range(seg_dev)]
    for k, owner in enumerate(arrival_order(here[0], n_adapter)):
        table[k * ENTRIES] = owner
        found, place = [jnp.int32(-1)] * MOST, [jnp.int32(0)] * MOST
        count = jnp.int32(0)
        for s, slot in enumerate(used):
            within = slot - owner * per_device
            hit = (within >= 0) & (within < per_device)
            for j in range(MOST):
                take = hit & (count == j)
                found[j] = jnp.where(take, s, found[j])
                place[j] = jnp.where(take, within, place[j])
            count = count + hit.astype(jnp.int32)
        for j in range(MOST):
            table[k * ENTRIES + 1 + 2 * j] = found[j]
            table[k * ENTRIES + 2 + 2 * j] = place[j]


def table_call(here, ids, slots, n_adapter, per_device):
    return pl.pallas_call(
        functools.partial(table_kernel, n_adapter, per_device),
        in_specs=[SMEM, SMEM, SMEM],
        out_specs=SMEM,
        out_shape=jax.ShapeDtypeStruct((n_adapter * ENTRIES,), jnp.int32),
        cost_estimate=cost(0, 4 * ids.shape[0]),
    )(here, ids, slots)


def diagonal():
    shape = (SEGMENT_ROWS, SEGMENT_ROWS)
    return lax.broadcasted_iota(jnp.int32, shape, 0) == lax.broadcasted_iota(jnp.int32, shape, 1)


WORDS = SEGMENT_ROWS * 3 // 4
QUARTER = SEGMENT_ROWS // 4


def coded_rows(segments):
    return segments * WORDS + 8


def encode(values, o_ref, unit, units):
    largest = jnp.maximum(jnp.max(jnp.abs(values), axis=1, keepdims=True), 2.0**-100)
    power = jnp.floor(jnp.log2(largest))
    whole = (values * jnp.exp2(21.0 - power) + MIDDLE).astype(jnp.int32) - int(MIDDLE)
    q = [whole[i * QUARTER : (i + 1) * QUARTER] for i in range(4)]
    for i in range(3):
        o_ref[unit * WORDS + i * QUARTER : unit * WORDS + (i + 1) * QUARTER, :] = (
            q[i] & 0xFFFFFF
        ) | ((q[3] >> (8 * i)) << 24)
    row = jnp.sum(jnp.where(diagonal(), power, 0.0), axis=0, keepdims=True)
    o_ref[units * WORDS + unit : units * WORDS + unit + 1, :SEGMENT_ROWS] = row.astype(jnp.int32)


def decode(ref, unit, units):
    w = [ref[unit * WORDS + i * QUARTER : unit * WORDS + (i + 1) * QUARTER, :] for i in range(3)]
    q = [(x << 8) >> 8 for x in w]
    q.append(((w[0] >> 24) & 0xFF) | (((w[1] >> 24) & 0xFF) << 8) | ((w[2] >> 24) << 16))
    row = ref[units * WORDS + unit : units * WORDS + unit + 1, :SEGMENT_ROWS].astype(jnp.float32)
    power = jnp.sum(jnp.where(diagonal(), row, 0.0), axis=1, keepdims=True)
    return jnp.concatenate(q, axis=0).astype(jnp.float32) * jnp.exp2(power - 21.0)


def load_base(first, segments, column, x_ref, w_ref, x, w, sems):
    width, columns = w.shape
    rows = segments * SEGMENT_ROWS
    start = pl.multiple_of(column * columns, columns)
    depth = width // PIECES
    blocks = [(r, min(BLOCK, rows - r)) for r in range(0, rows, BLOCK)]

    def x_copy(at, size, features, sem):
        return pltpu.make_async_copy(
            x_ref.at[pl.ds(first * SEGMENT_ROWS + at, size), features],
            x.at[pl.ds(at, size), features],
            sem,
        )

    work = []
    for i, (at, size) in enumerate(blocks):
        terms = []
        if i == 0:
            for p in range(PIECES):
                features = pl.ds(p * depth, depth)
                copies = (
                    pltpu.make_async_copy(
                        w_ref.at[features, pl.ds(start, columns)], w.at[features, :], sems.at[0, p]
                    ),
                    x_copy(0, size, features, sems.at[1, p]),
                )
                terms.append((copies, slice(p * depth, (p + 1) * depth)))
        else:
            terms.append(((x_copy(at, size, slice(None), sems.at[2, i]),), slice(None)))
        work.append((at, size, terms))
    for _, _, terms in work:
        for copies, _ in terms:
            for copy in copies:
                copy.start()
    return work


def block_product(x, w, at, size, terms):
    total = None
    for copies, features in terms:
        for copy in copies:
            copy.wait()
        term = jnp.dot(
            x[at : at + size, features], w[features, :], preferred_element_type=jnp.float32
        )
        total = term if total is None else total + term
    return total


def base_scratch(segments, width, columns):
    rows = segments * SEGMENT_ROWS
    return [
        pltpu.VMEM((rows, width), jnp.bfloat16),
        pltpu.VMEM((width, columns), jnp.bfloat16),
        pltpu.SemaphoreType.DMA((3, max(PIECES, rows // BLOCK + 1))),
    ]


def sent_kernel(first, sizes, column, x_ref, w_ref, *refs):
    outs, (x, w, sems) = refs[: len(sizes)], refs[len(sizes) :]
    work = load_base(first, sum(sizes), column[0], x_ref, w_ref, x, w, sems)
    unit_of = [(out, unit) for out, size in enumerate(sizes) for unit in range(size)]
    for out, size in zip(outs, sizes):
        out[size * WORDS :, :] = jnp.zeros((8, w.shape[1]), jnp.int32)
    for at, size, terms in work:
        product = block_product(x, w, at, size, terms)
        for r in range(0, size, SEGMENT_ROWS):
            out, unit = unit_of[(at + r) // SEGMENT_ROWS]
            encode(product[r : r + SEGMENT_ROWS], outs[out], unit, sizes[out])


def sent_call(tokens, weight, column, columns, first, sizes):
    width = tokens.shape[1]
    rows = sum(sizes) * SEGMENT_ROWS
    return pl.pallas_call(
        functools.partial(sent_kernel, first, sizes),
        in_specs=[SMEM, HBM, HBM],
        out_specs=[VMEM] * len(sizes),
        out_shape=[jax.ShapeDtypeStruct((coded_rows(n), columns), jnp.int32) for n in sizes],
        scratch_shapes=base_scratch(sum(sizes), width, columns),
        compiler_params=params(24),
        cost_estimate=cost(
            2 * rows * width * columns, 2 * rows * width + 2 * width * columns + 4 * rows * columns
        ),
    )(column.reshape(1), tokens, weight)


def shrink_into(o_ref, i, table, k, rows_of, buffers, owners, rank):
    for buffer, whose in zip(buffers, owners):

        @pl.when(whose == table[k * ENTRIES])
        def _(buffer=buffer):
            for j in range(MOST):
                _, _, within = segment_of(table, k, j)
                rows = rows_of(j)
                width = rows.shape[1]
                factor = buffer[pl.ds(pl.multiple_of(within * rank, rank), rank), :width]
                o_ref[i, :, j * rank : (j + 1) * rank] = lax.dot_general(
                    rows, factor, (((1,), (1,)), ((), ())), preferred_element_type=jnp.float32
                )


def stages_of(k):
    return range((k + 1) // 2, k + 1)


def own_kernel(n_adapter, rank, table, here, x_ref, w_ref, *refs):
    buffers, (o_ref, s_ref, kept_ref, x, w, sems, kept_sems) = refs[:3], refs[3:]
    work = load_base(0, x.shape[0] // SEGMENT_ROWS, here[2], x_ref, w_ref, x, w, sems)
    keeps = []
    for at, size, terms in work:
        o_ref[at : at + size, :] = block_product(x, w, at, size, terms)
    for k in range(2, n_adapter):
        for j in range(MOST):
            start, _, _ = segment_of(table, k, j)
            keeps.append(
                pltpu.make_async_copy(
                    x.at[pl.ds(start, SEGMENT_ROWS), :], kept_ref.at[k - 2, j], kept_sems.at[k - 2, j]
                )
            )
            keeps[-1].start()
    for k in range(2):

        def rows_of(j, k=k):
            start, _, _ = segment_of(table, k, j)
            return x[pl.ds(start, SEGMENT_ROWS), :]

        here_buffers = buffers[:1] if k == 0 else buffers[1:]
        shrink_into(s_ref, k, table, k, rows_of, here_buffers, buffer_owners(here, stages_of(k)), rank)
    for copy in keeps:
        copy.wait()


def own_call(table, here, tokens, weight, buffers, columns, n_adapter, rank):
    rows, width = tokens.shape
    segments = rows // SEGMENT_ROWS
    return pl.pallas_call(
        functools.partial(own_kernel, n_adapter, rank),
        in_specs=[SMEM, SMEM, HBM, HBM] + [VMEM] * len(buffers),
        out_specs=[VMEM] * 3,
        out_shape=[
            jax.ShapeDtypeStruct((rows, columns), jnp.float32),
            jax.ShapeDtypeStruct((2, SEGMENT_ROWS, MOST * rank), jnp.float32),
            jax.ShapeDtypeStruct((n_adapter - 2, MOST, SEGMENT_ROWS, width), jnp.bfloat16),
        ],
        scratch_shapes=base_scratch(segments, width, columns)
        + [pltpu.SemaphoreType.DMA((n_adapter - 2, MOST))],
        compiler_params=params(32),
        cost_estimate=cost(
            2 * rows * width * columns, 2 * rows * width + 2 * width * columns + 4 * rows * columns
        ),
    )(table, here, tokens, weight, *buffers)


def shrink_kernel(k, rank, table, here, kept_ref, *refs):
    buffers, o_ref = refs[:-1], refs[-1]
    shrink_into(
        o_ref, 0, table, k, lambda j: kept_ref[k - 2, j], buffers, buffer_owners(here, stages_of(k)), rank
    )


def shrink_call(k, table, here, kept, buffers, rank):
    width = kept.shape[3]
    return pl.pallas_call(
        functools.partial(shrink_kernel, k, rank),
        in_specs=[SMEM, SMEM, VMEM] + [VMEM] * len(buffers),
        out_specs=VMEM,
        out_shape=jax.ShapeDtypeStruct((1, SEGMENT_ROWS, MOST * rank), jnp.float32),
        compiler_params=params(16),
        cost_estimate=cost(MOST * 2 * SEGMENT_ROWS * width * 256, 4 * SEGMENT_ROWS * width),
    )(table, here, kept, *buffers)


def fetch_up(up, at, table, k, j, buffers, owners, rank):
    columns = up.shape[2]
    _, _, within = segment_of(table, k, j)
    for buffer, whose in zip(buffers, owners):

        @pl.when(whose == table[k * ENTRIES])
        def _(buffer=buffer):
            first = buffer.shape[1] - columns
            factor = buffer[pl.ds(pl.multiple_of(within * rank, rank), rank), first:]
            up[at, :rank, :] = factor
            up[at, rank:, :] = factor


def up_product(share, j, factor, rank):
    lane = lax.broadcasted_iota(jnp.int32, share.shape, 1)
    other = pltpu.roll(share, rank, 1)
    both = jnp.where((lane < rank) == (j == 0), share, other)
    high = both.astype(jnp.bfloat16).astype(jnp.float32)
    terms = jnp.where(lane < rank, high, both - high).astype(jnp.bfloat16)
    return jnp.dot(terms, factor, preferred_element_type=jnp.float32)


def early_kernel(n_adapter, n_tensor, rank, table, here, *refs):
    n_coded, n_calls = len(CHUNKS) * (n_tensor - 1), n_adapter - 2
    base_ref, coded_refs, refs = refs[0], refs[1 : 1 + n_coded], refs[1 + n_coded :]
    shrinks, refs = refs[: n_calls * n_tensor], refs[n_calls * n_tensor :]
    buffers, (o_ref, rest_ref, up, total) = refs[:-4], refs[-4:]
    for k in range(n_adapter - 1):
        at = 0 if k == 0 else 2 * stages_of(k)[0] - 1
        to = 2 * k + 1
        owners = buffer_owners(here, stages_of(k))
        for j in range(MOST):
            fetch_up(up, k * MOST + j, table, k, j, buffers[at:to], owners, rank)
    shares = []
    for call in range(n_calls):
        share = shrinks[call * n_tensor][...]
        for i in range(1, n_tensor):
            share = share + shrinks[call * n_tensor + i][...]
        shares += [share[i] for i in range(share.shape[0])]
    for chunk, (first, number) in enumerate(CHUNKS):
        for unit in range(number):
            here_rows = pl.ds((first + unit) * SEGMENT_ROWS, SEGMENT_ROWS)
            value = base_ref[here_rows, :]
            for i in range(n_tensor - 1):
                value = value + decode(coded_refs[chunk * (n_tensor - 1) + i], unit, number)
            total[here_rows, :] = value
    for k in range(n_adapter):
        for j in range(MOST):
            start, used, _ = segment_of(table, k, j)
            value = total[pl.ds(start, SEGMENT_ROWS), :]
            if k == n_adapter - 1:
                rest_ref[j] = value
                continue
            lora = up_product(shares[k], j, up[k * MOST + j], rank)

            @pl.when(used)
            def _(start=start, value=value, lora=lora):
                o_ref[pl.ds(start, SEGMENT_ROWS), :] = (value + adapter_scale * lora).astype(
                    jnp.bfloat16
                )


def early(n_adapter, n_tensor, table, here, base, coded, shrinks, buffers, rank):
    rows, columns = base.shape
    return pl.pallas_call(
        functools.partial(early_kernel, n_adapter, n_tensor, rank),
        in_specs=[SMEM] * 2 + [VMEM] * (1 + len(coded) + len(shrinks) + len(buffers)),
        out_specs=[VMEM, VMEM],
        out_shape=[
            jax.ShapeDtypeStruct((rows, columns), jnp.bfloat16),
            jax.ShapeDtypeStruct((MOST, SEGMENT_ROWS, columns), jnp.float32),
        ],
        scratch_shapes=[
            pltpu.VMEM(((n_adapter - 1) * MOST, 2 * rank, columns), jnp.bfloat16),
            pltpu.VMEM((rows, columns), jnp.float32),
        ],
        compiler_params=params(16),
        cost_estimate=cost(6 * rows * rank * columns, (4 * n_tensor + 2) * rows * columns),
    )(table, here, base, *coded, *shrinks, *buffers)


def late_kernel(k, n_tensor, rank, table, here, *refs):
    rest_ref, shrinks, refs = refs[0], refs[1 : 1 + n_tensor], refs[1 + n_tensor :]
    buffers, (_, o_ref, up, out, sems) = refs[:-5], refs[-5:]
    owners = buffer_owners(here, stages_of(k))
    share = shrinks[0][0]
    for r in shrinks[1:]:
        share = share + r[0]
    stores = []
    for j in range(MOST):
        fetch_up(up, j, table, k, j, buffers, owners, rank)
        start, used, _ = segment_of(table, k, j)
        lora = up_product(share, j, up[j], rank)
        out[j] = (rest_ref[j] + adapter_scale * lora).astype(jnp.bfloat16)
        store = pltpu.make_async_copy(out.at[j], o_ref.at[pl.ds(start, SEGMENT_ROWS), :], sems.at[j])
        pl.when(used)(store.start)
        stores.append((used, store))
    for used, store in stores:
        pl.when(used)(store.wait)


def late(k, n_tensor, table, here, rest, shrinks, buffers, value, rank):
    rows, columns = value.shape
    return pl.pallas_call(
        functools.partial(late_kernel, k, n_tensor, rank),
        in_specs=[SMEM] * 2 + [VMEM] * (1 + len(shrinks) + len(buffers)) + [ANY],
        out_specs=ANY,
        out_shape=jax.ShapeDtypeStruct((rows, columns), jnp.bfloat16),
        scratch_shapes=[
            pltpu.VMEM((MOST, 2 * rank, columns), jnp.bfloat16),
            pltpu.VMEM((MOST, SEGMENT_ROWS, columns), jnp.bfloat16),
            pltpu.SemaphoreType.DMA((MOST,)),
        ],
        input_output_aliases={3 + len(shrinks) + len(buffers): 0},
        compiler_params=params(8),
        cost_estimate=cost(
            6 * MOST * SEGMENT_ROWS * rank * columns, 8 * MOST * SEGMENT_ROWS * columns
        ),
    )(table, here, rest, *shrinks, *buffers, value)


def after(array, *others):
    return lax.optimization_barrier((array, *others))[0]


def on_device(
    tokens, value_weight, adapter_down_weight, adapter_up_weight, row_adapter_index, adapter_slot_of
):
    rows, width = tokens.shape
    per_device, _, rank = adapter_down_weight.shape
    n_adapter = lax.axis_size("adapter")
    n_tensor = lax.axis_size("tensor")
    me_t = lax.axis_index("tensor")
    here = jnp.stack([lax.axis_index("adapter"), lax.axis_index("dp"), me_t])
    columns = value_weight.shape[1] // n_tensor

    def swap_tensor(array, step):
        pairs = [(i, (i + step) % n_tensor) for i in range(n_tensor)]
        return lax.ppermute(array, "tensor", pairs)

    def along_line(array, stage):
        up = [(2 * i, 2 * (i + 1)) for i in range(stage - 1, n_adapter - 1)]
        down = [(2 * i + 1, 2 * (i - 1) + 1) for i in range(1, n_adapter - stage + 1)]
        return lax.ppermute(array, ("adapter", "dp"), up + down)

    def swap_cores(array):
        return lax.ppermute(array, "dp", [(0, 1), (1, 0)])

    down = jnp.swapaxes(adapter_down_weight, 1, 2).reshape(per_device * rank, width)
    up = adapter_up_weight.reshape(per_device * rank, value_weight.shape[1])
    tokens, value_weight, down, up = (
        pltpu.with_memory_space_constraint(a, pltpu.HBM) for a in (tokens, value_weight, down, up)
    )
    message = message_call(here, down, up, columns)
    table = table_call(here, row_adapter_index, adapter_slot_of, n_adapter, per_device)

    buffers, shrinks = [[message]], []

    def buffers_of(stages):
        return [b for stage in stages for b in buffers[stage]]

    def add_shrink(mine):
        shrinks.extend([mine] + [swap_tensor(mine, step) for step in range(1, n_tensor)])

    held = along_line(message, 1)
    others = range(1, n_tensor)

    def sent_for(step, chunks):
        sizes = [number for _, number in chunks]
        target = (me_t + step) % n_tensor
        return sent_call(tokens, value_weight, target, columns, chunks[0][0], sizes)

    parts = [[sent_for(step, CHUNKS[:1])[0] for step in others]]
    sent = [[swap_tensor(p, step) for step, p in zip(others, parts[0])]]
    rest_parts = [sent_for(step, CHUNKS[1:]) for step in others]
    parts += [[p[i] for p in rest_parts] for i in range(len(CHUNKS) - 1)]
    done = [table] + [p for group in parts for p in group] + sent[0]
    for stage in range(1, n_adapter):
        if stage < len(CHUNKS):
            sent.append([swap_tensor(after(p, held), step) for step, p in zip(others, parts[stage])])
        came = after(held, *done)
        done = sent[stage] if stage < len(CHUNKS) else []
        if stage < n_adapter - 1:
            held = along_line(came, stage + 1)
        buffers.append([came, swap_cores(came)])
        if stage == 1:
            base, mine, kept = own_call(
                table, here, tokens, value_weight, buffers_of(range(2)), columns, n_adapter, rank
            )
        else:
            mine = shrink_call(stage, table, here, kept, buffers_of(stages_of(stage)), rank)
        add_shrink(mine)
        done = done + [mine]

    value, remaining = early(
        n_adapter,
        n_tensor,
        table,
        here,
        base,
        [c for group in sent for c in group],
        shrinks[:-n_tensor],
        buffers_of(range(n_adapter - 1)),
        rank,
    )
    last = n_adapter - 1
    return late(
        last,
        n_tensor,
        table,
        here,
        remaining,
        shrinks[-n_tensor:],
        buffers_of(stages_of(last)),
        value,
        rank,
    )


def solution(mesh):
    return jax.shard_map(
        on_device,
        mesh=mesh,
        in_specs=(
            P(("groups", "adapter", "dp"), "tensor"),
            P("tensor", None),
            P(("groups", "adapter"), "tensor", None),
            P(("groups", "adapter"), None, None),
            P(("groups", "adapter", "dp")),
            P("groups"),
        ),
        out_specs=P(("groups", "adapter", "dp"), "tensor"),
        check_vma=False,
    )
```

```python
import functools

import jax
import jax.numpy as jnp
from jax import lax
from jax.experimental import pallas as pl
from jax.experimental.pallas import tpu as pltpu
from jax.sharding import PartitionSpec as P

SEGMENT_ROWS = 128
adapter_scale = 0.5
MOST = 2
BLOCK = 256
PIECES = 4
CHUNKS = ((6, 2), (0, 4), (4, 2))
ENTRIES = 8
MIDDLE = 1.5 * 2.0**23


def cost(flops, moved):
    return pl.CostEstimate(flops=int(flops), bytes_accessed=int(moved), transcendentals=0)


def params(mib):
    return pltpu.CompilerParams(vmem_limit_bytes=mib * 2**20)


ANY = pl.BlockSpec(memory_space=pl.ANY)
HBM = pl.BlockSpec(memory_space=pltpu.HBM)
SMEM = pl.BlockSpec(memory_space=pltpu.SMEM)
VMEM = pl.BlockSpec(memory_space=pltpu.VMEM)


def arrival_order(me, n_adapter):
    order = [me] + [jnp.int32(-1)] * (n_adapter - 1)
    count = jnp.int32(1)
    for distance in range(1, n_adapter):
        for other in (me - distance, me + distance):
            valid = (other >= 0) & (other < n_adapter)
            order = [jnp.where(valid & (count == k), other, o) for k, o in enumerate(order)]
            count = count + valid.astype(jnp.int32)
    return order


def buffer_owners(here, stages):
    owners = []
    for stage in stages:
        toward = jnp.where(here[1] == 0, -stage, stage)
        owners += [here[0] + toward, here[0] - toward] if stage > 0 else [here[0]]
    return owners


def segment_of(table, k, j):
    seg = table[k * ENTRIES + 1 + 2 * j]
    start = pl.multiple_of(jnp.maximum(seg, 0) * SEGMENT_ROWS, SEGMENT_ROWS)
    return start, seg >= 0, table[k * ENTRIES + 2 + 2 * j]


def message_kernel(here, down_ref, up_ref, o_ref, sems):
    width = down_ref.shape[1]
    columns = o_ref.shape[1] - width
    start = pl.multiple_of(here[2] * columns, columns)
    copies = [
        pltpu.make_async_copy(down_ref, o_ref.at[:, pl.ds(0, width)], sems.at[0]),
        pltpu.make_async_copy(
            up_ref.at[:, pl.ds(start, columns)], o_ref.at[:, pl.ds(width, columns)], sems.at[1]
        ),
    ]
    for copy in copies:
        copy.start()
    for copy in copies:
        copy.wait()


def message_call(here, down, up, columns):
    rows, width = down.shape
    return pl.pallas_call(
        message_kernel,
        in_specs=[SMEM, HBM, HBM],
        out_specs=VMEM,
        out_shape=jax.ShapeDtypeStruct((rows, width + columns), jnp.bfloat16),
        scratch_shapes=[pltpu.SemaphoreType.DMA((2,))],
        compiler_params=params(8),
        cost_estimate=cost(0, 4 * rows * (width + columns)),
    )(here, down, up)


def table_kernel(n_adapter, per_device, here, ids, slots, table):
    seg_dev = ids.shape[0] // SEGMENT_ROWS
    used = [slots[ids[s * SEGMENT_ROWS]] for s in range(seg_dev)]
    for k, owner in enumerate(arrival_order(here[0], n_adapter)):
        table[k * ENTRIES] = owner
        found, place = [jnp.int32(-1)] * MOST, [jnp.int32(0)] * MOST
        count = jnp.int32(0)
        for s, slot in enumerate(used):
            within = slot - owner * per_device
            hit = (within >= 0) & (within < per_device)
            for j in range(MOST):
                take = hit & (count == j)
                found[j] = jnp.where(take, s, found[j])
                place[j] = jnp.where(take, within, place[j])
            count = count + hit.astype(jnp.int32)
        for j in range(MOST):
            table[k * ENTRIES + 1 + 2 * j] = found[j]
            table[k * ENTRIES + 2 + 2 * j] = place[j]


def table_call(here, ids, slots, n_adapter, per_device):
    return pl.pallas_call(
        functools.partial(table_kernel, n_adapter, per_device),
        in_specs=[SMEM, SMEM, SMEM],
        out_specs=SMEM,
        out_shape=jax.ShapeDtypeStruct((n_adapter * ENTRIES,), jnp.int32),
        cost_estimate=cost(0, 4 * ids.shape[0]),
    )(here, ids, slots)


def diagonal():
    shape = (SEGMENT_ROWS, SEGMENT_ROWS)
    return lax.broadcasted_iota(jnp.int32, shape, 0) == lax.broadcasted_iota(jnp.int32, shape, 1)


GROUP = SEGMENT_ROWS // 8
WORDS = 5 * GROUP


def coded_rows(segments):
    return segments * WORDS + 8


def encode(values, o_ref, unit, units):
    largest = jnp.maximum(jnp.max(jnp.abs(values), axis=1, keepdims=True), 2.0**-100)
    power = jnp.floor(jnp.log2(largest))
    whole = (values * jnp.exp2(18.0 - power) + MIDDLE).astype(jnp.int32) - int(MIDDLE)
    whole = jnp.minimum(whole, 2**19 - 1)
    v = [whole[i * GROUP : (i + 1) * GROUP] for i in range(8)]
    over = [
        v[5] & 0xFFF,
        ((v[5] >> 12) & 0xFF) | ((v[6] & 0xF) << 8),
        (v[6] >> 4) & 0xFFF,
        ((v[6] >> 16) & 0xF) | ((v[7] & 0xFF) << 4),
        v[7] >> 8,
    ]
    for i in range(5):
        o_ref[unit * WORDS + i * GROUP : unit * WORDS + (i + 1) * GROUP, :] = (v[i] & 0xFFFFF) | (
            over[i] << 20
        )
    row = jnp.sum(jnp.where(diagonal(), power, 0.0), axis=0, keepdims=True)
    o_ref[units * WORDS + unit : units * WORDS + unit + 1, :SEGMENT_ROWS] = row.astype(jnp.int32)


def decode(ref, unit, units):
    w = [ref[unit * WORDS + i * GROUP : unit * WORDS + (i + 1) * GROUP, :] for i in range(5)]
    v = [(x << 12) >> 12 for x in w]
    v.append(((w[0] >> 20) & 0xFFF) | (((w[1] << 4) >> 24) << 12))
    v.append(((w[1] >> 28) & 0xF) | (((w[2] >> 20) & 0xFFF) << 4) | (((w[3] << 8) >> 28) << 16))
    v.append(((w[3] >> 24) & 0xFF) | ((w[4] >> 20) << 8))
    row = ref[units * WORDS + unit : units * WORDS + unit + 1, :SEGMENT_ROWS].astype(jnp.float32)
    power = jnp.sum(jnp.where(diagonal(), row, 0.0), axis=1, keepdims=True)
    return jnp.concatenate(v, axis=0).astype(jnp.float32) * jnp.exp2(power - 18.0)


def load_base(first, segments, column, x_ref, w_ref, x, w, sems):
    width, columns = w.shape
    rows = segments * SEGMENT_ROWS
    start = pl.multiple_of(column * columns, columns)
    depth = width // PIECES
    blocks = [(r, min(BLOCK, rows - r)) for r in range(0, rows, BLOCK)]

    def x_copy(at, size, features, sem):
        return pltpu.make_async_copy(
            x_ref.at[pl.ds(first * SEGMENT_ROWS + at, size), features],
            x.at[pl.ds(at, size), features],
            sem,
        )

    work = []
    for i, (at, size) in enumerate(blocks):
        terms = []
        if i == 0:
            for p in range(PIECES):
                features = pl.ds(p * depth, depth)
                copies = (
                    pltpu.make_async_copy(
                        w_ref.at[features, pl.ds(start, columns)], w.at[features, :], sems.at[0, p]
                    ),
                    x_copy(0, size, features, sems.at[1, p]),
                )
                terms.append((copies, slice(p * depth, (p + 1) * depth)))
        else:
            terms.append(((x_copy(at, size, slice(None), sems.at[2, i]),), slice(None)))
        work.append((at, size, terms))
    for _, _, terms in work:
        for copies, _ in terms:
            for copy in copies:
                copy.start()
    return work


def block_product(x, w, at, size, terms):
    total = None
    for copies, features in terms:
        for copy in copies:
            copy.wait()
        term = jnp.dot(
            x[at : at + size, features], w[features, :], preferred_element_type=jnp.float32
        )
        total = term if total is None else total + term
    return total


def base_scratch(segments, width, columns):
    rows = segments * SEGMENT_ROWS
    return [
        pltpu.VMEM((rows, width), jnp.bfloat16),
        pltpu.VMEM((width, columns), jnp.bfloat16),
        pltpu.SemaphoreType.DMA((3, max(PIECES, rows // BLOCK + 1))),
    ]


def sent_kernel(first, sizes, column, x_ref, w_ref, *refs):
    outs, (x, w, sems) = refs[: len(sizes)], refs[len(sizes) :]
    work = load_base(first, sum(sizes), column[0], x_ref, w_ref, x, w, sems)
    unit_of = [(out, unit) for out, size in enumerate(sizes) for unit in range(size)]
    for out, size in zip(outs, sizes):
        out[size * WORDS :, :] = jnp.zeros((8, w.shape[1]), jnp.int32)
    for at, size, terms in work:
        product = block_product(x, w, at, size, terms)
        for r in range(0, size, SEGMENT_ROWS):
            out, unit = unit_of[(at + r) // SEGMENT_ROWS]
            encode(product[r : r + SEGMENT_ROWS], outs[out], unit, sizes[out])


def sent_call(tokens, weight, column, columns, first, sizes):
    width = tokens.shape[1]
    rows = sum(sizes) * SEGMENT_ROWS
    return pl.pallas_call(
        functools.partial(sent_kernel, first, sizes),
        in_specs=[SMEM, HBM, HBM],
        out_specs=[VMEM] * len(sizes),
        out_shape=[jax.ShapeDtypeStruct((coded_rows(n), columns), jnp.int32) for n in sizes],
        scratch_shapes=base_scratch(sum(sizes), width, columns),
        compiler_params=params(24),
        cost_estimate=cost(
            2 * rows * width * columns, 2 * rows * width + 2 * width * columns + 4 * rows * columns
        ),
    )(column.reshape(1), tokens, weight)


def shrink_into(o_ref, i, table, k, rows_of, buffers, owners, rank):
    for buffer, whose in zip(buffers, owners):

        @pl.when(whose == table[k * ENTRIES])
        def _(buffer=buffer):
            for j in range(MOST):
                _, _, within = segment_of(table, k, j)
                rows = rows_of(j)
                width = rows.shape[1]
                factor = buffer[pl.ds(pl.multiple_of(within * rank, rank), rank), :width]
                o_ref[i, :, j * rank : (j + 1) * rank] = lax.dot_general(
                    rows, factor, (((1,), (1,)), ((), ())), preferred_element_type=jnp.float32
                )


def stages_of(k):
    return range((k + 1) // 2, k + 1)


def own_kernel(n_adapter, rank, table, here, x_ref, w_ref, message, *refs):
    o_ref, s_ref, kept_ref, x, w, sems, kept_sems = refs
    work = load_base(0, x.shape[0] // SEGMENT_ROWS, here[2], x_ref, w_ref, x, w, sems)
    keeps = []
    for at, size, terms in work:
        o_ref[at : at + size, :] = block_product(x, w, at, size, terms)
    for k in range(1, n_adapter):
        for j in range(MOST):
            start, _, _ = segment_of(table, k, j)
            keeps.append(
                pltpu.make_async_copy(
                    x.at[pl.ds(start, SEGMENT_ROWS), :], kept_ref.at[k - 1, j], kept_sems.at[k - 1, j]
                )
            )
            keeps[-1].start()

    def rows_of(j):
        start, _, _ = segment_of(table, 0, j)
        return x[pl.ds(start, SEGMENT_ROWS), :]

    shrink_into(s_ref, 0, table, 0, rows_of, [message], [here[0]], rank)
    for copy in keeps:
        copy.wait()


def own_call(table, here, tokens, weight, message, columns, n_adapter, rank):
    rows, width = tokens.shape
    segments = rows // SEGMENT_ROWS
    return pl.pallas_call(
        functools.partial(own_kernel, n_adapter, rank),
        in_specs=[SMEM, SMEM, HBM, HBM, VMEM],
        out_specs=[VMEM] * 3,
        out_shape=[
            jax.ShapeDtypeStruct((rows, columns), jnp.float32),
            jax.ShapeDtypeStruct((1, SEGMENT_ROWS, MOST * rank), jnp.float32),
            jax.ShapeDtypeStruct((n_adapter - 1, MOST, SEGMENT_ROWS, width), jnp.bfloat16),
        ],
        scratch_shapes=base_scratch(segments, width, columns)
        + [pltpu.SemaphoreType.DMA((n_adapter - 1, MOST))],
        compiler_params=params(32),
        cost_estimate=cost(
            2 * rows * width * columns, 2 * rows * width + 2 * width * columns + 4 * rows * columns
        ),
    )(table, here, tokens, weight, message)


def shrink_kernel(k, rank, n_before, table, here, kept_ref, *refs):
    buffers, o_ref = refs[n_before:-1], refs[-1]
    for r in refs[:n_before]:
        o_ref[:1] = r[...]
    rows_of = lambda j: kept_ref[k - 1, j]
    owners = buffer_owners(here, stages_of(k))
    shrink_into(o_ref, n_before, table, k, rows_of, buffers, owners, rank)


def shrink_call(k, table, here, kept, before, buffers, rank):
    width = kept.shape[3]
    n = 1 + len(before)
    return pl.pallas_call(
        functools.partial(shrink_kernel, k, rank, len(before)),
        in_specs=[SMEM, SMEM, VMEM] + [VMEM] * (n - 1 + len(buffers)),
        out_specs=VMEM,
        out_shape=jax.ShapeDtypeStruct((n, SEGMENT_ROWS, MOST * rank), jnp.float32),
        compiler_params=params(16),
        cost_estimate=cost(MOST * 2 * SEGMENT_ROWS * width * 256, 4 * SEGMENT_ROWS * width),
    )(table, here, kept, *before, *buffers)


def fetch_up(up, at, table, k, j, buffers, owners, rank):
    columns = up.shape[2]
    _, _, within = segment_of(table, k, j)
    for buffer, whose in zip(buffers, owners):

        @pl.when(whose == table[k * ENTRIES])
        def _(buffer=buffer):
            first = buffer.shape[1] - columns
            factor = buffer[pl.ds(pl.multiple_of(within * rank, rank), rank), first:]
            up[at, :rank, :] = factor
            up[at, rank:, :] = factor


def up_product(share, j, factor, rank):
    lane = lax.broadcasted_iota(jnp.int32, share.shape, 1)
    other = pltpu.roll(share, rank, 1)
    both = jnp.where((lane < rank) == (j == 0), share, other)
    high = both.astype(jnp.bfloat16).astype(jnp.float32)
    terms = jnp.where(lane < rank, high, both - high).astype(jnp.bfloat16)
    return jnp.dot(terms, factor, preferred_element_type=jnp.float32)


def early_kernel(n_adapter, n_tensor, rank, table, here, *refs):
    n_coded, n_buffers = len(CHUNKS) * (n_tensor - 1), 2 * n_adapter - 3
    base_ref, coded_refs, refs = refs[0], refs[1 : 1 + n_coded], refs[1 + n_coded :]
    shrinks, refs = refs[: -4 - n_buffers], refs[-4 - n_buffers :]
    buffers, (o_ref, rest_ref, up, total) = refs[:-4], refs[-4:]
    for k in range(n_adapter - 1):
        at = 0 if k == 0 else 2 * stages_of(k)[0] - 1
        to = 2 * k + 1
        owners = buffer_owners(here, stages_of(k))
        for j in range(MOST):
            fetch_up(up, k * MOST + j, table, k, j, buffers[at:to], owners, rank)
    shares = []
    for call in range(len(shrinks) // n_tensor):
        share = shrinks[call * n_tensor][...]
        for i in range(1, n_tensor):
            share = share + shrinks[call * n_tensor + i][...]
        shares += [share[i] for i in range(share.shape[0])]
    for chunk, (first, number) in enumerate(CHUNKS):
        for unit in range(number):
            here_rows = pl.ds((first + unit) * SEGMENT_ROWS, SEGMENT_ROWS)
            value = base_ref[here_rows, :]
            for i in range(n_tensor - 1):
                value = value + decode(coded_refs[chunk * (n_tensor - 1) + i], unit, number)
            total[here_rows, :] = value
    for k in range(n_adapter):
        for j in range(MOST):
            start, used, _ = segment_of(table, k, j)
            value = total[pl.ds(start, SEGMENT_ROWS), :]
            if k == n_adapter - 1:
                rest_ref[j] = value
                continue
            lora = up_product(shares[k], j, up[k * MOST + j], rank)

            @pl.when(used)
            def _(start=start, value=value, lora=lora):
                o_ref[pl.ds(start, SEGMENT_ROWS), :] = (value + adapter_scale * lora).astype(
                    jnp.bfloat16
                )


def early(n_adapter, n_tensor, table, here, base, coded, shrinks, buffers, rank):
    rows, columns = base.shape
    return pl.pallas_call(
        functools.partial(early_kernel, n_adapter, n_tensor, rank),
        in_specs=[SMEM] * 2 + [VMEM] * (1 + len(coded) + len(shrinks) + len(buffers)),
        out_specs=[VMEM, VMEM],
        out_shape=[
            jax.ShapeDtypeStruct((rows, columns), jnp.bfloat16),
            jax.ShapeDtypeStruct((MOST, SEGMENT_ROWS, columns), jnp.float32),
        ],
        scratch_shapes=[
            pltpu.VMEM(((n_adapter - 1) * MOST, 2 * rank, columns), jnp.bfloat16),
            pltpu.VMEM((rows, columns), jnp.float32),
        ],
        compiler_params=params(16),
        cost_estimate=cost(6 * rows * rank * columns, (4 * n_tensor + 2) * rows * columns),
    )(table, here, base, *coded, *shrinks, *buffers)


def late_kernel(k, n_tensor, rank, table, here, *refs):
    rest_ref, shrinks, refs = refs[0], refs[1 : 1 + n_tensor], refs[1 + n_tensor :]
    buffers, (_, o_ref, up, out, sems) = refs[:-5], refs[-5:]
    owners = buffer_owners(here, stages_of(k))
    share = shrinks[0][0]
    for r in shrinks[1:]:
        share = share + r[0]
    stores = []
    for j in range(MOST):
        fetch_up(up, j, table, k, j, buffers, owners, rank)
        start, used, _ = segment_of(table, k, j)
        lora = up_product(share, j, up[j], rank)
        out[j] = (rest_ref[j] + adapter_scale * lora).astype(jnp.bfloat16)
        store = pltpu.make_async_copy(out.at[j], o_ref.at[pl.ds(start, SEGMENT_ROWS), :], sems.at[j])
        pl.when(used)(store.start)
        stores.append((used, store))
    for used, store in stores:
        pl.when(used)(store.wait)


def late(k, n_tensor, table, here, rest, shrinks, buffers, value, rank):
    rows, columns = value.shape
    return pl.pallas_call(
        functools.partial(late_kernel, k, n_tensor, rank),
        in_specs=[SMEM] * 2 + [VMEM] * (1 + len(shrinks) + len(buffers)) + [ANY],
        out_specs=ANY,
        out_shape=jax.ShapeDtypeStruct((rows, columns), jnp.bfloat16),
        scratch_shapes=[
            pltpu.VMEM((MOST, 2 * rank, columns), jnp.bfloat16),
            pltpu.VMEM((MOST, SEGMENT_ROWS, columns), jnp.bfloat16),
            pltpu.SemaphoreType.DMA((MOST,)),
        ],
        input_output_aliases={3 + len(shrinks) + len(buffers): 0},
        compiler_params=params(8),
        cost_estimate=cost(
            6 * MOST * SEGMENT_ROWS * rank * columns, 8 * MOST * SEGMENT_ROWS * columns
        ),
    )(table, here, rest, *shrinks, *buffers, value)


def after(array, *others):
    return lax.optimization_barrier((array, *others))[0]


def on_device(
    tokens, value_weight, adapter_down_weight, adapter_up_weight, row_adapter_index, adapter_slot_of
):
    rows, width = tokens.shape
    per_device, _, rank = adapter_down_weight.shape
    n_adapter = lax.axis_size("adapter")
    n_tensor = lax.axis_size("tensor")
    me_t = lax.axis_index("tensor")
    here = jnp.stack([lax.axis_index("adapter"), lax.axis_index("dp"), me_t])
    columns = value_weight.shape[1] // n_tensor

    def swap_tensor(array, step):
        pairs = [(i, (i + step) % n_tensor) for i in range(n_tensor)]
        return lax.ppermute(array, "tensor", pairs)

    def along_line(array, stage):
        up = [(2 * i, 2 * (i + 1)) for i in range(stage - 1, n_adapter - 1)]
        down = [(2 * i + 1, 2 * (i - 1) + 1) for i in range(1, n_adapter - stage + 1)]
        return lax.ppermute(array, ("adapter", "dp"), up + down)

    def swap_cores(array):
        return lax.ppermute(array, "dp", [(0, 1), (1, 0)])

    down = jnp.swapaxes(adapter_down_weight, 1, 2).reshape(per_device * rank, width)
    up = adapter_up_weight.reshape(per_device * rank, value_weight.shape[1])
    tokens, value_weight, down, up = (
        pltpu.with_memory_space_constraint(a, pltpu.HBM) for a in (tokens, value_weight, down, up)
    )
    message = message_call(here, down, up, columns)
    table = table_call(here, row_adapter_index, adapter_slot_of, n_adapter, per_device)

    buffers, shrinks = [[message]], []

    def buffers_of(stages):
        return [b for stage in stages for b in buffers[stage]]

    def add_shrink(mine):
        shrinks.extend([mine] + [swap_tensor(mine, step) for step in range(1, n_tensor)])

    held = along_line(message, 1)
    others = range(1, n_tensor)

    def sent_for(step, chunks):
        sizes = [number for _, number in chunks]
        target = (me_t + step) % n_tensor
        return sent_call(tokens, value_weight, target, columns, chunks[0][0], sizes)

    parts = [[sent_for(step, CHUNKS[:1])[0] for step in others]]
    rest_parts = [sent_for(step, CHUNKS[1:]) for step in others]
    parts += [[p[i] for p in rest_parts] for i in range(len(CHUNKS) - 1)]
    sent = [[swap_tensor(p, step) for step, p in zip(others, parts[0])]]
    last = n_adapter - 1
    done = [table] + [p for group in parts for p in group] + sent[0]
    before = None
    for stage in range(1, last):
        came = after(held, *done)
        held = along_line(came, stage + 1)
        if stage < len(CHUNKS):
            sent.append([swap_tensor(after(p, came), step) for step, p in zip(others, parts[stage])])
        if stage == 1:
            base, before, kept = own_call(
                after(table, came), here, tokens, value_weight, message, columns, n_adapter, rank
            )
            add_shrink(before)
            done = sent[1] + [before]
        else:
            before = shrink_call(
                stage - 1, table, here, after(kept, came), [], buffers_of(stages_of(stage - 1)), rank
            )
            if stage < last - 1:
                add_shrink(before)
            done = []
        buffers.append([came, swap_cores(came)])
    merged = shrink_call(
        last - 1, table, here, kept, [before], buffers_of(stages_of(last - 1)), rank
    )
    add_shrink(merged)
    value, remaining = early(
        n_adapter,
        n_tensor,
        table,
        here,
        base,
        [c for group in sent for c in group],
        shrinks,
        buffers_of(range(last)),
        rank,
    )
    came = after(held, value)
    buffers.append([came, swap_cores(came)])
    add_shrink(shrink_call(last, table, here, kept, [], buffers_of(stages_of(last)), rank))
    return late(
        last,
        n_tensor,
        table,
        here,
        remaining,
        shrinks[-n_tensor:],
        buffers_of(stages_of(last)),
        value,
        rank,
    )


def solution(mesh):
    return jax.shard_map(
        on_device,
        mesh=mesh,
        in_specs=(
            P(("groups", "adapter", "dp"), "tensor"),
            P("tensor", None),
            P(("groups", "adapter"), "tensor", None),
            P(("groups", "adapter"), None, None),
            P(("groups", "adapter", "dp")),
            P("groups"),
        ),
        out_specs=P(("groups", "adapter", "dp"), "tensor"),
        check_vma=False,
    )
```

```python
import functools

import jax
import jax.numpy as jnp
from jax import lax
from jax.experimental import pallas as pl
from jax.experimental.pallas import tpu as pltpu
from jax.sharding import PartitionSpec as P

SEGMENT_ROWS = 128
adapter_scale = 0.5
MOST = 2
BLOCK = 256
PIECES = 4
CHUNKS = ((6, 2), (0, 4), (4, 2))
ENTRIES = 8
MIDDLE = 1.5 * 2.0**23


def cost(flops, moved):
    return pl.CostEstimate(flops=int(flops), bytes_accessed=int(moved), transcendentals=0)


def params(mib):
    return pltpu.CompilerParams(vmem_limit_bytes=mib * 2**20)


ANY = pl.BlockSpec(memory_space=pl.ANY)
HBM = pl.BlockSpec(memory_space=pltpu.HBM)
SMEM = pl.BlockSpec(memory_space=pltpu.SMEM)
VMEM = pl.BlockSpec(memory_space=pltpu.VMEM)


def arrival_order(me, n_adapter):
    order = [me] + [jnp.int32(-1)] * (n_adapter - 1)
    count = jnp.int32(1)
    for distance in range(1, n_adapter):
        for other in (me - distance, me + distance):
            valid = (other >= 0) & (other < n_adapter)
            order = [jnp.where(valid & (count == k), other, o) for k, o in enumerate(order)]
            count = count + valid.astype(jnp.int32)
    return order


def buffer_owners(here, stages):
    owners = []
    for stage in stages:
        toward = jnp.where(here[1] == 0, -stage, stage)
        owners += [here[0] + toward, here[0] - toward] if stage > 0 else [here[0]]
    return owners


def segment_of(table, k, j):
    seg = table[k * ENTRIES + 1 + 2 * j]
    start = pl.multiple_of(jnp.maximum(seg, 0) * SEGMENT_ROWS, SEGMENT_ROWS)
    return start, seg >= 0, table[k * ENTRIES + 2 + 2 * j]


def message_kernel(here, down_ref, up_ref, o_ref, sems):
    width = down_ref.shape[1]
    columns = o_ref.shape[1] - width
    start = pl.multiple_of(here[2] * columns, columns)
    rows = down_ref.shape[0] // PIECES
    copies = [
        pltpu.make_async_copy(
            down_ref.at[pl.ds(p * rows, rows), :],
            o_ref.at[pl.ds(p * rows, rows), pl.ds(0, width)],
            sems.at[p],
        )
        for p in range(PIECES)
    ]
    copies.append(
        pltpu.make_async_copy(
            up_ref.at[:, pl.ds(start, columns)], o_ref.at[:, pl.ds(width, columns)], sems.at[PIECES]
        )
    )
    for copy in copies:
        copy.start()
    for copy in copies:
        copy.wait()


def message_call(here, down, up, columns):
    rows, width = down.shape
    return pl.pallas_call(
        message_kernel,
        in_specs=[SMEM, HBM, HBM],
        out_specs=VMEM,
        out_shape=jax.ShapeDtypeStruct((rows, width + columns), jnp.bfloat16),
        scratch_shapes=[pltpu.SemaphoreType.DMA((PIECES + 1,))],
        compiler_params=params(8),
        cost_estimate=cost(0, 4 * rows * (width + columns)),
    )(here, down, up)


def table_kernel(n_adapter, per_device, here, ids, slots, table):
    seg_dev = ids.shape[0] // SEGMENT_ROWS
    used = [slots[ids[s * SEGMENT_ROWS]] for s in range(seg_dev)]
    for k, owner in enumerate(arrival_order(here[0], n_adapter)):
        table[k * ENTRIES] = owner
        found, place = [jnp.int32(-1)] * MOST, [jnp.int32(0)] * MOST
        count = jnp.int32(0)
        for s, slot in enumerate(used):
            within = slot - owner * per_device
            hit = (within >= 0) & (within < per_device)
            for j in range(MOST):
                take = hit & (count == j)
                found[j] = jnp.where(take, s, found[j])
                place[j] = jnp.where(take, within, place[j])
            count = count + hit.astype(jnp.int32)
        for j in range(MOST):
            table[k * ENTRIES + 1 + 2 * j] = found[j]
            table[k * ENTRIES + 2 + 2 * j] = place[j]


def table_call(here, ids, slots, n_adapter, per_device):
    return pl.pallas_call(
        functools.partial(table_kernel, n_adapter, per_device),
        in_specs=[SMEM, SMEM, SMEM],
        out_specs=SMEM,
        out_shape=jax.ShapeDtypeStruct((n_adapter * ENTRIES,), jnp.int32),
        cost_estimate=cost(0, 4 * ids.shape[0]),
    )(here, ids, slots)


def diagonal():
    shape = (SEGMENT_ROWS, SEGMENT_ROWS)
    return lax.broadcasted_iota(jnp.int32, shape, 0) == lax.broadcasted_iota(jnp.int32, shape, 1)


GROUP = SEGMENT_ROWS // 8
WORDS = 5 * GROUP


def coded_rows(segments):
    return segments * WORDS + 8


def encode(values, o_ref, unit, units):
    largest = jnp.maximum(jnp.max(jnp.abs(values), axis=1, keepdims=True), 2.0**-100)
    power = jnp.floor(jnp.log2(largest))
    whole = (values * jnp.exp2(18.0 - power) + MIDDLE).astype(jnp.int32) - int(MIDDLE)
    whole = jnp.minimum(whole, 2**19 - 1)
    v = [whole[i * GROUP : (i + 1) * GROUP] for i in range(8)]
    over = [
        v[5] & 0xFFF,
        ((v[5] >> 12) & 0xFF) | ((v[6] & 0xF) << 8),
        (v[6] >> 4) & 0xFFF,
        ((v[6] >> 16) & 0xF) | ((v[7] & 0xFF) << 4),
        v[7] >> 8,
    ]
    for i in range(5):
        o_ref[unit * WORDS + i * GROUP : unit * WORDS + (i + 1) * GROUP, :] = (v[i] & 0xFFFFF) | (
            over[i] << 20
        )
    row = jnp.sum(jnp.where(diagonal(), power, 0.0), axis=0, keepdims=True)
    o_ref[units * WORDS + unit : units * WORDS + unit + 1, :SEGMENT_ROWS] = row.astype(jnp.int32)


def decode(ref, unit, units):
    w = [ref[unit * WORDS + i * GROUP : unit * WORDS + (i + 1) * GROUP, :] for i in range(5)]
    v = [(x << 12) >> 12 for x in w]
    v.append(((w[0] >> 20) & 0xFFF) | (((w[1] << 4) >> 24) << 12))
    v.append(((w[1] >> 28) & 0xF) | (((w[2] >> 20) & 0xFFF) << 4) | (((w[3] << 8) >> 28) << 16))
    v.append(((w[3] >> 24) & 0xFF) | ((w[4] >> 20) << 8))
    row = ref[units * WORDS + unit : units * WORDS + unit + 1, :SEGMENT_ROWS].astype(jnp.float32)
    power = jnp.sum(jnp.where(diagonal(), row, 0.0), axis=1, keepdims=True)
    return jnp.concatenate(v, axis=0).astype(jnp.float32) * jnp.exp2(power - 18.0)


def add_decoded(sums, chunk, refs):
    first, number = CHUNKS[chunk]
    for unit in range(number):
        rows = pl.ds((first + unit) * SEGMENT_ROWS, SEGMENT_ROWS)
        value = sums[rows, :]
        for ref in refs:
            value = value + decode(ref, unit, number)
        sums[rows, :] = value


def load_base(first, segments, column, x_ref, w_ref, x, w, sems):
    width, columns = w.shape
    rows = segments * SEGMENT_ROWS
    start = pl.multiple_of(column * columns, columns)
    depth = width // PIECES
    blocks = [(r, min(BLOCK, rows - r)) for r in range(0, rows, BLOCK)]

    def x_copy(at, size, features, sem):
        return pltpu.make_async_copy(
            x_ref.at[pl.ds(first * SEGMENT_ROWS + at, size), features],
            x.at[pl.ds(at, size), features],
            sem,
        )

    work = []
    for i, (at, size) in enumerate(blocks):
        terms = []
        if i == 0:
            for p in range(PIECES):
                features = pl.ds(p * depth, depth)
                copies = (
                    pltpu.make_async_copy(
                        w_ref.at[features, pl.ds(start, columns)], w.at[features, :], sems.at[0, p]
                    ),
                    x_copy(0, size, features, sems.at[1, p]),
                )
                terms.append((copies, slice(p * depth, (p + 1) * depth)))
        else:
            terms.append(((x_copy(at, size, slice(None), sems.at[2, i]),), slice(None)))
        work.append((at, size, terms))
    for _, _, terms in work:
        for copies, _ in terms:
            for copy in copies:
                copy.start()
    return work


def block_product(x, w, at, size, terms):
    total = None
    for copies, features in terms:
        for copy in copies:
            copy.wait()
        term = jnp.dot(
            x[at : at + size, features], w[features, :], preferred_element_type=jnp.float32
        )
        total = term if total is None else total + term
    return total


def base_scratch(segments, width, columns):
    rows = segments * SEGMENT_ROWS
    return [
        pltpu.VMEM((rows, width), jnp.bfloat16),
        pltpu.VMEM((width, columns), jnp.bfloat16),
        pltpu.SemaphoreType.DMA((3, max(PIECES, rows // BLOCK + 1))),
    ]


def sent_kernel(first, sizes, column, x_ref, w_ref, *refs):
    outs, (x, w, sems) = refs[: len(sizes)], refs[len(sizes) :]
    work = load_base(first, sum(sizes), column[0], x_ref, w_ref, x, w, sems)
    unit_of = [(out, unit) for out, size in enumerate(sizes) for unit in range(size)]
    for out, size in zip(outs, sizes):
        out[size * WORDS :, :] = jnp.zeros((8, w.shape[1]), jnp.int32)
    for at, size, terms in work:
        product = block_product(x, w, at, size, terms)
        for r in range(0, size, SEGMENT_ROWS):
            out, unit = unit_of[(at + r) // SEGMENT_ROWS]
            encode(product[r : r + SEGMENT_ROWS], outs[out], unit, sizes[out])


def sent_call(tokens, weight, column, columns, first, sizes):
    width = tokens.shape[1]
    rows = sum(sizes) * SEGMENT_ROWS
    return pl.pallas_call(
        functools.partial(sent_kernel, first, sizes),
        in_specs=[SMEM, HBM, HBM],
        out_specs=[VMEM] * len(sizes),
        out_shape=[jax.ShapeDtypeStruct((coded_rows(n), columns), jnp.int32) for n in sizes],
        scratch_shapes=base_scratch(sum(sizes), width, columns),
        compiler_params=params(24),
        cost_estimate=cost(
            2 * rows * width * columns, 2 * rows * width + 2 * width * columns + 4 * rows * columns
        ),
    )(column.reshape(1), tokens, weight)


def add_kernel(chunk, base_ref, *refs):
    coded_refs, o_ref = refs[:-1], refs[-1]
    o_ref[...] = base_ref[...]
    add_decoded(o_ref, chunk, coded_refs)


def add_call(chunk, base, coded):
    return pl.pallas_call(
        functools.partial(add_kernel, chunk),
        in_specs=[VMEM] * (1 + len(coded)),
        out_specs=VMEM,
        out_shape=jax.ShapeDtypeStruct(base.shape, base.dtype),
        compiler_params=params(8),
        cost_estimate=cost(0, 4 * base.size),
    )(base, *coded)


def shrink_into(o_ref, i, table, k, rows_of, buffers, owners, rank):
    for buffer, whose in zip(buffers, owners):

        @pl.when(whose == table[k * ENTRIES])
        def _(buffer=buffer):
            for j in range(MOST):
                _, _, within = segment_of(table, k, j)
                rows = rows_of(j)
                width = rows.shape[1]
                factor = buffer[pl.ds(pl.multiple_of(within * rank, rank), rank), :width]
                o_ref[i, :, j * rank : (j + 1) * rank] = lax.dot_general(
                    rows, factor, (((1,), (1,)), ((), ())), preferred_element_type=jnp.float32
                )


def stages_of(k):
    return range((k + 1) // 2, k + 1)


def own_kernel(n_adapter, rank, table, here, x_ref, w_ref, message, *refs):
    coded_refs, (o_ref, s_ref, kept_ref, x, w, sems, kept_sems) = refs[:-7], refs[-7:]
    work = load_base(0, x.shape[0] // SEGMENT_ROWS, here[2], x_ref, w_ref, x, w, sems)
    keeps = []
    for at, size, terms in work:
        o_ref[at : at + size, :] = block_product(x, w, at, size, terms)
    add_decoded(o_ref, 0, coded_refs)
    for k in range(1, n_adapter):
        for j in range(MOST):
            start, _, _ = segment_of(table, k, j)
            keeps.append(
                pltpu.make_async_copy(
                    x.at[pl.ds(start, SEGMENT_ROWS), :], kept_ref.at[k - 1, j], kept_sems.at[k - 1, j]
                )
            )
            keeps[-1].start()

    def rows_of(j):
        start, _, _ = segment_of(table, 0, j)
        return x[pl.ds(start, SEGMENT_ROWS), :]

    shrink_into(s_ref, 0, table, 0, rows_of, [message], [here[0]], rank)
    for copy in keeps:
        copy.wait()


def own_call(table, here, tokens, weight, message, coded, columns, n_adapter, rank):
    rows, width = tokens.shape
    segments = rows // SEGMENT_ROWS
    return pl.pallas_call(
        functools.partial(own_kernel, n_adapter, rank),
        in_specs=[SMEM, SMEM, HBM, HBM] + [VMEM] * (1 + len(coded)),
        out_specs=[VMEM] * 3,
        out_shape=[
            jax.ShapeDtypeStruct((rows, columns), jnp.float32),
            jax.ShapeDtypeStruct((1, SEGMENT_ROWS, MOST * rank), jnp.float32),
            jax.ShapeDtypeStruct((n_adapter - 1, MOST, SEGMENT_ROWS, width), jnp.bfloat16),
        ],
        scratch_shapes=base_scratch(segments, width, columns)
        + [pltpu.SemaphoreType.DMA((n_adapter - 1, MOST))],
        compiler_params=params(32),
        cost_estimate=cost(
            2 * rows * width * columns, 2 * rows * width + 2 * width * columns + 4 * rows * columns
        ),
    )(table, here, tokens, weight, message, *coded)


def shrink_kernel(k, rank, n_before, table, here, kept_ref, *refs):
    buffers, o_ref = refs[n_before:-1], refs[-1]
    for r in refs[:n_before]:
        o_ref[:1] = r[...]
    rows_of = lambda j: kept_ref[k - 1, j]
    owners = buffer_owners(here, stages_of(k))
    shrink_into(o_ref, n_before, table, k, rows_of, buffers, owners, rank)


def shrink_call(k, table, here, kept, before, buffers, rank):
    width = kept.shape[3]
    n = 1 + len(before)
    return pl.pallas_call(
        functools.partial(shrink_kernel, k, rank, len(before)),
        in_specs=[SMEM, SMEM, VMEM] + [VMEM] * (n - 1 + len(buffers)),
        out_specs=VMEM,
        out_shape=jax.ShapeDtypeStruct((n, SEGMENT_ROWS, MOST * rank), jnp.float32),
        compiler_params=params(16),
        cost_estimate=cost(MOST * 2 * SEGMENT_ROWS * width * 256, 4 * SEGMENT_ROWS * width),
    )(table, here, kept, *before, *buffers)


def fetch_up(up, at, table, k, j, buffers, owners, rank):
    columns = up.shape[2]
    _, _, within = segment_of(table, k, j)
    for buffer, whose in zip(buffers, owners):

        @pl.when(whose == table[k * ENTRIES])
        def _(buffer=buffer):
            first = buffer.shape[1] - columns
            factor = buffer[pl.ds(pl.multiple_of(within * rank, rank), rank), first:]
            up[at, :rank, :] = factor
            up[at, rank:, :] = factor


def up_product(share, j, factor, rank):
    lane = lax.broadcasted_iota(jnp.int32, share.shape, 1)
    other = pltpu.roll(share, rank, 1)
    both = jnp.where((lane < rank) == (j == 0), share, other)
    high = both.astype(jnp.bfloat16).astype(jnp.float32)
    terms = jnp.where(lane < rank, high, both - high).astype(jnp.bfloat16)
    return jnp.dot(terms, factor, preferred_element_type=jnp.float32)


def early_kernel(n_adapter, n_tensor, rank, table, here, *refs):
    n_coded, n_buffers = n_tensor - 1, 2 * n_adapter - 3
    base_ref, coded_refs, refs = refs[0], refs[1 : 1 + n_coded], refs[1 + n_coded :]
    shrinks, refs = refs[: -4 - n_buffers], refs[-4 - n_buffers :]
    buffers, (o_ref, rest_ref, up, total) = refs[:-4], refs[-4:]
    for k in range(n_adapter - 1):
        at = 0 if k == 0 else 2 * stages_of(k)[0] - 1
        to = 2 * k + 1
        owners = buffer_owners(here, stages_of(k))
        for j in range(MOST):
            fetch_up(up, k * MOST + j, table, k, j, buffers[at:to], owners, rank)
    shares = []
    for call in range(len(shrinks) // n_tensor):
        share = shrinks[call * n_tensor][...]
        for i in range(1, n_tensor):
            share = share + shrinks[call * n_tensor + i][...]
        shares += [share[i] for i in range(share.shape[0])]
    total[...] = base_ref[...]
    add_decoded(total, len(CHUNKS) - 1, coded_refs)
    for k in range(n_adapter):
        for j in range(MOST):
            start, used, _ = segment_of(table, k, j)
            value = total[pl.ds(start, SEGMENT_ROWS), :]
            if k == n_adapter - 1:
                rest_ref[j] = value
                continue
            lora = up_product(shares[k], j, up[k * MOST + j], rank)

            @pl.when(used)
            def _(start=start, value=value, lora=lora):
                o_ref[pl.ds(start, SEGMENT_ROWS), :] = (value + adapter_scale * lora).astype(
                    jnp.bfloat16
                )


def early(n_adapter, n_tensor, table, here, base, coded, shrinks, buffers, rank):
    rows, columns = base.shape
    return pl.pallas_call(
        functools.partial(early_kernel, n_adapter, n_tensor, rank),
        in_specs=[SMEM] * 2 + [VMEM] * (1 + len(coded) + len(shrinks) + len(buffers)),
        out_specs=[VMEM, VMEM],
        out_shape=[
            jax.ShapeDtypeStruct((rows, columns), jnp.bfloat16),
            jax.ShapeDtypeStruct((MOST, SEGMENT_ROWS, columns), jnp.float32),
        ],
        scratch_shapes=[
            pltpu.VMEM(((n_adapter - 1) * MOST, 2 * rank, columns), jnp.bfloat16),
            pltpu.VMEM((rows, columns), jnp.float32),
        ],
        compiler_params=params(16),
        cost_estimate=cost(6 * rows * rank * columns, (4 * n_tensor + 2) * rows * columns),
    )(table, here, base, *coded, *shrinks, *buffers)


def late_kernel(k, n_tensor, rank, table, here, *refs):
    rest_ref, shrinks, refs = refs[0], refs[1 : 1 + n_tensor], refs[1 + n_tensor :]
    buffers, (_, o_ref, up, out, sems) = refs[:-5], refs[-5:]
    owners = buffer_owners(here, stages_of(k))
    share = shrinks[0][0]
    for r in shrinks[1:]:
        share = share + r[0]
    stores = []
    for j in range(MOST):
        fetch_up(up, j, table, k, j, buffers, owners, rank)
        start, used, _ = segment_of(table, k, j)
        lora = up_product(share, j, up[j], rank)
        out[j] = (rest_ref[j] + adapter_scale * lora).astype(jnp.bfloat16)
        store = pltpu.make_async_copy(out.at[j], o_ref.at[pl.ds(start, SEGMENT_ROWS), :], sems.at[j])
        pl.when(used)(store.start)
        stores.append((used, store))
    for used, store in stores:
        pl.when(used)(store.wait)


def late(k, n_tensor, table, here, rest, shrinks, buffers, value, rank):
    rows, columns = value.shape
    return pl.pallas_call(
        functools.partial(late_kernel, k, n_tensor, rank),
        in_specs=[SMEM] * 2 + [VMEM] * (1 + len(shrinks) + len(buffers)) + [ANY],
        out_specs=ANY,
        out_shape=jax.ShapeDtypeStruct((rows, columns), jnp.bfloat16),
        scratch_shapes=[
            pltpu.VMEM((MOST, 2 * rank, columns), jnp.bfloat16),
            pltpu.VMEM((MOST, SEGMENT_ROWS, columns), jnp.bfloat16),
            pltpu.SemaphoreType.DMA((MOST,)),
        ],
        input_output_aliases={3 + len(shrinks) + len(buffers): 0},
        compiler_params=params(8),
        cost_estimate=cost(
            6 * MOST * SEGMENT_ROWS * rank * columns, 8 * MOST * SEGMENT_ROWS * columns
        ),
    )(table, here, rest, *shrinks, *buffers, value)


def after(array, *others):
    return lax.optimization_barrier((array, *others))[0]


def on_device(
    tokens, value_weight, adapter_down_weight, adapter_up_weight, row_adapter_index, adapter_slot_of
):
    rows, width = tokens.shape
    per_device, _, rank = adapter_down_weight.shape
    n_adapter = lax.axis_size("adapter")
    n_tensor = lax.axis_size("tensor")
    me_t = lax.axis_index("tensor")
    here = jnp.stack([lax.axis_index("adapter"), lax.axis_index("dp"), me_t])
    columns = value_weight.shape[1] // n_tensor

    def swap_tensor(array, step):
        pairs = [(i, (i + step) % n_tensor) for i in range(n_tensor)]
        return lax.ppermute(array, "tensor", pairs)

    def along_line(array, stage):
        up = [(2 * i, 2 * (i + 1)) for i in range(stage - 1, n_adapter - 1)]
        down = [(2 * i + 1, 2 * (i - 1) + 1) for i in range(1, n_adapter - stage + 1)]
        return lax.ppermute(array, ("adapter", "dp"), up + down)

    def swap_cores(array):
        return lax.ppermute(array, "dp", [(0, 1), (1, 0)])

    down = jnp.swapaxes(adapter_down_weight, 1, 2).reshape(per_device * rank, width)
    up = adapter_up_weight.reshape(per_device * rank, value_weight.shape[1])
    tokens, value_weight, down, up = (
        pltpu.with_memory_space_constraint(a, pltpu.HBM) for a in (tokens, value_weight, down, up)
    )
    message = message_call(here, down, up, columns)
    table = table_call(here, row_adapter_index, adapter_slot_of, n_adapter, per_device)

    buffers, shrinks = [[message]], []

    def buffers_of(stages):
        return [b for stage in stages for b in buffers[stage]]

    def add_shrink(mine):
        shrinks.extend([mine] + [swap_tensor(mine, step) for step in range(1, n_tensor)])

    held = along_line(message, 1)
    others = range(1, n_tensor)

    def sent_for(step, chunks):
        sizes = [number for _, number in chunks]
        target = (me_t + step) % n_tensor
        return sent_call(tokens, value_weight, target, columns, chunks[0][0], sizes)

    parts = [[sent_for(step, CHUNKS[:1])[0] for step in others]]
    rest_parts = [sent_for(step, CHUNKS[1:]) for step in others]
    parts += [[p[i] for p in rest_parts] for i in range(len(CHUNKS) - 1)]
    sent = [[swap_tensor(p, step) for step, p in zip(others, parts[0])]]
    last = n_adapter - 1
    done = [table] + [p for group in parts for p in group] + sent[0]
    before = None
    for stage in range(1, last):
        came = after(held, *done)
        held = along_line(came, stage + 1)
        if stage < len(CHUNKS):
            sent.append([swap_tensor(after(p, came), step) for step, p in zip(others, parts[stage])])
        if stage == 1:
            base, before, kept = own_call(
                after(table, came), here, tokens, value_weight, message, sent[0], columns, n_adapter, rank
            )
            add_shrink(before)
            done = sent[1] + shrinks
        else:
            if stage == 2:
                base = add_call(1, after(base, came), sent[1])
            before = shrink_call(
                stage - 1, table, here, after(kept, came), [], buffers_of(stages_of(stage - 1)), rank
            )
            if stage < last - 1:
                add_shrink(before)
            done = []
        buffers.append([came, swap_cores(came)])
    merged = shrink_call(
        last - 1, table, here, kept, [before], buffers_of(stages_of(last - 1)), rank
    )
    add_shrink(merged)
    value, remaining = early(
        n_adapter,
        n_tensor,
        table,
        here,
        base,
        sent[2],
        shrinks,
        buffers_of(range(last)),
        rank,
    )
    came = after(held, value)
    buffers.append([came, swap_cores(came)])
    add_shrink(shrink_call(last, table, here, kept, [], buffers_of(stages_of(last)), rank))
    return late(
        last,
        n_tensor,
        table,
        here,
        remaining,
        shrinks[-n_tensor:],
        buffers_of(stages_of(last)),
        value,
        rank,
    )


def solution(mesh):
    return jax.shard_map(
        on_device,
        mesh=mesh,
        in_specs=(
            P(("groups", "adapter", "dp"), "tensor"),
            P("tensor", None),
            P(("groups", "adapter"), "tensor", None),
            P(("groups", "adapter"), None, None),
            P(("groups", "adapter", "dp")),
            P("groups"),
        ),
        out_specs=P(("groups", "adapter", "dp"), "tensor"),
        check_vma=False,
    )
```

```python
import functools

import jax
import jax.numpy as jnp
from jax import lax
from jax.experimental import pallas as pl
from jax.experimental.pallas import tpu as pltpu
from jax.sharding import PartitionSpec as P

SEGMENT_ROWS = 128
adapter_scale = 0.5
MOST = 2
BLOCK = 256
PIECES = 4
CHUNKS = ((6, 2), (0, 4), (4, 2))
ENTRIES = 8
MIDDLE = 1.5 * 2.0**23


def cost(flops, moved):
    return pl.CostEstimate(flops=int(flops), bytes_accessed=int(moved), transcendentals=0)


def params(mib):
    return pltpu.CompilerParams(vmem_limit_bytes=mib * 2**20)


ANY = pl.BlockSpec(memory_space=pl.ANY)
HBM = pl.BlockSpec(memory_space=pltpu.HBM)
SMEM = pl.BlockSpec(memory_space=pltpu.SMEM)
VMEM = pl.BlockSpec(memory_space=pltpu.VMEM)


def arrival_order(me, n_adapter):
    order = [me] + [jnp.int32(-1)] * (n_adapter - 1)
    count = jnp.int32(1)
    for distance in range(1, n_adapter):
        for other in (me - distance, me + distance):
            valid = (other >= 0) & (other < n_adapter)
            order = [jnp.where(valid & (count == k), other, o) for k, o in enumerate(order)]
            count = count + valid.astype(jnp.int32)
    return order


def buffer_tags(here, stages, per_device):
    tags = []
    for stage in stages:
        for i in range(per_device):
            toward = jnp.where(here[1] == i % 2, -stage, stage)
            tags += [(here[0] + toward, i), (here[0] - toward, i)] if stage > 0 else [(here[0], i)]
    return tags


def segment_of(table, k, j):
    seg = table[k * ENTRIES + 1 + 2 * j]
    start = pl.multiple_of(jnp.maximum(seg, 0) * SEGMENT_ROWS, SEGMENT_ROWS)
    return start, seg >= 0, table[k * ENTRIES + 2 + 2 * j]


def message_kernel(here, down_ref, up_ref, *refs):
    outs, sems = refs[:-1], refs[-1]
    rank = outs[0].shape[0]
    width = down_ref.shape[1]
    columns = outs[0].shape[1] - width
    start = pl.multiple_of(here[2] * columns, columns)
    copies = []
    for i, out in enumerate(outs):
        rows = pl.ds(i * rank, rank)
        copies += [
            pltpu.make_async_copy(down_ref.at[rows, :], out.at[:, pl.ds(0, width)], sems.at[0, i]),
            pltpu.make_async_copy(
                up_ref.at[rows, pl.ds(start, columns)], out.at[:, pl.ds(width, columns)], sems.at[1, i]
            ),
        ]
    for copy in copies:
        copy.start()
    for copy in copies:
        copy.wait()


def message_call(here, down, up, columns, per_device):
    rows, width = down.shape
    shape = jax.ShapeDtypeStruct((rows // per_device, width + columns), jnp.bfloat16)
    return pl.pallas_call(
        message_kernel,
        in_specs=[SMEM, HBM, HBM],
        out_specs=[VMEM] * per_device,
        out_shape=[shape] * per_device,
        scratch_shapes=[pltpu.SemaphoreType.DMA((2, per_device))],
        compiler_params=params(8),
        cost_estimate=cost(0, 4 * rows * (width + columns)),
    )(here, down, up)


def table_kernel(n_adapter, per_device, here, ids, slots, table):
    seg_dev = ids.shape[0] // SEGMENT_ROWS
    used = [slots[ids[s * SEGMENT_ROWS]] for s in range(seg_dev)]
    for k, owner in enumerate(arrival_order(here[0], n_adapter)):
        table[k * ENTRIES] = owner
        found, place = [jnp.int32(-1)] * MOST, [jnp.int32(0)] * MOST
        count = jnp.int32(0)
        for s, slot in enumerate(used):
            within = slot - owner * per_device
            hit = (within >= 0) & (within < per_device)
            for j in range(MOST):
                take = hit & (count == j)
                found[j] = jnp.where(take, s, found[j])
                place[j] = jnp.where(take, within, place[j])
            count = count + hit.astype(jnp.int32)
        for j in range(MOST):
            table[k * ENTRIES + 1 + 2 * j] = found[j]
            table[k * ENTRIES + 2 + 2 * j] = place[j]


def table_call(here, ids, slots, n_adapter, per_device):
    return pl.pallas_call(
        functools.partial(table_kernel, n_adapter, per_device),
        in_specs=[SMEM, SMEM, SMEM],
        out_specs=SMEM,
        out_shape=jax.ShapeDtypeStruct((n_adapter * ENTRIES,), jnp.int32),
        cost_estimate=cost(0, 4 * ids.shape[0]),
    )(here, ids, slots)


def diagonal():
    shape = (SEGMENT_ROWS, SEGMENT_ROWS)
    return lax.broadcasted_iota(jnp.int32, shape, 0) == lax.broadcasted_iota(jnp.int32, shape, 1)


GROUP = SEGMENT_ROWS // 8
WORDS = 5 * GROUP


def coded_rows(segments):
    return segments * WORDS + 8


def encode(values, o_ref, unit, units):
    largest = jnp.maximum(jnp.max(jnp.abs(values), axis=1, keepdims=True), 2.0**-100)
    power = jnp.floor(jnp.log2(largest))
    whole = (values * jnp.exp2(18.0 - power) + MIDDLE).astype(jnp.int32) - int(MIDDLE)
    whole = jnp.minimum(whole, 2**19 - 1)
    v = [whole[i * GROUP : (i + 1) * GROUP] for i in range(8)]
    over = [
        v[5] & 0xFFF,
        ((v[5] >> 12) & 0xFF) | ((v[6] & 0xF) << 8),
        (v[6] >> 4) & 0xFFF,
        ((v[6] >> 16) & 0xF) | ((v[7] & 0xFF) << 4),
        v[7] >> 8,
    ]
    for i in range(5):
        o_ref[unit * WORDS + i * GROUP : unit * WORDS + (i + 1) * GROUP, :] = (v[i] & 0xFFFFF) | (
            over[i] << 20
        )
    row = jnp.sum(jnp.where(diagonal(), power, 0.0), axis=0, keepdims=True)
    o_ref[units * WORDS + unit : units * WORDS + unit + 1, :SEGMENT_ROWS] = row.astype(jnp.int32)


def decode(ref, unit, units):
    w = [ref[unit * WORDS + i * GROUP : unit * WORDS + (i + 1) * GROUP, :] for i in range(5)]
    v = [(x << 12) >> 12 for x in w]
    v.append(((w[0] >> 20) & 0xFFF) | (((w[1] << 4) >> 24) << 12))
    v.append(((w[1] >> 28) & 0xF) | (((w[2] >> 20) & 0xFFF) << 4) | (((w[3] << 8) >> 28) << 16))
    v.append(((w[3] >> 24) & 0xFF) | ((w[4] >> 20) << 8))
    row = ref[units * WORDS + unit : units * WORDS + unit + 1, :SEGMENT_ROWS].astype(jnp.float32)
    power = jnp.sum(jnp.where(diagonal(), row, 0.0), axis=1, keepdims=True)
    return jnp.concatenate(v, axis=0).astype(jnp.float32) * jnp.exp2(power - 18.0)


def add_decoded(sums, chunk, refs):
    first, number = CHUNKS[chunk]
    for unit in range(number):
        rows = pl.ds((first + unit) * SEGMENT_ROWS, SEGMENT_ROWS)
        value = sums[rows, :]
        for ref in refs:
            value = value + decode(ref, unit, number)
        sums[rows, :] = value


def load_base(first, segments, column, x_ref, w_ref, x, w, sems):
    width, columns = w.shape
    rows = segments * SEGMENT_ROWS
    start = pl.multiple_of(column * columns, columns)
    depth = width // PIECES
    blocks = [(r, min(BLOCK, rows - r)) for r in range(0, rows, BLOCK)]

    def x_copy(at, size, features, sem):
        return pltpu.make_async_copy(
            x_ref.at[pl.ds(first * SEGMENT_ROWS + at, size), features],
            x.at[pl.ds(at, size), features],
            sem,
        )

    work = []
    for i, (at, size) in enumerate(blocks):
        terms = []
        if i == 0:
            for p in range(PIECES):
                features = pl.ds(p * depth, depth)
                copies = (
                    pltpu.make_async_copy(
                        w_ref.at[features, pl.ds(start, columns)], w.at[features, :], sems.at[0, p]
                    ),
                    x_copy(0, size, features, sems.at[1, p]),
                )
                terms.append((copies, slice(p * depth, (p + 1) * depth)))
        else:
            terms.append(((x_copy(at, size, slice(None), sems.at[2, i]),), slice(None)))
        work.append((at, size, terms))
    for _, _, terms in work:
        for copies, _ in terms:
            for copy in copies:
                copy.start()
    return work


def block_product(x, w, at, size, terms):
    total = None
    for copies, features in terms:
        for copy in copies:
            copy.wait()
        term = jnp.dot(
            x[at : at + size, features], w[features, :], preferred_element_type=jnp.float32
        )
        total = term if total is None else total + term
    return total


def base_scratch(segments, width, columns):
    rows = segments * SEGMENT_ROWS
    return [
        pltpu.VMEM((rows, width), jnp.bfloat16),
        pltpu.VMEM((width, columns), jnp.bfloat16),
        pltpu.SemaphoreType.DMA((3, max(PIECES, rows // BLOCK + 1))),
    ]


def sent_kernel(first, sizes, column, x_ref, w_ref, *refs):
    outs, (x, w, sems) = refs[: len(sizes)], refs[len(sizes) :]
    work = load_base(first, sum(sizes), column[0], x_ref, w_ref, x, w, sems)
    unit_of = [(out, unit) for out, size in enumerate(sizes) for unit in range(size)]
    for out, size in zip(outs, sizes):
        out[size * WORDS :, :] = jnp.zeros((8, w.shape[1]), jnp.int32)
    for at, size, terms in work:
        product = block_product(x, w, at, size, terms)
        for r in range(0, size, SEGMENT_ROWS):
            out, unit = unit_of[(at + r) // SEGMENT_ROWS]
            encode(product[r : r + SEGMENT_ROWS], outs[out], unit, sizes[out])


def sent_call(tokens, weight, column, columns, first, sizes):
    width = tokens.shape[1]
    rows = sum(sizes) * SEGMENT_ROWS
    return pl.pallas_call(
        functools.partial(sent_kernel, first, sizes),
        in_specs=[SMEM, HBM, HBM],
        out_specs=[VMEM] * len(sizes),
        out_shape=[jax.ShapeDtypeStruct((coded_rows(n), columns), jnp.int32) for n in sizes],
        scratch_shapes=base_scratch(sum(sizes), width, columns),
        compiler_params=params(24),
        cost_estimate=cost(
            2 * rows * width * columns, 2 * rows * width + 2 * width * columns + 4 * rows * columns
        ),
    )(column.reshape(1), tokens, weight)


def add_kernel(chunk, base_ref, *refs):
    coded_refs, o_ref = refs[:-1], refs[-1]
    o_ref[...] = base_ref[...]
    add_decoded(o_ref, chunk, coded_refs)


def add_call(chunk, base, coded):
    return pl.pallas_call(
        functools.partial(add_kernel, chunk),
        in_specs=[VMEM] * (1 + len(coded)),
        out_specs=VMEM,
        out_shape=jax.ShapeDtypeStruct(base.shape, base.dtype),
        compiler_params=params(8),
        cost_estimate=cost(0, 4 * base.size),
    )(base, *coded)


def own_kernel(column, x_ref, w_ref, *refs):
    coded_refs, (o_ref, x, w, sems) = refs[:-4], refs[-4:]
    work = load_base(0, x.shape[0] // SEGMENT_ROWS, column[0], x_ref, w_ref, x, w, sems)
    for at, size, terms in work:
        o_ref[at : at + size, :] = block_product(x, w, at, size, terms)
    add_decoded(o_ref, 0, coded_refs)


def own_call(tokens, weight, column, coded, columns):
    rows, width = tokens.shape
    x, *scratch = base_scratch(rows // SEGMENT_ROWS, width, columns)
    return pl.pallas_call(
        own_kernel,
        in_specs=[SMEM, HBM, HBM] + [VMEM] * len(coded),
        out_specs=[VMEM, VMEM],
        out_shape=[
            jax.ShapeDtypeStruct((rows, columns), jnp.float32),
            jax.ShapeDtypeStruct(x.shape, x.dtype),
        ],
        scratch_shapes=scratch,
        compiler_params=params(24),
        cost_estimate=cost(
            2 * rows * width * columns, 2 * rows * width + 2 * width * columns + 4 * rows * columns
        ),
    )(column.reshape(1), tokens, weight, *coded)


def stages_of(k):
    return range((k + 1) // 2, k + 1)


def stages_of_all(ks):
    return range(stages_of(ks[0])[0], ks[-1] + 1)


def shrink_kernel(ks, stages, per_device, rank, n_before, table, here, x, *refs):
    buffers, o_ref = refs[n_before:-1], refs[-1]
    width = x.shape[1]
    for r in refs[:n_before]:
        o_ref[: r.shape[0]] = r[...]
    tags = buffer_tags(here, stages, per_device)
    for at, k in enumerate(ks, o_ref.shape[0] - len(ks)):
        for j in range(MOST):
            start, _, within = segment_of(table, k, j)
            for buffer, (whose, i) in zip(buffers, tags):

                @pl.when((whose == table[k * ENTRIES]) & (within == i))
                def _(at=at, j=j, start=start, buffer=buffer):
                    o_ref[at, :, j * rank : (j + 1) * rank] = lax.dot_general(
                        x[pl.ds(start, SEGMENT_ROWS), :],
                        buffer[:, :width],
                        (((1,), (1,)), ((), ())),
                        preferred_element_type=jnp.float32,
                    )


def shrink_call(ks, table, here, x, before, buffers, per_device, rank):
    n = len(ks) + sum(b.shape[0] for b in before)
    return pl.pallas_call(
        functools.partial(shrink_kernel, ks, stages_of_all(ks), per_device, rank, len(before)),
        in_specs=[SMEM, SMEM, VMEM] + [VMEM] * (len(before) + len(buffers)),
        out_specs=VMEM,
        out_shape=jax.ShapeDtypeStruct((n, SEGMENT_ROWS, MOST * rank), jnp.float32),
        compiler_params=params(16),
        cost_estimate=cost(
            len(ks) * MOST * 2 * SEGMENT_ROWS * x.shape[1] * 256,
            len(ks) * 4 * SEGMENT_ROWS * x.shape[1],
        ),
    )(table, here, x, *before, *buffers)


def fetch_up(up, at, table, k, j, buffers, tags, rank):
    columns = up.shape[2]
    _, _, within = segment_of(table, k, j)
    for buffer, (whose, i) in zip(buffers, tags):

        @pl.when((whose == table[k * ENTRIES]) & (within == i))
        def _(buffer=buffer):
            factor = buffer[:, buffer.shape[1] - columns :]
            up[at, :rank, :] = factor
            up[at, rank:, :] = factor


def up_product(share, j, factor, rank):
    lane = lax.broadcasted_iota(jnp.int32, share.shape, 1)
    other = pltpu.roll(share, rank, 1)
    both = jnp.where((lane < rank) == (j == 0), share, other)
    high = both.astype(jnp.bfloat16).astype(jnp.float32)
    terms = jnp.where(lane < rank, high, both - high).astype(jnp.bfloat16)
    return jnp.dot(terms, factor, preferred_element_type=jnp.float32)


LATE = 2


def total_shrinks(shrinks, n_tensor):
    shares = []
    for call in range(0, len(shrinks), n_tensor):
        share = shrinks[call][...]
        for r in shrinks[call + 1 : call + n_tensor]:
            share = share + r[...]
        shares += [share[i] for i in range(share.shape[0])]
    return shares


def early_kernel(n_adapter, n_tensor, per_device, rank, n_shrinks, table, here, *refs):
    base_ref, coded_refs, refs = refs[0], refs[1:n_tensor], refs[n_tensor:]
    shrinks, refs = refs[:n_shrinks], refs[n_shrinks:]
    buffers, (o_ref, rest_ref, up, total) = refs[:-4], refs[-4:]
    first = n_adapter - LATE
    tags = buffer_tags(here, range(first), per_device)
    for k in range(first):
        for j in range(MOST):
            fetch_up(up, k * MOST + j, table, k, j, buffers, tags, rank)
    shares = total_shrinks(shrinks, n_tensor)
    total[...] = base_ref[...]
    add_decoded(total, len(CHUNKS) - 1, coded_refs)
    for k in range(n_adapter):
        for j in range(MOST):
            start, used, _ = segment_of(table, k, j)
            value = total[pl.ds(start, SEGMENT_ROWS), :]
            if k >= first:
                rest_ref[k - first, j] = value
                continue
            lora = up_product(shares[k], j, up[k * MOST + j], rank)

            @pl.when(used)
            def _(start=start, value=value, lora=lora):
                o_ref[pl.ds(start, SEGMENT_ROWS), :] = (value + adapter_scale * lora).astype(
                    jnp.bfloat16
                )


def early(n_adapter, n_tensor, table, here, base, coded, shrinks, buffers, per_device, rank):
    rows, columns = base.shape
    return pl.pallas_call(
        functools.partial(early_kernel, n_adapter, n_tensor, per_device, rank, len(shrinks)),
        in_specs=[SMEM] * 2 + [VMEM] * (1 + len(coded) + len(shrinks) + len(buffers)),
        out_specs=[VMEM, VMEM],
        out_shape=[
            jax.ShapeDtypeStruct((rows, columns), jnp.bfloat16),
            jax.ShapeDtypeStruct((LATE, MOST, SEGMENT_ROWS, columns), jnp.float32),
        ],
        scratch_shapes=[
            pltpu.VMEM(((n_adapter - LATE) * MOST, 2 * rank, columns), jnp.bfloat16),
            pltpu.VMEM((rows, columns), jnp.float32),
        ],
        compiler_params=params(16),
        cost_estimate=cost(6 * rows * rank * columns, (4 * n_tensor + 2) * rows * columns),
    )(table, here, base, *coded, *shrinks, *buffers)


def late_kernel(ks, n_tensor, per_device, rank, table, here, *refs):
    rest_ref, shrinks, refs = refs[0], refs[1 : 1 + n_tensor], refs[1 + n_tensor :]
    buffers, (_, o_ref, up, out, sems) = refs[:-5], refs[-5:]
    tags = buffer_tags(here, stages_of_all(ks), per_device)
    shares = total_shrinks(shrinks, n_tensor)
    stores = []
    for i, k in enumerate(ks):
        for j in range(MOST):
            fetch_up(up, i * MOST + j, table, k, j, buffers, tags, rank)
            start, used, _ = segment_of(table, k, j)
            lora = up_product(shares[i], j, up[i * MOST + j], rank)
            out[i, j] = (rest_ref[i, j] + adapter_scale * lora).astype(jnp.bfloat16)
            store = pltpu.make_async_copy(
                out.at[i, j], o_ref.at[pl.ds(start, SEGMENT_ROWS), :], sems.at[i, j]
            )
            pl.when(used)(store.start)
            stores.append((used, store))
    for used, store in stores:
        pl.when(used)(store.wait)


def late(ks, n_tensor, table, here, rest, shrinks, buffers, value, per_device, rank):
    rows, columns = value.shape
    return pl.pallas_call(
        functools.partial(late_kernel, ks, n_tensor, per_device, rank),
        in_specs=[SMEM] * 2 + [VMEM] * (1 + len(shrinks) + len(buffers)) + [ANY],
        out_specs=ANY,
        out_shape=jax.ShapeDtypeStruct((rows, columns), jnp.bfloat16),
        scratch_shapes=[
            pltpu.VMEM((LATE * MOST, 2 * rank, columns), jnp.bfloat16),
            pltpu.VMEM((LATE, MOST, SEGMENT_ROWS, columns), jnp.bfloat16),
            pltpu.SemaphoreType.DMA((LATE, MOST)),
        ],
        input_output_aliases={3 + len(shrinks) + len(buffers): 0},
        compiler_params=params(8),
        cost_estimate=cost(
            6 * LATE * MOST * SEGMENT_ROWS * rank * columns,
            8 * LATE * MOST * SEGMENT_ROWS * columns,
        ),
    )(table, here, rest, *shrinks, *buffers, value)


def after(array, *others):
    return lax.optimization_barrier((array, *others))[0]


def on_device(
    tokens, value_weight, adapter_down_weight, adapter_up_weight, row_adapter_index, adapter_slot_of
):
    rows, width = tokens.shape
    per_device, _, rank = adapter_down_weight.shape
    n_adapter = lax.axis_size("adapter")
    n_tensor = lax.axis_size("tensor")
    me_t = lax.axis_index("tensor")
    here = jnp.stack([lax.axis_index("adapter"), lax.axis_index("dp"), me_t])
    columns = value_weight.shape[1] // n_tensor

    def swap_tensor(array, step):
        pairs = [(i, (i + step) % n_tensor) for i in range(n_tensor)]
        return lax.ppermute(array, "tensor", pairs)

    def along_line(arrays, stage):
        moved = []
        for i, array in enumerate(arrays):
            up, down = i % 2, 1 - i % 2
            pairs = [(2 * z + up, 2 * (z + 1) + up) for z in range(stage - 1, n_adapter - 1)]
            pairs += [(2 * z + down, 2 * (z - 1) + down) for z in range(1, n_adapter - stage + 1)]
            moved.append(lax.ppermute(array, ("adapter", "dp"), pairs))
        return moved

    def swap_cores(arrays):
        return [lax.ppermute(a, "dp", [(0, 1), (1, 0)]) for a in arrays]

    down = jnp.swapaxes(adapter_down_weight, 1, 2).reshape(per_device * rank, width)
    up = adapter_up_weight.reshape(per_device * rank, value_weight.shape[1])
    tokens, value_weight, down, up = (
        pltpu.with_memory_space_constraint(a, pltpu.HBM) for a in (tokens, value_weight, down, up)
    )
    messages = message_call(here, down, up, columns, per_device)
    buffers = [[[m] for m in messages]]

    def buffers_of(stages):
        return [b for stage in stages for pair in buffers[stage] for b in pair]

    def swapped(mine):
        return [mine] + [swap_tensor(mine, step) for step in range(1, n_tensor)]

    def shrink(ks, x, before=()):
        mine = buffers_of(stages_of_all(ks))
        return shrink_call(ks, table, here, x, list(before), mine, per_device, rank)

    others = range(1, n_tensor)

    def sent_for(step, chunks):
        sizes = [number for _, number in chunks]
        target = (me_t + step) % n_tensor
        return sent_call(tokens, value_weight, target, columns, chunks[0][0], sizes)

    held = along_line(messages, 1)
    parts = [[sent_for(step, CHUNKS[:1])[0] for step in others]]
    rest_parts = [sent_for(step, CHUNKS[1:]) for step in others]
    parts += [[p[i] for p in rest_parts] for i in range(len(CHUNKS) - 1)]
    sent = [[swap_tensor(p, step) for step, p in zip(others, parts[0])]]
    done = [p for group in parts for p in group] + sent[0]
    shrinks = []
    for stage in range(1, n_adapter):
        if stage == n_adapter - 1:
            value, remaining = early(
                n_adapter,
                n_tensor,
                table,
                here,
                base,
                sent[2],
                shrinks,
                buffers_of(range(n_adapter - LATE)),
                per_device,
                rank,
            )
            done = [value]
        came = list(lax.optimization_barrier((*held, *done)))[:per_device]
        if stage < n_adapter - 1:
            held = along_line(came, stage + 1)
        buffers.append([list(pair) for pair in zip(came, swap_cores(came))])
        if stage < len(CHUNKS):
            sent.append([swap_tensor(after(p, *came), step) for step, p in zip(others, parts[stage])])
        if stage == 1:
            base, x = own_call(tokens, value_weight, after(me_t, *came), sent[0], columns)
            done = sent[1] + [base]
        elif stage < n_adapter - 1:
            done = []
            if stage == 2:
                table = table_call(
                    after(here, *came), row_adapter_index, adapter_slot_of, n_adapter, per_device
                )
                base = add_call(1, after(base, *came), sent[1])
            shrinks += swapped(shrink([0, 1] if stage == 2 else [stage - 1], x))
    last = [n_adapter - 2, n_adapter - 1]
    mine = shrink(last[:1], after(x, *came))
    mine = shrink(last[1:], x, [mine])
    return late(
        last,
        n_tensor,
        table,
        here,
        remaining,
        swapped(mine),
        buffers_of(stages_of_all(last)),
        value,
        per_device,
        rank,
    )


def solution(mesh):
    return jax.shard_map(
        on_device,
        mesh=mesh,
        in_specs=(
            P(("groups", "adapter", "dp"), "tensor"),
            P("tensor", None),
            P(("groups", "adapter"), "tensor", None),
            P(("groups", "adapter"), None, None),
            P(("groups", "adapter", "dp")),
            P("groups"),
        ),
        out_specs=P(("groups", "adapter", "dp"), "tensor"),
        check_vma=False,
    )
```

```python
import functools

import jax
import jax.numpy as jnp
from jax import lax
from jax.experimental import pallas as pl
from jax.experimental.pallas import tpu as pltpu
from jax.sharding import PartitionSpec as P

SEGMENT_ROWS = 128
adapter_scale = 0.5
MOST = 2
BLOCK = 256
PIECES = 4
CHUNKS = ((6, 2), (0, 3), (3, 3))
ENTRIES = 8
MIDDLE = 1.5 * 2.0**23


def cost(flops, moved):
    return pl.CostEstimate(flops=int(flops), bytes_accessed=int(moved), transcendentals=0)


def params(mib):
    return pltpu.CompilerParams(vmem_limit_bytes=mib * 2**20)


ANY = pl.BlockSpec(memory_space=pl.ANY)
HBM = pl.BlockSpec(memory_space=pltpu.HBM)
SMEM = pl.BlockSpec(memory_space=pltpu.SMEM)
VMEM = pl.BlockSpec(memory_space=pltpu.VMEM)


def arrival_order(me, n_adapter):
    order = [me] + [jnp.int32(-1)] * (n_adapter - 1)
    count = jnp.int32(1)
    for distance in range(1, n_adapter):
        for other in (me - distance, me + distance):
            valid = (other >= 0) & (other < n_adapter)
            order = [jnp.where(valid & (count == k), other, o) for k, o in enumerate(order)]
            count = count + valid.astype(jnp.int32)
    return order


def buffer_owners(here, stages):
    owners = []
    for stage in stages:
        toward = jnp.where(here[1] == 0, -stage, stage)
        owners += [here[0] + toward, here[0] - toward] if stage > 0 else [here[0]]
    return owners


def segment_of(table, k, j):
    seg = table[k * ENTRIES + 1 + 2 * j]
    start = pl.multiple_of(jnp.maximum(seg, 0) * SEGMENT_ROWS, SEGMENT_ROWS)
    return start, seg >= 0, table[k * ENTRIES + 2 + 2 * j]


def message_kernel(here, down_ref, up_ref, o_ref, sems):
    width = down_ref.shape[1]
    columns = o_ref.shape[1] - width
    start = pl.multiple_of(here[2] * columns, columns)
    rows = down_ref.shape[0] // PIECES
    copies = [
        pltpu.make_async_copy(
            down_ref.at[pl.ds(p * rows, rows), :],
            o_ref.at[pl.ds(p * rows, rows), pl.ds(0, width)],
            sems.at[p],
        )
        for p in range(PIECES)
    ]
    copies.append(
        pltpu.make_async_copy(
            up_ref.at[:, pl.ds(start, columns)], o_ref.at[:, pl.ds(width, columns)], sems.at[PIECES]
        )
    )
    for copy in copies:
        copy.start()
    for copy in copies:
        copy.wait()


def message_call(here, down, up, columns):
    rows, width = down.shape
    return pl.pallas_call(
        message_kernel,
        in_specs=[SMEM, HBM, HBM],
        out_specs=VMEM,
        out_shape=jax.ShapeDtypeStruct((rows, width + columns), jnp.bfloat16),
        scratch_shapes=[pltpu.SemaphoreType.DMA((PIECES + 1,))],
        compiler_params=params(8),
        cost_estimate=cost(0, 4 * rows * (width + columns)),
    )(here, down, up)


def table_kernel(n_adapter, per_device, here, ids, slots, table):
    seg_dev = ids.shape[0] // SEGMENT_ROWS
    used = [slots[ids[s * SEGMENT_ROWS]] for s in range(seg_dev)]
    for k, owner in enumerate(arrival_order(here[0], n_adapter)):
        table[k * ENTRIES] = owner
        found, place = [jnp.int32(-1)] * MOST, [jnp.int32(0)] * MOST
        count = jnp.int32(0)
        for s, slot in enumerate(used):
            within = slot - owner * per_device
            hit = (within >= 0) & (within < per_device)
            for j in range(MOST):
                take = hit & (count == j)
                found[j] = jnp.where(take, s, found[j])
                place[j] = jnp.where(take, within, place[j])
            count = count + hit.astype(jnp.int32)
        for j in range(MOST):
            table[k * ENTRIES + 1 + 2 * j] = found[j]
            table[k * ENTRIES + 2 + 2 * j] = place[j]


def table_call(here, ids, slots, n_adapter, per_device):
    return pl.pallas_call(
        functools.partial(table_kernel, n_adapter, per_device),
        in_specs=[SMEM, SMEM, SMEM],
        out_specs=SMEM,
        out_shape=jax.ShapeDtypeStruct((n_adapter * ENTRIES,), jnp.int32),
        cost_estimate=cost(0, 4 * ids.shape[0]),
    )(here, ids, slots)


def diagonal():
    shape = (SEGMENT_ROWS, SEGMENT_ROWS)
    return lax.broadcasted_iota(jnp.int32, shape, 0) == lax.broadcasted_iota(jnp.int32, shape, 1)


GROUP = SEGMENT_ROWS // 8
WORDS = 5 * GROUP


def coded_rows(segments):
    return segments * WORDS + 8


def encode(values, o_ref, unit, units):
    largest = jnp.maximum(jnp.max(jnp.abs(values), axis=1, keepdims=True), 2.0**-100)
    power = jnp.floor(jnp.log2(largest))
    whole = (values * jnp.exp2(18.0 - power) + MIDDLE).astype(jnp.int32) - int(MIDDLE)
    whole = jnp.minimum(whole, 2**19 - 1)
    v = [whole[i * GROUP : (i + 1) * GROUP] for i in range(8)]
    over = [
        v[5] & 0xFFF,
        ((v[5] >> 12) & 0xFF) | ((v[6] & 0xF) << 8),
        (v[6] >> 4) & 0xFFF,
        ((v[6] >> 16) & 0xF) | ((v[7] & 0xFF) << 4),
        v[7] >> 8,
    ]
    for i in range(5):
        o_ref[unit * WORDS + i * GROUP : unit * WORDS + (i + 1) * GROUP, :] = (v[i] & 0xFFFFF) | (
            over[i] << 20
        )
    row = jnp.sum(jnp.where(diagonal(), power, 0.0), axis=0, keepdims=True)
    o_ref[units * WORDS + unit : units * WORDS + unit + 1, :SEGMENT_ROWS] = row.astype(jnp.int32)


def decode(ref, unit, units):
    w = [ref[unit * WORDS + i * GROUP : unit * WORDS + (i + 1) * GROUP, :] for i in range(5)]
    v = [(x << 12) >> 12 for x in w]
    v.append(((w[0] >> 20) & 0xFFF) | (((w[1] << 4) >> 24) << 12))
    v.append(((w[1] >> 28) & 0xF) | (((w[2] >> 20) & 0xFFF) << 4) | (((w[3] << 8) >> 28) << 16))
    v.append(((w[3] >> 24) & 0xFF) | ((w[4] >> 20) << 8))
    row = ref[units * WORDS + unit : units * WORDS + unit + 1, :SEGMENT_ROWS].astype(jnp.float32)
    power = jnp.sum(jnp.where(diagonal(), row, 0.0), axis=1, keepdims=True)
    return jnp.concatenate(v, axis=0).astype(jnp.float32) * jnp.exp2(power - 18.0)


def add_decoded(sums, chunk, refs):
    first, number = CHUNKS[chunk]
    for unit in range(number):
        rows = pl.ds((first + unit) * SEGMENT_ROWS, SEGMENT_ROWS)
        value = sums[rows, :]
        for ref in refs:
            value = value + decode(ref, unit, number)
        sums[rows, :] = value


def load_base(first, segments, column, x_ref, w_ref, x, w, sems):
    width, columns = w.shape
    rows = segments * SEGMENT_ROWS
    start = pl.multiple_of(column * columns, columns)
    depth = width // PIECES
    blocks = [(r, min(BLOCK, rows - r)) for r in range(0, rows, BLOCK)]

    def x_copy(at, size, features, sem):
        return pltpu.make_async_copy(
            x_ref.at[pl.ds(first * SEGMENT_ROWS + at, size), features],
            x.at[pl.ds(at, size), features],
            sem,
        )

    work = []
    for i, (at, size) in enumerate(blocks):
        terms = []
        if i == 0:
            for p in range(PIECES):
                features = pl.ds(p * depth, depth)
                copies = (
                    pltpu.make_async_copy(
                        w_ref.at[features, pl.ds(start, columns)], w.at[features, :], sems.at[0, p]
                    ),
                    x_copy(0, size, features, sems.at[1, p]),
                )
                terms.append((copies, slice(p * depth, (p + 1) * depth)))
        else:
            terms.append(((x_copy(at, size, slice(None), sems.at[2, i]),), slice(None)))
        work.append((at, size, terms))
    for _, _, terms in work:
        for copies, _ in terms:
            for copy in copies:
                copy.start()
    return work


def block_product(x, w, at, size, terms):
    total = None
    for copies, features in terms:
        for copy in copies:
            copy.wait()
        term = jnp.dot(
            x[at : at + size, features], w[features, :], preferred_element_type=jnp.float32
        )
        total = term if total is None else total + term
    return total


def base_scratch(segments, width, columns):
    rows = segments * SEGMENT_ROWS
    return [
        pltpu.VMEM((rows, width), jnp.bfloat16),
        pltpu.VMEM((width, columns), jnp.bfloat16),
        pltpu.SemaphoreType.DMA((3, max(PIECES, rows // BLOCK + 1))),
    ]


def sent_kernel(first, sizes, column, x_ref, w_ref, *refs):
    outs, (x, w, sems) = refs[: len(sizes)], refs[len(sizes) :]
    work = load_base(first, sum(sizes), column[0], x_ref, w_ref, x, w, sems)
    unit_of = [(out, unit) for out, size in enumerate(sizes) for unit in range(size)]
    for out, size in zip(outs, sizes):
        out[size * WORDS :, :] = jnp.zeros((8, w.shape[1]), jnp.int32)
    for at, size, terms in work:
        product = block_product(x, w, at, size, terms)
        for r in range(0, size, SEGMENT_ROWS):
            out, unit = unit_of[(at + r) // SEGMENT_ROWS]
            encode(product[r : r + SEGMENT_ROWS], outs[out], unit, sizes[out])


def sent_call(tokens, weight, column, columns, first, sizes):
    width = tokens.shape[1]
    rows = sum(sizes) * SEGMENT_ROWS
    return pl.pallas_call(
        functools.partial(sent_kernel, first, sizes),
        in_specs=[SMEM, HBM, HBM],
        out_specs=[VMEM] * len(sizes),
        out_shape=[jax.ShapeDtypeStruct((coded_rows(n), columns), jnp.int32) for n in sizes],
        scratch_shapes=base_scratch(sum(sizes), width, columns),
        compiler_params=params(24),
        cost_estimate=cost(
            2 * rows * width * columns, 2 * rows * width + 2 * width * columns + 4 * rows * columns
        ),
    )(column.reshape(1), tokens, weight)


def add_kernel(chunk, base_ref, *refs):
    coded_refs, o_ref = refs[:-1], refs[-1]
    o_ref[...] = base_ref[...]
    add_decoded(o_ref, chunk, coded_refs)


def add_call(chunk, base, coded):
    return pl.pallas_call(
        functools.partial(add_kernel, chunk),
        in_specs=[VMEM] * (1 + len(coded)),
        out_specs=VMEM,
        out_shape=jax.ShapeDtypeStruct(base.shape, base.dtype),
        compiler_params=params(8),
        cost_estimate=cost(0, 4 * base.size),
    )(base, *coded)


def shrink_into(o_ref, i, table, k, rows_of, buffers, owners, rank):
    for buffer, whose in zip(buffers, owners):

        @pl.when(whose == table[k * ENTRIES])
        def _(buffer=buffer):
            for j in range(MOST):
                _, _, within = segment_of(table, k, j)
                rows = rows_of(j)
                width = rows.shape[1]
                factor = buffer[pl.ds(pl.multiple_of(within * rank, rank), rank), :width]
                o_ref[i, :, j * rank : (j + 1) * rank] = lax.dot_general(
                    rows, factor, (((1,), (1,)), ((), ())), preferred_element_type=jnp.float32
                )


def stages_of(k):
    return range((k + 1) // 2, k + 1)


def own_kernel(n_adapter, rank, table, here, x_ref, w_ref, message, *refs):
    coded_refs, (o_ref, s_ref, kept_ref, x, w, sems, kept_sems) = refs[:-7], refs[-7:]
    work = load_base(0, x.shape[0] // SEGMENT_ROWS, here[2], x_ref, w_ref, x, w, sems)
    keeps = []
    for at, size, terms in work:
        o_ref[at : at + size, :] = block_product(x, w, at, size, terms)
    add_decoded(o_ref, 0, coded_refs)
    for k in range(1, n_adapter):
        for j in range(MOST):
            start, _, _ = segment_of(table, k, j)
            keeps.append(
                pltpu.make_async_copy(
                    x.at[pl.ds(start, SEGMENT_ROWS), :], kept_ref.at[k - 1, j], kept_sems.at[k - 1, j]
                )
            )
            keeps[-1].start()

    def rows_of(j):
        start, _, _ = segment_of(table, 0, j)
        return x[pl.ds(start, SEGMENT_ROWS), :]

    shrink_into(s_ref, 0, table, 0, rows_of, [message], [here[0]], rank)
    for copy in keeps:
        copy.wait()


def own_call(table, here, tokens, weight, message, coded, columns, n_adapter, rank):
    rows, width = tokens.shape
    segments = rows // SEGMENT_ROWS
    return pl.pallas_call(
        functools.partial(own_kernel, n_adapter, rank),
        in_specs=[SMEM, SMEM, HBM, HBM] + [VMEM] * (1 + len(coded)),
        out_specs=[VMEM] * 3,
        out_shape=[
            jax.ShapeDtypeStruct((rows, columns), jnp.float32),
            jax.ShapeDtypeStruct((1, SEGMENT_ROWS, MOST * rank), jnp.float32),
            jax.ShapeDtypeStruct((n_adapter - 1, MOST, SEGMENT_ROWS, width), jnp.bfloat16),
        ],
        scratch_shapes=base_scratch(segments, width, columns)
        + [pltpu.SemaphoreType.DMA((n_adapter - 1, MOST))],
        compiler_params=params(32),
        cost_estimate=cost(
            2 * rows * width * columns, 2 * rows * width + 2 * width * columns + 4 * rows * columns
        ),
    )(table, here, tokens, weight, message, *coded)


def shrink_kernel(k, rank, n_before, table, here, kept_ref, *refs):
    buffers, o_ref = refs[n_before:-1], refs[-1]
    for r in refs[:n_before]:
        o_ref[:1] = r[...]
    rows_of = lambda j: kept_ref[k - 1, j]
    owners = buffer_owners(here, stages_of(k))
    shrink_into(o_ref, n_before, table, k, rows_of, buffers, owners, rank)


def shrink_call(k, table, here, kept, before, buffers, rank):
    width = kept.shape[3]
    n = 1 + len(before)
    return pl.pallas_call(
        functools.partial(shrink_kernel, k, rank, len(before)),
        in_specs=[SMEM, SMEM, VMEM] + [VMEM] * (n - 1 + len(buffers)),
        out_specs=VMEM,
        out_shape=jax.ShapeDtypeStruct((n, SEGMENT_ROWS, MOST * rank), jnp.float32),
        compiler_params=params(16),
        cost_estimate=cost(MOST * 2 * SEGMENT_ROWS * width * 256, 4 * SEGMENT_ROWS * width),
    )(table, here, kept, *before, *buffers)


def fetch_up(up, at, table, k, j, buffers, owners, rank):
    columns = up.shape[2]
    _, _, within = segment_of(table, k, j)
    for buffer, whose in zip(buffers, owners):

        @pl.when(whose == table[k * ENTRIES])
        def _(buffer=buffer):
            first = buffer.shape[1] - columns
            factor = buffer[pl.ds(pl.multiple_of(within * rank, rank), rank), first:]
            up[at, :rank, :] = factor
            up[at, rank:, :] = factor


def up_product(share, j, factor, rank):
    lane = lax.broadcasted_iota(jnp.int32, share.shape, 1)
    other = pltpu.roll(share, rank, 1)
    both = jnp.where((lane < rank) == (j == 0), share, other)
    high = both.astype(jnp.bfloat16).astype(jnp.float32)
    terms = jnp.where(lane < rank, high, both - high).astype(jnp.bfloat16)
    return jnp.dot(terms, factor, preferred_element_type=jnp.float32)


def early_kernel(n_adapter, n_tensor, rank, table, here, *refs):
    n_coded, n_buffers = n_tensor - 1, 2 * n_adapter - 3
    base_ref, coded_refs, refs = refs[0], refs[1 : 1 + n_coded], refs[1 + n_coded :]
    shrinks, refs = refs[: -4 - n_buffers], refs[-4 - n_buffers :]
    buffers, (o_ref, rest_ref, up, total) = refs[:-4], refs[-4:]
    for k in range(n_adapter - 1):
        at = 0 if k == 0 else 2 * stages_of(k)[0] - 1
        to = 2 * k + 1
        owners = buffer_owners(here, stages_of(k))
        for j in range(MOST):
            fetch_up(up, k * MOST + j, table, k, j, buffers[at:to], owners, rank)
    shares = []
    for call in range(len(shrinks) // n_tensor):
        share = shrinks[call * n_tensor][...]
        for i in range(1, n_tensor):
            share = share + shrinks[call * n_tensor + i][...]
        shares += [share[i] for i in range(share.shape[0])]
    total[...] = base_ref[...]
    add_decoded(total, len(CHUNKS) - 1, coded_refs)
    for k in range(n_adapter):
        for j in range(MOST):
            start, used, _ = segment_of(table, k, j)
            value = total[pl.ds(start, SEGMENT_ROWS), :]
            if k == n_adapter - 1:
                rest_ref[j] = value
                continue
            lora = up_product(shares[k], j, up[k * MOST + j], rank)

            @pl.when(used)
            def _(start=start, value=value, lora=lora):
                o_ref[pl.ds(start, SEGMENT_ROWS), :] = (value + adapter_scale * lora).astype(
                    jnp.bfloat16
                )


def early(n_adapter, n_tensor, table, here, base, coded, shrinks, buffers, rank):
    rows, columns = base.shape
    return pl.pallas_call(
        functools.partial(early_kernel, n_adapter, n_tensor, rank),
        in_specs=[SMEM] * 2 + [VMEM] * (1 + len(coded) + len(shrinks) + len(buffers)),
        out_specs=[VMEM, VMEM],
        out_shape=[
            jax.ShapeDtypeStruct((rows, columns), jnp.bfloat16),
            jax.ShapeDtypeStruct((MOST, SEGMENT_ROWS, columns), jnp.float32),
        ],
        scratch_shapes=[
            pltpu.VMEM(((n_adapter - 1) * MOST, 2 * rank, columns), jnp.bfloat16),
            pltpu.VMEM((rows, columns), jnp.float32),
        ],
        compiler_params=params(16),
        cost_estimate=cost(6 * rows * rank * columns, (4 * n_tensor + 2) * rows * columns),
    )(table, here, base, *coded, *shrinks, *buffers)


def late_kernel(k, n_tensor, rank, table, here, *refs):
    rest_ref, shrinks, refs = refs[0], refs[1 : 1 + n_tensor], refs[1 + n_tensor :]
    buffers, (_, o_ref, up, out, sems) = refs[:-5], refs[-5:]
    owners = buffer_owners(here, stages_of(k))
    share = shrinks[0][0]
    for r in shrinks[1:]:
        share = share + r[0]
    stores = []
    for j in range(MOST):
        fetch_up(up, j, table, k, j, buffers, owners, rank)
        start, used, _ = segment_of(table, k, j)
        lora = up_product(share, j, up[j], rank)
        out[j] = (rest_ref[j] + adapter_scale * lora).astype(jnp.bfloat16)
        store = pltpu.make_async_copy(out.at[j], o_ref.at[pl.ds(start, SEGMENT_ROWS), :], sems.at[j])
        pl.when(used)(store.start)
        stores.append((used, store))
    for used, store in stores:
        pl.when(used)(store.wait)


def late(k, n_tensor, table, here, rest, shrinks, buffers, value, rank):
    rows, columns = value.shape
    return pl.pallas_call(
        functools.partial(late_kernel, k, n_tensor, rank),
        in_specs=[SMEM] * 2 + [VMEM] * (1 + len(shrinks) + len(buffers)) + [ANY],
        out_specs=ANY,
        out_shape=jax.ShapeDtypeStruct((rows, columns), jnp.bfloat16),
        scratch_shapes=[
            pltpu.VMEM((MOST, 2 * rank, columns), jnp.bfloat16),
            pltpu.VMEM((MOST, SEGMENT_ROWS, columns), jnp.bfloat16),
            pltpu.SemaphoreType.DMA((MOST,)),
        ],
        input_output_aliases={3 + len(shrinks) + len(buffers): 0},
        compiler_params=params(8),
        cost_estimate=cost(
            6 * MOST * SEGMENT_ROWS * rank * columns, 8 * MOST * SEGMENT_ROWS * columns
        ),
    )(table, here, rest, *shrinks, *buffers, value)


def after(array, *others):
    return lax.optimization_barrier((array, *others))[0]


def on_device(
    tokens, value_weight, adapter_down_weight, adapter_up_weight, row_adapter_index, adapter_slot_of
):
    rows, width = tokens.shape
    per_device, _, rank = adapter_down_weight.shape
    n_adapter = lax.axis_size("adapter")
    n_tensor = lax.axis_size("tensor")
    me_t = lax.axis_index("tensor")
    here = jnp.stack([lax.axis_index("adapter"), lax.axis_index("dp"), me_t])
    columns = value_weight.shape[1] // n_tensor

    def swap_tensor(array, step):
        pairs = [(i, (i + step) % n_tensor) for i in range(n_tensor)]
        return lax.ppermute(array, "tensor", pairs)

    def along_line(array, stage):
        up = [(2 * i, 2 * (i + 1)) for i in range(stage - 1, n_adapter - 1)]
        down = [(2 * i + 1, 2 * (i - 1) + 1) for i in range(1, n_adapter - stage + 1)]
        return lax.ppermute(array, ("adapter", "dp"), up + down)

    def swap_cores(array):
        return lax.ppermute(array, "dp", [(0, 1), (1, 0)])

    down = jnp.swapaxes(adapter_down_weight, 1, 2).reshape(per_device * rank, width)
    up = adapter_up_weight.reshape(per_device * rank, value_weight.shape[1])
    tokens, value_weight, down, up = (
        pltpu.with_memory_space_constraint(a, pltpu.HBM) for a in (tokens, value_weight, down, up)
    )
    message = message_call(here, down, up, columns)
    table = table_call(here, row_adapter_index, adapter_slot_of, n_adapter, per_device)

    buffers, shrinks = [[message]], []

    def buffers_of(stages):
        return [b for stage in stages for b in buffers[stage]]

    def add_shrink(mine):
        shrinks.extend([mine] + [swap_tensor(mine, step) for step in range(1, n_tensor)])

    held = along_line(message, 1)
    others = range(1, n_tensor)

    def sent_for(step, chunks):
        sizes = [number for _, number in chunks]
        target = (me_t + step) % n_tensor
        return sent_call(tokens, value_weight, target, columns, chunks[0][0], sizes)

    parts = [[sent_for(step, CHUNKS[:1])[0] for step in others]]
    rest_parts = [sent_for(step, CHUNKS[1:]) for step in others]
    parts += [[p[i] for p in rest_parts] for i in range(len(CHUNKS) - 1)]
    sent = [[swap_tensor(p, step) for step, p in zip(others, parts[0])]]
    last = n_adapter - 1
    done = [table] + [p for group in parts for p in group] + sent[0]
    before = None
    for stage in range(1, last):
        came = after(held, *done)
        held = along_line(came, stage + 1)
        if stage < len(CHUNKS):
            sent.append([swap_tensor(after(p, came), step) for step, p in zip(others, parts[stage])])
        if stage == 1:
            base, before, kept = own_call(
                after(table, came), here, tokens, value_weight, message, sent[0], columns, n_adapter, rank
            )
            add_shrink(before)
            done = sent[1] + [base]
        else:
            if stage == 2:
                base = add_call(1, after(base, came), sent[1])
            before = shrink_call(
                stage - 1, table, here, after(kept, came), [], buffers_of(stages_of(stage - 1)), rank
            )
            if stage < last - 1:
                add_shrink(before)
            done = []
        buffers.append([came, swap_cores(came)])
    merged = shrink_call(
        last - 1, table, here, kept, [before], buffers_of(stages_of(last - 1)), rank
    )
    add_shrink(merged)
    value, remaining = early(
        n_adapter,
        n_tensor,
        table,
        here,
        base,
        sent[2],
        shrinks,
        buffers_of(range(last)),
        rank,
    )
    came = after(held, *shrinks, *sent[2])
    buffers.append([came, swap_cores(came)])
    add_shrink(shrink_call(last, table, here, after(kept, value), [], buffers_of(stages_of(last)), rank))
    return late(
        last,
        n_tensor,
        table,
        here,
        remaining,
        shrinks[-n_tensor:],
        buffers_of(stages_of(last)),
        value,
        rank,
    )


def solution(mesh):
    return jax.shard_map(
        on_device,
        mesh=mesh,
        in_specs=(
            P(("groups", "adapter", "dp"), "tensor"),
            P("tensor", None),
            P(("groups", "adapter"), "tensor", None),
            P(("groups", "adapter"), None, None),
            P(("groups", "adapter", "dp")),
            P("groups"),
        ),
        out_specs=P(("groups", "adapter", "dp"), "tensor"),
        check_vma=False,
    )
```

```python
import functools

import jax
import jax.numpy as jnp
from jax import lax
from jax.experimental import pallas as pl
from jax.experimental.pallas import tpu as pltpu
from jax.sharding import PartitionSpec as P

SEGMENT_ROWS = 128
adapter_scale = 0.5
MOST = 2
BLOCK = 256
PIECES = 4
CHUNKS = ((6, 2), (0, 6))
ENTRIES = 8
MIDDLE = 1.5 * 2.0**23


def cost(flops, moved):
    return pl.CostEstimate(flops=int(flops), bytes_accessed=int(moved), transcendentals=0)


def params(mib):
    return pltpu.CompilerParams(vmem_limit_bytes=mib * 2**20)


ANY = pl.BlockSpec(memory_space=pl.ANY)
HBM = pl.BlockSpec(memory_space=pltpu.HBM)
SMEM = pl.BlockSpec(memory_space=pltpu.SMEM)
VMEM = pl.BlockSpec(memory_space=pltpu.VMEM)


def arrival_order(me, n_adapter):
    order = [me] + [jnp.int32(-1)] * (n_adapter - 1)
    count = jnp.int32(1)
    for distance in range(1, n_adapter):
        for other in (me - distance, me + distance):
            valid = (other >= 0) & (other < n_adapter)
            order = [jnp.where(valid & (count == k), other, o) for k, o in enumerate(order)]
            count = count + valid.astype(jnp.int32)
    return order


def buffer_tags(here, stages, per_device):
    tags = []
    for stage in stages:
        for i in range(per_device):
            toward = jnp.where(here[1] == 0, -stage, stage)
            tags += [(here[0] + toward, i), (here[0] - toward, i)] if stage > 0 else [(here[0], i)]
    return tags


def segment_of(table, k, j):
    seg = table[k * ENTRIES + 1 + 2 * j]
    start = pl.multiple_of(jnp.maximum(seg, 0) * SEGMENT_ROWS, SEGMENT_ROWS)
    return start, seg >= 0, table[k * ENTRIES + 2 + 2 * j]


def message_kernel(here, down_ref, up_ref, *refs):
    outs, sems = refs[:-1], refs[-1]
    rank = outs[0].shape[0]
    width = down_ref.shape[1]
    columns = outs[0].shape[1] - width
    start = pl.multiple_of(here[2] * columns, columns)
    copies = []
    for i, out in enumerate(outs):
        rows = pl.ds(i * rank, rank)
        copies += [
            pltpu.make_async_copy(down_ref.at[rows, :], out.at[:, pl.ds(0, width)], sems.at[0, i]),
            pltpu.make_async_copy(
                up_ref.at[rows, pl.ds(start, columns)], out.at[:, pl.ds(width, columns)], sems.at[1, i]
            ),
        ]
    for copy in copies:
        copy.start()
    for copy in copies:
        copy.wait()


def message_call(here, down, up, columns, per_device):
    rows, width = down.shape
    shape = jax.ShapeDtypeStruct((rows // per_device, width + columns), jnp.bfloat16)
    return pl.pallas_call(
        message_kernel,
        in_specs=[SMEM, HBM, HBM],
        out_specs=[VMEM] * per_device,
        out_shape=[shape] * per_device,
        scratch_shapes=[pltpu.SemaphoreType.DMA((2, per_device))],
        compiler_params=params(8),
        cost_estimate=cost(0, 4 * rows * (width + columns)),
    )(here, down, up)


def table_kernel(n_adapter, per_device, here, ids, slots, table):
    seg_dev = ids.shape[0] // SEGMENT_ROWS
    used = [slots[ids[s * SEGMENT_ROWS]] for s in range(seg_dev)]
    for k, owner in enumerate(arrival_order(here[0], n_adapter)):
        table[k * ENTRIES] = owner
        found, place = [jnp.int32(-1)] * MOST, [jnp.int32(0)] * MOST
        count = jnp.int32(0)
        for s, slot in enumerate(used):
            within = slot - owner * per_device
            hit = (within >= 0) & (within < per_device)
            for j in range(MOST):
                take = hit & (count == j)
                found[j] = jnp.where(take, s, found[j])
                place[j] = jnp.where(take, within, place[j])
            count = count + hit.astype(jnp.int32)
        for j in range(MOST):
            table[k * ENTRIES + 1 + 2 * j] = found[j]
            table[k * ENTRIES + 2 + 2 * j] = place[j]


def table_call(here, ids, slots, n_adapter, per_device):
    return pl.pallas_call(
        functools.partial(table_kernel, n_adapter, per_device),
        in_specs=[SMEM, SMEM, SMEM],
        out_specs=SMEM,
        out_shape=jax.ShapeDtypeStruct((n_adapter * ENTRIES,), jnp.int32),
        cost_estimate=cost(0, 4 * ids.shape[0]),
    )(here, ids, slots)


def diagonal():
    shape = (SEGMENT_ROWS, SEGMENT_ROWS)
    return lax.broadcasted_iota(jnp.int32, shape, 0) == lax.broadcasted_iota(jnp.int32, shape, 1)


GROUP = SEGMENT_ROWS // 8
WORDS = 5 * GROUP


def coded_rows(segments):
    return segments * WORDS + 8


def encode(values, o_ref, unit, units):
    largest = jnp.maximum(jnp.max(jnp.abs(values), axis=1, keepdims=True), 2.0**-100)
    power = jnp.floor(jnp.log2(largest))
    whole = (values * jnp.exp2(18.0 - power) + MIDDLE).astype(jnp.int32) - int(MIDDLE)
    whole = jnp.minimum(whole, 2**19 - 1)
    v = [whole[i * GROUP : (i + 1) * GROUP] for i in range(8)]
    over = [
        v[5] & 0xFFF,
        ((v[5] >> 12) & 0xFF) | ((v[6] & 0xF) << 8),
        (v[6] >> 4) & 0xFFF,
        ((v[6] >> 16) & 0xF) | ((v[7] & 0xFF) << 4),
        v[7] >> 8,
    ]
    for i in range(5):
        o_ref[unit * WORDS + i * GROUP : unit * WORDS + (i + 1) * GROUP, :] = (v[i] & 0xFFFFF) | (
            over[i] << 20
        )
    row = jnp.sum(jnp.where(diagonal(), power, 0.0), axis=0, keepdims=True)
    o_ref[units * WORDS + unit : units * WORDS + unit + 1, :SEGMENT_ROWS] = row.astype(jnp.int32)


def decode(ref, unit, units):
    w = [ref[unit * WORDS + i * GROUP : unit * WORDS + (i + 1) * GROUP, :] for i in range(5)]
    v = [(x << 12) >> 12 for x in w]
    v.append(((w[0] >> 20) & 0xFFF) | (((w[1] << 4) >> 24) << 12))
    v.append(((w[1] >> 28) & 0xF) | (((w[2] >> 20) & 0xFFF) << 4) | (((w[3] << 8) >> 28) << 16))
    v.append(((w[3] >> 24) & 0xFF) | ((w[4] >> 20) << 8))
    row = ref[units * WORDS + unit : units * WORDS + unit + 1, :SEGMENT_ROWS].astype(jnp.float32)
    power = jnp.sum(jnp.where(diagonal(), row, 0.0), axis=1, keepdims=True)
    return jnp.concatenate(v, axis=0).astype(jnp.float32) * jnp.exp2(power - 18.0)


def add_decoded(sums, chunk, refs):
    first, number = CHUNKS[chunk]
    for unit in range(number):
        rows = pl.ds((first + unit) * SEGMENT_ROWS, SEGMENT_ROWS)
        value = sums[rows, :]
        for ref in refs:
            value = value + decode(ref, unit, number)
        sums[rows, :] = value


def load_base(first, segments, column, x_ref, w_ref, x, w, sems):
    width, columns = w.shape
    rows = segments * SEGMENT_ROWS
    start = pl.multiple_of(column * columns, columns)
    depth = width // PIECES
    blocks = [(r, min(BLOCK, rows - r)) for r in range(0, rows, BLOCK)]

    def x_copy(at, size, features, sem):
        return pltpu.make_async_copy(
            x_ref.at[pl.ds(first * SEGMENT_ROWS + at, size), features],
            x.at[pl.ds(at, size), features],
            sem,
        )

    work = []
    for i, (at, size) in enumerate(blocks):
        terms = []
        if i == 0:
            for p in range(PIECES):
                features = pl.ds(p * depth, depth)
                copies = (
                    pltpu.make_async_copy(
                        w_ref.at[features, pl.ds(start, columns)], w.at[features, :], sems.at[0, p]
                    ),
                    x_copy(0, size, features, sems.at[1, p]),
                )
                terms.append((copies, slice(p * depth, (p + 1) * depth)))
        else:
            terms.append(((x_copy(at, size, slice(None), sems.at[2, i]),), slice(None)))
        work.append((at, size, terms))
    for _, _, terms in work:
        for copies, _ in terms:
            for copy in copies:
                copy.start()
    return work


def block_product(x, w, at, size, terms):
    total = None
    for copies, features in terms:
        for copy in copies:
            copy.wait()
        term = jnp.dot(
            x[at : at + size, features], w[features, :], preferred_element_type=jnp.float32
        )
        total = term if total is None else total + term
    return total


def base_scratch(segments, width, columns):
    rows = segments * SEGMENT_ROWS
    return [
        pltpu.VMEM((rows, width), jnp.bfloat16),
        pltpu.VMEM((width, columns), jnp.bfloat16),
        pltpu.SemaphoreType.DMA((3, max(PIECES, rows // BLOCK + 1))),
    ]


def sent_kernel(first, sizes, column, x_ref, w_ref, *refs):
    outs, (x, w, sems) = refs[: len(sizes)], refs[len(sizes) :]
    work = load_base(first, sum(sizes), column[0], x_ref, w_ref, x, w, sems)
    unit_of = [(out, unit) for out, size in enumerate(sizes) for unit in range(size)]
    for out, size in zip(outs, sizes):
        out[size * WORDS :, :] = jnp.zeros((8, w.shape[1]), jnp.int32)
    for at, size, terms in work:
        product = block_product(x, w, at, size, terms)
        for r in range(0, size, SEGMENT_ROWS):
            out, unit = unit_of[(at + r) // SEGMENT_ROWS]
            encode(product[r : r + SEGMENT_ROWS], outs[out], unit, sizes[out])


def sent_call(tokens, weight, column, columns, first, sizes):
    width = tokens.shape[1]
    rows = sum(sizes) * SEGMENT_ROWS
    return pl.pallas_call(
        functools.partial(sent_kernel, first, sizes),
        in_specs=[SMEM, HBM, HBM],
        out_specs=[VMEM] * len(sizes),
        out_shape=[jax.ShapeDtypeStruct((coded_rows(n), columns), jnp.int32) for n in sizes],
        scratch_shapes=base_scratch(sum(sizes), width, columns),
        compiler_params=params(24),
        cost_estimate=cost(
            2 * rows * width * columns, 2 * rows * width + 2 * width * columns + 4 * rows * columns
        ),
    )(column.reshape(1), tokens, weight)


def add_kernel(chunk, base_ref, *refs):
    coded_refs, o_ref = refs[:-1], refs[-1]
    o_ref[...] = base_ref[...]
    add_decoded(o_ref, chunk, coded_refs)


def add_call(chunk, base, coded):
    return pl.pallas_call(
        functools.partial(add_kernel, chunk),
        in_specs=[VMEM] * (1 + len(coded)),
        out_specs=VMEM,
        out_shape=jax.ShapeDtypeStruct(base.shape, base.dtype),
        compiler_params=params(8),
        cost_estimate=cost(20000 * base.size, 12 * base.size),
    )(base, *coded)


def shrink_into(o_ref, at, table, k, rows_of, buffers, tags, rank):
    for j in range(MOST):
        _, _, within = segment_of(table, k, j)
        for buffer, (whose, i) in zip(buffers, tags):

            @pl.when((whose == table[k * ENTRIES]) & (within == i))
            def _(j=j, buffer=buffer):
                rows = rows_of(j)
                o_ref[at, :, j * rank : (j + 1) * rank] = lax.dot_general(
                    rows,
                    buffer[:, : rows.shape[1]],
                    (((1,), (1,)), ((), ())),
                    preferred_element_type=jnp.float32,
                )


def stages_of(k):
    return range((k + 1) // 2, k + 1)


def own_kernel(n_adapter, per_device, rank, table, here, x_ref, w_ref, *refs):
    messages, refs = refs[:per_device], refs[per_device:]
    coded_refs, (o_ref, s_ref, kept_ref, x, w, sems, kept_sems) = refs[:-7], refs[-7:]
    work = load_base(0, x.shape[0] // SEGMENT_ROWS, here[2], x_ref, w_ref, x, w, sems)
    keeps = []
    for at, size, terms in work:
        o_ref[at : at + size, :] = block_product(x, w, at, size, terms)
    add_decoded(o_ref, 0, coded_refs)
    for k in range(1, n_adapter):
        for j in range(MOST):
            start, _, _ = segment_of(table, k, j)
            keeps.append(
                pltpu.make_async_copy(
                    x.at[pl.ds(start, SEGMENT_ROWS), :], kept_ref.at[k - 1, j], kept_sems.at[k - 1, j]
                )
            )
            keeps[-1].start()

    def rows_of(j):
        start, _, _ = segment_of(table, 0, j)
        return x[pl.ds(start, SEGMENT_ROWS), :]

    shrink_into(s_ref, 0, table, 0, rows_of, messages, buffer_tags(here, [0], per_device), rank)
    for copy in keeps:
        copy.wait()


def own_call(table, here, tokens, weight, messages, coded, columns, n_adapter):
    rows, width = tokens.shape
    segments = rows // SEGMENT_ROWS
    per_device, rank = len(messages), messages[0].shape[0]
    return pl.pallas_call(
        functools.partial(own_kernel, n_adapter, per_device, rank),
        in_specs=[SMEM, SMEM, HBM, HBM] + [VMEM] * (per_device + len(coded)),
        out_specs=[VMEM] * 3,
        out_shape=[
            jax.ShapeDtypeStruct((rows, columns), jnp.float32),
            jax.ShapeDtypeStruct((1, SEGMENT_ROWS, MOST * rank), jnp.float32),
            jax.ShapeDtypeStruct((n_adapter - 1, MOST, SEGMENT_ROWS, width), jnp.bfloat16),
        ],
        scratch_shapes=base_scratch(segments, width, columns)
        + [pltpu.SemaphoreType.DMA((n_adapter - 1, MOST))],
        compiler_params=params(32),
        cost_estimate=cost(
            2 * rows * width * columns, 2 * rows * width + 2 * width * columns + 4 * rows * columns
        ),
    )(table, here, tokens, weight, *messages, *coded)


def shrink_kernel(k, per_device, rank, at, table, here, kept_ref, *refs):
    buffers, o_ref = refs[1 if at else 0 : -1], refs[-1]
    if at:
        o_ref[:at] = refs[0][...]
    tags = buffer_tags(here, stages_of(k), per_device)
    shrink_into(o_ref, at, table, k, lambda j: kept_ref[k - 1, j], buffers, tags, rank)


def shrink_call(k, table, here, kept, before, buffers, per_device, rank):
    width = kept.shape[3]
    at = sum(b.shape[0] for b in before)
    return pl.pallas_call(
        functools.partial(shrink_kernel, k, per_device, rank, at),
        in_specs=[SMEM, SMEM, VMEM] + [VMEM] * (len(before) + len(buffers)),
        out_specs=VMEM,
        out_shape=jax.ShapeDtypeStruct((at + 1, SEGMENT_ROWS, MOST * rank), jnp.float32),
        compiler_params=params(16),
        cost_estimate=cost(MOST * 2 * SEGMENT_ROWS * width * 256, 4 * SEGMENT_ROWS * width),
    )(table, here, kept, *before, *buffers)


def fetch_up(up, at, table, k, j, buffers, tags, rank):
    columns = up.shape[2]
    _, _, within = segment_of(table, k, j)
    for buffer, (whose, i) in zip(buffers, tags):

        @pl.when((whose == table[k * ENTRIES]) & (within == i))
        def _(buffer=buffer):
            factor = buffer[:, buffer.shape[1] - columns :]
            up[at, :rank, :] = factor
            up[at, rank:, :] = factor


def up_product(share, j, factor, rank):
    lane = lax.broadcasted_iota(jnp.int32, share.shape, 1)
    other = pltpu.roll(share, rank, 1)
    both = jnp.where((lane < rank) == (j == 0), share, other)
    high = both.astype(jnp.bfloat16).astype(jnp.float32)
    terms = jnp.where(lane < rank, high, both - high).astype(jnp.bfloat16)
    return jnp.dot(terms, factor, preferred_element_type=jnp.float32)


def early_kernel(n_adapter, n_tensor, per_device, rank, n_shrinks, table, here, *refs):
    base_ref, refs = refs[0], refs[1:]
    shrinks, refs = refs[:n_shrinks], refs[n_shrinks:]
    buffers, (o_ref, rest_ref, up) = refs[:-3], refs[-3:]
    tags = buffer_tags(here, range(n_adapter - 1), per_device)
    for k in range(n_adapter - 1):
        at = per_device * (0 if k == 0 else 2 * stages_of(k)[0] - 1)
        to = per_device * (2 * k + 1)
        for j in range(MOST):
            fetch_up(up, k * MOST + j, table, k, j, buffers[at:to], tags[at:to], rank)
    shares = []
    for call in range(0, n_shrinks, n_tensor):
        share = shrinks[call][...]
        for r in shrinks[call + 1 : call + n_tensor]:
            share = share + r[...]
        shares += [share[i] for i in range(share.shape[0])]
    for k in range(n_adapter):
        for j in range(MOST):
            start, used, _ = segment_of(table, k, j)
            value = base_ref[pl.ds(start, SEGMENT_ROWS), :]
            if k == n_adapter - 1:
                rest_ref[j] = value
                continue
            lora = up_product(shares[k], j, up[k * MOST + j], rank)

            @pl.when(used)
            def _(start=start, value=value, lora=lora):
                o_ref[pl.ds(start, SEGMENT_ROWS), :] = (value + adapter_scale * lora).astype(
                    jnp.bfloat16
                )


def early(n_adapter, n_tensor, table, here, base, shrinks, buffers, per_device, rank):
    rows, columns = base.shape
    return pl.pallas_call(
        functools.partial(early_kernel, n_adapter, n_tensor, per_device, rank, len(shrinks)),
        in_specs=[SMEM] * 2 + [VMEM] * (1 + len(shrinks) + len(buffers)),
        out_specs=[VMEM, VMEM],
        out_shape=[
            jax.ShapeDtypeStruct((rows, columns), jnp.bfloat16),
            jax.ShapeDtypeStruct((MOST, SEGMENT_ROWS, columns), jnp.float32),
        ],
        scratch_shapes=[
            pltpu.VMEM(((n_adapter - 1) * MOST, 2 * rank, columns), jnp.bfloat16),
        ],
        compiler_params=params(16),
        cost_estimate=cost(6 * rows * rank * columns, (4 * n_tensor + 2) * rows * columns),
    )(table, here, base, *shrinks, *buffers)


def late_kernel(k, n_tensor, per_device, rank, table, here, *refs):
    rest_ref, shrinks, refs = refs[0], refs[1 : 1 + n_tensor], refs[1 + n_tensor :]
    buffers, (_, o_ref, up, out, sems) = refs[:-5], refs[-5:]
    tags = buffer_tags(here, stages_of(k), per_device)
    share = shrinks[0][0]
    for r in shrinks[1:]:
        share = share + r[0]
    stores = []
    for j in range(MOST):
        fetch_up(up, j, table, k, j, buffers, tags, rank)
        start, used, _ = segment_of(table, k, j)
        lora = up_product(share, j, up[j], rank)
        out[j] = (rest_ref[j] + adapter_scale * lora).astype(jnp.bfloat16)
        store = pltpu.make_async_copy(out.at[j], o_ref.at[pl.ds(start, SEGMENT_ROWS), :], sems.at[j])
        pl.when(used)(store.start)
        stores.append((used, store))
    for used, store in stores:
        pl.when(used)(store.wait)


def late(k, n_tensor, table, here, rest, shrinks, buffers, value, per_device, rank):
    rows, columns = value.shape
    return pl.pallas_call(
        functools.partial(late_kernel, k, n_tensor, per_device, rank),
        in_specs=[SMEM] * 2 + [VMEM] * (1 + len(shrinks) + len(buffers)) + [ANY],
        out_specs=ANY,
        out_shape=jax.ShapeDtypeStruct((rows, columns), jnp.bfloat16),
        scratch_shapes=[
            pltpu.VMEM((MOST, 2 * rank, columns), jnp.bfloat16),
            pltpu.VMEM((MOST, SEGMENT_ROWS, columns), jnp.bfloat16),
            pltpu.SemaphoreType.DMA((MOST,)),
        ],
        input_output_aliases={3 + len(shrinks) + len(buffers): 0},
        compiler_params=params(8),
        cost_estimate=cost(
            6 * MOST * SEGMENT_ROWS * rank * columns, 8 * MOST * SEGMENT_ROWS * columns
        ),
    )(table, here, rest, *shrinks, *buffers, value)


def after(array, *others):
    return lax.optimization_barrier((array, *others))[0]


def on_device(
    tokens, value_weight, adapter_down_weight, adapter_up_weight, row_adapter_index, adapter_slot_of
):
    rows, width = tokens.shape
    per_device, _, rank = adapter_down_weight.shape
    n_adapter = lax.axis_size("adapter")
    n_tensor = lax.axis_size("tensor")
    me_t = lax.axis_index("tensor")
    here = jnp.stack([lax.axis_index("adapter"), lax.axis_index("dp"), me_t])
    columns = value_weight.shape[1] // n_tensor

    def swap_tensor(array, step):
        pairs = [(i, (i + step) % n_tensor) for i in range(n_tensor)]
        return lax.ppermute(array, "tensor", pairs)

    def along_line(array, stage):
        up = [(2 * z, 2 * (z + 1)) for z in range(stage - 1, n_adapter - 1)]
        down = [(2 * z + 1, 2 * (z - 1) + 1) for z in range(1, n_adapter - stage + 1)]
        return lax.ppermute(array, ("adapter", "dp"), up + down)

    def swap_cores(array):
        return lax.ppermute(array, "dp", [(0, 1), (1, 0)])

    down = jnp.swapaxes(adapter_down_weight, 1, 2).reshape(per_device * rank, width)
    up = adapter_up_weight.reshape(per_device * rank, value_weight.shape[1])
    tokens, value_weight, down, up = (
        pltpu.with_memory_space_constraint(a, pltpu.HBM) for a in (tokens, value_weight, down, up)
    )
    messages = message_call(here, down, up, columns, per_device)
    table = table_call(here, row_adapter_index, adapter_slot_of, n_adapter, per_device)
    buffers, shrinks = [[[m] for m in messages]], []

    def buffers_of(stages):
        return [b for stage in stages for pair in buffers[stage] for b in pair]

    def add_shrink(mine):
        shrinks.extend([mine] + [swap_tensor(mine, step) for step in range(1, n_tensor)])

    def shrink(k, kept, before=()):
        mine = buffers_of(stages_of(k))
        return shrink_call(k, table, here, kept, list(before), mine, per_device, rank)

    others = range(1, n_tensor)

    def sent_for(step, chunks, *ahead):
        sizes = [number for _, number in chunks]
        target = after((me_t + step) % n_tensor, *ahead)
        return sent_call(tokens, value_weight, target, columns, chunks[0][0], sizes)

    def send(parts, *ahead):
        return [swap_tensor(after(p, *ahead), step) for step, p in zip(others, parts)]

    last = n_adapter - 1
    held = [along_line(m, 1) for m in messages]
    part_a = [sent_for(step, CHUNKS[:1])[0] for step in others]
    sent = [send(part_a)]
    part_b = [sent_for(step, CHUNKS[1:], held[0], *part_a)[0] for step in others]
    sent.append(send(part_b))
    for stage in range(1, last):
        came = held
        if stage == 1:
            came = [after(held[0], *part_a)] + [after(h, *part_b, *sent[0]) for h in held[1:]]
        if stage == 2:
            came = held[:1] + [after(h, base) for h in held[1:]]
        held = [along_line(c, stage + 1) for c in came]
        swapped = [swap_cores(after(c, base) if stage == 2 else c) for c in came]
        buffers.append([list(pair) for pair in zip(came, swapped)])
        if stage == 1:
            base, before, kept = own_call(
                after(table, held[0]),
                here,
                tokens,
                value_weight,
                messages,
                sent[0],
                columns,
                n_adapter,
            )
        else:
            ready = kept
            if stage == 2:
                base = add_call(1, after(base, held[0], *came), sent[1])
                ready = after(kept, base, *held[1:])
            before = shrink(stage - 1, ready, [before])
    merged = shrink(last - 1, kept, [before])
    add_shrink(merged)
    value, remaining = early(
        n_adapter,
        n_tensor,
        table,
        here,
        base,
        shrinks,
        buffers_of(range(last)),
        per_device,
        rank,
    )
    buffers.append([[h, swap_cores(h)] for h in held])
    add_shrink(shrink(last, kept))
    return late(
        last,
        n_tensor,
        table,
        here,
        remaining,
        shrinks[-n_tensor:],
        buffers_of(stages_of(last)),
        value,
        per_device,
        rank,
    )


def solution(mesh):
    return jax.shard_map(
        on_device,
        mesh=mesh,
        in_specs=(
            P(("groups", "adapter", "dp"), "tensor"),
            P("tensor", None),
            P(("groups", "adapter"), "tensor", None),
            P(("groups", "adapter"), None, None),
            P(("groups", "adapter", "dp")),
            P("groups"),
        ),
        out_specs=P(("groups", "adapter", "dp"), "tensor"),
        check_vma=False,
    )
```

```python
import functools

import jax
import jax.numpy as jnp
from jax import lax
from jax.experimental import pallas as pl
from jax.experimental.pallas import tpu as pltpu
from jax.sharding import PartitionSpec as P

SEGMENT_ROWS = 128
adapter_scale = 0.5
MOST = 2
BLOCK = 256
PIECES = 4
CHUNKS = ((6, 2), (0, 4), (4, 2))
ENTRIES = 8
MIDDLE = 1.5 * 2.0**23


def cost(flops, moved):
    return pl.CostEstimate(flops=int(flops), bytes_accessed=int(moved), transcendentals=0)


def params(mib):
    return pltpu.CompilerParams(vmem_limit_bytes=mib * 2**20)


ANY = pl.BlockSpec(memory_space=pl.ANY)
HBM = pl.BlockSpec(memory_space=pltpu.HBM)
SMEM = pl.BlockSpec(memory_space=pltpu.SMEM)
VMEM = pl.BlockSpec(memory_space=pltpu.VMEM)


def arrival_order(me, n_adapter):
    order = [me] + [jnp.int32(-1)] * (n_adapter - 1)
    count = jnp.int32(1)
    for distance in range(1, n_adapter):
        for other in (me - distance, me + distance):
            valid = (other >= 0) & (other < n_adapter)
            order = [jnp.where(valid & (count == k), other, o) for k, o in enumerate(order)]
            count = count + valid.astype(jnp.int32)
    return order


def buffer_owners(here, stages):
    owners = []
    for stage in stages:
        toward = jnp.where(here[1] == 0, -stage, stage)
        owners += [here[0] + toward, here[0] - toward] if stage > 0 else [here[0]]
    return owners


def segment_of(table, k, j):
    seg = table[k * ENTRIES + 1 + 2 * j]
    start = pl.multiple_of(jnp.maximum(seg, 0) * SEGMENT_ROWS, SEGMENT_ROWS)
    return start, seg >= 0, table[k * ENTRIES + 2 + 2 * j]


def message_kernel(down_ref, up_ref, o_ref, sems):
    width = down_ref.shape[1]
    columns = o_ref.shape[1] - width
    start = pl.multiple_of(lax.axis_index("tensor") * columns, columns)
    rows = down_ref.shape[0] // PIECES
    copies = [
        pltpu.make_async_copy(
            down_ref.at[pl.ds(p * rows, rows), :],
            o_ref.at[pl.ds(p * rows, rows), pl.ds(0, width)],
            sems.at[p],
        )
        for p in range(PIECES)
    ]
    copies.append(
        pltpu.make_async_copy(
            up_ref.at[:, pl.ds(start, columns)], o_ref.at[:, pl.ds(width, columns)], sems.at[PIECES]
        )
    )
    for copy in copies:
        copy.start()
    for copy in copies:
        copy.wait()


def message_call(down, up, columns):
    rows, width = down.shape
    return pl.pallas_call(
        message_kernel,
        in_specs=[HBM, HBM],
        out_specs=VMEM,
        out_shape=jax.ShapeDtypeStruct((rows, width + columns), jnp.bfloat16),
        scratch_shapes=[pltpu.SemaphoreType.DMA((PIECES + 1,))],
        compiler_params=params(8),
        cost_estimate=cost(0, 4 * rows * (width + columns)),
    )(down, up)


def table_kernel(n_adapter, per_device, here, ids, slots, table):
    seg_dev = ids.shape[0] // SEGMENT_ROWS
    used = [slots[ids[s * SEGMENT_ROWS]] for s in range(seg_dev)]
    for k, owner in enumerate(arrival_order(here[0], n_adapter)):
        table[k * ENTRIES] = owner
        found, place = [jnp.int32(-1)] * MOST, [jnp.int32(0)] * MOST
        count = jnp.int32(0)
        for s, slot in enumerate(used):
            within = slot - owner * per_device
            hit = (within >= 0) & (within < per_device)
            for j in range(MOST):
                take = hit & (count == j)
                found[j] = jnp.where(take, s, found[j])
                place[j] = jnp.where(take, within, place[j])
            count = count + hit.astype(jnp.int32)
        for j in range(MOST):
            table[k * ENTRIES + 1 + 2 * j] = found[j]
            table[k * ENTRIES + 2 + 2 * j] = place[j]


def table_call(here, ids, slots, n_adapter, per_device):
    return pl.pallas_call(
        functools.partial(table_kernel, n_adapter, per_device),
        in_specs=[SMEM, SMEM, SMEM],
        out_specs=SMEM,
        out_shape=jax.ShapeDtypeStruct((n_adapter * ENTRIES,), jnp.int32),
        cost_estimate=cost(0, 4 * ids.shape[0]),
    )(here, ids, slots)


def diagonal():
    shape = (SEGMENT_ROWS, SEGMENT_ROWS)
    return lax.broadcasted_iota(jnp.int32, shape, 0) == lax.broadcasted_iota(jnp.int32, shape, 1)


GROUP = SEGMENT_ROWS // 8
WORDS = 5 * GROUP


def coded_rows(segments):
    return segments * WORDS + 8


def encode(values, o_ref, unit, units):
    largest = jnp.maximum(jnp.max(jnp.abs(values), axis=1, keepdims=True), 2.0**-100)
    power = jnp.floor(jnp.log2(largest))
    whole = (values * jnp.exp2(18.0 - power) + MIDDLE).astype(jnp.int32) - int(MIDDLE)
    whole = jnp.minimum(whole, 2**19 - 1)
    v = [whole[i * GROUP : (i + 1) * GROUP] for i in range(8)]
    over = [
        v[5] & 0xFFF,
        ((v[5] >> 12) & 0xFF) | ((v[6] & 0xF) << 8),
        (v[6] >> 4) & 0xFFF,
        ((v[6] >> 16) & 0xF) | ((v[7] & 0xFF) << 4),
        v[7] >> 8,
    ]
    for i in range(5):
        o_ref[unit * WORDS + i * GROUP : unit * WORDS + (i + 1) * GROUP, :] = (v[i] & 0xFFFFF) | (
            over[i] << 20
        )
    row = jnp.sum(jnp.where(diagonal(), power, 0.0), axis=0, keepdims=True)
    o_ref[units * WORDS + unit : units * WORDS + unit + 1, :SEGMENT_ROWS] = row.astype(jnp.int32)


def decode(ref, unit, units):
    w = [ref[unit * WORDS + i * GROUP : unit * WORDS + (i + 1) * GROUP, :] for i in range(5)]
    v = [(x << 12) >> 12 for x in w]
    v.append(((w[0] >> 20) & 0xFFF) | (((w[1] << 4) >> 24) << 12))
    v.append(((w[1] >> 28) & 0xF) | (((w[2] >> 20) & 0xFFF) << 4) | (((w[3] << 8) >> 28) << 16))
    v.append(((w[3] >> 24) & 0xFF) | ((w[4] >> 20) << 8))
    row = ref[units * WORDS + unit : units * WORDS + unit + 1, :SEGMENT_ROWS].astype(jnp.float32)
    power = jnp.sum(jnp.where(diagonal(), row, 0.0), axis=1, keepdims=True)
    return jnp.concatenate(v, axis=0).astype(jnp.float32) * jnp.exp2(power - 18.0)


def add_decoded(sums, chunk, refs):
    first, number = CHUNKS[chunk]
    for unit in range(number):
        rows = pl.ds((first + unit) * SEGMENT_ROWS, SEGMENT_ROWS)
        value = sums[rows, :]
        for ref in refs:
            value = value + decode(ref, unit, number)
        sums[rows, :] = value


def load_base(first, segments, column, x_ref, w_ref, x, w, sems):
    width, columns = w.shape
    rows = segments * SEGMENT_ROWS
    start = pl.multiple_of(column * columns, columns)
    depth = width // PIECES
    blocks = [(r, min(BLOCK, rows - r)) for r in range(0, rows, BLOCK)]

    def x_copy(at, size, features, sem):
        return pltpu.make_async_copy(
            x_ref.at[pl.ds(first * SEGMENT_ROWS + at, size), features],
            x.at[pl.ds(at, size), features],
            sem,
        )

    work = []
    for i, (at, size) in enumerate(blocks):
        terms = []
        if i == 0:
            for p in range(PIECES):
                features = pl.ds(p * depth, depth)
                copies = (
                    pltpu.make_async_copy(
                        w_ref.at[features, pl.ds(start, columns)], w.at[features, :], sems.at[0, p]
                    ),
                    x_copy(0, size, features, sems.at[1, p]),
                )
                terms.append((copies, slice(p * depth, (p + 1) * depth)))
        else:
            terms.append(((x_copy(at, size, slice(None), sems.at[2, i]),), slice(None)))
        work.append((at, size, terms))
    for _, _, terms in work:
        for copies, _ in terms:
            for copy in copies:
                copy.start()
    return work


def block_product(x, w, at, size, terms):
    total = None
    for copies, features in terms:
        for copy in copies:
            copy.wait()
        term = jnp.dot(
            x[at : at + size, features], w[features, :], preferred_element_type=jnp.float32
        )
        total = term if total is None else total + term
    return total


def base_scratch(segments, width, columns):
    rows = segments * SEGMENT_ROWS
    return [
        pltpu.VMEM((rows, width), jnp.bfloat16),
        pltpu.VMEM((width, columns), jnp.bfloat16),
        pltpu.SemaphoreType.DMA((3, max(PIECES, rows // BLOCK + 1))),
    ]


def sent_kernel(first, sizes, step, n_tensor, x_ref, w_ref, *refs):
    outs, (x, w, sems) = refs[: len(sizes)], refs[len(sizes) :]
    column = lax.rem(lax.axis_index("tensor") + step, n_tensor)
    work = load_base(first, sum(sizes), column, x_ref, w_ref, x, w, sems)
    unit_of = [(out, unit) for out, size in enumerate(sizes) for unit in range(size)]
    for out, size in zip(outs, sizes):
        out[size * WORDS :, :] = jnp.zeros((8, w.shape[1]), jnp.int32)
    for at, size, terms in work:
        product = block_product(x, w, at, size, terms)
        for r in range(0, size, SEGMENT_ROWS):
            out, unit = unit_of[(at + r) // SEGMENT_ROWS]
            encode(product[r : r + SEGMENT_ROWS], outs[out], unit, sizes[out])


def sent_call(tokens, weight, step, n_tensor, columns, first, sizes):
    width = tokens.shape[1]
    rows = sum(sizes) * SEGMENT_ROWS
    return pl.pallas_call(
        functools.partial(sent_kernel, first, sizes, step, n_tensor),
        in_specs=[HBM, HBM],
        out_specs=[VMEM] * len(sizes),
        out_shape=[jax.ShapeDtypeStruct((coded_rows(n), columns), jnp.int32) for n in sizes],
        scratch_shapes=base_scratch(sum(sizes), width, columns),
        compiler_params=params(24),
        cost_estimate=cost(
            2 * rows * width * columns, 2 * rows * width + 2 * width * columns + 4 * rows * columns
        ),
    )(tokens, weight)


def add_kernel(chunk, base_ref, *refs):
    coded_refs, o_ref = refs[:-1], refs[-1]
    o_ref[...] = base_ref[...]
    add_decoded(o_ref, chunk, coded_refs)


def add_call(chunk, base, coded):
    return pl.pallas_call(
        functools.partial(add_kernel, chunk),
        in_specs=[VMEM] * (1 + len(coded)),
        out_specs=VMEM,
        out_shape=jax.ShapeDtypeStruct(base.shape, base.dtype),
        compiler_params=params(8),
        cost_estimate=cost(0, 4 * base.size),
    )(base, *coded)


def shrink_into(o_ref, i, table, k, rows_of, buffers, owners, rank):
    for buffer, whose in zip(buffers, owners):

        @pl.when(whose == table[k * ENTRIES])
        def _(buffer=buffer):
            for j in range(MOST):
                _, _, within = segment_of(table, k, j)
                rows = rows_of(j)
                width = rows.shape[1]
                factor = buffer[pl.ds(pl.multiple_of(within * rank, rank), rank), :width]
                o_ref[i, :, j * rank : (j + 1) * rank] = lax.dot_general(
                    rows, factor, (((1,), (1,)), ((), ())), preferred_element_type=jnp.float32
                )


def stages_of(k):
    return range((k + 1) // 2, k + 1)


def own_kernel(n_adapter, rank, table, here, x_ref, w_ref, message, *refs):
    coded_refs, (o_ref, s_ref, kept_ref, x, w, sems, kept_sems) = refs[:-7], refs[-7:]
    work = load_base(0, x.shape[0] // SEGMENT_ROWS, here[2], x_ref, w_ref, x, w, sems)
    keeps = []
    for at, size, terms in work:
        o_ref[at : at + size, :] = block_product(x, w, at, size, terms)
    add_decoded(o_ref, 0, coded_refs)
    for k in range(1, n_adapter):
        for j in range(MOST):
            start, _, _ = segment_of(table, k, j)
            keeps.append(
                pltpu.make_async_copy(
                    x.at[pl.ds(start, SEGMENT_ROWS), :], kept_ref.at[k - 1, j], kept_sems.at[k - 1, j]
                )
            )
            keeps[-1].start()

    def rows_of(j):
        start, _, _ = segment_of(table, 0, j)
        return x[pl.ds(start, SEGMENT_ROWS), :]

    shrink_into(s_ref, 0, table, 0, rows_of, [message], [here[0]], rank)
    for copy in keeps:
        copy.wait()


def own_call(table, here, tokens, weight, message, coded, columns, n_adapter, rank):
    rows, width = tokens.shape
    segments = rows // SEGMENT_ROWS
    return pl.pallas_call(
        functools.partial(own_kernel, n_adapter, rank),
        in_specs=[SMEM, SMEM, HBM, HBM] + [VMEM] * (1 + len(coded)),
        out_specs=[VMEM] * 3,
        out_shape=[
            jax.ShapeDtypeStruct((rows, columns), jnp.float32),
            jax.ShapeDtypeStruct((1, SEGMENT_ROWS, MOST * rank), jnp.float32),
            jax.ShapeDtypeStruct((n_adapter - 1, MOST, SEGMENT_ROWS, width), jnp.bfloat16),
        ],
        scratch_shapes=base_scratch(segments, width, columns)
        + [pltpu.SemaphoreType.DMA((n_adapter - 1, MOST))],
        compiler_params=params(32),
        cost_estimate=cost(
            2 * rows * width * columns, 2 * rows * width + 2 * width * columns + 4 * rows * columns
        ),
    )(table, here, tokens, weight, message, *coded)


def shrink_kernel(k, rank, at, table, here, kept_ref, *refs):
    buffers, o_ref = refs[1 if at else 0 : -1], refs[-1]
    if at:
        o_ref[:at] = refs[0][...]
    owners = buffer_owners(here, stages_of(k))
    shrink_into(o_ref, at, table, k, lambda j: kept_ref[k - 1, j], buffers, owners, rank)


def shrink_call(k, table, here, kept, before, buffers, rank):
    width = kept.shape[3]
    at = sum(b.shape[0] for b in before)
    return pl.pallas_call(
        functools.partial(shrink_kernel, k, rank, at),
        in_specs=[SMEM, SMEM, VMEM] + [VMEM] * (len(before) + len(buffers)),
        out_specs=VMEM,
        out_shape=jax.ShapeDtypeStruct((at + 1, SEGMENT_ROWS, MOST * rank), jnp.float32),
        compiler_params=params(16),
        cost_estimate=cost(MOST * 2 * SEGMENT_ROWS * width * 256, 4 * SEGMENT_ROWS * width),
    )(table, here, kept, *before, *buffers)


def fetch_up(up, at, table, k, j, buffers, owners, rank):
    columns = up.shape[2]
    _, _, within = segment_of(table, k, j)
    for buffer, whose in zip(buffers, owners):

        @pl.when(whose == table[k * ENTRIES])
        def _(buffer=buffer):
            first = buffer.shape[1] - columns
            factor = buffer[pl.ds(pl.multiple_of(within * rank, rank), rank), first:]
            up[at, :rank, :] = factor
            up[at, rank:, :] = factor


def up_product(share, j, factor, rank):
    lane = lax.broadcasted_iota(jnp.int32, share.shape, 1)
    other = pltpu.roll(share, rank, 1)
    both = jnp.where((lane < rank) == (j == 0), share, other)
    high = both.astype(jnp.bfloat16).astype(jnp.float32)
    terms = jnp.where(lane < rank, high, both - high).astype(jnp.bfloat16)
    return jnp.dot(terms, factor, preferred_element_type=jnp.float32)


LATE = 2


def early_kernel(n_adapter, n_tensor, rank, table, here, *refs):
    first = n_adapter - LATE
    n_buffers = 2 * first - 1
    base_ref, coded_refs, refs = refs[0], refs[1:n_tensor], refs[n_tensor:]
    shrinks, refs = refs[: -4 - n_buffers], refs[-4 - n_buffers :]
    buffers, (o_ref, rest_ref, up, total) = refs[:-4], refs[-4:]
    for k in range(first):
        at = 0 if k == 0 else 2 * stages_of(k)[0] - 1
        to = 2 * k + 1
        owners = buffer_owners(here, stages_of(k))
        for j in range(MOST):
            fetch_up(up, k * MOST + j, table, k, j, buffers[at:to], owners, rank)
    shares = []
    for call in range(len(shrinks) // n_tensor):
        share = shrinks[call * n_tensor][...]
        for i in range(1, n_tensor):
            share = share + shrinks[call * n_tensor + i][...]
        shares += [share[i] for i in range(share.shape[0])]
    total[...] = base_ref[...]
    add_decoded(total, len(CHUNKS) - 1, coded_refs)
    for k in range(n_adapter):
        for j in range(MOST):
            start, used, _ = segment_of(table, k, j)
            value = total[pl.ds(start, SEGMENT_ROWS), :]
            if k >= first:
                rest_ref[k - first, j] = value
                continue
            lora = up_product(shares[k], j, up[k * MOST + j], rank)

            @pl.when(used)
            def _(start=start, value=value, lora=lora):
                o_ref[pl.ds(start, SEGMENT_ROWS), :] = (value + adapter_scale * lora).astype(
                    jnp.bfloat16
                )


def early(n_adapter, n_tensor, table, here, base, coded, shrinks, buffers, rank):
    rows, columns = base.shape
    return pl.pallas_call(
        functools.partial(early_kernel, n_adapter, n_tensor, rank),
        in_specs=[SMEM] * 2 + [VMEM] * (1 + len(coded) + len(shrinks) + len(buffers)),
        out_specs=[VMEM, VMEM],
        out_shape=[
            jax.ShapeDtypeStruct((rows, columns), jnp.bfloat16),
            jax.ShapeDtypeStruct((LATE, MOST, SEGMENT_ROWS, columns), jnp.float32),
        ],
        scratch_shapes=[
            pltpu.VMEM(((n_adapter - LATE) * MOST, 2 * rank, columns), jnp.bfloat16),
            pltpu.VMEM((rows, columns), jnp.float32),
        ],
        compiler_params=params(16),
        cost_estimate=cost(6 * rows * rank * columns, (4 * n_tensor + 2) * rows * columns),
    )(table, here, base, *coded, *shrinks, *buffers)


def late_kernel(k, number, n_tensor, rank, table, here, *refs):
    rest_ref, shrinks, refs = refs[0], refs[1 : 1 + n_tensor], refs[1 + n_tensor :]
    buffers, (_, o_ref, up, out, sems) = refs[:-5], refs[-5:]
    owners = buffer_owners(here, stages_of(k))
    share = shrinks[0][0]
    for r in shrinks[1:]:
        share = share + r[0]
    stores = []
    for j in range(MOST):
        fetch_up(up, j, table, k, j, buffers, owners, rank)
        start, used, _ = segment_of(table, k, j)
        lora = up_product(share, j, up[j], rank)
        out[j] = (rest_ref[number, j] + adapter_scale * lora).astype(jnp.bfloat16)
        store = pltpu.make_async_copy(out.at[j], o_ref.at[pl.ds(start, SEGMENT_ROWS), :], sems.at[j])
        pl.when(used)(store.start)
        stores.append((used, store))
    for used, store in stores:
        pl.when(used)(store.wait)


def late(k, number, n_tensor, table, here, rest, shrinks, buffers, value, rank):
    rows, columns = value.shape
    return pl.pallas_call(
        functools.partial(late_kernel, k, number, n_tensor, rank),
        in_specs=[SMEM] * 2 + [VMEM] * (1 + len(shrinks) + len(buffers)) + [ANY],
        out_specs=ANY,
        out_shape=jax.ShapeDtypeStruct((rows, columns), jnp.bfloat16),
        scratch_shapes=[
            pltpu.VMEM((MOST, 2 * rank, columns), jnp.bfloat16),
            pltpu.VMEM((MOST, SEGMENT_ROWS, columns), jnp.bfloat16),
            pltpu.SemaphoreType.DMA((MOST,)),
        ],
        input_output_aliases={3 + len(shrinks) + len(buffers): 0},
        compiler_params=params(8),
        cost_estimate=cost(
            6 * MOST * SEGMENT_ROWS * rank * columns, 8 * MOST * SEGMENT_ROWS * columns
        ),
    )(table, here, rest, *shrinks, *buffers, value)


def after(array, *others):
    return lax.optimization_barrier((array, *others))[0]


def on_device(
    tokens, value_weight, adapter_down_weight, adapter_up_weight, row_adapter_index, adapter_slot_of
):
    rows, width = tokens.shape
    per_device, _, rank = adapter_down_weight.shape
    n_adapter = lax.axis_size("adapter")
    n_tensor = lax.axis_size("tensor")
    me_t = lax.axis_index("tensor")
    here = jnp.stack([lax.axis_index("adapter"), lax.axis_index("dp"), me_t])
    columns = value_weight.shape[1] // n_tensor

    def swap_tensor(array, step):
        pairs = [(i, (i + step) % n_tensor) for i in range(n_tensor)]
        return lax.ppermute(array, "tensor", pairs)

    def along_line(array, stage):
        up = [(2 * i, 2 * (i + 1)) for i in range(stage - 1, n_adapter - 1)]
        down = [(2 * i + 1, 2 * (i - 1) + 1) for i in range(1, n_adapter - stage + 1)]
        return lax.ppermute(array, ("adapter", "dp"), up + down)

    def swap_cores(array):
        return lax.ppermute(array, "dp", [(0, 1), (1, 0)])

    down = jnp.swapaxes(adapter_down_weight, 1, 2).reshape(per_device * rank, width)
    up = adapter_up_weight.reshape(per_device * rank, value_weight.shape[1])
    tokens, value_weight, down, up = (
        pltpu.with_memory_space_constraint(a, pltpu.HBM) for a in (tokens, value_weight, down, up)
    )
    message = message_call(down, up, columns)
    table = table_call(here, row_adapter_index, adapter_slot_of, n_adapter, per_device)

    buffers, shrinks = [[message]], []

    def buffers_of(stages):
        return [b for stage in stages for b in buffers[stage]]

    def shrink(k, kept, before):
        return shrink_call(k, table, here, kept, before, buffers_of(stages_of(k)), rank)

    def add_shrink(mine):
        shrinks.extend([mine] + [swap_tensor(mine, step) for step in range(1, n_tensor)])

    held = along_line(message, 1)
    others = range(1, n_tensor)

    def sent_for(step, chunks):
        sizes = [number for _, number in chunks]
        return sent_call(tokens, value_weight, step, n_tensor, columns, chunks[0][0], sizes)

    parts = [[sent_for(step, CHUNKS[:1])[0] for step in others]]
    rest_parts = [sent_for(step, CHUNKS[1:]) for step in others]
    parts += [[p[i] for p in rest_parts] for i in range(len(CHUNKS) - 1)]
    sent = [[swap_tensor(p, step) for step, p in zip(others, parts[0])]]
    last = n_adapter - 1
    done = [table] + [p for group in parts for p in group] + sent[0]
    for stage in range(1, last):
        came = after(held, *done)
        held = along_line(came, stage + 1)
        buffers.append([came, swap_cores(came)])
        if stage < len(CHUNKS):
            sent.append([swap_tensor(after(p, came), step) for step, p in zip(others, parts[stage])])
        if stage == 1:
            base, before, kept = own_call(
                after(table, came), here, tokens, value_weight, message, sent[0], columns, n_adapter, rank
            )
            done = sent[1] + [base]
        else:
            if stage == 2:
                base = add_call(1, after(base, came), sent[1])
            before = shrink(stage - 1, after(kept, came), [before])
            done = []
    add_shrink(before)
    value, remaining = early(
        n_adapter,
        n_tensor,
        table,
        here,
        base,
        sent[2],
        shrinks,
        buffers_of(range(last - 1)),
        rank,
    )
    came = after(held, value)
    buffers.append([came, swap_cores(came)])
    ready = after(kept, came)
    for k in (last - 1, last):
        mine = shrink(k, ready, [])
        add_shrink(mine)
        ready = after(kept, mine)
    for number, k in enumerate((last - 1, last)):
        value = late(
            k,
            number,
            n_tensor,
            table,
            here,
            remaining,
            shrinks[(number - LATE) * n_tensor :][:n_tensor],
            buffers_of(stages_of(k)),
            value,
            rank,
        )
    return value


def solution(mesh):
    return jax.shard_map(
        on_device,
        mesh=mesh,
        in_specs=(
            P(("groups", "adapter", "dp"), "tensor"),
            P("tensor", None),
            P(("groups", "adapter"), "tensor", None),
            P(("groups", "adapter"), None, None),
            P(("groups", "adapter", "dp")),
            P("groups"),
        ),
        out_specs=P(("groups", "adapter", "dp"), "tensor"),
        check_vma=False,
    )
```

```python
import functools

import jax
import jax.numpy as jnp
from jax import lax
from jax.experimental import pallas as pl
from jax.experimental.pallas import tpu as pltpu
from jax.sharding import PartitionSpec as P

SEGMENT_ROWS = 128
adapter_scale = 0.5
MOST = 2
BLOCK = 256
PIECES = 4
CHUNKS = ((6, 2), (0, 4), (4, 2))
ENTRIES = 8
MIDDLE = 1.5 * 2.0**23


def cost(flops, moved):
    return pl.CostEstimate(flops=int(flops), bytes_accessed=int(moved), transcendentals=0)


def params(mib):
    return pltpu.CompilerParams(vmem_limit_bytes=mib * 2**20)


ANY = pl.BlockSpec(memory_space=pl.ANY)
HBM = pl.BlockSpec(memory_space=pltpu.HBM)
SMEM = pl.BlockSpec(memory_space=pltpu.SMEM)
VMEM = pl.BlockSpec(memory_space=pltpu.VMEM)


def arrival_order(me, n_adapter):
    order = [me] + [jnp.int32(-1)] * (n_adapter - 1)
    count = jnp.int32(1)
    for distance in range(1, n_adapter):
        for other in (me - distance, me + distance):
            valid = (other >= 0) & (other < n_adapter)
            order = [jnp.where(valid & (count == k), other, o) for k, o in enumerate(order)]
            count = count + valid.astype(jnp.int32)
    return order


def views_of(refs, stages, layout, rank):
    me, core = lax.axis_index("adapter"), lax.axis_index("dp")
    refs, views = list(refs), []
    for stage in stages:
        came, swapped = layout[stage]
        toward = jnp.where(core == 0, -stage, stage)
        for i in range(came):
            views.append((refs.pop(0), 0, me + toward if stage > 0 else me, i))
        for i in range(swapped):
            ref = refs.pop(0)
            for part in range(came // swapped):
                views.append((ref, part * rank, me - toward, i + part))
    return views


def segment_of(table, k, j):
    seg = table[k * ENTRIES + 1 + 2 * j]
    start = pl.multiple_of(jnp.maximum(seg, 0) * SEGMENT_ROWS, SEGMENT_ROWS)
    return start, seg >= 0, table[k * ENTRIES + 2 + 2 * j]


def message_kernel(down_ref, up_ref, *refs):
    outs, sems = refs[:-1], refs[-1]
    rank = outs[0].shape[0]
    width = down_ref.shape[1]
    columns = outs[0].shape[1] - width
    start = pl.multiple_of(lax.axis_index("tensor") * columns, columns)
    copies = []
    for i, out in enumerate(outs):
        rows = pl.ds(i * rank, rank)
        copies += [
            pltpu.make_async_copy(down_ref.at[rows, :], out.at[:, pl.ds(0, width)], sems.at[0, i]),
            pltpu.make_async_copy(
                up_ref.at[rows, pl.ds(start, columns)], out.at[:, pl.ds(width, columns)], sems.at[1, i]
            ),
        ]
    for copy in copies:
        copy.start()
    for copy in copies:
        copy.wait()


def message_call(down, up, columns, per_device):
    rows, width = down.shape
    shape = jax.ShapeDtypeStruct((rows // per_device, width + columns), jnp.bfloat16)
    return pl.pallas_call(
        message_kernel,
        in_specs=[HBM, HBM],
        out_specs=[VMEM] * per_device,
        out_shape=[shape] * per_device,
        scratch_shapes=[pltpu.SemaphoreType.DMA((2, per_device))],
        compiler_params=params(8),
        cost_estimate=cost(0, 4 * rows * (width + columns)),
    )(down, up)


def table_kernel(n_adapter, per_device, ids, slots, table):
    seg_dev = ids.shape[0] // SEGMENT_ROWS
    used = [slots[ids[s * SEGMENT_ROWS]] for s in range(seg_dev)]
    for k, owner in enumerate(arrival_order(lax.axis_index("adapter"), n_adapter)):
        table[k * ENTRIES] = owner
        found, place = [jnp.int32(-1)] * MOST, [jnp.int32(0)] * MOST
        count = jnp.int32(0)
        for s, slot in enumerate(used):
            within = slot - owner * per_device
            hit = (within >= 0) & (within < per_device)
            for j in range(MOST):
                take = hit & (count == j)
                found[j] = jnp.where(take, s, found[j])
                place[j] = jnp.where(take, within, place[j])
            count = count + hit.astype(jnp.int32)
        for j in range(MOST):
            table[k * ENTRIES + 1 + 2 * j] = found[j]
            table[k * ENTRIES + 2 + 2 * j] = place[j]


def table_call(ids, slots, n_adapter, per_device):
    return pl.pallas_call(
        functools.partial(table_kernel, n_adapter, per_device),
        in_specs=[SMEM, SMEM],
        out_specs=SMEM,
        out_shape=jax.ShapeDtypeStruct((n_adapter * ENTRIES,), jnp.int32),
        cost_estimate=cost(0, 4 * ids.shape[0]),
    )(ids, slots)


def diagonal():
    shape = (SEGMENT_ROWS, SEGMENT_ROWS)
    return lax.broadcasted_iota(jnp.int32, shape, 0) == lax.broadcasted_iota(jnp.int32, shape, 1)


GROUP = SEGMENT_ROWS // 8
WORDS = 5 * GROUP


def coded_rows(segments):
    return segments * WORDS + 8


def encode(values, o_ref, unit, units):
    largest = jnp.maximum(jnp.max(jnp.abs(values), axis=1, keepdims=True), 2.0**-100)
    power = jnp.floor(jnp.log2(largest))
    whole = (values * jnp.exp2(18.0 - power) + MIDDLE).astype(jnp.int32) - int(MIDDLE)
    whole = jnp.minimum(whole, 2**19 - 1)
    v = [whole[i * GROUP : (i + 1) * GROUP] for i in range(8)]
    over = [
        v[5] & 0xFFF,
        ((v[5] >> 12) & 0xFF) | ((v[6] & 0xF) << 8),
        (v[6] >> 4) & 0xFFF,
        ((v[6] >> 16) & 0xF) | ((v[7] & 0xFF) << 4),
        v[7] >> 8,
    ]
    for i in range(5):
        o_ref[unit * WORDS + i * GROUP : unit * WORDS + (i + 1) * GROUP, :] = (v[i] & 0xFFFFF) | (
            over[i] << 20
        )
    row = jnp.sum(jnp.where(diagonal(), power, 0.0), axis=0, keepdims=True)
    o_ref[units * WORDS + unit : units * WORDS + unit + 1, :SEGMENT_ROWS] = row.astype(jnp.int32)


def decode(ref, unit, units):
    w = [ref[unit * WORDS + i * GROUP : unit * WORDS + (i + 1) * GROUP, :] for i in range(5)]
    v = [(x << 12) >> 12 for x in w]
    v.append(((w[0] >> 20) & 0xFFF) | (((w[1] << 4) >> 24) << 12))
    v.append(((w[1] >> 28) & 0xF) | (((w[2] >> 20) & 0xFFF) << 4) | (((w[3] << 8) >> 28) << 16))
    v.append(((w[3] >> 24) & 0xFF) | ((w[4] >> 20) << 8))
    row = ref[units * WORDS + unit : units * WORDS + unit + 1, :SEGMENT_ROWS].astype(jnp.float32)
    power = jnp.sum(jnp.where(diagonal(), row, 0.0), axis=1, keepdims=True)
    return jnp.concatenate(v, axis=0).astype(jnp.float32) * jnp.exp2(power - 18.0)


def add_decoded(sums, chunk, refs):
    first, number = CHUNKS[chunk]
    for unit in range(number):
        rows = pl.ds((first + unit) * SEGMENT_ROWS, SEGMENT_ROWS)
        value = sums[rows, :]
        for ref in refs:
            value = value + decode(ref, unit, number)
        sums[rows, :] = value


def load_base(first, segments, column, x_ref, w_ref, x, w, sems):
    width, columns = w.shape
    rows = segments * SEGMENT_ROWS
    start = pl.multiple_of(column * columns, columns)
    depth = width // PIECES
    blocks = [(r, min(BLOCK, rows - r)) for r in range(0, rows, BLOCK)]

    def x_copy(at, size, features, sem):
        return pltpu.make_async_copy(
            x_ref.at[pl.ds(first * SEGMENT_ROWS + at, size), features],
            x.at[pl.ds(at, size), features],
            sem,
        )

    work = []
    for i, (at, size) in enumerate(blocks):
        terms = []
        if i == 0:
            for p in range(PIECES):
                features = pl.ds(p * depth, depth)
                copies = (
                    pltpu.make_async_copy(
                        w_ref.at[features, pl.ds(start, columns)], w.at[features, :], sems.at[0, p]
                    ),
                    x_copy(0, size, features, sems.at[1, p]),
                )
                terms.append((copies, slice(p * depth, (p + 1) * depth)))
        else:
            terms.append(((x_copy(at, size, slice(None), sems.at[2, i]),), slice(None)))
        work.append((at, size, terms))
    for _, _, terms in work:
        for copies, _ in terms:
            for copy in copies:
                copy.start()
    return work


def block_product(x, w, at, size, terms):
    total = None
    for copies, features in terms:
        for copy in copies:
            copy.wait()
        term = jnp.dot(
            x[at : at + size, features], w[features, :], preferred_element_type=jnp.float32
        )
        total = term if total is None else total + term
    return total


def base_scratch(segments, width, columns):
    rows = segments * SEGMENT_ROWS
    return [
        pltpu.VMEM((rows, width), jnp.bfloat16),
        pltpu.VMEM((width, columns), jnp.bfloat16),
        pltpu.SemaphoreType.DMA((3, max(PIECES, rows // BLOCK + 1))),
    ]


def sent_kernel(first, sizes, step, n_tensor, x_ref, w_ref, *refs):
    outs, (x, w, sems) = refs[: len(sizes)], refs[len(sizes) :]
    column = lax.rem(lax.axis_index("tensor") + step, n_tensor)
    work = load_base(first, sum(sizes), column, x_ref, w_ref, x, w, sems)
    unit_of = [(out, unit) for out, size in enumerate(sizes) for unit in range(size)]
    for out, size in zip(outs, sizes):
        out[size * WORDS :, :] = jnp.zeros((8, w.shape[1]), jnp.int32)
    for at, size, terms in work:
        product = block_product(x, w, at, size, terms)
        for r in range(0, size, SEGMENT_ROWS):
            out, unit = unit_of[(at + r) // SEGMENT_ROWS]
            encode(product[r : r + SEGMENT_ROWS], outs[out], unit, sizes[out])


def sent_call(tokens, weight, step, n_tensor, columns, first, sizes):
    width = tokens.shape[1]
    rows = sum(sizes) * SEGMENT_ROWS
    return pl.pallas_call(
        functools.partial(sent_kernel, first, sizes, step, n_tensor),
        in_specs=[HBM, HBM],
        out_specs=[VMEM] * len(sizes),
        out_shape=[jax.ShapeDtypeStruct((coded_rows(n), columns), jnp.int32) for n in sizes],
        scratch_shapes=base_scratch(sum(sizes), width, columns),
        compiler_params=params(16),
        cost_estimate=cost(
            2 * rows * width * columns, 2 * rows * width + 2 * width * columns + 4 * rows * columns
        ),
    )(tokens, weight)


def add_kernel(chunk, base_ref, *refs):
    coded_refs, o_ref = refs[:-1], refs[-1]
    o_ref[...] = base_ref[...]
    add_decoded(o_ref, chunk, coded_refs)


def add_call(chunk, base, coded):
    return pl.pallas_call(
        functools.partial(add_kernel, chunk),
        in_specs=[VMEM] * (1 + len(coded)),
        out_specs=VMEM,
        out_shape=jax.ShapeDtypeStruct(base.shape, base.dtype),
        compiler_params=params(8),
        cost_estimate=cost(20 * base.size, 12 * base.size),
    )(base, *coded)


def shrink_into(o_ref, at, table, k, rows_of, views, rank):
    for j in range(MOST):
        _, _, within = segment_of(table, k, j)
        for ref, first, whose, i in views:

            @pl.when((whose == table[k * ENTRIES]) & (within == i))
            def _(j=j, ref=ref, first=first):
                rows = rows_of(j)
                o_ref[at, :, j * rank : (j + 1) * rank] = lax.dot_general(
                    rows,
                    ref[first : first + rank, : rows.shape[1]],
                    (((1,), (1,)), ((), ())),
                    preferred_element_type=jnp.float32,
                )


def join_copies(halves, whole, sems):
    copies, rank = [], halves[0].shape[0]
    for i, half in enumerate(halves):
        copies.append(
            pltpu.make_async_copy(half, whole.at[pl.ds(i * rank, rank), :], sems.at[i])
        )
        copies[-1].start()
    return copies


def stages_of(k):
    return range((k + 1) // 2, k + 1)


def own_kernel(n_adapter, per_device, rank, table, x_ref, w_ref, *refs):
    messages, refs = refs[:per_device], refs[per_device:]
    coded_refs, (o_ref, s_ref, kept_ref, x, w, sems, kept_sems) = refs[:-7], refs[-7:]
    work = load_base(0, x.shape[0] // SEGMENT_ROWS, lax.axis_index("tensor"), x_ref, w_ref, x, w, sems)
    keeps = []
    for at, size, terms in work:
        o_ref[at : at + size, :] = block_product(x, w, at, size, terms)
    add_decoded(o_ref, 0, coded_refs)
    for k in range(1, n_adapter):
        for j in range(MOST):
            start, _, _ = segment_of(table, k, j)
            keeps.append(
                pltpu.make_async_copy(
                    x.at[pl.ds(start, SEGMENT_ROWS), :], kept_ref.at[k - 1, j], kept_sems.at[k - 1, j]
                )
            )
            keeps[-1].start()

    def rows_of(j):
        start, _, _ = segment_of(table, 0, j)
        return x[pl.ds(start, SEGMENT_ROWS), :]

    views = views_of(messages, [0], [(per_device, 0)], rank)
    shrink_into(s_ref, 0, table, 0, rows_of, views, rank)
    for copy in keeps:
        copy.wait()


def own_call(table, tokens, weight, messages, coded, columns, n_adapter):
    rows, width = tokens.shape
    per_device, rank = len(messages), messages[0].shape[0]
    return pl.pallas_call(
        functools.partial(own_kernel, n_adapter, per_device, rank),
        in_specs=[SMEM, HBM, HBM] + [VMEM] * (per_device + len(coded)),
        out_specs=[VMEM] * 3,
        out_shape=[
            jax.ShapeDtypeStruct((rows, columns), jnp.float32),
            jax.ShapeDtypeStruct((1, SEGMENT_ROWS, MOST * rank), jnp.float32),
            jax.ShapeDtypeStruct((n_adapter - 1, MOST, SEGMENT_ROWS, width), jnp.bfloat16),
        ],
        scratch_shapes=base_scratch(rows // SEGMENT_ROWS, width, columns)
        + [pltpu.SemaphoreType.DMA((n_adapter - 1, MOST))],
        compiler_params=params(20),
        cost_estimate=cost(
            2 * rows * width * columns, 2 * rows * width + 2 * width * columns + 4 * rows * columns
        ),
    )(table, tokens, weight, *messages, *coded)


def shrink_kernel(k, rank, at, layout, n_halves, table, kept_ref, *refs):
    before, refs = refs[: 1 if at else 0], refs[1 if at else 0 :]
    halves, refs = refs[:n_halves], refs[n_halves:]
    joins = []
    if n_halves:
        refs, whole_ref, sems = refs[:-2], refs[-2], refs[-1]
        joins = join_copies(halves, whole_ref, sems)
    buffers, o_ref = refs[:-1], refs[-1]
    for r in before:
        o_ref[:at] = r[...]
    views = views_of(buffers, stages_of(k), layout, rank)
    shrink_into(o_ref, at, table, k, lambda j: kept_ref[k - 1, j], views, rank)
    for copy in joins:
        copy.wait()


def shrink_call(k, table, kept, before, halves, buffers, layout, rank):
    width = kept.shape[3]
    at = sum(b.shape[0] for b in before)
    shapes = [jax.ShapeDtypeStruct((at + 1, SEGMENT_ROWS, MOST * rank), jnp.float32)]
    if halves:
        shapes.append(jax.ShapeDtypeStruct((len(halves) * rank, halves[0].shape[1]), jnp.bfloat16))
    return pl.pallas_call(
        functools.partial(shrink_kernel, k, rank, at, layout, len(halves)),
        in_specs=[SMEM] + [VMEM] * (1 + len(before) + len(halves) + len(buffers)),
        out_specs=[VMEM] * len(shapes),
        out_shape=shapes,
        scratch_shapes=[pltpu.SemaphoreType.DMA((len(halves),))] if halves else [],
        compiler_params=params(4),
        cost_estimate=cost(MOST * 2 * SEGMENT_ROWS * width * 256, 4 * SEGMENT_ROWS * width),
    )(table, kept, *before, *halves, *buffers)


def fetch_up(up, at, table, k, j, views, rank):
    columns = up.shape[2]
    _, _, within = segment_of(table, k, j)
    for ref, first, whose, i in views:

        @pl.when((whose == table[k * ENTRIES]) & (within == i))
        def _(ref=ref, first=first):
            factor = ref[first : first + rank, ref.shape[1] - columns :]
            up[at, :rank, :] = factor
            up[at, rank:, :] = factor


def up_product(share, j, factor, rank):
    lane = lax.broadcasted_iota(jnp.int32, share.shape, 1)
    other = pltpu.roll(share, rank, 1)
    both = jnp.where((lane < rank) == (j == 0), share, other)
    high = both.astype(jnp.bfloat16).astype(jnp.float32)
    terms = jnp.where(lane < rank, high, both - high).astype(jnp.bfloat16)
    return jnp.dot(terms, factor, preferred_element_type=jnp.float32)


LATE = 2


def early_kernel(n_adapter, n_tensor, rank, layout, n_buffers, table, *refs):
    first = n_adapter - LATE
    base_ref, coded_refs, refs = refs[0], refs[1:n_tensor], refs[n_tensor:]
    shrinks, refs = refs[: -4 - n_buffers], refs[-4 - n_buffers :]
    buffers, (o_ref, rest_ref, up, total) = refs[:-4], refs[-4:]
    views = views_of(buffers, range(first), layout, rank)
    for k in range(first):
        for j in range(MOST):
            fetch_up(up, k * MOST + j, table, k, j, views, rank)
    shares = []
    for call in range(len(shrinks) // n_tensor):
        share = shrinks[call * n_tensor][...]
        for i in range(1, n_tensor):
            share = share + shrinks[call * n_tensor + i][...]
        shares += [share[i] for i in range(share.shape[0])]
    total[...] = base_ref[...]
    add_decoded(total, len(CHUNKS) - 1, coded_refs)
    for k in range(n_adapter):
        for j in range(MOST):
            start, used, _ = segment_of(table, k, j)
            value = total[pl.ds(start, SEGMENT_ROWS), :]
            if k >= first:
                rest_ref[k - first, j] = value
                continue
            lora = up_product(shares[k], j, up[k * MOST + j], rank)

            @pl.when(used)
            def _(start=start, value=value, lora=lora):
                o_ref[pl.ds(start, SEGMENT_ROWS), :] = (value + adapter_scale * lora).astype(
                    jnp.bfloat16
                )


def early(n_adapter, n_tensor, table, base, coded, shrinks, buffers, layout, rank):
    rows, columns = base.shape
    return pl.pallas_call(
        functools.partial(early_kernel, n_adapter, n_tensor, rank, layout, len(buffers)),
        in_specs=[SMEM] + [VMEM] * (1 + len(coded) + len(shrinks) + len(buffers)),
        out_specs=[VMEM, VMEM],
        out_shape=[
            jax.ShapeDtypeStruct((rows, columns), jnp.bfloat16),
            jax.ShapeDtypeStruct((LATE, MOST, SEGMENT_ROWS, columns), jnp.float32),
        ],
        scratch_shapes=[
            pltpu.VMEM(((n_adapter - LATE) * MOST, 2 * rank, columns), jnp.bfloat16),
            pltpu.VMEM((rows, columns), jnp.float32),
        ],
        compiler_params=params(16),
        cost_estimate=cost(6 * rows * rank * columns, (4 * n_tensor + 2) * rows * columns),
    )(table, base, *coded, *shrinks, *buffers)


def late_kernel(k, number, n_tensor, rank, layout, table, *refs):
    rest_ref, shrinks, refs = refs[0], refs[1 : 1 + n_tensor], refs[1 + n_tensor :]
    buffers, (_, o_ref, up, out, sems) = refs[:-5], refs[-5:]
    views = views_of(buffers, stages_of(k), layout, rank)
    share = shrinks[0][0]
    for r in shrinks[1:]:
        share = share + r[0]
    stores = []
    for j in range(MOST):
        fetch_up(up, j, table, k, j, views, rank)
        start, used, _ = segment_of(table, k, j)
        lora = up_product(share, j, up[j], rank)
        out[j] = (rest_ref[number, j] + adapter_scale * lora).astype(jnp.bfloat16)
        store = pltpu.make_async_copy(out.at[j], o_ref.at[pl.ds(start, SEGMENT_ROWS), :], sems.at[j])
        pl.when(used)(store.start)
        stores.append((used, store))
    for used, store in stores:
        pl.when(used)(store.wait)


def late(k, number, n_tensor, table, rest, shrinks, buffers, value, layout, rank):
    rows, columns = value.shape
    return pl.pallas_call(
        functools.partial(late_kernel, k, number, n_tensor, rank, layout),
        in_specs=[SMEM] + [VMEM] * (1 + len(shrinks) + len(buffers)) + [ANY],
        out_specs=ANY,
        out_shape=jax.ShapeDtypeStruct((rows, columns), jnp.bfloat16),
        scratch_shapes=[
            pltpu.VMEM((MOST, 2 * rank, columns), jnp.bfloat16),
            pltpu.VMEM((MOST, SEGMENT_ROWS, columns), jnp.bfloat16),
            pltpu.SemaphoreType.DMA((MOST,)),
        ],
        input_output_aliases={2 + len(shrinks) + len(buffers): 0},
        compiler_params=params(8),
        cost_estimate=cost(
            6 * MOST * SEGMENT_ROWS * rank * columns, 8 * MOST * SEGMENT_ROWS * columns
        ),
    )(table, rest, *shrinks, *buffers, value)


def after(array, *others):
    return lax.optimization_barrier((array, *others))[0]


def on_device(
    tokens, value_weight, adapter_down_weight, adapter_up_weight, row_adapter_index, adapter_slot_of
):
    rows, width = tokens.shape
    per_device, _, rank = adapter_down_weight.shape
    n_adapter = lax.axis_size("adapter")
    n_tensor = lax.axis_size("tensor")
    columns = value_weight.shape[1] // n_tensor

    def swap_tensor(array, step):
        pairs = [(i, (i + step) % n_tensor) for i in range(n_tensor)]
        return lax.ppermute(array, "tensor", pairs)

    def along_line(array, stage):
        up = [(2 * i, 2 * (i + 1)) for i in range(stage - 1, n_adapter - 1)]
        down = [(2 * i + 1, 2 * (i - 1) + 1) for i in range(1, n_adapter - stage + 1)]
        return lax.ppermute(array, ("adapter", "dp"), up + down)

    def swap_cores(array):
        return lax.ppermute(array, "dp", [(0, 1), (1, 0)])

    down = jnp.swapaxes(adapter_down_weight, 1, 2).reshape(per_device * rank, width)
    up = adapter_up_weight.reshape(per_device * rank, value_weight.shape[1])
    tokens, value_weight, down, up = (
        pltpu.with_memory_space_constraint(a, pltpu.HBM) for a in (tokens, value_weight, down, up)
    )
    messages = message_call(down, up, columns, per_device)
    table = table_call(row_adapter_index, adapter_slot_of, n_adapter, per_device)
    last = n_adapter - 1
    buffers, shrinks = [list(messages)], []
    layout = [(per_device, 0)] + [(per_device, per_device)] * last

    def buffers_of(stages):
        return [b for stage in stages for b in buffers[stage]]

    def shrink(k, kept, before=(), halves=()):
        mine = buffers_of(stages_of(k))
        return shrink_call(k, table, kept, list(before), list(halves), mine, layout, rank)

    def add_shrink(mine):
        shrinks.extend([mine] + [swap_tensor(mine, step) for step in range(1, n_tensor)])

    others = range(1, n_tensor)

    def sent_for(step, chunks, rows):
        sizes = [number for _, number in chunks]
        return sent_call(rows, value_weight, step, n_tensor, columns, chunks[0][0], sizes)

    def send(parts, *ahead):
        return [swap_tensor(after(p, *ahead), step) for step, p in zip(others, parts)]

    held = [along_line(m, 1) for m in messages]
    part_a = [sent_for(step, CHUNKS[:1], tokens)[0] for step in others]
    sent = [send(part_a)]
    first = after(held[0], table, *part_a)
    rest_parts = [sent_for(step, CHUNKS[1:], after(tokens, first)) for step in others]
    parts = [[p[i] for p in rest_parts] for i in range(len(CHUNKS) - 1)]
    part_b = [p for group in parts for p in group]
    held1 = held
    for stage in range(1, last):
        came = held
        if stage == 1:
            came = [first] + [after(h, *part_b, *sent[0]) for h in held[1:]]
            sent.append(send(parts[0], *came))
        if stage == 2:
            came = held[:1] + [after(h, base) for h in held[1:]]
            sent.append(send(parts[1], base, *sent[1]))
        held = [along_line(c, stage + 1) for c in came]
        if stage == 1:
            base, before, kept = own_call(
                after(table, held[0]),
                tokens,
                value_weight,
                messages,
                sent[0],
                columns,
                n_adapter,
            )
        else:
            ready = kept
            if stage == 2:
                base = add_call(1, after(base, held[0], *came), sent[1])
                ready = after(kept, base)
            before = shrink(stage - 1, ready, [before])[0]
        buffers.append([*came, *[swap_cores(h) for h in (held1 if stage == 1 else came)]])
    add_shrink(before)
    value, remaining = early(
        n_adapter,
        n_tensor,
        table,
        base,
        sent[2],
        shrinks,
        buffers_of(range(last - 1)),
        layout,
        rank,
    )
    buffers.append([*held, *[swap_cores(after(h, before, *sent[2])) for h in held]])
    ready = after(kept, *held)
    for k in (last - 1, last):
        mine = shrink(k, ready)[0]
        add_shrink(mine)
        ready = after(kept, mine)
    for number, k in enumerate((last - 1, last)):
        value = late(
            k,
            number,
            n_tensor,
            table,
            remaining,
            shrinks[(number - LATE) * n_tensor :][:n_tensor],
            buffers_of(stages_of(k)),
            value,
            layout,
            rank,
        )
    return value


def solution(mesh):
    return jax.shard_map(
        on_device,
        mesh=mesh,
        in_specs=(
            P(("groups", "adapter", "dp"), "tensor"),
            P("tensor", None),
            P(("groups", "adapter"), "tensor", None),
            P(("groups", "adapter"), None, None),
            P(("groups", "adapter", "dp")),
            P("groups"),
        ),
        out_specs=P(("groups", "adapter", "dp"), "tensor"),
        check_vma=False,
    )
```

```python
import functools

import jax
import jax.numpy as jnp
from jax import lax
from jax.experimental import pallas as pl
from jax.experimental.pallas import tpu as pltpu
from jax.sharding import PartitionSpec as P

SEGMENT_ROWS = 128
adapter_scale = 0.5
MOST = 2
BLOCK = 256
PIECES = 4
CHUNKS = ((5, 3), (0, 5))
ENTRIES = 8
MIDDLE = 1.5 * 2.0**23


def cost(flops, moved):
    return pl.CostEstimate(flops=int(flops), bytes_accessed=int(moved), transcendentals=0)


def params(mib):
    return pltpu.CompilerParams(vmem_limit_bytes=mib * 2**20)


ANY = pl.BlockSpec(memory_space=pl.ANY)
HBM = pl.BlockSpec(memory_space=pltpu.HBM)
SMEM = pl.BlockSpec(memory_space=pltpu.SMEM)
VMEM = pl.BlockSpec(memory_space=pltpu.VMEM)


def arrival_order(me, n_adapter):
    order = [me] + [jnp.int32(-1)] * (n_adapter - 1)
    count = jnp.int32(1)
    for distance in range(1, n_adapter):
        for other in (me - distance, me + distance):
            valid = (other >= 0) & (other < n_adapter)
            order = [jnp.where(valid & (count == k), other, o) for k, o in enumerate(order)]
            count = count + valid.astype(jnp.int32)
    return order


def views_of(refs, stages, layout, rank):
    me, core = lax.axis_index("adapter"), lax.axis_index("dp")
    refs, views = list(refs), []
    for stage in stages:
        came, swapped = layout[stage]
        toward = jnp.where(core == 0, -stage, stage)
        for i in range(came):
            views.append((refs.pop(0), 0, me + toward if stage > 0 else me, i))
        for i in range(swapped):
            ref = refs.pop(0)
            for part in range(came // swapped):
                views.append((ref, part * rank, me - toward, i + part))
    return views


def segment_of(table, k, j):
    seg = table[k * ENTRIES + 1 + 2 * j]
    start = pl.multiple_of(jnp.maximum(seg, 0) * SEGMENT_ROWS, SEGMENT_ROWS)
    return start, seg >= 0, table[k * ENTRIES + 2 + 2 * j]


def message_kernel(down_ref, up_ref, *refs):
    outs, sems = refs[:-1], refs[-1]
    rank = outs[0].shape[0]
    width = down_ref.shape[1]
    columns = outs[0].shape[1] - width
    start = pl.multiple_of(lax.axis_index("tensor") * columns, columns)
    copies = []
    for i, out in enumerate(outs):
        rows = pl.ds(i * rank, rank)
        copies += [
            pltpu.make_async_copy(down_ref.at[rows, :], out.at[:, pl.ds(0, width)], sems.at[0, i]),
            pltpu.make_async_copy(
                up_ref.at[rows, pl.ds(start, columns)], out.at[:, pl.ds(width, columns)], sems.at[1, i]
            ),
        ]
    for copy in copies:
        copy.start()
    for copy in copies:
        copy.wait()


def message_call(down, up, columns, per_device):
    rows, width = down.shape
    shape = jax.ShapeDtypeStruct((rows // per_device, width + columns), jnp.bfloat16)
    return pl.pallas_call(
        message_kernel,
        in_specs=[HBM, HBM],
        out_specs=[VMEM] * per_device,
        out_shape=[shape] * per_device,
        scratch_shapes=[pltpu.SemaphoreType.DMA((2, per_device))],
        compiler_params=params(8),
        cost_estimate=cost(0, 4 * rows * (width + columns)),
    )(down, up)


def table_kernel(n_adapter, per_device, ids, slots, table):
    seg_dev = ids.shape[0] // SEGMENT_ROWS
    used = [slots[ids[s * SEGMENT_ROWS]] for s in range(seg_dev)]
    for k, owner in enumerate(arrival_order(lax.axis_index("adapter"), n_adapter)):
        table[k * ENTRIES] = owner
        found, place = [jnp.int32(-1)] * MOST, [jnp.int32(0)] * MOST
        count = jnp.int32(0)
        for s, slot in enumerate(used):
            within = slot - owner * per_device
            hit = (within >= 0) & (within < per_device)
            for j in range(MOST):
                take = hit & (count == j)
                found[j] = jnp.where(take, s, found[j])
                place[j] = jnp.where(take, within, place[j])
            count = count + hit.astype(jnp.int32)
        for j in range(MOST):
            table[k * ENTRIES + 1 + 2 * j] = found[j]
            table[k * ENTRIES + 2 + 2 * j] = place[j]


def table_call(ids, slots, n_adapter, per_device):
    return pl.pallas_call(
        functools.partial(table_kernel, n_adapter, per_device),
        in_specs=[SMEM, SMEM],
        out_specs=SMEM,
        out_shape=jax.ShapeDtypeStruct((n_adapter * ENTRIES,), jnp.int32),
        cost_estimate=cost(0, 4 * ids.shape[0]),
    )(ids, slots)


def diagonal():
    shape = (SEGMENT_ROWS, SEGMENT_ROWS)
    return lax.broadcasted_iota(jnp.int32, shape, 0) == lax.broadcasted_iota(jnp.int32, shape, 1)


GROUP = SEGMENT_ROWS // 8
WORDS = 5 * GROUP


def coded_rows(segments):
    return segments * WORDS + 8


def encode(values, o_ref, unit, units):
    largest = jnp.maximum(jnp.max(jnp.abs(values), axis=1, keepdims=True), 2.0**-100)
    power = jnp.floor(jnp.log2(largest))
    whole = (values * jnp.exp2(18.0 - power) + MIDDLE).astype(jnp.int32) - int(MIDDLE)
    whole = jnp.minimum(whole, 2**19 - 1)
    v = [whole[i * GROUP : (i + 1) * GROUP] for i in range(8)]
    over = [
        v[5] & 0xFFF,
        ((v[5] >> 12) & 0xFF) | ((v[6] & 0xF) << 8),
        (v[6] >> 4) & 0xFFF,
        ((v[6] >> 16) & 0xF) | ((v[7] & 0xFF) << 4),
        v[7] >> 8,
    ]
    for i in range(5):
        o_ref[unit * WORDS + i * GROUP : unit * WORDS + (i + 1) * GROUP, :] = (v[i] & 0xFFFFF) | (
            over[i] << 20
        )
    row = jnp.sum(jnp.where(diagonal(), power, 0.0), axis=0, keepdims=True)
    o_ref[units * WORDS + unit : units * WORDS + unit + 1, :SEGMENT_ROWS] = row.astype(jnp.int32)


def decode(ref, unit, units):
    w = [ref[unit * WORDS + i * GROUP : unit * WORDS + (i + 1) * GROUP, :] for i in range(5)]
    v = [(x << 12) >> 12 for x in w]
    v.append(((w[0] >> 20) & 0xFFF) | (((w[1] << 4) >> 24) << 12))
    v.append(((w[1] >> 28) & 0xF) | (((w[2] >> 20) & 0xFFF) << 4) | (((w[3] << 8) >> 28) << 16))
    v.append(((w[3] >> 24) & 0xFF) | ((w[4] >> 20) << 8))
    row = ref[units * WORDS + unit : units * WORDS + unit + 1, :SEGMENT_ROWS].astype(jnp.float32)
    power = jnp.sum(jnp.where(diagonal(), row, 0.0), axis=1, keepdims=True)
    return jnp.concatenate(v, axis=0).astype(jnp.float32) * jnp.exp2(power - 18.0)


def add_decoded(sums, chunk, refs, above):
    first, number = CHUNKS[chunk]
    for unit in range(number):
        at = first + unit - above
        if at < 0 or at >= sums.shape[0] // SEGMENT_ROWS:
            continue
        rows = pl.ds(at * SEGMENT_ROWS, SEGMENT_ROWS)
        value = sums[rows, :]
        for ref in refs:
            value = value + decode(ref, unit, number)
        sums[rows, :] = value


def load_base(first, segments, column, x_ref, w_ref, x, w, sems):
    width, columns = w.shape
    rows = segments * SEGMENT_ROWS
    start = pl.multiple_of(column * columns, columns)
    depth = width // PIECES
    blocks = [(r, min(BLOCK, rows - r)) for r in range(0, rows, BLOCK)]

    def x_copy(at, size, features, sem):
        return pltpu.make_async_copy(
            x_ref.at[pl.ds(first * SEGMENT_ROWS + at, size), features],
            x.at[pl.ds(at, size), features],
            sem,
        )

    work = []
    for i, (at, size) in enumerate(blocks):
        terms = []
        if i == 0:
            for p in range(PIECES):
                features = pl.ds(p * depth, depth)
                copies = (
                    pltpu.make_async_copy(
                        w_ref.at[features, pl.ds(start, columns)], w.at[features, :], sems.at[0, p]
                    ),
                    x_copy(0, size, features, sems.at[1, p]),
                )
                terms.append((copies, slice(p * depth, (p + 1) * depth)))
        else:
            terms.append(((x_copy(at, size, slice(None), sems.at[2, i]),), slice(None)))
        work.append((at, size, terms))
    for _, _, terms in work:
        for copies, _ in terms:
            for copy in copies:
                copy.start()
    return work


def block_product(x, w, at, size, terms):
    total = None
    for copies, features in terms:
        for copy in copies:
            copy.wait()
        term = jnp.dot(
            x[at : at + size, features], w[features, :], preferred_element_type=jnp.float32
        )
        total = term if total is None else total + term
    return total


def base_scratch(segments, width, columns):
    rows = segments * SEGMENT_ROWS
    return [
        pltpu.VMEM((rows, width), jnp.bfloat16),
        pltpu.VMEM((width, columns), jnp.bfloat16),
        pltpu.SemaphoreType.DMA((3, max(PIECES, rows // BLOCK + 1))),
    ]


def sent_kernel(first, sizes, step, n_tensor, x_ref, w_ref, *refs):
    outs, (x, w, sems) = refs[: len(sizes)], refs[len(sizes) :]
    column = lax.rem(lax.axis_index("tensor") + step, n_tensor)
    work = load_base(first, sum(sizes), column, x_ref, w_ref, x, w, sems)
    unit_of = [(out, unit) for out, size in enumerate(sizes) for unit in range(size)]
    for out, size in zip(outs, sizes):
        out[size * WORDS :, :] = jnp.zeros((8, w.shape[1]), jnp.int32)
    for at, size, terms in work:
        product = block_product(x, w, at, size, terms)
        for r in range(0, size, SEGMENT_ROWS):
            out, unit = unit_of[(at + r) // SEGMENT_ROWS]
            encode(product[r : r + SEGMENT_ROWS], outs[out], unit, sizes[out])


def sent_call(tokens, weight, step, n_tensor, columns, first, sizes):
    width = tokens.shape[1]
    rows = sum(sizes) * SEGMENT_ROWS
    return pl.pallas_call(
        functools.partial(sent_kernel, first, sizes, step, n_tensor),
        in_specs=[HBM, HBM],
        out_specs=[VMEM] * len(sizes),
        out_shape=[jax.ShapeDtypeStruct((coded_rows(n), columns), jnp.int32) for n in sizes],
        scratch_shapes=base_scratch(sum(sizes), width, columns),
        compiler_params=params(16),
        cost_estimate=cost(
            2 * rows * width * columns, 2 * rows * width + 2 * width * columns + 4 * rows * columns
        ),
    )(tokens, weight)


def add_kernel(chunk, above, sums_ref, *refs):
    coded_refs, o_ref = refs[:-1], refs[-1]
    o_ref[...] = sums_ref[...]
    add_decoded(o_ref, chunk, coded_refs, above)


def add_call(chunk, above, sums, coded):
    return pl.pallas_call(
        functools.partial(add_kernel, chunk, above),
        in_specs=[VMEM] * (1 + len(coded)),
        out_specs=VMEM,
        out_shape=jax.ShapeDtypeStruct(sums.shape, sums.dtype),
        compiler_params=params(8),
        cost_estimate=cost(40000 * sums.size, 12 * sums.size),
    )(sums, *coded)


def shrink_into(o_ref, at, table, k, rows_of, views, rank):
    for j in range(MOST):
        _, _, within = segment_of(table, k, j)
        for ref, first, whose, i in views:

            @pl.when((whose == table[k * ENTRIES]) & (within == i))
            def _(j=j, ref=ref, first=first):
                rows = rows_of(j)
                o_ref[at, :, j * rank : (j + 1) * rank] = lax.dot_general(
                    rows,
                    ref[first : first + rank, : rows.shape[1]],
                    (((1,), (1,)), ((), ())),
                    preferred_element_type=jnp.float32,
                )


def join_copies(halves, whole, sems):
    copies, rank = [], halves[0].shape[0]
    for i, half in enumerate(halves):
        copies.append(
            pltpu.make_async_copy(half, whole.at[pl.ds(i * rank, rank), :], sems.at[i])
        )
        copies[-1].start()
    return copies


def stages_of(k):
    return range((k + 1) // 2, k + 1)


def upper_kernel(n_adapter, table, x_ref, w_ref, o_ref, kept_ref, x, w, sems, kept_sems):
    work = load_base(0, x.shape[0] // SEGMENT_ROWS, lax.axis_index("tensor"), x_ref, w_ref, x, w, sems)
    keeps = []
    for k in range(1, n_adapter):
        for j in range(MOST):
            start, _, _ = segment_of(table, k, j)
            keeps.append(
                pltpu.make_async_copy(
                    x_ref.at[pl.ds(start, SEGMENT_ROWS), :],
                    kept_ref.at[k - 1, j],
                    kept_sems.at[k - 1, j],
                )
            )
            keeps[-1].start()
    for at, size, terms in work:
        o_ref[at : at + size, :] = block_product(x, w, at, size, terms)
    for copy in keeps:
        copy.wait()


def upper_call(table, tokens, weight, columns, n_adapter):
    rows, width = tokens.shape
    half = rows // 2
    return pl.pallas_call(
        functools.partial(upper_kernel, n_adapter),
        in_specs=[SMEM, HBM, HBM],
        out_specs=[VMEM] * 2,
        out_shape=[
            jax.ShapeDtypeStruct((half, columns), jnp.float32),
            jax.ShapeDtypeStruct((n_adapter - 1, MOST, SEGMENT_ROWS, width), jnp.bfloat16),
        ],
        scratch_shapes=base_scratch(half // SEGMENT_ROWS, width, columns)
        + [pltpu.SemaphoreType.DMA((n_adapter - 1, MOST))],
        compiler_params=params(12),
        cost_estimate=cost(2 * half * width * columns, 2 * rows * width + 2 * width * columns),
    )(table, tokens, weight)


def lower_kernel(per_device, rank, table, x_ref, w_ref, *refs):
    messages, halves, refs = refs[:per_device], refs[per_device : 2 * per_device], refs[2 * per_device :]
    coded_refs, (o_ref, s_ref, whole_ref, x, w, sems, mine, mine_sems, join_sems) = refs[:-9], refs[-9:]
    above = x.shape[0] // SEGMENT_ROWS
    work = load_base(above, above, lax.axis_index("tensor"), x_ref, w_ref, x, w, sems)
    joins = join_copies(halves, whole_ref, join_sems)
    loads = []
    for j in range(MOST):
        start, _, _ = segment_of(table, 0, j)
        loads.append(
            pltpu.make_async_copy(
                x_ref.at[pl.ds(start, SEGMENT_ROWS), :], mine.at[j], mine_sems.at[j]
            )
        )
        loads[-1].start()
    for at, size, terms in work:
        o_ref[at : at + size, :] = block_product(x, w, at, size, terms)
    add_decoded(o_ref, 0, coded_refs, above)
    for copy in loads:
        copy.wait()
    views = views_of(messages, [0], [(per_device, 0)], rank)
    shrink_into(s_ref, 0, table, 0, lambda j: mine[j], views, rank)
    for copy in joins:
        copy.wait()


def lower_call(table, tokens, weight, messages, halves, coded, columns):
    rows, width = tokens.shape
    half = rows // 2
    per_device, (rank, long) = len(messages), messages[0].shape
    return pl.pallas_call(
        functools.partial(lower_kernel, per_device, rank),
        in_specs=[SMEM, HBM, HBM] + [VMEM] * (2 * per_device + len(coded)),
        out_specs=[VMEM] * 3,
        out_shape=[
            jax.ShapeDtypeStruct((half, columns), jnp.float32),
            jax.ShapeDtypeStruct((1, SEGMENT_ROWS, MOST * rank), jnp.float32),
            jax.ShapeDtypeStruct((per_device * rank, long), jnp.bfloat16),
        ],
        scratch_shapes=base_scratch(half // SEGMENT_ROWS, width, columns)
        + [
            pltpu.VMEM((MOST, SEGMENT_ROWS, width), jnp.bfloat16),
            pltpu.SemaphoreType.DMA((MOST,)),
            pltpu.SemaphoreType.DMA((per_device,)),
        ],
        compiler_params=params(14),
        cost_estimate=cost(0 * half * width * columns, 4 * rows * columns),
    )(table, tokens, weight, *messages, *halves, *coded)


def shrink_kernel(k, rank, at, layout, n_halves, table, kept_ref, *refs):
    before, refs = refs[: 1 if at else 0], refs[1 if at else 0 :]
    halves, refs = refs[:n_halves], refs[n_halves:]
    joins = []
    if n_halves:
        refs, whole_ref, sems = refs[:-2], refs[-2], refs[-1]
        joins = join_copies(halves, whole_ref, sems)
    buffers, o_ref = refs[:-1], refs[-1]
    for r in before:
        o_ref[:at] = r[...]
    views = views_of(buffers, stages_of(k), layout, rank)
    shrink_into(o_ref, at, table, k, lambda j: kept_ref[k - 1, j], views, rank)
    for copy in joins:
        copy.wait()


def shrink_call(k, table, kept, before, halves, buffers, layout, rank):
    width = kept.shape[3]
    at = sum(b.shape[0] for b in before)
    shapes = [jax.ShapeDtypeStruct((at + 1, SEGMENT_ROWS, MOST * rank), jnp.float32)]
    if halves:
        shapes.append(jax.ShapeDtypeStruct((len(halves) * rank, halves[0].shape[1]), jnp.bfloat16))
    return pl.pallas_call(
        functools.partial(shrink_kernel, k, rank, at, layout, len(halves)),
        in_specs=[SMEM] + [VMEM] * (1 + len(before) + len(halves) + len(buffers)),
        out_specs=[VMEM] * len(shapes),
        out_shape=shapes,
        scratch_shapes=[pltpu.SemaphoreType.DMA((len(halves),))] if halves else [],
        compiler_params=params(4),
        cost_estimate=cost(MOST * 2 * SEGMENT_ROWS * width * 256, 4 * SEGMENT_ROWS * width),
    )(table, kept, *before, *halves, *buffers)


def fetch_up(up, at, table, k, j, views, rank):
    columns = up.shape[2]
    _, _, within = segment_of(table, k, j)
    for ref, first, whose, i in views:

        @pl.when((whose == table[k * ENTRIES]) & (within == i))
        def _(ref=ref, first=first):
            factor = ref[first : first + rank, ref.shape[1] - columns :]
            up[at, :rank, :] = factor
            up[at, rank:, :] = factor


def up_product(share, j, factor, rank):
    lane = lax.broadcasted_iota(jnp.int32, share.shape, 1)
    other = pltpu.roll(share, rank, 1)
    both = jnp.where((lane < rank) == (j == 0), share, other)
    high = both.astype(jnp.bfloat16).astype(jnp.float32)
    terms = jnp.where(lane < rank, high, both - high).astype(jnp.bfloat16)
    return jnp.dot(terms, factor, preferred_element_type=jnp.float32)


LATE = 2


def early_kernel(n_adapter, n_tensor, rank, layout, n_buffers, table, *refs):
    first = n_adapter - LATE
    upper_ref, lower_ref, refs = refs[0], refs[1], refs[2:]
    shrinks, refs = refs[: -4 - n_buffers], refs[-4 - n_buffers :]
    buffers, (o_ref, rest_ref, up, base_ref) = refs[:-4], refs[-4:]
    rows = upper_ref.shape[0]
    base_ref[:rows, :] = upper_ref[...]
    base_ref[rows:, :] = lower_ref[...]
    views = views_of(buffers, range(first), layout, rank)
    for k in range(first):
        for j in range(MOST):
            fetch_up(up, k * MOST + j, table, k, j, views, rank)
    shares = []
    for call in range(len(shrinks) // n_tensor):
        share = shrinks[call * n_tensor][...]
        for i in range(1, n_tensor):
            share = share + shrinks[call * n_tensor + i][...]
        shares += [share[i] for i in range(share.shape[0])]
    for k in range(n_adapter):
        for j in range(MOST):
            start, used, _ = segment_of(table, k, j)
            value = base_ref[pl.ds(start, SEGMENT_ROWS), :]
            if k >= first:
                rest_ref[k - first, j] = value
                continue
            lora = up_product(shares[k], j, up[k * MOST + j], rank)

            @pl.when(used)
            def _(start=start, value=value, lora=lora):
                o_ref[pl.ds(start, SEGMENT_ROWS), :] = (value + adapter_scale * lora).astype(
                    jnp.bfloat16
                )


def early(n_adapter, n_tensor, table, upper, lower, shrinks, buffers, layout, rank):
    rows, columns = upper.shape[0] + lower.shape[0], upper.shape[1]
    return pl.pallas_call(
        functools.partial(early_kernel, n_adapter, n_tensor, rank, layout, len(buffers)),
        in_specs=[SMEM] + [VMEM] * (2 + len(shrinks) + len(buffers)),
        out_specs=[VMEM, VMEM],
        out_shape=[
            jax.ShapeDtypeStruct((rows, columns), jnp.bfloat16),
            jax.ShapeDtypeStruct((LATE, MOST, SEGMENT_ROWS, columns), jnp.float32),
        ],
        scratch_shapes=[
            pltpu.VMEM(((n_adapter - LATE) * MOST, 2 * rank, columns), jnp.bfloat16),
            pltpu.VMEM((rows, columns), jnp.float32),
        ],
        compiler_params=params(16),
        cost_estimate=cost(6 * rows * rank * columns, (4 * n_tensor + 2) * rows * columns),
    )(table, upper, lower, *shrinks, *buffers)


def late_kernel(ks, n_tensor, rank, layout, table, *refs):
    rest_ref, shrinks, refs = refs[0], refs[1 : 1 + len(ks) * n_tensor], refs[1 + len(ks) * n_tensor :]
    buffers, (_, o_ref, up, out, sems) = refs[:-5], refs[-5:]
    views = views_of(buffers, stages_of_all(ks), layout, rank)
    stores = []
    for i, k in enumerate(ks):
        share = shrinks[i * n_tensor][0]
        for r in shrinks[i * n_tensor + 1 : (i + 1) * n_tensor]:
            share = share + r[0]
        for j in range(MOST):
            fetch_up(up, i * MOST + j, table, k, j, views, rank)
            start, used, _ = segment_of(table, k, j)
            lora = up_product(share, j, up[i * MOST + j], rank)
            out[i, j] = (rest_ref[i, j] + adapter_scale * lora).astype(jnp.bfloat16)
            store = pltpu.make_async_copy(
                out.at[i, j], o_ref.at[pl.ds(start, SEGMENT_ROWS), :], sems.at[i, j]
            )
            pl.when(used)(store.start)
            stores.append((used, store))
    for used, store in stores:
        pl.when(used)(store.wait)


def stages_of_all(ks):
    return range(stages_of(ks[0])[0], ks[-1] + 1)


def late(ks, n_tensor, table, rest, shrinks, buffers, value, layout, rank):
    rows, columns = value.shape
    return pl.pallas_call(
        functools.partial(late_kernel, ks, n_tensor, rank, layout),
        in_specs=[SMEM] + [VMEM] * (1 + len(shrinks) + len(buffers)) + [ANY],
        out_specs=ANY,
        out_shape=jax.ShapeDtypeStruct((rows, columns), jnp.bfloat16),
        scratch_shapes=[
            pltpu.VMEM((LATE * MOST, 2 * rank, columns), jnp.bfloat16),
            pltpu.VMEM((LATE, MOST, SEGMENT_ROWS, columns), jnp.bfloat16),
            pltpu.SemaphoreType.DMA((LATE, MOST)),
        ],
        input_output_aliases={2 + len(shrinks) + len(buffers): 0},
        compiler_params=params(8),
        cost_estimate=cost(
            6 * LATE * MOST * SEGMENT_ROWS * rank * columns,
            8 * LATE * MOST * SEGMENT_ROWS * columns,
        ),
    )(table, rest, *shrinks, *buffers, value)


def after(array, *others):
    return lax.optimization_barrier((array, *others))[0]


def on_device(
    tokens, value_weight, adapter_down_weight, adapter_up_weight, row_adapter_index, adapter_slot_of
):
    rows, width = tokens.shape
    per_device, _, rank = adapter_down_weight.shape
    n_adapter = lax.axis_size("adapter")
    n_tensor = lax.axis_size("tensor")
    columns = value_weight.shape[1] // n_tensor

    def swap_tensor(array, step):
        pairs = [(i, (i + step) % n_tensor) for i in range(n_tensor)]
        return lax.ppermute(array, "tensor", pairs)

    def along_line(array, stage):
        up = [(2 * i, 2 * (i + 1)) for i in range(stage - 1, n_adapter - 1)]
        down = [(2 * i + 1, 2 * (i - 1) + 1) for i in range(1, n_adapter - stage + 1)]
        return lax.ppermute(array, ("adapter", "dp"), up + down)

    def swap_cores(array):
        return lax.ppermute(array, "dp", [(0, 1), (1, 0)])

    down = jnp.swapaxes(adapter_down_weight, 1, 2).reshape(per_device * rank, width)
    up = adapter_up_weight.reshape(per_device * rank, value_weight.shape[1])
    tokens, value_weight, down, up = (
        pltpu.with_memory_space_constraint(a, pltpu.HBM) for a in (tokens, value_weight, down, up)
    )
    messages = message_call(down, up, columns, per_device)
    table = table_call(row_adapter_index, adapter_slot_of, n_adapter, per_device)
    last = n_adapter - 1
    buffers, shrinks = [list(messages)], []
    layout = [(per_device, 0), (per_device, 1)] + [(per_device, per_device)] * (last - 1)

    def buffers_of(stages):
        return [b for stage in stages for b in buffers[stage]]

    def shrink(k, kept, before=(), halves=()):
        mine = buffers_of(stages_of(k))
        return shrink_call(k, table, kept, list(before), list(halves), mine, layout, rank)

    def add_shrink(mine):
        shrinks.extend([mine] + [swap_tensor(mine, step) for step in range(1, n_tensor)])

    others = range(1, n_tensor)

    def sent_for(step, chunks, rows):
        sizes = [number for _, number in chunks]
        return sent_call(rows, value_weight, step, n_tensor, columns, chunks[0][0], sizes)

    def send(parts, *ahead):
        return [swap_tensor(after(p, *ahead), step) for step, p in zip(others, parts)]

    held = [along_line(m, 1) for m in messages]
    part_a = [sent_for(step, CHUNKS[:1], tokens)[0] for step in others]
    sent = [send(part_a)]
    first = after(held[0], table, *part_a)
    rest_parts = [sent_for(step, CHUNKS[1:], after(tokens, first)) for step in others]
    parts = [[p[i] for p in rest_parts] for i in range(len(CHUNKS) - 1)]
    part_b = [p for group in parts for p in group]
    for stage in range(1, last):
        came = held
        if stage == 1:
            came = [first] + [after(h, *part_b) for h in held[1:]]
            sent.append(send(parts[0], *came, *sent[0]))
        if stage == 2:
            came = held[:1] + [after(h, upper) for h in held[1:]]
        held = [along_line(c, stage + 1) for c in came]
        if stage == 1:
            upper, kept = upper_call(
                after(table, held[0], *came), tokens, value_weight, columns, n_adapter
            )
        elif stage == 2:
            lower, before, joined = lower_call(
                after(table, *came), tokens, value_weight, messages, buffers[1], sent[0], columns
            )
            buffers[1] += [swap_cores(joined)]
            free = lower
            above = rows // SEGMENT_ROWS // 2
            upper = add_call(1, 0, after(upper, held[0]), sent[1])
            lower = add_call(1, above, after(lower, upper, *held[1:]), sent[1])
            before = shrink(1, after(kept, lower), [before])[0]
        else:
            before = shrink(stage - 1, kept, [before])[0]
        ahead = [free] if stage == 2 else []
        swapped = [swap_cores(after(c, *ahead)) for c in came] if stage > 1 else []
        buffers.append([*came, *swapped])
    add_shrink(before)
    value, remaining = early(
        n_adapter,
        n_tensor,
        table,
        upper,
        lower,
        shrinks,
        buffers_of(range(last - 1)),
        layout,
        rank,
    )
    buffers.append([*held, *[swap_cores(h) for h in held]])
    ready = after(kept, *held)
    for k in (last - 1, last):
        mine = shrink(k, ready)[0]
        add_shrink(mine)
        ready = after(kept, mine)
    ks = (last - 1, last)
    return late(
        ks,
        n_tensor,
        table,
        remaining,
        shrinks[-LATE * n_tensor :],
        buffers_of(stages_of_all(ks)),
        value,
        layout,
        rank,
    )


def solution(mesh):
    return jax.shard_map(
        on_device,
        mesh=mesh,
        in_specs=(
            P(("groups", "adapter", "dp"), "tensor"),
            P("tensor", None),
            P(("groups", "adapter"), "tensor", None),
            P(("groups", "adapter"), None, None),
            P(("groups", "adapter", "dp")),
            P("groups"),
        ),
        out_specs=P(("groups", "adapter", "dp"), "tensor"),
        check_vma=False,
    )
```

```python
import functools

import jax
import jax.numpy as jnp
from jax import lax
from jax.experimental import pallas as pl
from jax.experimental.pallas import tpu as pltpu
from jax.sharding import PartitionSpec as P

SEGMENT_ROWS = 128
adapter_scale = 0.5
MOST = 2
BLOCK = 256
PIECES = 4
CHUNKS = ((6, 2), (0, 6))
UPPER = 3
ENTRIES = 8
MIDDLE = 1.5 * 2.0**23


def cost(flops, moved):
    return pl.CostEstimate(flops=int(flops), bytes_accessed=int(moved), transcendentals=0)


def params(mib):
    return pltpu.CompilerParams(vmem_limit_bytes=mib * 2**20)


ANY = pl.BlockSpec(memory_space=pl.ANY)
HBM = pl.BlockSpec(memory_space=pltpu.HBM)
SMEM = pl.BlockSpec(memory_space=pltpu.SMEM)
VMEM = pl.BlockSpec(memory_space=pltpu.VMEM)


def arrival_order(me, n_adapter):
    order = [me] + [jnp.int32(-1)] * (n_adapter - 1)
    count = jnp.int32(1)
    for distance in range(1, n_adapter):
        for other in (me - distance, me + distance):
            valid = (other >= 0) & (other < n_adapter)
            order = [jnp.where(valid & (count == k), other, o) for k, o in enumerate(order)]
            count = count + valid.astype(jnp.int32)
    return order


def views_of(refs, stages, layout, rank):
    me, core = lax.axis_index("adapter"), lax.axis_index("dp")
    refs, views = list(refs), []
    for stage in stages:
        came, swapped = layout[stage]
        toward = jnp.where(core == 0, -stage, stage)
        for i in range(came):
            views.append((stage, refs.pop(0), 0, me + toward if stage > 0 else me, i))
        for i in range(swapped):
            ref = refs.pop(0)
            for part in range(came // swapped):
                views.append((stage, ref, part * rank, me - toward, i + part))
    return views


def segment_of(table, k, j):
    seg = table[k * ENTRIES + 1 + 2 * j]
    start = pl.multiple_of(jnp.maximum(seg, 0) * SEGMENT_ROWS, SEGMENT_ROWS)
    return start, seg >= 0, table[k * ENTRIES + 2 + 2 * j]


def message_kernel(down_ref, up_ref, *refs):
    outs, sems = refs[:-1], refs[-1]
    rank = outs[0].shape[0]
    width = down_ref.shape[1]
    columns = outs[0].shape[1] - width
    start = pl.multiple_of(lax.axis_index("tensor") * columns, columns)
    copies = []
    for i, out in enumerate(outs):
        rows = pl.ds(i * rank, rank)
        copies += [
            pltpu.make_async_copy(down_ref.at[rows, :], out.at[:, pl.ds(0, width)], sems.at[0, i]),
            pltpu.make_async_copy(
                up_ref.at[rows, pl.ds(start, columns)], out.at[:, pl.ds(width, columns)], sems.at[1, i]
            ),
        ]
    for copy in copies:
        copy.start()
    for copy in copies:
        copy.wait()


def message_call(down, up, columns, per_device):
    rows, width = down.shape
    shape = jax.ShapeDtypeStruct((rows // per_device, width + columns), jnp.bfloat16)
    return pl.pallas_call(
        message_kernel,
        in_specs=[HBM, HBM],
        out_specs=[VMEM] * per_device,
        out_shape=[shape] * per_device,
        scratch_shapes=[pltpu.SemaphoreType.DMA((2, per_device))],
        compiler_params=params(8),
        cost_estimate=cost(0, 4 * rows * (width + columns)),
    )(down, up)


def table_kernel(n_adapter, per_device, ids, slots, table):
    seg_dev = ids.shape[0] // SEGMENT_ROWS
    used = [slots[ids[s * SEGMENT_ROWS]] for s in range(seg_dev)]
    for k, owner in enumerate(arrival_order(lax.axis_index("adapter"), n_adapter)):
        table[k * ENTRIES] = owner
        found, place = [jnp.int32(-1)] * MOST, [jnp.int32(0)] * MOST
        count = jnp.int32(0)
        for s, slot in enumerate(used):
            within = slot - owner * per_device
            hit = (within >= 0) & (within < per_device)
            for j in range(MOST):
                take = hit & (count == j)
                found[j] = jnp.where(take, s, found[j])
                place[j] = jnp.where(take, within, place[j])
            count = count + hit.astype(jnp.int32)
        for j in range(MOST):
            table[k * ENTRIES + 1 + 2 * j] = found[j]
            table[k * ENTRIES + 2 + 2 * j] = place[j]


def table_call(ids, slots, n_adapter, per_device):
    return pl.pallas_call(
        functools.partial(table_kernel, n_adapter, per_device),
        in_specs=[SMEM, SMEM],
        out_specs=SMEM,
        out_shape=jax.ShapeDtypeStruct((n_adapter * ENTRIES,), jnp.int32),
        cost_estimate=cost(0, 4 * ids.shape[0]),
    )(ids, slots)


def diagonal():
    shape = (SEGMENT_ROWS, SEGMENT_ROWS)
    return lax.broadcasted_iota(jnp.int32, shape, 0) == lax.broadcasted_iota(jnp.int32, shape, 1)


GROUP = SEGMENT_ROWS // 8
WORDS = 5 * GROUP


def coded_rows(segments):
    return segments * WORDS + 8


def encode(values, o_ref, unit, units):
    largest = jnp.maximum(jnp.max(jnp.abs(values), axis=1, keepdims=True), 2.0**-100)
    power = jnp.floor(jnp.log2(largest))
    whole = (values * jnp.exp2(18.0 - power) + MIDDLE).astype(jnp.int32) - int(MIDDLE)
    whole = jnp.minimum(whole, 2**19 - 1)
    v = [whole[i * GROUP : (i + 1) * GROUP] for i in range(8)]
    over = [
        v[5] & 0xFFF,
        ((v[5] >> 12) & 0xFF) | ((v[6] & 0xF) << 8),
        (v[6] >> 4) & 0xFFF,
        ((v[6] >> 16) & 0xF) | ((v[7] & 0xFF) << 4),
        v[7] >> 8,
    ]
    for i in range(5):
        o_ref[unit * WORDS + i * GROUP : unit * WORDS + (i + 1) * GROUP, :] = (v[i] & 0xFFFFF) | (
            over[i] << 20
        )
    row = jnp.sum(jnp.where(diagonal(), power, 0.0), axis=0, keepdims=True)
    o_ref[units * WORDS + unit : units * WORDS + unit + 1, :SEGMENT_ROWS] = row.astype(jnp.int32)


def decode(ref, unit, units):
    w = [ref[unit * WORDS + i * GROUP : unit * WORDS + (i + 1) * GROUP, :] for i in range(5)]
    v = [(x << 12) >> 12 for x in w]
    v.append(((w[0] >> 20) & 0xFFF) | (((w[1] << 4) >> 24) << 12))
    v.append(((w[1] >> 28) & 0xF) | (((w[2] >> 20) & 0xFFF) << 4) | (((w[3] << 8) >> 28) << 16))
    v.append(((w[3] >> 24) & 0xFF) | ((w[4] >> 20) << 8))
    row = ref[units * WORDS + unit : units * WORDS + unit + 1, :SEGMENT_ROWS].astype(jnp.float32)
    power = jnp.sum(jnp.where(diagonal(), row, 0.0), axis=1, keepdims=True)
    return jnp.concatenate(v, axis=0).astype(jnp.float32) * jnp.exp2(power - 18.0)


def add_decoded(sums, chunk, refs, above):
    first, number = CHUNKS[chunk]
    for unit in range(number):
        at = first + unit - above
        if at < 0 or at >= sums.shape[0] // SEGMENT_ROWS:
            continue
        rows = pl.ds(at * SEGMENT_ROWS, SEGMENT_ROWS)
        value = sums[rows, :]
        for ref in refs:
            value = value + decode(ref, unit, number)
        sums[rows, :] = value


def load_base(first, segments, column, x_ref, w_ref, x, w, sems):
    width, columns = w.shape
    rows = segments * SEGMENT_ROWS
    start = pl.multiple_of(column * columns, columns)
    depth = width // PIECES
    blocks = [(r, min(BLOCK, rows - r)) for r in range(0, rows, BLOCK)]

    def x_copy(at, size, features, sem):
        return pltpu.make_async_copy(
            x_ref.at[pl.ds(first * SEGMENT_ROWS + at, size), features],
            x.at[pl.ds(at, size), features],
            sem,
        )

    work = []
    for i, (at, size) in enumerate(blocks):
        terms = []
        if i == 0:
            for p in range(PIECES):
                features = pl.ds(p * depth, depth)
                copies = (
                    pltpu.make_async_copy(
                        w_ref.at[features, pl.ds(start, columns)], w.at[features, :], sems.at[0, p]
                    ),
                    x_copy(0, size, features, sems.at[1, p]),
                )
                terms.append((copies, slice(p * depth, (p + 1) * depth)))
        else:
            terms.append(((x_copy(at, size, slice(None), sems.at[2, i]),), slice(None)))
        work.append((at, size, terms))
    for _, _, terms in work:
        for copies, _ in terms:
            for copy in copies:
                copy.start()
    return work


def block_product(x, w, at, size, terms):
    total = None
    for copies, features in terms:
        for copy in copies:
            copy.wait()
        term = jnp.dot(
            x[at : at + size, features], w[features, :], preferred_element_type=jnp.float32
        )
        total = term if total is None else total + term
    return total


def base_scratch(segments, width, columns):
    rows = segments * SEGMENT_ROWS
    return [
        pltpu.VMEM((rows, width), jnp.bfloat16),
        pltpu.VMEM((width, columns), jnp.bfloat16),
        pltpu.SemaphoreType.DMA((3, max(PIECES, rows // BLOCK + 1))),
    ]


def sent_kernel(first, sizes, step, n_tensor, x_ref, w_ref, *refs):
    outs, (x, w, sems) = refs[: len(sizes)], refs[len(sizes) :]
    column = lax.rem(lax.axis_index("tensor") + step, n_tensor)
    work = load_base(first, sum(sizes), column, x_ref, w_ref, x, w, sems)
    unit_of = [(out, unit) for out, size in enumerate(sizes) for unit in range(size)]
    for out, size in zip(outs, sizes):
        out[size * WORDS :, :] = jnp.zeros((8, w.shape[1]), jnp.int32)
    for at, size, terms in work:
        product = block_product(x, w, at, size, terms)
        for r in range(0, size, SEGMENT_ROWS):
            out, unit = unit_of[(at + r) // SEGMENT_ROWS]
            encode(product[r : r + SEGMENT_ROWS], outs[out], unit, sizes[out])


def sent_call(tokens, weight, step, n_tensor, columns, first, sizes):
    width = tokens.shape[1]
    rows = sum(sizes) * SEGMENT_ROWS
    return pl.pallas_call(
        functools.partial(sent_kernel, first, sizes, step, n_tensor),
        in_specs=[HBM, HBM],
        out_specs=[VMEM] * len(sizes),
        out_shape=[jax.ShapeDtypeStruct((coded_rows(n), columns), jnp.int32) for n in sizes],
        scratch_shapes=base_scratch(sum(sizes), width, columns),
        compiler_params=params(16),
        cost_estimate=cost(
            2 * rows * width * columns, 2 * rows * width + 2 * width * columns + 4 * rows * columns
        ),
    )(tokens, weight)


def add_kernel(chunk, above, sums_ref, *refs):
    coded_refs, o_ref = refs[:-1], refs[-1]
    o_ref[...] = sums_ref[...]
    add_decoded(o_ref, chunk, coded_refs, above)


def add_call(chunk, above, sums, coded):
    return pl.pallas_call(
        functools.partial(add_kernel, chunk, above),
        in_specs=[VMEM] * (1 + len(coded)),
        out_specs=VMEM,
        out_shape=jax.ShapeDtypeStruct(sums.shape, sums.dtype),
        compiler_params=params(8),
        cost_estimate=cost(40000 * sums.size, 12 * sums.size),
    )(sums, *coded)


def shrink_into(o_ref, at, table, k, rows_of, views, rank):
    for j in range(MOST):
        _, _, within = segment_of(table, k, j)
        for stage, ref, first, whose, i in views:
            if stage not in stages_of(k):
                continue

            @pl.when((whose == table[k * ENTRIES]) & (within == i))
            def _(j=j, ref=ref, first=first):
                rows = rows_of(j)
                o_ref[at, :, j * rank : (j + 1) * rank] = lax.dot_general(
                    rows,
                    ref[first : first + rank, : rows.shape[1]],
                    (((1,), (1,)), ((), ())),
                    preferred_element_type=jnp.float32,
                )


def join_copies(halves, whole, sems):
    copies, rank = [], halves[0].shape[0]
    for i, half in enumerate(halves):
        copies.append(
            pltpu.make_async_copy(half, whole.at[pl.ds(i * rank, rank), :], sems.at[i])
        )
        copies[-1].start()
    return copies


def stages_of(k):
    return range((k + 1) // 2, k + 1)


def stages_of_all(ks):
    return range(stages_of(ks[0])[0], ks[-1] + 1)


def upper_kernel(n_adapter, table, x_ref, w_ref, o_ref, kept_ref, x, w, sems, kept_sems):
    work = load_base(0, x.shape[0] // SEGMENT_ROWS, lax.axis_index("tensor"), x_ref, w_ref, x, w, sems)
    keeps = []
    for k in range(1, n_adapter):
        for j in range(MOST):
            start, _, _ = segment_of(table, k, j)
            keeps.append(
                pltpu.make_async_copy(
                    x_ref.at[pl.ds(start, SEGMENT_ROWS), :],
                    kept_ref.at[k - 1, j],
                    kept_sems.at[k - 1, j],
                )
            )
            keeps[-1].start()
    for at, size, terms in work:
        o_ref[at : at + size, :] = block_product(x, w, at, size, terms)
    for copy in keeps:
        copy.wait()


def upper_call(table, tokens, weight, columns, n_adapter):
    rows, width = tokens.shape
    half = UPPER * SEGMENT_ROWS
    return pl.pallas_call(
        functools.partial(upper_kernel, n_adapter),
        in_specs=[SMEM, HBM, HBM],
        out_specs=[VMEM] * 2,
        out_shape=[
            jax.ShapeDtypeStruct((half, columns), jnp.float32),
            jax.ShapeDtypeStruct((n_adapter - 1, MOST, SEGMENT_ROWS, width), jnp.bfloat16),
        ],
        scratch_shapes=base_scratch(half // SEGMENT_ROWS, width, columns)
        + [pltpu.SemaphoreType.DMA((n_adapter - 1, MOST))],
        compiler_params=params(12),
        cost_estimate=cost(2 * half * width * columns, 2 * rows * width + 2 * width * columns),
    )(table, tokens, weight)


def lower_kernel(per_device, rank, table, x_ref, w_ref, *refs):
    messages, halves, refs = refs[:per_device], refs[per_device : 2 * per_device], refs[2 * per_device :]
    coded_refs, (o_ref, s_ref, whole_ref, x, w, sems, mine, mine_sems, join_sems) = refs[:-9], refs[-9:]
    work = load_base(UPPER, x.shape[0] // SEGMENT_ROWS, lax.axis_index("tensor"), x_ref, w_ref, x, w, sems)
    joins = join_copies(halves, whole_ref, join_sems)
    loads = []
    for j in range(MOST):
        start, _, _ = segment_of(table, 0, j)
        loads.append(
            pltpu.make_async_copy(
                x_ref.at[pl.ds(start, SEGMENT_ROWS), :], mine.at[j], mine_sems.at[j]
            )
        )
        loads[-1].start()
    for at, size, terms in work:
        o_ref[at : at + size, :] = block_product(x, w, at, size, terms)
    add_decoded(o_ref, 0, coded_refs, UPPER)
    for copy in loads:
        copy.wait()
    views = views_of(messages, [0], [(per_device, 0)], rank)
    shrink_into(s_ref, 0, table, 0, lambda j: mine[j], views, rank)
    for copy in joins:
        copy.wait()


def lower_call(table, tokens, weight, messages, halves, coded, columns):
    rows, width = tokens.shape
    half = rows - UPPER * SEGMENT_ROWS
    per_device, (rank, long) = len(messages), messages[0].shape
    return pl.pallas_call(
        functools.partial(lower_kernel, per_device, rank),
        in_specs=[SMEM, HBM, HBM] + [VMEM] * (2 * per_device + len(coded)),
        out_specs=[VMEM] * 3,
        out_shape=[
            jax.ShapeDtypeStruct((half, columns), jnp.float32),
            jax.ShapeDtypeStruct((1, SEGMENT_ROWS, MOST * rank), jnp.float32),
            jax.ShapeDtypeStruct((per_device * rank, long), jnp.bfloat16),
        ],
        scratch_shapes=base_scratch(half // SEGMENT_ROWS, width, columns)
        + [
            pltpu.VMEM((MOST, SEGMENT_ROWS, width), jnp.bfloat16),
            pltpu.SemaphoreType.DMA((MOST,)),
            pltpu.SemaphoreType.DMA((per_device,)),
        ],
        compiler_params=params(14),
        cost_estimate=cost(0 * half * width * columns, 4 * rows * columns),
    )(table, tokens, weight, *messages, *halves, *coded)


def shrink_kernel(ks, rank, at, layout, table, kept_ref, *refs):
    buffers, o_ref = refs[1 if at else 0 : -1], refs[-1]
    if at:
        o_ref[:at] = refs[0][...]
    views = views_of(buffers, stages_of_all(ks), layout, rank)
    for i, k in enumerate(ks):
        shrink_into(o_ref, at + i, table, k, lambda j, k=k: kept_ref[k - 1, j], views, rank)


def shrink_call(ks, table, kept, before, buffers, layout, rank):
    width = kept.shape[3]
    at = sum(b.shape[0] for b in before)
    return pl.pallas_call(
        functools.partial(shrink_kernel, ks, rank, at, layout),
        in_specs=[SMEM] + [VMEM] * (1 + len(before) + len(buffers)),
        out_specs=VMEM,
        out_shape=jax.ShapeDtypeStruct((at + len(ks), SEGMENT_ROWS, MOST * rank), jnp.float32),
        compiler_params=params(4),
        cost_estimate=cost(
            len(ks) * MOST * 2 * SEGMENT_ROWS * width * 256, len(ks) * 4 * SEGMENT_ROWS * width
        ),
    )(table, kept, *before, *buffers)


def fetch_up(up, at, table, k, j, views, rank):
    columns = up.shape[2]
    _, _, within = segment_of(table, k, j)
    for stage, ref, first, whose, i in views:
        if stage not in stages_of(k):
            continue

        @pl.when((whose == table[k * ENTRIES]) & (within == i))
        def _(ref=ref, first=first):
            factor = ref[first : first + rank, ref.shape[1] - columns :]
            up[at, :rank, :] = factor
            up[at, rank:, :] = factor


def up_product(share, j, factor, rank):
    lane = lax.broadcasted_iota(jnp.int32, share.shape, 1)
    other = pltpu.roll(share, rank, 1)
    both = jnp.where((lane < rank) == (j == 0), share, other)
    high = both.astype(jnp.bfloat16).astype(jnp.float32)
    terms = jnp.where(lane < rank, high, both - high).astype(jnp.bfloat16)
    return jnp.dot(terms, factor, preferred_element_type=jnp.float32)


LATE = 2


def early_kernel(n_adapter, n_tensor, rank, layout, n_buffers, table, *refs):
    first = n_adapter - LATE
    upper_ref, lower_ref, refs = refs[0], refs[1], refs[2:]
    shrinks, refs = refs[: -4 - n_buffers], refs[-4 - n_buffers :]
    buffers, (o_ref, rest_ref, up, sums) = refs[:-4], refs[-4:]
    views = views_of(buffers, range(first), layout, rank)
    for k in range(first):
        for j in range(MOST):
            fetch_up(up, k * MOST + j, table, k, j, views, rank)
    shares = []
    for call in range(len(shrinks) // n_tensor):
        share = shrinks[call * n_tensor][...]
        for i in range(1, n_tensor):
            share = share + shrinks[call * n_tensor + i][...]
        shares += [share[i] for i in range(share.shape[0])]
    for k in range(n_adapter):
        for j in range(MOST):
            start, used, _ = segment_of(table, k, j)
            upper_rows = upper_ref.shape[0]

            @pl.when(start < upper_rows)
            def _(start=start):
                at = pl.multiple_of(jnp.minimum(start, upper_rows - SEGMENT_ROWS), SEGMENT_ROWS)
                sums[...] = upper_ref[pl.ds(at, SEGMENT_ROWS), :]

            @pl.when(start >= upper_rows)
            def _(start=start):
                at = pl.multiple_of(jnp.maximum(start - upper_rows, 0), SEGMENT_ROWS)
                sums[...] = lower_ref[pl.ds(at, SEGMENT_ROWS), :]

            value = sums[...]
            if k >= first:
                rest_ref[k - first, j] = value
                continue
            lora = up_product(shares[k], j, up[k * MOST + j], rank)

            @pl.when(used)
            def _(start=start, value=value, lora=lora):
                o_ref[pl.ds(start, SEGMENT_ROWS), :] = (value + adapter_scale * lora).astype(
                    jnp.bfloat16
                )


def early(n_adapter, n_tensor, table, upper, lower, shrinks, buffers, layout, rank):
    rows, columns = upper.shape[0] + lower.shape[0], upper.shape[1]
    return pl.pallas_call(
        functools.partial(early_kernel, n_adapter, n_tensor, rank, layout, len(buffers)),
        in_specs=[SMEM] + [VMEM] * (2 + len(shrinks) + len(buffers)),
        out_specs=[VMEM, VMEM],
        out_shape=[
            jax.ShapeDtypeStruct((rows, columns), jnp.bfloat16),
            jax.ShapeDtypeStruct((LATE, MOST, SEGMENT_ROWS, columns), jnp.float32),
        ],
        scratch_shapes=[
            pltpu.VMEM(((n_adapter - LATE) * MOST, 2 * rank, columns), jnp.bfloat16),
            pltpu.VMEM((SEGMENT_ROWS, columns), jnp.float32),
        ],
        compiler_params=params(16),
        cost_estimate=cost(6 * rows * rank * columns, (4 * n_tensor + 2) * rows * columns),
    )(table, upper, lower, *shrinks, *buffers)


def late_kernel(ks, n_tensor, rank, layout, table, *refs):
    rest_ref, shrinks, refs = refs[0], refs[1 : 1 + n_tensor], refs[1 + n_tensor :]
    buffers, (_, o_ref, up, out, sems) = refs[:-5], refs[-5:]
    views = views_of(buffers, stages_of_all(ks), layout, rank)
    stores = []
    for i, k in enumerate(ks):
        share = shrinks[0][i]
        for r in shrinks[1:]:
            share = share + r[i]
        for j in range(MOST):
            fetch_up(up, i * MOST + j, table, k, j, views, rank)
            start, used, _ = segment_of(table, k, j)
            lora = up_product(share, j, up[i * MOST + j], rank)
            out[i, j] = (rest_ref[i, j] + adapter_scale * lora).astype(jnp.bfloat16)
            store = pltpu.make_async_copy(
                out.at[i, j], o_ref.at[pl.ds(start, SEGMENT_ROWS), :], sems.at[i, j]
            )
            pl.when(used)(store.start)
            stores.append((used, store))
    for used, store in stores:
        pl.when(used)(store.wait)


def late(ks, n_tensor, table, rest, shrinks, buffers, value, layout, rank):
    rows, columns = value.shape
    return pl.pallas_call(
        functools.partial(late_kernel, ks, n_tensor, rank, layout),
        in_specs=[SMEM] + [VMEM] * (1 + len(shrinks) + len(buffers)) + [ANY],
        out_specs=ANY,
        out_shape=jax.ShapeDtypeStruct((rows, columns), jnp.bfloat16),
        scratch_shapes=[
            pltpu.VMEM((LATE * MOST, 2 * rank, columns), jnp.bfloat16),
            pltpu.VMEM((LATE, MOST, SEGMENT_ROWS, columns), jnp.bfloat16),
            pltpu.SemaphoreType.DMA((LATE, MOST)),
        ],
        input_output_aliases={2 + len(shrinks) + len(buffers): 0},
        compiler_params=params(8),
        cost_estimate=cost(
            6 * LATE * MOST * SEGMENT_ROWS * rank * columns,
            8 * LATE * MOST * SEGMENT_ROWS * columns,
        ),
    )(table, rest, *shrinks, *buffers, value)


def after(array, *others):
    return lax.optimization_barrier((array, *others))[0]


def on_device(
    tokens, value_weight, adapter_down_weight, adapter_up_weight, row_adapter_index, adapter_slot_of
):
    rows, width = tokens.shape
    per_device, _, rank = adapter_down_weight.shape
    n_adapter = lax.axis_size("adapter")
    n_tensor = lax.axis_size("tensor")
    columns = value_weight.shape[1] // n_tensor

    def swap_tensor(array, step):
        pairs = [(i, (i + step) % n_tensor) for i in range(n_tensor)]
        return lax.ppermute(array, "tensor", pairs)

    def along_line(array, stage):
        up = [(2 * i, 2 * (i + 1)) for i in range(stage - 1, n_adapter - 1)]
        down = [(2 * i + 1, 2 * (i - 1) + 1) for i in range(1, n_adapter - stage + 1)]
        return lax.ppermute(array, ("adapter", "dp"), up + down)

    def swap_cores(array):
        return lax.ppermute(array, "dp", [(0, 1), (1, 0)])

    down = jnp.swapaxes(adapter_down_weight, 1, 2).reshape(per_device * rank, width)
    up = adapter_up_weight.reshape(per_device * rank, value_weight.shape[1])
    tokens, value_weight, down, up = (
        pltpu.with_memory_space_constraint(a, pltpu.HBM) for a in (tokens, value_weight, down, up)
    )
    messages = message_call(down, up, columns, per_device)
    table = table_call(row_adapter_index, adapter_slot_of, n_adapter, per_device)
    last = n_adapter - 1
    buffers, shrinks = [list(messages)], []
    layout = [(per_device, 0), (per_device, 1)] + [(per_device, per_device)] * (last - 1)

    def buffers_of(stages):
        return [b for stage in stages for b in buffers[stage]]

    def shrink(ks, kept, before=()):
        mine = buffers_of(stages_of_all(ks))
        return shrink_call(ks, table, kept, list(before), mine, layout, rank)

    def add_shrink(mine):
        shrinks.extend([mine] + [swap_tensor(mine, step) for step in range(1, n_tensor)])

    others = range(1, n_tensor)

    def sent_for(step, chunks, rows):
        sizes = [number for _, number in chunks]
        return sent_call(rows, value_weight, step, n_tensor, columns, chunks[0][0], sizes)

    def send(parts, *ahead):
        return [swap_tensor(after(p, *ahead), step) for step, p in zip(others, parts)]

    held = [along_line(m, 1) for m in messages]
    part_a = [sent_for(step, CHUNKS[:1], tokens)[0] for step in others]
    sent = [send(part_a)]
    first = after(held[0], table, *part_a)
    rest_parts = [sent_for(step, CHUNKS[1:], after(tokens, first)) for step in others]
    parts = [[p[i] for p in rest_parts] for i in range(len(CHUNKS) - 1)]
    part_b = [p for group in parts for p in group]
    for stage in range(1, last):
        came = held
        if stage == 1:
            came = [first] + [after(h, *part_b) for h in held[1:]]
            sent.append(send(parts[0], *came, *sent[0]))
        if stage == 2:
            came = held[:1] + [after(h, upper) for h in held[1:]]
        held = [along_line(c, stage + 1) for c in came]
        if stage == 1:
            upper, kept = upper_call(
                after(table, held[0], *came), tokens, value_weight, columns, n_adapter
            )
        elif stage == 2:
            lower, before, joined = lower_call(
                after(table, *came), tokens, value_weight, messages, buffers[1], sent[0], columns
            )
            buffers[1] += [swap_cores(joined)]
            free = lower
            upper = add_call(1, 0, after(upper, held[0]), sent[1])
            lower = add_call(1, UPPER, after(lower, upper, *held[1:]), sent[1])
            before = shrink([1], after(kept, lower), [before])
        else:
            before = shrink([stage - 1], kept, [before])
        ahead = [free] if stage == 2 else []
        swapped = [swap_cores(after(c, *ahead)) for c in came] if stage > 1 else []
        buffers.append([*came, *swapped])
    add_shrink(before)
    value, remaining = early(
        n_adapter,
        n_tensor,
        table,
        upper,
        lower,
        shrinks,
        buffers_of(range(last - 1)),
        layout,
        rank,
    )
    buffers.append([*held, *[swap_cores(h) for h in held]])
    ks = (last - 1, last)
    add_shrink(shrink(ks, after(kept, *held)))
    return late(
        ks,
        n_tensor,
        table,
        remaining,
        shrinks[-n_tensor:],
        buffers_of(stages_of_all(ks)),
        value,
        layout,
        rank,
    )


def solution(mesh):
    return jax.shard_map(
        on_device,
        mesh=mesh,
        in_specs=(
            P(("groups", "adapter", "dp"), "tensor"),
            P("tensor", None),
            P(("groups", "adapter"), "tensor", None),
            P(("groups", "adapter"), None, None),
            P(("groups", "adapter", "dp")),
            P("groups"),
        ),
        out_specs=P(("groups", "adapter", "dp"), "tensor"),
        check_vma=False,
    )
```

```python
import functools

import jax
import jax.numpy as jnp
from jax import lax
from jax.experimental import pallas as pl
from jax.experimental.pallas import tpu as pltpu
from jax.sharding import PartitionSpec as P

SEGMENT_ROWS = 128
adapter_scale = 0.5
MOST = 2
BLOCK = 256
PIECES = 4
CHUNKS = ((6, 2), (0, 6))
UPPER = 3
ENTRIES = 8
MIDDLE = 1.5 * 2.0**23


def cost(flops, moved):
    return pl.CostEstimate(flops=int(flops), bytes_accessed=int(moved), transcendentals=0)


def params(mib):
    return pltpu.CompilerParams(vmem_limit_bytes=mib * 2**20)


ANY = pl.BlockSpec(memory_space=pl.ANY)
HBM = pl.BlockSpec(memory_space=pltpu.HBM)
SMEM = pl.BlockSpec(memory_space=pltpu.SMEM)
VMEM = pl.BlockSpec(memory_space=pltpu.VMEM)


def arrival_order(me, n_adapter):
    order = [me] + [jnp.int32(-1)] * (n_adapter - 1)
    count = jnp.int32(1)
    for distance in range(1, n_adapter):
        for other in (me - distance, me + distance):
            valid = (other >= 0) & (other < n_adapter)
            order = [jnp.where(valid & (count == k), other, o) for k, o in enumerate(order)]
            count = count + valid.astype(jnp.int32)
    return order


def views_of(refs, stages, layout, rank):
    me, core = lax.axis_index("adapter"), lax.axis_index("dp")
    refs, views = list(refs), []
    for stage in stages:
        came, swapped = layout[stage]
        toward = jnp.where(core == 0, -stage, stage)
        for i in range(came):
            views.append((stage, refs.pop(0), 0, me + toward if stage > 0 else me, i))
        for i in range(swapped):
            ref = refs.pop(0)
            for part in range(came // swapped):
                views.append((stage, ref, part * rank, me - toward, i + part))
    return views


def segment_of(table, k, j):
    seg = table[k * ENTRIES + 1 + 2 * j]
    start = pl.multiple_of(jnp.maximum(seg, 0) * SEGMENT_ROWS, SEGMENT_ROWS)
    return start, seg >= 0, table[k * ENTRIES + 2 + 2 * j]


def message_kernel(down_ref, up_ref, *refs):
    outs, sems = refs[:-1], refs[-1]
    rank = outs[0].shape[0]
    width = down_ref.shape[1]
    columns = outs[0].shape[1] - width
    start = pl.multiple_of(lax.axis_index("tensor") * columns, columns)
    copies = []
    for i, out in enumerate(outs):
        rows = pl.ds(i * rank, rank)
        copies += [
            pltpu.make_async_copy(down_ref.at[rows, :], out.at[:, pl.ds(0, width)], sems.at[0, i]),
            pltpu.make_async_copy(
                up_ref.at[rows, pl.ds(start, columns)], out.at[:, pl.ds(width, columns)], sems.at[1, i]
            ),
        ]
    for copy in copies:
        copy.start()
    for copy in copies:
        copy.wait()


def message_call(down, up, columns, per_device):
    rows, width = down.shape
    shape = jax.ShapeDtypeStruct((rows // per_device, width + columns), jnp.bfloat16)
    return pl.pallas_call(
        message_kernel,
        in_specs=[HBM, HBM],
        out_specs=[VMEM] * per_device,
        out_shape=[shape] * per_device,
        scratch_shapes=[pltpu.SemaphoreType.DMA((2, per_device))],
        compiler_params=params(8),
        cost_estimate=cost(0, 4 * rows * (width + columns)),
    )(down, up)


def table_kernel(n_adapter, per_device, ids, slots, table):
    seg_dev = ids.shape[0] // SEGMENT_ROWS
    used = [slots[ids[s * SEGMENT_ROWS]] for s in range(seg_dev)]
    for k, owner in enumerate(arrival_order(lax.axis_index("adapter"), n_adapter)):
        table[k * ENTRIES] = owner
        found, place = [jnp.int32(-1)] * MOST, [jnp.int32(0)] * MOST
        count = jnp.int32(0)
        for s, slot in enumerate(used):
            within = slot - owner * per_device
            hit = (within >= 0) & (within < per_device)
            for j in range(MOST):
                take = hit & (count == j)
                found[j] = jnp.where(take, s, found[j])
                place[j] = jnp.where(take, within, place[j])
            count = count + hit.astype(jnp.int32)
        for j in range(MOST):
            table[k * ENTRIES + 1 + 2 * j] = found[j]
            table[k * ENTRIES + 2 + 2 * j] = place[j]


def table_call(ids, slots, n_adapter, per_device):
    return pl.pallas_call(
        functools.partial(table_kernel, n_adapter, per_device),
        in_specs=[SMEM, SMEM],
        out_specs=SMEM,
        out_shape=jax.ShapeDtypeStruct((n_adapter * ENTRIES,), jnp.int32),
        cost_estimate=cost(0, 4 * ids.shape[0]),
    )(ids, slots)


def diagonal():
    shape = (SEGMENT_ROWS, SEGMENT_ROWS)
    return lax.broadcasted_iota(jnp.int32, shape, 0) == lax.broadcasted_iota(jnp.int32, shape, 1)


GROUP = SEGMENT_ROWS // 8
WORDS = 5 * GROUP


def coded_rows(segments):
    return segments * WORDS + 8


def encode(values, o_ref, unit, units):
    largest = jnp.maximum(jnp.max(jnp.abs(values), axis=1, keepdims=True), 2.0**-100)
    power = jnp.floor(jnp.log2(largest))
    whole = (values * jnp.exp2(18.0 - power) + MIDDLE).astype(jnp.int32) - int(MIDDLE)
    whole = jnp.minimum(whole, 2**19 - 1)
    v = [whole[i * GROUP : (i + 1) * GROUP] for i in range(8)]
    over = [
        v[5] & 0xFFF,
        ((v[5] >> 12) & 0xFF) | ((v[6] & 0xF) << 8),
        (v[6] >> 4) & 0xFFF,
        ((v[6] >> 16) & 0xF) | ((v[7] & 0xFF) << 4),
        v[7] >> 8,
    ]
    for i in range(5):
        o_ref[unit * WORDS + i * GROUP : unit * WORDS + (i + 1) * GROUP, :] = (v[i] & 0xFFFFF) | (
            over[i] << 20
        )
    row = jnp.sum(jnp.where(diagonal(), power, 0.0), axis=0, keepdims=True)
    o_ref[units * WORDS + unit : units * WORDS + unit + 1, :SEGMENT_ROWS] = row.astype(jnp.int32)


def decode(ref, unit, units):
    w = [ref[unit * WORDS + i * GROUP : unit * WORDS + (i + 1) * GROUP, :] for i in range(5)]
    v = [(x << 12) >> 12 for x in w]
    v.append(((w[0] >> 20) & 0xFFF) | (((w[1] << 4) >> 24) << 12))
    v.append(((w[1] >> 28) & 0xF) | (((w[2] >> 20) & 0xFFF) << 4) | (((w[3] << 8) >> 28) << 16))
    v.append(((w[3] >> 24) & 0xFF) | ((w[4] >> 20) << 8))
    row = ref[units * WORDS + unit : units * WORDS + unit + 1, :SEGMENT_ROWS].astype(jnp.float32)
    power = jnp.sum(jnp.where(diagonal(), row, 0.0), axis=1, keepdims=True)
    return jnp.concatenate(v, axis=0).astype(jnp.float32) * jnp.exp2(power - 18.0)


def add_decoded(sums, chunk, refs, above):
    first, number = CHUNKS[chunk]
    for unit in range(number):
        at = first + unit - above
        if at < 0 or at >= sums.shape[0] // SEGMENT_ROWS:
            continue
        rows = pl.ds(at * SEGMENT_ROWS, SEGMENT_ROWS)
        value = sums[rows, :]
        for ref in refs:
            value = value + decode(ref, unit, number)
        sums[rows, :] = value


def load_base(first, segments, column, x_ref, w_ref, x, w, sems):
    width, columns = w.shape
    rows = segments * SEGMENT_ROWS
    start = pl.multiple_of(column * columns, columns)
    depth = width // PIECES
    blocks = [(r, min(BLOCK, rows - r)) for r in range(0, rows, BLOCK)]

    def x_copy(at, size, features, sem):
        return pltpu.make_async_copy(
            x_ref.at[pl.ds(first * SEGMENT_ROWS + at, size), features],
            x.at[pl.ds(at, size), features],
            sem,
        )

    work = []
    for i, (at, size) in enumerate(blocks):
        terms = []
        if i == 0:
            for p in range(PIECES):
                features = pl.ds(p * depth, depth)
                copies = (
                    pltpu.make_async_copy(
                        w_ref.at[features, pl.ds(start, columns)], w.at[features, :], sems.at[0, p]
                    ),
                    x_copy(0, size, features, sems.at[1, p]),
                )
                terms.append((copies, slice(p * depth, (p + 1) * depth)))
        else:
            terms.append(((x_copy(at, size, slice(None), sems.at[2, i]),), slice(None)))
        work.append((at, size, terms))
    for _, _, terms in work:
        for copies, _ in terms:
            for copy in copies:
                copy.start()
    return work


def block_product(x, w, at, size, terms):
    total = None
    for copies, features in terms:
        for copy in copies:
            copy.wait()
        term = jnp.dot(
            x[at : at + size, features], w[features, :], preferred_element_type=jnp.float32
        )
        total = term if total is None else total + term
    return total


def base_scratch(segments, width, columns):
    rows = segments * SEGMENT_ROWS
    return [
        pltpu.VMEM((rows, width), jnp.bfloat16),
        pltpu.VMEM((width, columns), jnp.bfloat16),
        pltpu.SemaphoreType.DMA((3, max(PIECES, rows // BLOCK + 1))),
    ]


def sent_kernel(first, sizes, step, n_tensor, x_ref, w_ref, *refs):
    outs, (x, w, sems) = refs[: len(sizes)], refs[len(sizes) :]
    column = lax.rem(lax.axis_index("tensor") + step, n_tensor)
    work = load_base(first, sum(sizes), column, x_ref, w_ref, x, w, sems)
    unit_of = [(out, unit) for out, size in enumerate(sizes) for unit in range(size)]
    for out, size in zip(outs, sizes):
        out[size * WORDS :, :] = jnp.zeros((8, w.shape[1]), jnp.int32)
    for at, size, terms in work:
        product = block_product(x, w, at, size, terms)
        for r in range(0, size, SEGMENT_ROWS):
            out, unit = unit_of[(at + r) // SEGMENT_ROWS]
            encode(product[r : r + SEGMENT_ROWS], outs[out], unit, sizes[out])


def sent_call(tokens, weight, step, n_tensor, columns, first, sizes):
    width = tokens.shape[1]
    rows = sum(sizes) * SEGMENT_ROWS
    return pl.pallas_call(
        functools.partial(sent_kernel, first, sizes, step, n_tensor),
        in_specs=[HBM, HBM],
        out_specs=[VMEM] * len(sizes),
        out_shape=[jax.ShapeDtypeStruct((coded_rows(n), columns), jnp.int32) for n in sizes],
        scratch_shapes=base_scratch(sum(sizes), width, columns),
        compiler_params=params(16),
        cost_estimate=cost(
            2 * rows * width * columns, 2 * rows * width + 2 * width * columns + 4 * rows * columns
        ),
    )(tokens, weight)


def add_kernel(chunk, above, sums_ref, *refs):
    coded_refs, o_ref = refs[:-1], refs[-1]
    o_ref[...] = sums_ref[...]
    add_decoded(o_ref, chunk, coded_refs, above)


def add_call(chunk, above, sums, coded):
    return pl.pallas_call(
        functools.partial(add_kernel, chunk, above),
        in_specs=[VMEM] * (1 + len(coded)),
        out_specs=VMEM,
        out_shape=jax.ShapeDtypeStruct(sums.shape, sums.dtype),
        compiler_params=params(8),
        cost_estimate=cost(40000 * sums.size, 12 * sums.size),
    )(sums, *coded)


def shrink_into(o_ref, at, table, k, rows_of, views, rank):
    for j in range(MOST):
        _, _, within = segment_of(table, k, j)
        for stage, ref, first, whose, i in views:
            if stage not in stages_of(k):
                continue

            @pl.when((whose == table[k * ENTRIES]) & (within == i))
            def _(j=j, ref=ref, first=first):
                rows = rows_of(j)
                o_ref[at, :, j * rank : (j + 1) * rank] = lax.dot_general(
                    rows,
                    ref[first : first + rank, : rows.shape[1]],
                    (((1,), (1,)), ((), ())),
                    preferred_element_type=jnp.float32,
                )


SPLIT = 2


def split_copies(halves, quarters, sems):
    copies, rows = [], quarters[0].shape[0]
    for i, quarter in enumerate(quarters):
        part = halves[i // SPLIT].at[pl.ds(i % SPLIT * rows, rows), :]
        copies.append(pltpu.make_async_copy(part, quarter, sems.at[i]))
        copies[-1].start()
    return copies


def join_copies(quarters, whole, sems):
    copies, rows = [], quarters[0].shape[0]
    for i, quarter in enumerate(quarters):
        copies.append(
            pltpu.make_async_copy(quarter, whole.at[pl.ds(i * rows, rows), :], sems.at[i])
        )
        copies[-1].start()
    return copies


def stages_of(k):
    return range((k + 1) // 2, k + 1)


def stages_of_all(ks):
    return range(stages_of(ks[0])[0], ks[-1] + 1)


def upper_kernel(n_adapter, table, x_ref, w_ref, o_ref, kept_ref, x, w, sems, kept_sems):
    work = load_base(0, x.shape[0] // SEGMENT_ROWS, lax.axis_index("tensor"), x_ref, w_ref, x, w, sems)
    keeps = []
    for k in range(1, n_adapter):
        for j in range(MOST):
            start, _, _ = segment_of(table, k, j)
            keeps.append(
                pltpu.make_async_copy(
                    x_ref.at[pl.ds(start, SEGMENT_ROWS), :],
                    kept_ref.at[k - 1, j],
                    kept_sems.at[k - 1, j],
                )
            )
            keeps[-1].start()
    for at, size, terms in work:
        o_ref[at : at + size, :] = block_product(x, w, at, size, terms)
    for copy in keeps:
        copy.wait()


def upper_call(table, tokens, weight, columns, n_adapter):
    rows, width = tokens.shape
    half = UPPER * SEGMENT_ROWS
    return pl.pallas_call(
        functools.partial(upper_kernel, n_adapter),
        in_specs=[SMEM, HBM, HBM],
        out_specs=[VMEM] * 2,
        out_shape=[
            jax.ShapeDtypeStruct((half, columns), jnp.float32),
            jax.ShapeDtypeStruct((n_adapter - 1, MOST, SEGMENT_ROWS, width), jnp.bfloat16),
        ],
        scratch_shapes=base_scratch(half // SEGMENT_ROWS, width, columns)
        + [pltpu.SemaphoreType.DMA((n_adapter - 1, MOST))],
        compiler_params=params(12),
        cost_estimate=cost(2 * half * width * columns, 2 * rows * width + 2 * width * columns),
    )(table, tokens, weight)


def lower_kernel(per_device, rank, table, x_ref, w_ref, *refs):
    messages, halves, refs = refs[:per_device], refs[per_device : 2 * per_device], refs[2 * per_device :]
    coded_refs, (o_ref, s_ref, *refs) = refs[: -8 - SPLIT * per_device], refs[-8 - SPLIT * per_device :]
    quarters, (x, w, sems, mine, mine_sems, join_sems) = refs[:-6], refs[-6:]
    work = load_base(UPPER, x.shape[0] // SEGMENT_ROWS, lax.axis_index("tensor"), x_ref, w_ref, x, w, sems)
    joins = split_copies(halves, quarters, join_sems)
    loads = []
    for j in range(MOST):
        start, _, _ = segment_of(table, 0, j)
        loads.append(
            pltpu.make_async_copy(
                x_ref.at[pl.ds(start, SEGMENT_ROWS), :], mine.at[j], mine_sems.at[j]
            )
        )
        loads[-1].start()
    for at, size, terms in work:
        o_ref[at : at + size, :] = block_product(x, w, at, size, terms)
    add_decoded(o_ref, 0, coded_refs, UPPER)
    for copy in loads:
        copy.wait()
    views = views_of(messages, [0], [(per_device, 0)], rank)
    shrink_into(s_ref, 0, table, 0, lambda j: mine[j], views, rank)
    for copy in joins:
        copy.wait()


def lower_call(table, tokens, weight, messages, halves, coded, columns):
    rows, width = tokens.shape
    half = rows - UPPER * SEGMENT_ROWS
    per_device, (rank, long) = len(messages), messages[0].shape
    return pl.pallas_call(
        functools.partial(lower_kernel, per_device, rank),
        in_specs=[SMEM, HBM, HBM] + [VMEM] * (2 * per_device + len(coded)),
        out_specs=[VMEM] * (2 + SPLIT * per_device),
        out_shape=[
            jax.ShapeDtypeStruct((half, columns), jnp.float32),
            jax.ShapeDtypeStruct((1, SEGMENT_ROWS, MOST * rank), jnp.float32),
        ]
        + [jax.ShapeDtypeStruct((rank // SPLIT, long), jnp.bfloat16)] * (SPLIT * per_device),
        scratch_shapes=base_scratch(half // SEGMENT_ROWS, width, columns)
        + [
            pltpu.VMEM((MOST, SEGMENT_ROWS, width), jnp.bfloat16),
            pltpu.SemaphoreType.DMA((MOST,)),
            pltpu.SemaphoreType.DMA((SPLIT * per_device,)),
        ],
        compiler_params=params(14),
        cost_estimate=cost(0 * half * width * columns, 4 * rows * columns),
    )(table, tokens, weight, *messages, *halves, *coded)


def shrink_kernel(ks, rank, at, layout, n_quarters, table, kept_ref, *refs):
    before, refs = refs[: 1 if at else 0], refs[1 if at else 0 :]
    quarters, refs = refs[:n_quarters], refs[n_quarters:]
    if n_quarters:
        buffers, (o_ref, whole_ref, sems) = refs[:-3], refs[-3:]
        joins = join_copies(quarters, whole_ref, sems)
        buffers = [*buffers, whole_ref]
    else:
        buffers, o_ref, joins = refs[:-1], refs[-1], []
    for r in before:
        o_ref[:at] = r[...]
    for copy in joins:
        copy.wait()
    views = views_of(buffers, stages_of_all(ks), layout, rank)
    for i, k in enumerate(ks):
        shrink_into(o_ref, at + i, table, k, lambda j, k=k: kept_ref[k - 1, j], views, rank)


def shrink_call(ks, table, kept, before, quarters, buffers, layout, rank):
    width = kept.shape[3]
    at = sum(b.shape[0] for b in before)
    n = len(quarters)
    shapes = [jax.ShapeDtypeStruct((at + len(ks), SEGMENT_ROWS, MOST * rank), jnp.float32)]
    if n:
        rows, long = quarters[0].shape
        shapes.append(jax.ShapeDtypeStruct((n * rows, long), jnp.bfloat16))
    return pl.pallas_call(
        functools.partial(shrink_kernel, ks, rank, at, layout, n),
        in_specs=[SMEM] + [VMEM] * (1 + len(before) + n + len(buffers)),
        out_specs=[VMEM] * len(shapes),
        out_shape=shapes,
        scratch_shapes=[pltpu.SemaphoreType.DMA((n,))] if n else [],
        compiler_params=params(4),
        cost_estimate=cost(
            len(ks) * MOST * 2 * SEGMENT_ROWS * width * 256, len(ks) * 4 * SEGMENT_ROWS * width
        ),
    )(table, kept, *before, *quarters, *buffers)


def fetch_up(up, at, table, k, j, views, rank):
    columns = up.shape[2]
    _, _, within = segment_of(table, k, j)
    for stage, ref, first, whose, i in views:
        if stage not in stages_of(k):
            continue

        @pl.when((whose == table[k * ENTRIES]) & (within == i))
        def _(ref=ref, first=first):
            factor = ref[first : first + rank, ref.shape[1] - columns :]
            up[at, :rank, :] = factor
            up[at, rank:, :] = factor


def up_product(share, j, factor, rank):
    lane = lax.broadcasted_iota(jnp.int32, share.shape, 1)
    other = pltpu.roll(share, rank, 1)
    both = jnp.where((lane < rank) == (j == 0), share, other)
    high = both.astype(jnp.bfloat16).astype(jnp.float32)
    terms = jnp.where(lane < rank, high, both - high).astype(jnp.bfloat16)
    return jnp.dot(terms, factor, preferred_element_type=jnp.float32)


LATE = 2


def early_kernel(n_adapter, n_tensor, rank, layout, n_buffers, table, *refs):
    first = n_adapter - LATE
    upper_ref, lower_ref, refs = refs[0], refs[1], refs[2:]
    shrinks, refs = refs[: -4 - n_buffers], refs[-4 - n_buffers :]
    buffers, (o_ref, rest_ref, up, sums) = refs[:-4], refs[-4:]
    views = views_of(buffers, range(first), layout, rank)
    for k in range(first):
        for j in range(MOST):
            fetch_up(up, k * MOST + j, table, k, j, views, rank)
    shares = []
    for call in range(len(shrinks) // n_tensor):
        share = shrinks[call * n_tensor][...]
        for i in range(1, n_tensor):
            share = share + shrinks[call * n_tensor + i][...]
        shares += [share[i] for i in range(share.shape[0])]
    for k in range(n_adapter):
        for j in range(MOST):
            start, used, _ = segment_of(table, k, j)
            upper_rows = upper_ref.shape[0]

            @pl.when(start < upper_rows)
            def _(start=start):
                at = pl.multiple_of(jnp.minimum(start, upper_rows - SEGMENT_ROWS), SEGMENT_ROWS)
                sums[...] = upper_ref[pl.ds(at, SEGMENT_ROWS), :]

            @pl.when(start >= upper_rows)
            def _(start=start):
                at = pl.multiple_of(jnp.maximum(start - upper_rows, 0), SEGMENT_ROWS)
                sums[...] = lower_ref[pl.ds(at, SEGMENT_ROWS), :]

            value = sums[...]
            if k >= first:
                rest_ref[k - first, j] = value
                continue
            lora = up_product(shares[k], j, up[k * MOST + j], rank)

            @pl.when(used)
            def _(start=start, value=value, lora=lora):
                o_ref[pl.ds(start, SEGMENT_ROWS), :] = (value + adapter_scale * lora).astype(
                    jnp.bfloat16
                )


def early(n_adapter, n_tensor, table, upper, lower, shrinks, buffers, layout, rank):
    rows, columns = upper.shape[0] + lower.shape[0], upper.shape[1]
    return pl.pallas_call(
        functools.partial(early_kernel, n_adapter, n_tensor, rank, layout, len(buffers)),
        in_specs=[SMEM] + [VMEM] * (2 + len(shrinks) + len(buffers)),
        out_specs=[VMEM, VMEM],
        out_shape=[
            jax.ShapeDtypeStruct((rows, columns), jnp.bfloat16),
            jax.ShapeDtypeStruct((LATE, MOST, SEGMENT_ROWS, columns), jnp.float32),
        ],
        scratch_shapes=[
            pltpu.VMEM(((n_adapter - LATE) * MOST, 2 * rank, columns), jnp.bfloat16),
            pltpu.VMEM((SEGMENT_ROWS, columns), jnp.float32),
        ],
        compiler_params=params(16),
        cost_estimate=cost(6 * rows * rank * columns, (4 * n_tensor + 2) * rows * columns),
    )(table, upper, lower, *shrinks, *buffers)


def late_kernel(ks, n_tensor, rank, layout, table, *refs):
    rest_ref, shrinks, refs = refs[0], refs[1 : 1 + n_tensor], refs[1 + n_tensor :]
    buffers, (_, o_ref, up, out, sems) = refs[:-5], refs[-5:]
    views = views_of(buffers, stages_of_all(ks), layout, rank)
    stores = []
    for i, k in enumerate(ks):
        share = shrinks[0][i]
        for r in shrinks[1:]:
            share = share + r[i]
        for j in range(MOST):
            fetch_up(up, i * MOST + j, table, k, j, views, rank)
            start, used, _ = segment_of(table, k, j)
            lora = up_product(share, j, up[i * MOST + j], rank)
            out[i, j] = (rest_ref[i, j] + adapter_scale * lora).astype(jnp.bfloat16)
            store = pltpu.make_async_copy(
                out.at[i, j], o_ref.at[pl.ds(start, SEGMENT_ROWS), :], sems.at[i, j]
            )
            pl.when(used)(store.start)
            stores.append((used, store))
    for used, store in stores:
        pl.when(used)(store.wait)


def late(ks, n_tensor, table, rest, shrinks, buffers, value, layout, rank):
    rows, columns = value.shape
    return pl.pallas_call(
        functools.partial(late_kernel, ks, n_tensor, rank, layout),
        in_specs=[SMEM] + [VMEM] * (1 + len(shrinks) + len(buffers)) + [ANY],
        out_specs=ANY,
        out_shape=jax.ShapeDtypeStruct((rows, columns), jnp.bfloat16),
        scratch_shapes=[
            pltpu.VMEM((LATE * MOST, 2 * rank, columns), jnp.bfloat16),
            pltpu.VMEM((LATE, MOST, SEGMENT_ROWS, columns), jnp.bfloat16),
            pltpu.SemaphoreType.DMA((LATE, MOST)),
        ],
        input_output_aliases={2 + len(shrinks) + len(buffers): 0},
        compiler_params=params(8),
        cost_estimate=cost(
            6 * LATE * MOST * SEGMENT_ROWS * rank * columns,
            8 * LATE * MOST * SEGMENT_ROWS * columns,
        ),
    )(table, rest, *shrinks, *buffers, value)


def after(array, *others):
    return lax.optimization_barrier((array, *others))[0]


def on_device(
    tokens, value_weight, adapter_down_weight, adapter_up_weight, row_adapter_index, adapter_slot_of
):
    rows, width = tokens.shape
    per_device, _, rank = adapter_down_weight.shape
    n_adapter = lax.axis_size("adapter")
    n_tensor = lax.axis_size("tensor")
    columns = value_weight.shape[1] // n_tensor

    def swap_tensor(array, step):
        pairs = [(i, (i + step) % n_tensor) for i in range(n_tensor)]
        return lax.ppermute(array, "tensor", pairs)

    def along_line(array, stage):
        up = [(2 * i, 2 * (i + 1)) for i in range(stage - 1, n_adapter - 1)]
        down = [(2 * i + 1, 2 * (i - 1) + 1) for i in range(1, n_adapter - stage + 1)]
        return lax.ppermute(array, ("adapter", "dp"), up + down)

    def swap_cores(array):
        return lax.ppermute(array, "dp", [(0, 1), (1, 0)])

    down = jnp.swapaxes(adapter_down_weight, 1, 2).reshape(per_device * rank, width)
    up = adapter_up_weight.reshape(per_device * rank, value_weight.shape[1])
    tokens, value_weight, down, up = (
        pltpu.with_memory_space_constraint(a, pltpu.HBM) for a in (tokens, value_weight, down, up)
    )
    messages = message_call(down, up, columns, per_device)
    table = table_call(row_adapter_index, adapter_slot_of, n_adapter, per_device)
    last = n_adapter - 1
    buffers, shrinks = [list(messages)], []
    layout = [(per_device, 0), (per_device, 1)] + [(per_device, per_device)] * (last - 1)

    def buffers_of(stages):
        return [b for stage in stages for b in buffers[stage]]

    def shrink(ks, kept, before=(), quarters=()):
        mine = buffers_of(stages_of_all(ks))
        return shrink_call(ks, table, kept, list(before), list(quarters), mine, layout, rank)

    def add_shrink(mine):
        shrinks.extend([mine] + [swap_tensor(mine, step) for step in range(1, n_tensor)])

    others = range(1, n_tensor)

    def sent_for(step, chunks, rows):
        sizes = [number for _, number in chunks]
        return sent_call(rows, value_weight, step, n_tensor, columns, chunks[0][0], sizes)

    def send(parts, *ahead):
        return [swap_tensor(after(p, *ahead), step) for step, p in zip(others, parts)]

    held = [along_line(m, 1) for m in messages]
    part_a = [sent_for(step, CHUNKS[:1], tokens)[0] for step in others]
    sent = [send(part_a)]
    first = after(held[0], table, *part_a)
    rest_parts = [sent_for(step, CHUNKS[1:], after(tokens, first)) for step in others]
    parts = [[p[i] for p in rest_parts] for i in range(len(CHUNKS) - 1)]
    part_b = [p for group in parts for p in group]
    for stage in range(1, last):
        came = held
        if stage == 1:
            came = [first] + [after(h, *part_b) for h in held[1:]]
            sent.append(send(parts[0], *came, *sent[0]))
        if stage == 2:
            came = held[:1] + [after(h, upper) for h in held[1:]]
        held = [along_line(c, stage + 1) for c in came]
        if stage == 1:
            upper, kept = upper_call(
                after(table, held[0], *came), tokens, value_weight, columns, n_adapter
            )
        elif stage == 2:
            lower, before, *quarters = lower_call(
                after(table, *came), tokens, value_weight, messages, buffers[1], sent[0], columns
            )
            quarters = [swap_cores(q) for q in quarters]
            free = lower
            upper = add_call(1, 0, after(upper, held[0]), sent[1])
            lower = add_call(1, UPPER, after(lower, upper), sent[1])
            before, joined = shrink([1], after(kept, lower), [before], quarters)
            buffers[1].append(joined)
        else:
            before = shrink([stage - 1], kept, [before])[0]
        ahead = [free] if stage == 2 else []
        swapped = [swap_cores(after(c, *ahead)) for c in came] if stage > 1 else []
        buffers.append([*came, *swapped])
    add_shrink(before)
    value, remaining = early(
        n_adapter,
        n_tensor,
        table,
        upper,
        lower,
        shrinks,
        buffers_of(range(last - 1)),
        layout,
        rank,
    )
    buffers.append([*held, *[swap_cores(after(h, before)) for h in held]])
    ks = (last - 1, last)
    add_shrink(shrink(ks, after(kept, *held))[0])
    return late(
        ks,
        n_tensor,
        table,
        remaining,
        shrinks[-n_tensor:],
        buffers_of(stages_of_all(ks)),
        value,
        layout,
        rank,
    )


def solution(mesh):
    return jax.shard_map(
        on_device,
        mesh=mesh,
        in_specs=(
            P(("groups", "adapter", "dp"), "tensor"),
            P("tensor", None),
            P(("groups", "adapter"), "tensor", None),
            P(("groups", "adapter"), None, None),
            P(("groups", "adapter", "dp")),
            P("groups"),
        ),
        out_specs=P(("groups", "adapter", "dp"), "tensor"),
        check_vma=False,
    )
```

```python
import functools

import jax
import jax.numpy as jnp
from jax import lax
from jax.experimental import pallas as pl
from jax.experimental.pallas import tpu as pltpu
from jax.sharding import PartitionSpec as P

SEGMENT_ROWS = 128
adapter_scale = 0.5
MOST = 2
BLOCK = 256
PIECES = 4
CHUNKS = ((6, 2), (0, 6))
UPPER = 3
ENTRIES = 8
MIDDLE = 1.5 * 2.0**23


def cost(flops, moved):
    return pl.CostEstimate(flops=int(flops), bytes_accessed=int(moved), transcendentals=0)


def params(mib):
    return pltpu.CompilerParams(vmem_limit_bytes=mib * 2**20)


ANY = pl.BlockSpec(memory_space=pl.ANY)
HBM = pl.BlockSpec(memory_space=pltpu.HBM)
SMEM = pl.BlockSpec(memory_space=pltpu.SMEM)
VMEM = pl.BlockSpec(memory_space=pltpu.VMEM)


def arrival_order(me, n_adapter):
    order = [me] + [jnp.int32(-1)] * (n_adapter - 1)
    count = jnp.int32(1)
    for distance in range(1, n_adapter):
        for other in (me - distance, me + distance):
            valid = (other >= 0) & (other < n_adapter)
            order = [jnp.where(valid & (count == k), other, o) for k, o in enumerate(order)]
            count = count + valid.astype(jnp.int32)
    return order


def views_of(refs, stages, layout, rank):
    me, core = lax.axis_index("adapter"), lax.axis_index("dp")
    refs, views = list(refs), []
    for stage in stages:
        came, swapped = layout[stage]
        toward = jnp.where(core == 0, -stage, stage)
        for i in range(came):
            views.append((stage, refs.pop(0), 0, me + toward if stage > 0 else me, i))
        for i in range(swapped):
            ref = refs.pop(0)
            for part in range(came // swapped):
                views.append((stage, ref, part * rank, me - toward, i + part))
    return views


def segment_of(table, k, j):
    seg = table[k * ENTRIES + 1 + 2 * j]
    start = pl.multiple_of(jnp.maximum(seg, 0) * SEGMENT_ROWS, SEGMENT_ROWS)
    return start, seg >= 0, table[k * ENTRIES + 2 + 2 * j]


def message_kernel(down_ref, up_ref, *refs):
    outs, sems = refs[:-1], refs[-1]
    rank = outs[0].shape[0]
    width = down_ref.shape[1]
    columns = outs[0].shape[1] - width
    start = pl.multiple_of(lax.axis_index("tensor") * columns, columns)
    copies = []
    for i, out in enumerate(outs):
        rows = pl.ds(i * rank, rank)
        copies += [
            pltpu.make_async_copy(down_ref.at[rows, :], out.at[:, pl.ds(0, width)], sems.at[0, i]),
            pltpu.make_async_copy(
                up_ref.at[rows, pl.ds(start, columns)], out.at[:, pl.ds(width, columns)], sems.at[1, i]
            ),
        ]
    for copy in copies:
        copy.start()
    for copy in copies:
        copy.wait()


def message_call(down, up, columns, per_device):
    rows, width = down.shape
    shape = jax.ShapeDtypeStruct((rows // per_device, width + columns), jnp.bfloat16)
    return pl.pallas_call(
        message_kernel,
        in_specs=[HBM, HBM],
        out_specs=[VMEM] * per_device,
        out_shape=[shape] * per_device,
        scratch_shapes=[pltpu.SemaphoreType.DMA((2, per_device))],
        compiler_params=params(8),
        cost_estimate=cost(0, 4 * rows * (width + columns)),
    )(down, up)


def table_kernel(n_adapter, per_device, ids, slots, table):
    seg_dev = ids.shape[0] // SEGMENT_ROWS
    used = [slots[ids[s * SEGMENT_ROWS]] for s in range(seg_dev)]
    for k, owner in enumerate(arrival_order(lax.axis_index("adapter"), n_adapter)):
        table[k * ENTRIES] = owner
        found, place = [jnp.int32(-1)] * MOST, [jnp.int32(0)] * MOST
        count = jnp.int32(0)
        for s, slot in enumerate(used):
            within = slot - owner * per_device
            hit = (within >= 0) & (within < per_device)
            for j in range(MOST):
                take = hit & (count == j)
                found[j] = jnp.where(take, s, found[j])
                place[j] = jnp.where(take, within, place[j])
            count = count + hit.astype(jnp.int32)
        for j in range(MOST):
            table[k * ENTRIES + 1 + 2 * j] = found[j]
            table[k * ENTRIES + 2 + 2 * j] = place[j]


def table_call(ids, slots, n_adapter, per_device):
    return pl.pallas_call(
        functools.partial(table_kernel, n_adapter, per_device),
        in_specs=[SMEM, SMEM],
        out_specs=SMEM,
        out_shape=jax.ShapeDtypeStruct((n_adapter * ENTRIES,), jnp.int32),
        cost_estimate=cost(0, 4 * ids.shape[0]),
    )(ids, slots)


def diagonal():
    shape = (SEGMENT_ROWS, SEGMENT_ROWS)
    return lax.broadcasted_iota(jnp.int32, shape, 0) == lax.broadcasted_iota(jnp.int32, shape, 1)


GROUP = SEGMENT_ROWS // 8
WORDS = 5 * GROUP


def coded_rows(segments):
    return segments * WORDS + 8


def encode(values, o_ref, unit, units):
    largest = jnp.maximum(jnp.max(jnp.abs(values), axis=1, keepdims=True), 2.0**-100)
    power = jnp.floor(jnp.log2(largest))
    whole = (values * jnp.exp2(18.0 - power) + MIDDLE).astype(jnp.int32) - int(MIDDLE)
    whole = jnp.minimum(whole, 2**19 - 1)
    v = [whole[i * GROUP : (i + 1) * GROUP] for i in range(8)]
    over = [
        v[5] & 0xFFF,
        ((v[5] >> 12) & 0xFF) | ((v[6] & 0xF) << 8),
        (v[6] >> 4) & 0xFFF,
        ((v[6] >> 16) & 0xF) | ((v[7] & 0xFF) << 4),
        v[7] >> 8,
    ]
    for i in range(5):
        o_ref[unit * WORDS + i * GROUP : unit * WORDS + (i + 1) * GROUP, :] = (v[i] & 0xFFFFF) | (
            over[i] << 20
        )
    row = jnp.sum(jnp.where(diagonal(), power, 0.0), axis=0, keepdims=True)
    o_ref[units * WORDS + unit : units * WORDS + unit + 1, :SEGMENT_ROWS] = row.astype(jnp.int32)


def decode(ref, unit, units):
    w = [ref[unit * WORDS + i * GROUP : unit * WORDS + (i + 1) * GROUP, :] for i in range(5)]
    v = [(x << 12) >> 12 for x in w]
    v.append(((w[0] >> 20) & 0xFFF) | (((w[1] << 4) >> 24) << 12))
    v.append(((w[1] >> 28) & 0xF) | (((w[2] >> 20) & 0xFFF) << 4) | (((w[3] << 8) >> 28) << 16))
    v.append(((w[3] >> 24) & 0xFF) | ((w[4] >> 20) << 8))
    row = ref[units * WORDS + unit : units * WORDS + unit + 1, :SEGMENT_ROWS].astype(jnp.float32)
    power = jnp.sum(jnp.where(diagonal(), row, 0.0), axis=1, keepdims=True)
    return jnp.concatenate(v, axis=0).astype(jnp.float32) * jnp.exp2(power - 18.0)


def add_decoded(sums, chunk, refs, above):
    first, number = CHUNKS[chunk]
    for unit in range(number):
        at = first + unit - above
        if at < 0 or at >= sums.shape[0] // SEGMENT_ROWS:
            continue
        rows = pl.ds(at * SEGMENT_ROWS, SEGMENT_ROWS)
        value = sums[rows, :]
        for ref in refs:
            value = value + decode(ref, unit, number)
        sums[rows, :] = value


def load_base(first, segments, column, x_ref, w_ref, x, w, sems):
    width, columns = w.shape
    rows = segments * SEGMENT_ROWS
    start = pl.multiple_of(column * columns, columns)
    depth = width // PIECES
    blocks = [(r, min(BLOCK, rows - r)) for r in range(0, rows, BLOCK)]

    def x_copy(at, size, features, sem):
        return pltpu.make_async_copy(
            x_ref.at[pl.ds(first * SEGMENT_ROWS + at, size), features],
            x.at[pl.ds(at, size), features],
            sem,
        )

    work = []
    for i, (at, size) in enumerate(blocks):
        terms = []
        if i == 0:
            for p in range(PIECES):
                features = pl.ds(p * depth, depth)
                copies = (
                    pltpu.make_async_copy(
                        w_ref.at[features, pl.ds(start, columns)], w.at[features, :], sems.at[0, p]
                    ),
                    x_copy(0, size, features, sems.at[1, p]),
                )
                terms.append((copies, slice(p * depth, (p + 1) * depth)))
        else:
            terms.append(((x_copy(at, size, slice(None), sems.at[2, i]),), slice(None)))
        work.append((at, size, terms))
    for _, _, terms in work:
        for copies, _ in terms:
            for copy in copies:
                copy.start()
    return work


def block_product(x, w, at, size, terms):
    total = None
    for copies, features in terms:
        for copy in copies:
            copy.wait()
        term = jnp.dot(
            x[at : at + size, features], w[features, :], preferred_element_type=jnp.float32
        )
        total = term if total is None else total + term
    return total


def base_scratch(segments, width, columns):
    rows = segments * SEGMENT_ROWS
    return [
        pltpu.VMEM((rows, width), jnp.bfloat16),
        pltpu.VMEM((width, columns), jnp.bfloat16),
        pltpu.SemaphoreType.DMA((3, max(PIECES, rows // BLOCK + 1))),
    ]


def sent_kernel(first, sizes, step, n_tensor, x_ref, w_ref, *refs):
    outs, (x, w, sems) = refs[: len(sizes)], refs[len(sizes) :]
    column = lax.rem(lax.axis_index("tensor") + step, n_tensor)
    work = load_base(first, sum(sizes), column, x_ref, w_ref, x, w, sems)
    unit_of = [(out, unit) for out, size in enumerate(sizes) for unit in range(size)]
    for out, size in zip(outs, sizes):
        out[size * WORDS :, :] = jnp.zeros((8, w.shape[1]), jnp.int32)
    for at, size, terms in work:
        product = block_product(x, w, at, size, terms)
        for r in range(0, size, SEGMENT_ROWS):
            out, unit = unit_of[(at + r) // SEGMENT_ROWS]
            encode(product[r : r + SEGMENT_ROWS], outs[out], unit, sizes[out])


def sent_call(tokens, weight, step, n_tensor, columns, first, sizes):
    width = tokens.shape[1]
    rows = sum(sizes) * SEGMENT_ROWS
    return pl.pallas_call(
        functools.partial(sent_kernel, first, sizes, step, n_tensor),
        in_specs=[HBM, HBM],
        out_specs=[VMEM] * len(sizes),
        out_shape=[jax.ShapeDtypeStruct((coded_rows(n), columns), jnp.int32) for n in sizes],
        scratch_shapes=base_scratch(sum(sizes), width, columns),
        compiler_params=params(16),
        cost_estimate=cost(
            2 * rows * width * columns, 2 * rows * width + 2 * width * columns + 4 * rows * columns
        ),
    )(tokens, weight)


def add_kernel(chunk, above, sums_ref, *refs):
    coded_refs, o_ref = refs[:-1], refs[-1]
    o_ref[...] = sums_ref[...]
    add_decoded(o_ref, chunk, coded_refs, above)


def add_call(chunk, above, sums, coded):
    return pl.pallas_call(
        functools.partial(add_kernel, chunk, above),
        in_specs=[VMEM] * (1 + len(coded)),
        out_specs=VMEM,
        out_shape=jax.ShapeDtypeStruct(sums.shape, sums.dtype),
        compiler_params=params(8),
        cost_estimate=cost(40000 * sums.size, 12 * sums.size),
    )(sums, *coded)


def shrink_into(o_ref, at, table, k, rows_of, views, rank):
    for j in range(MOST):
        _, _, within = segment_of(table, k, j)
        for stage, ref, first, whose, i in views:
            if stage not in stages_of(k):
                continue

            @pl.when((whose == table[k * ENTRIES]) & (within == i))
            def _(j=j, ref=ref, first=first):
                rows = rows_of(j)
                o_ref[at, :, j * rank : (j + 1) * rank] = lax.dot_general(
                    rows,
                    ref[first : first + rank, : rows.shape[1]],
                    (((1,), (1,)), ((), ())),
                    preferred_element_type=jnp.float32,
                )


def join_copies(halves, whole, sems):
    copies, rank = [], halves[0].shape[0]
    for i, half in enumerate(halves):
        copies.append(
            pltpu.make_async_copy(half, whole.at[pl.ds(i * rank, rank), :], sems.at[i])
        )
        copies[-1].start()
    return copies


def stages_of(k):
    return range((k + 1) // 2, k + 1)


def stages_of_all(ks):
    return range(stages_of(ks[0])[0], ks[-1] + 1)


def upper_kernel(n_adapter, table, x_ref, w_ref, o_ref, kept_ref, x, w, sems, kept_sems):
    work = load_base(0, x.shape[0] // SEGMENT_ROWS, lax.axis_index("tensor"), x_ref, w_ref, x, w, sems)
    keeps = []
    for k in range(1, n_adapter):
        for j in range(MOST):
            start, _, _ = segment_of(table, k, j)
            keeps.append(
                pltpu.make_async_copy(
                    x_ref.at[pl.ds(start, SEGMENT_ROWS), :],
                    kept_ref.at[k - 1, j],
                    kept_sems.at[k - 1, j],
                )
            )
            keeps[-1].start()
    for at, size, terms in work:
        o_ref[at : at + size, :] = block_product(x, w, at, size, terms)
    for copy in keeps:
        copy.wait()


def upper_call(table, tokens, weight, columns, n_adapter):
    rows, width = tokens.shape
    half = UPPER * SEGMENT_ROWS
    return pl.pallas_call(
        functools.partial(upper_kernel, n_adapter),
        in_specs=[SMEM, HBM, HBM],
        out_specs=[VMEM] * 2,
        out_shape=[
            jax.ShapeDtypeStruct((half, columns), jnp.float32),
            jax.ShapeDtypeStruct((n_adapter - 1, MOST, SEGMENT_ROWS, width), jnp.bfloat16),
        ],
        scratch_shapes=base_scratch(half // SEGMENT_ROWS, width, columns)
        + [pltpu.SemaphoreType.DMA((n_adapter - 1, MOST))],
        compiler_params=params(12),
        cost_estimate=cost(2 * half * width * columns, 2 * rows * width + 2 * width * columns),
    )(table, tokens, weight)


def lower_kernel(per_device, rank, table, x_ref, w_ref, *refs):
    messages, halves, refs = refs[:per_device], refs[per_device : 2 * per_device], refs[2 * per_device :]
    coded_refs, (o_ref, s_ref, whole_ref, x, w, sems, mine, mine_sems, join_sems) = refs[:-9], refs[-9:]
    work = load_base(UPPER, x.shape[0] // SEGMENT_ROWS, lax.axis_index("tensor"), x_ref, w_ref, x, w, sems)
    joins = join_copies(halves, whole_ref, join_sems)
    loads = []
    for j in range(MOST):
        start, _, _ = segment_of(table, 0, j)
        loads.append(
            pltpu.make_async_copy(
                x_ref.at[pl.ds(start, SEGMENT_ROWS), :], mine.at[j], mine_sems.at[j]
            )
        )
        loads[-1].start()
    for at, size, terms in work:
        o_ref[at : at + size, :] = block_product(x, w, at, size, terms)
    add_decoded(o_ref, 0, coded_refs, UPPER)
    for copy in loads:
        copy.wait()
    views = views_of(messages, [0], [(per_device, 0)], rank)
    shrink_into(s_ref, 0, table, 0, lambda j: mine[j], views, rank)
    for copy in joins:
        copy.wait()


def lower_call(table, tokens, weight, messages, halves, coded, columns):
    rows, width = tokens.shape
    half = rows - UPPER * SEGMENT_ROWS
    per_device, (rank, long) = len(messages), messages[0].shape
    return pl.pallas_call(
        functools.partial(lower_kernel, per_device, rank),
        in_specs=[SMEM, HBM, HBM] + [VMEM] * (2 * per_device + len(coded)),
        out_specs=[VMEM] * 3,
        out_shape=[
            jax.ShapeDtypeStruct((half, columns), jnp.float32),
            jax.ShapeDtypeStruct((1, SEGMENT_ROWS, MOST * rank), jnp.float32),
            jax.ShapeDtypeStruct((per_device * rank, long), jnp.bfloat16),
        ],
        scratch_shapes=base_scratch(half // SEGMENT_ROWS, width, columns)
        + [
            pltpu.VMEM((MOST, SEGMENT_ROWS, width), jnp.bfloat16),
            pltpu.SemaphoreType.DMA((MOST,)),
            pltpu.SemaphoreType.DMA((per_device,)),
        ],
        compiler_params=params(14),
        cost_estimate=cost(0 * half * width * columns, 4 * rows * columns),
    )(table, tokens, weight, *messages, *halves, *coded)


def shrink_kernel(ks, rank, at, layout, table, kept_ref, *refs):
    buffers, o_ref = refs[1 if at else 0 : -1], refs[-1]
    if at:
        o_ref[:at] = refs[0][...]
    views = views_of(buffers, stages_of_all(ks), layout, rank)
    for i, k in enumerate(ks):
        shrink_into(o_ref, at + i, table, k, lambda j, k=k: kept_ref[k - 1, j], views, rank)


def shrink_call(ks, table, kept, before, buffers, layout, rank):
    width = kept.shape[3]
    at = sum(b.shape[0] for b in before)
    return pl.pallas_call(
        functools.partial(shrink_kernel, ks, rank, at, layout),
        in_specs=[SMEM] + [VMEM] * (1 + len(before) + len(buffers)),
        out_specs=VMEM,
        out_shape=jax.ShapeDtypeStruct((at + len(ks), SEGMENT_ROWS, MOST * rank), jnp.float32),
        compiler_params=params(4),
        cost_estimate=cost(
            len(ks) * MOST * 2 * SEGMENT_ROWS * width * 256, len(ks) * 4 * SEGMENT_ROWS * width
        ),
    )(table, kept, *before, *buffers)


def fetch_up(up, at, table, k, j, views, rank):
    columns = up.shape[2]
    _, _, within = segment_of(table, k, j)
    for stage, ref, first, whose, i in views:
        if stage not in stages_of(k):
            continue

        @pl.when((whose == table[k * ENTRIES]) & (within == i))
        def _(ref=ref, first=first):
            factor = ref[first : first + rank, ref.shape[1] - columns :]
            up[at, :rank, :] = factor
            up[at, rank:, :] = factor


def up_product(share, j, factor, rank):
    lane = lax.broadcasted_iota(jnp.int32, share.shape, 1)
    other = pltpu.roll(share, rank, 1)
    both = jnp.where((lane < rank) == (j == 0), share, other)
    high = both.astype(jnp.bfloat16).astype(jnp.float32)
    terms = jnp.where(lane < rank, high, both - high).astype(jnp.bfloat16)
    return jnp.dot(terms, factor, preferred_element_type=jnp.float32)


LATE = 2


def pick_sums(sums, upper_ref, lower_ref, start):
    upper_rows = upper_ref.shape[0]

    @pl.when(start < upper_rows)
    def _():
        at = pl.multiple_of(jnp.minimum(start, upper_rows - SEGMENT_ROWS), SEGMENT_ROWS)
        sums[...] = upper_ref[pl.ds(at, SEGMENT_ROWS), :]

    @pl.when(start >= upper_rows)
    def _():
        at = pl.multiple_of(jnp.maximum(start - upper_rows, 0), SEGMENT_ROWS)
        sums[...] = lower_ref[pl.ds(at, SEGMENT_ROWS), :]


def early_kernel(n_adapter, n_tensor, rank, layout, n_buffers, table, *refs):
    first = n_adapter - LATE
    upper_ref, lower_ref, refs = refs[0], refs[1], refs[2:]
    shrinks, refs = refs[: -3 - n_buffers], refs[-3 - n_buffers :]
    buffers, (o_ref, up, sums) = refs[:-3], refs[-3:]
    views = views_of(buffers, range(first), layout, rank)
    for k in range(first):
        for j in range(MOST):
            fetch_up(up, k * MOST + j, table, k, j, views, rank)
    shares = []
    for call in range(len(shrinks) // n_tensor):
        share = shrinks[call * n_tensor][...]
        for i in range(1, n_tensor):
            share = share + shrinks[call * n_tensor + i][...]
        shares += [share[i] for i in range(share.shape[0])]
    for k in range(first):
        for j in range(MOST):
            start, used, _ = segment_of(table, k, j)
            pick_sums(sums, upper_ref, lower_ref, start)
            value = sums[...]
            lora = up_product(shares[k], j, up[k * MOST + j], rank)

            @pl.when(used)
            def _(start=start, value=value, lora=lora):
                o_ref[pl.ds(start, SEGMENT_ROWS), :] = (value + adapter_scale * lora).astype(
                    jnp.bfloat16
                )


def early(n_adapter, n_tensor, table, upper, lower, shrinks, buffers, layout, rank):
    rows, columns = upper.shape[0] + lower.shape[0], upper.shape[1]
    return pl.pallas_call(
        functools.partial(early_kernel, n_adapter, n_tensor, rank, layout, len(buffers)),
        in_specs=[SMEM] + [VMEM] * (2 + len(shrinks) + len(buffers)),
        out_specs=VMEM,
        out_shape=jax.ShapeDtypeStruct((rows, columns), jnp.bfloat16),
        scratch_shapes=[
            pltpu.VMEM(((n_adapter - LATE) * MOST, 2 * rank, columns), jnp.bfloat16),
            pltpu.VMEM((SEGMENT_ROWS, columns), jnp.float32),
        ],
        compiler_params=params(16),
        cost_estimate=cost(600 * rows * rank * columns, (4 * n_tensor + 2) * rows * columns),
    )(table, upper, lower, *shrinks, *buffers)


def late_kernel(ks, n_tensor, rank, layout, table, *refs):
    upper_ref, lower_ref, shrinks, refs = refs[0], refs[1], refs[2 : 2 + n_tensor], refs[2 + n_tensor :]
    buffers, (_, o_ref, up, sums, out, sems) = refs[:-6], refs[-6:]
    views = views_of(buffers, stages_of_all(ks), layout, rank)
    stores = []
    for i, k in enumerate(ks):
        share = shrinks[0][i]
        for r in shrinks[1:]:
            share = share + r[i]
        for j in range(MOST):
            fetch_up(up, i * MOST + j, table, k, j, views, rank)
            start, used, _ = segment_of(table, k, j)
            lora = up_product(share, j, up[i * MOST + j], rank)
            pick_sums(sums, upper_ref, lower_ref, start)
            out[i, j] = (sums[...] + adapter_scale * lora).astype(jnp.bfloat16)
            store = pltpu.make_async_copy(
                out.at[i, j], o_ref.at[pl.ds(start, SEGMENT_ROWS), :], sems.at[i, j]
            )
            pl.when(used)(store.start)
            stores.append((used, store))
    for used, store in stores:
        pl.when(used)(store.wait)


def late(ks, n_tensor, table, upper, lower, shrinks, buffers, value, layout, rank):
    rows, columns = value.shape
    return pl.pallas_call(
        functools.partial(late_kernel, ks, n_tensor, rank, layout),
        in_specs=[SMEM] + [VMEM] * (2 + len(shrinks) + len(buffers)) + [ANY],
        out_specs=ANY,
        out_shape=jax.ShapeDtypeStruct((rows, columns), jnp.bfloat16),
        scratch_shapes=[
            pltpu.VMEM((LATE * MOST, 2 * rank, columns), jnp.bfloat16),
            pltpu.VMEM((SEGMENT_ROWS, columns), jnp.float32),
            pltpu.VMEM((LATE, MOST, SEGMENT_ROWS, columns), jnp.bfloat16),
            pltpu.SemaphoreType.DMA((LATE, MOST)),
        ],
        input_output_aliases={3 + len(shrinks) + len(buffers): 0},
        compiler_params=params(8),
        cost_estimate=cost(
            6 * LATE * MOST * SEGMENT_ROWS * rank * columns,
            8 * LATE * MOST * SEGMENT_ROWS * columns,
        ),
    )(table, upper, lower, *shrinks, *buffers, value)


def after(array, *others):
    return lax.optimization_barrier((array, *others))[0]


def on_device(
    tokens, value_weight, adapter_down_weight, adapter_up_weight, row_adapter_index, adapter_slot_of
):
    rows, width = tokens.shape
    per_device, _, rank = adapter_down_weight.shape
    n_adapter = lax.axis_size("adapter")
    n_tensor = lax.axis_size("tensor")
    columns = value_weight.shape[1] // n_tensor

    def swap_tensor(array, step):
        pairs = [(i, (i + step) % n_tensor) for i in range(n_tensor)]
        return lax.ppermute(array, "tensor", pairs)

    def along_line(array, stage):
        up = [(2 * i, 2 * (i + 1)) for i in range(stage - 1, n_adapter - 1)]
        down = [(2 * i + 1, 2 * (i - 1) + 1) for i in range(1, n_adapter - stage + 1)]
        return lax.ppermute(array, ("adapter", "dp"), up + down)

    def swap_cores(array):
        return lax.ppermute(array, "dp", [(0, 1), (1, 0)])

    down = jnp.swapaxes(adapter_down_weight, 1, 2).reshape(per_device * rank, width)
    up = adapter_up_weight.reshape(per_device * rank, value_weight.shape[1])
    tokens, value_weight, down, up = (
        pltpu.with_memory_space_constraint(a, pltpu.HBM) for a in (tokens, value_weight, down, up)
    )
    messages = message_call(down, up, columns, per_device)
    table = table_call(row_adapter_index, adapter_slot_of, n_adapter, per_device)
    last = n_adapter - 1
    buffers, shrinks = [list(messages)], []
    layout = [(per_device, 0), (per_device, 1)] + [(per_device, per_device)] * (last - 1)

    def buffers_of(stages):
        return [b for stage in stages for b in buffers[stage]]

    def shrink(ks, kept, before=()):
        mine = buffers_of(stages_of_all(ks))
        return shrink_call(ks, table, kept, list(before), mine, layout, rank)

    def add_shrink(mine):
        shrinks.extend([mine] + [swap_tensor(mine, step) for step in range(1, n_tensor)])

    others = range(1, n_tensor)

    def sent_for(step, chunks, rows):
        sizes = [number for _, number in chunks]
        return sent_call(rows, value_weight, step, n_tensor, columns, chunks[0][0], sizes)

    def send(parts, *ahead):
        return [swap_tensor(after(p, *ahead), step) for step, p in zip(others, parts)]

    held = [along_line(m, 1) for m in messages]
    part_a = [sent_for(step, CHUNKS[:1], tokens)[0] for step in others]
    sent = [send(part_a)]
    first = after(held[0], table, *part_a)
    rest_parts = [sent_for(step, CHUNKS[1:], after(tokens, first)) for step in others]
    parts = [[p[i] for p in rest_parts] for i in range(len(CHUNKS) - 1)]
    part_b = [p for group in parts for p in group]
    for stage in range(1, last):
        came = held
        if stage == 1:
            came = [first] + [after(h, *part_b) for h in held[1:]]
            sent.append(send(parts[0], *came, *sent[0]))
        if stage == 2:
            came = held[:1] + [after(h, upper) for h in held[1:]]
        held = [along_line(c, stage + 1) for c in came]
        if stage == 1:
            upper, kept = upper_call(
                after(table, held[0], *came), tokens, value_weight, columns, n_adapter
            )
        elif stage == 2:
            lower, before, joined = lower_call(
                after(table, *came), tokens, value_weight, messages, buffers[1], sent[0], columns
            )
            buffers[1] += [swap_cores(joined)]
            free = lower
            upper = add_call(1, 0, after(upper, held[0]), sent[1])
            add_shrink(before)
            lower = add_call(1, UPPER, after(lower, upper, *held[1:], *shrinks), sent[1])
            before = shrink([1], after(kept, lower))
        else:
            before = shrink([stage - 1], kept, [before])
        ahead = [free] if stage == 2 else []
        swapped = [swap_cores(after(c, *ahead)) for c in came] if stage > 1 else []
        buffers.append([*came, *swapped])
    add_shrink(before)
    value = early(
        n_adapter,
        n_tensor,
        table,
        upper,
        lower,
        shrinks,
        buffers_of(range(last - 1)),
        layout,
        rank,
    )
    buffers.append([*held, *[swap_cores(h) for h in held]])
    ks = (last - 1, last)
    add_shrink(shrink(ks, after(kept, *held, before)))
    return late(
        ks,
        n_tensor,
        table,
        upper,
        lower,
        shrinks[-n_tensor:],
        buffers_of(stages_of_all(ks)),
        value,
        layout,
        rank,
    )


def solution(mesh):
    return jax.shard_map(
        on_device,
        mesh=mesh,
        in_specs=(
            P(("groups", "adapter", "dp"), "tensor"),
            P("tensor", None),
            P(("groups", "adapter"), "tensor", None),
            P(("groups", "adapter"), None, None),
            P(("groups", "adapter", "dp")),
            P("groups"),
        ),
        out_specs=P(("groups", "adapter", "dp"), "tensor"),
        check_vma=False,
    )
```

```python
import functools

import jax
import jax.numpy as jnp
from jax import lax
from jax.experimental import pallas as pl
from jax.experimental.pallas import tpu as pltpu
from jax.sharding import PartitionSpec as P

SEGMENT_ROWS = 128
adapter_scale = 0.5
MOST = 2
BLOCK = 256
PIECES = 4
CHUNKS = ((6, 2), (0, 6))
UPPER = 3
ENTRIES = 8
MIDDLE = 1.5 * 2.0**23


def cost(flops, moved):
    return pl.CostEstimate(flops=int(flops), bytes_accessed=int(moved), transcendentals=0)


def params(mib):
    return pltpu.CompilerParams(vmem_limit_bytes=mib * 2**20)


ANY = pl.BlockSpec(memory_space=pl.ANY)
HBM = pl.BlockSpec(memory_space=pltpu.HBM)
SMEM = pl.BlockSpec(memory_space=pltpu.SMEM)
VMEM = pl.BlockSpec(memory_space=pltpu.VMEM)


def arrival_order(me, n_adapter):
    order = [me] + [jnp.int32(-1)] * (n_adapter - 1)
    count = jnp.int32(1)
    for distance in range(1, n_adapter):
        for other in (me - distance, me + distance):
            valid = (other >= 0) & (other < n_adapter)
            order = [jnp.where(valid & (count == k), other, o) for k, o in enumerate(order)]
            count = count + valid.astype(jnp.int32)
    return order


def views_of(refs, stages, layout, rank):
    me, core = lax.axis_index("adapter"), lax.axis_index("dp")
    refs, views = list(refs), []
    for stage in stages:
        came, swapped = layout[stage]
        toward = jnp.where(core == 0, -stage, stage)
        for i in range(came):
            views.append((stage, refs.pop(0), 0, me + toward if stage > 0 else me, i))
        for i in range(swapped):
            ref = refs.pop(0)
            for part in range(came // swapped):
                views.append((stage, ref, part * rank, me - toward, i + part))
    return views


def segment_of(table, k, j):
    seg = table[k * ENTRIES + 1 + 2 * j]
    start = pl.multiple_of(jnp.maximum(seg, 0) * SEGMENT_ROWS, SEGMENT_ROWS)
    return start, seg >= 0, table[k * ENTRIES + 2 + 2 * j]


def message_kernel(down_ref, up_ref, *refs):
    outs, sems = refs[:-1], refs[-1]
    rank = outs[0].shape[0]
    width = down_ref.shape[1]
    columns = outs[0].shape[1] - width
    start = pl.multiple_of(lax.axis_index("tensor") * columns, columns)
    copies = []
    for i, out in enumerate(outs):
        rows = pl.ds(i * rank, rank)
        copies += [
            pltpu.make_async_copy(down_ref.at[rows, :], out.at[:, pl.ds(0, width)], sems.at[0, i]),
            pltpu.make_async_copy(
                up_ref.at[rows, pl.ds(start, columns)], out.at[:, pl.ds(width, columns)], sems.at[1, i]
            ),
        ]
    for copy in copies:
        copy.start()
    for copy in copies:
        copy.wait()


def message_call(down, up, columns, per_device):
    rows, width = down.shape
    shape = jax.ShapeDtypeStruct((rows // per_device, width + columns), jnp.bfloat16)
    return pl.pallas_call(
        message_kernel,
        in_specs=[HBM, HBM],
        out_specs=[VMEM] * per_device,
        out_shape=[shape] * per_device,
        scratch_shapes=[pltpu.SemaphoreType.DMA((2, per_device))],
        compiler_params=params(8),
        cost_estimate=cost(0, 4 * rows * (width + columns)),
    )(down, up)


def table_kernel(n_adapter, per_device, ids, slots, table):
    seg_dev = ids.shape[0] // SEGMENT_ROWS
    used = [slots[ids[s * SEGMENT_ROWS]] for s in range(seg_dev)]
    for k, owner in enumerate(arrival_order(lax.axis_index("adapter"), n_adapter)):
        table[k * ENTRIES] = owner
        found, place = [jnp.int32(-1)] * MOST, [jnp.int32(0)] * MOST
        count = jnp.int32(0)
        for s, slot in enumerate(used):
            within = slot - owner * per_device
            hit = (within >= 0) & (within < per_device)
            for j in range(MOST):
                take = hit & (count == j)
                found[j] = jnp.where(take, s, found[j])
                place[j] = jnp.where(take, within, place[j])
            count = count + hit.astype(jnp.int32)
        for j in range(MOST):
            table[k * ENTRIES + 1 + 2 * j] = found[j]
            table[k * ENTRIES + 2 + 2 * j] = place[j]


def table_call(ids, slots, n_adapter, per_device):
    return pl.pallas_call(
        functools.partial(table_kernel, n_adapter, per_device),
        in_specs=[SMEM, SMEM],
        out_specs=SMEM,
        out_shape=jax.ShapeDtypeStruct((n_adapter * ENTRIES,), jnp.int32),
        cost_estimate=cost(0, 4 * ids.shape[0]),
    )(ids, slots)


def diagonal():
    shape = (SEGMENT_ROWS, SEGMENT_ROWS)
    return lax.broadcasted_iota(jnp.int32, shape, 0) == lax.broadcasted_iota(jnp.int32, shape, 1)


GROUP = SEGMENT_ROWS // 8
WORDS = 5 * GROUP


def coded_rows(segments):
    return segments * WORDS + 8


def encode(values, o_ref, unit, units):
    largest = jnp.maximum(jnp.max(jnp.abs(values), axis=1, keepdims=True), 2.0**-100)
    power = jnp.floor(jnp.log2(largest))
    whole = (values * jnp.exp2(18.0 - power) + MIDDLE).astype(jnp.int32) - int(MIDDLE)
    whole = jnp.clip(whole, -(2**19), 2**19 - 1)
    v = [whole[i * GROUP : (i + 1) * GROUP] for i in range(8)]
    over = [
        v[5] & 0xFFF,
        ((v[5] >> 12) & 0xFF) | ((v[6] & 0xF) << 8),
        (v[6] >> 4) & 0xFFF,
        ((v[6] >> 16) & 0xF) | ((v[7] & 0xFF) << 4),
        v[7] >> 8,
    ]
    for i in range(5):
        o_ref[unit * WORDS + i * GROUP : unit * WORDS + (i + 1) * GROUP, :] = (v[i] & 0xFFFFF) | (
            over[i] << 20
        )
    row = jnp.sum(jnp.where(diagonal(), power, 0.0), axis=0, keepdims=True)
    o_ref[units * WORDS + unit : units * WORDS + unit + 1, :SEGMENT_ROWS] = row.astype(jnp.int32)


def decode(ref, unit, units):
    w = [ref[unit * WORDS + i * GROUP : unit * WORDS + (i + 1) * GROUP, :] for i in range(5)]
    v = [(x << 12) >> 12 for x in w]
    v.append(((w[0] >> 20) & 0xFFF) | (((w[1] << 4) >> 24) << 12))
    v.append(((w[1] >> 28) & 0xF) | (((w[2] >> 20) & 0xFFF) << 4) | (((w[3] << 8) >> 28) << 16))
    v.append(((w[3] >> 24) & 0xFF) | ((w[4] >> 20) << 8))
    row = ref[units * WORDS + unit : units * WORDS + unit + 1, :SEGMENT_ROWS].astype(jnp.float32)
    power = jnp.sum(jnp.where(diagonal(), row, 0.0), axis=1, keepdims=True)
    return jnp.concatenate(v, axis=0).astype(jnp.float32) * jnp.exp2(power - 18.0)


def add_decoded(sums, chunk, refs, above):
    first, number = CHUNKS[chunk]
    for unit in range(number):
        at = first + unit - above
        if at < 0 or at >= sums.shape[0] // SEGMENT_ROWS:
            continue
        rows = pl.ds(at * SEGMENT_ROWS, SEGMENT_ROWS)
        value = sums[rows, :]
        for ref in refs:
            value = value + decode(ref, unit, number)
        sums[rows, :] = value


def load_base(first, segments, column, x_ref, w_ref, x, w, sems):
    width, columns = w.shape
    rows = segments * SEGMENT_ROWS
    start = pl.multiple_of(column * columns, columns)
    depth = width // PIECES
    blocks = [(r, min(BLOCK, rows - r)) for r in range(0, rows, BLOCK)]

    def x_copy(at, size, features, sem):
        return pltpu.make_async_copy(
            x_ref.at[pl.ds(first * SEGMENT_ROWS + at, size), features],
            x.at[pl.ds(at, size), features],
            sem,
        )

    work = []
    for i, (at, size) in enumerate(blocks):
        terms = []
        if i == 0:
            for p in range(PIECES):
                features = pl.ds(p * depth, depth)
                copies = (
                    pltpu.make_async_copy(
                        w_ref.at[features, pl.ds(start, columns)], w.at[features, :], sems.at[0, p]
                    ),
                    x_copy(0, size, features, sems.at[1, p]),
                )
                terms.append((copies, slice(p * depth, (p + 1) * depth)))
        else:
            terms.append(((x_copy(at, size, slice(None), sems.at[2, i]),), slice(None)))
        work.append((at, size, terms))
    for _, _, terms in work:
        for copies, _ in terms:
            for copy in copies:
                copy.start()
    return work


def block_product(x, w, at, size, terms):
    total = None
    for copies, features in terms:
        for copy in copies:
            copy.wait()
        term = jnp.dot(
            x[at : at + size, features], w[features, :], preferred_element_type=jnp.float32
        )
        total = term if total is None else total + term
    return total


def base_scratch(segments, width, columns):
    rows = segments * SEGMENT_ROWS
    return [
        pltpu.VMEM((rows, width), jnp.bfloat16),
        pltpu.VMEM((width, columns), jnp.bfloat16),
        pltpu.SemaphoreType.DMA((3, max(PIECES, rows // BLOCK + 1))),
    ]


def sent_kernel(first, sizes, step, n_tensor, x_ref, w_ref, *refs):
    outs, (x, w, sems) = refs[: len(sizes)], refs[len(sizes) :]
    column = lax.rem(lax.axis_index("tensor") + step, n_tensor)
    work = load_base(first, sum(sizes), column, x_ref, w_ref, x, w, sems)
    unit_of = [(out, unit) for out, size in enumerate(sizes) for unit in range(size)]
    for out, size in zip(outs, sizes):
        out[size * WORDS :, :] = jnp.zeros((8, w.shape[1]), jnp.int32)
    for at, size, terms in work:
        product = block_product(x, w, at, size, terms)
        for r in range(0, size, SEGMENT_ROWS):
            out, unit = unit_of[(at + r) // SEGMENT_ROWS]
            encode(product[r : r + SEGMENT_ROWS], outs[out], unit, sizes[out])


def sent_call(tokens, weight, step, n_tensor, columns, first, sizes):
    width = tokens.shape[1]
    rows = sum(sizes) * SEGMENT_ROWS
    return pl.pallas_call(
        functools.partial(sent_kernel, first, sizes, step, n_tensor),
        in_specs=[HBM, HBM],
        out_specs=[VMEM] * len(sizes),
        out_shape=[jax.ShapeDtypeStruct((coded_rows(n), columns), jnp.int32) for n in sizes],
        scratch_shapes=base_scratch(sum(sizes), width, columns),
        compiler_params=params(16),
        cost_estimate=cost(
            2 * rows * width * columns, 2 * rows * width + 2 * width * columns + 4 * rows * columns
        ),
    )(tokens, weight)


def add_kernel(chunk, above, sums_ref, *refs):
    coded_refs, o_ref = refs[:-1], refs[-1]
    o_ref[...] = sums_ref[...]
    add_decoded(o_ref, chunk, coded_refs, above)


def add_call(chunk, above, sums, coded):
    return pl.pallas_call(
        functools.partial(add_kernel, chunk, above),
        in_specs=[VMEM] * (1 + len(coded)),
        out_specs=VMEM,
        out_shape=jax.ShapeDtypeStruct(sums.shape, sums.dtype),
        compiler_params=params(8),
        cost_estimate=cost(40000 * sums.size, 12 * sums.size),
    )(sums, *coded)


def shrink_into(o_ref, at, table, k, rows_of, views, rank):
    for j in range(MOST):
        _, _, within = segment_of(table, k, j)
        for stage, ref, first, whose, i in views:
            if stage not in stages_of(k):
                continue

            @pl.when((whose == table[k * ENTRIES]) & (within == i))
            def _(j=j, ref=ref, first=first):
                rows = rows_of(j)
                o_ref[at, :, j * rank : (j + 1) * rank] = lax.dot_general(
                    rows,
                    ref[first : first + rank, : rows.shape[1]],
                    (((1,), (1,)), ((), ())),
                    preferred_element_type=jnp.float32,
                )


def join_copies(halves, whole, sems):
    copies, rank = [], halves[0].shape[0]
    for i, half in enumerate(halves):
        copies.append(
            pltpu.make_async_copy(half, whole.at[pl.ds(i * rank, rank), :], sems.at[i])
        )
        copies[-1].start()
    return copies


def stages_of(k):
    return range((k + 1) // 2, k + 1)


def stages_of_all(ks):
    return range(stages_of(ks[0])[0], ks[-1] + 1)


def upper_kernel(n_adapter, table, x_ref, w_ref, o_ref, kept_ref, x, w, sems, kept_sems):
    work = load_base(0, x.shape[0] // SEGMENT_ROWS, lax.axis_index("tensor"), x_ref, w_ref, x, w, sems)
    keeps = []
    for k in range(1, n_adapter):
        for j in range(MOST):
            start, _, _ = segment_of(table, k, j)
            keeps.append(
                pltpu.make_async_copy(
                    x_ref.at[pl.ds(start, SEGMENT_ROWS), :],
                    kept_ref.at[k - 1, j],
                    kept_sems.at[k - 1, j],
                )
            )
            keeps[-1].start()
    for at, size, terms in work:
        o_ref[at : at + size, :] = block_product(x, w, at, size, terms)
    for copy in keeps:
        copy.wait()


def upper_call(table, tokens, weight, columns, n_adapter):
    rows, width = tokens.shape
    half = UPPER * SEGMENT_ROWS
    return pl.pallas_call(
        functools.partial(upper_kernel, n_adapter),
        in_specs=[SMEM, HBM, HBM],
        out_specs=[VMEM] * 2,
        out_shape=[
            jax.ShapeDtypeStruct((half, columns), jnp.float32),
            jax.ShapeDtypeStruct((n_adapter - 1, MOST, SEGMENT_ROWS, width), jnp.bfloat16),
        ],
        scratch_shapes=base_scratch(half // SEGMENT_ROWS, width, columns)
        + [pltpu.SemaphoreType.DMA((n_adapter - 1, MOST))],
        compiler_params=params(12),
        cost_estimate=cost(2 * half * width * columns, 2 * rows * width + 2 * width * columns),
    )(table, tokens, weight)


def lower_kernel(per_device, rank, table, x_ref, w_ref, *refs):
    messages, halves, refs = refs[:per_device], refs[per_device : 2 * per_device], refs[2 * per_device :]
    coded_refs, (o_ref, s_ref, whole_ref, x, w, sems, mine, mine_sems, join_sems) = refs[:-9], refs[-9:]
    work = load_base(UPPER, x.shape[0] // SEGMENT_ROWS, lax.axis_index("tensor"), x_ref, w_ref, x, w, sems)
    joins = join_copies(halves, whole_ref, join_sems)
    loads = []
    for j in range(MOST):
        start, _, _ = segment_of(table, 0, j)
        loads.append(
            pltpu.make_async_copy(
                x_ref.at[pl.ds(start, SEGMENT_ROWS), :], mine.at[j], mine_sems.at[j]
            )
        )
        loads[-1].start()
    for at, size, terms in work:
        o_ref[at : at + size, :] = block_product(x, w, at, size, terms)
    add_decoded(o_ref, 0, coded_refs, UPPER)
    for copy in loads:
        copy.wait()
    views = views_of(messages, [0], [(per_device, 0)], rank)
    shrink_into(s_ref, 0, table, 0, lambda j: mine[j], views, rank)
    for copy in joins:
        copy.wait()


def lower_call(table, tokens, weight, messages, halves, coded, columns):
    rows, width = tokens.shape
    half = rows - UPPER * SEGMENT_ROWS
    per_device, (rank, long) = len(messages), messages[0].shape
    return pl.pallas_call(
        functools.partial(lower_kernel, per_device, rank),
        in_specs=[SMEM, HBM, HBM] + [VMEM] * (2 * per_device + len(coded)),
        out_specs=[VMEM] * 3,
        out_shape=[
            jax.ShapeDtypeStruct((half, columns), jnp.float32),
            jax.ShapeDtypeStruct((1, SEGMENT_ROWS, MOST * rank), jnp.float32),
            jax.ShapeDtypeStruct((per_device * rank, long), jnp.bfloat16),
        ],
        scratch_shapes=base_scratch(half // SEGMENT_ROWS, width, columns)
        + [
            pltpu.VMEM((MOST, SEGMENT_ROWS, width), jnp.bfloat16),
            pltpu.SemaphoreType.DMA((MOST,)),
            pltpu.SemaphoreType.DMA((per_device,)),
        ],
        compiler_params=params(14),
        cost_estimate=cost(0 * half * width * columns, 4 * rows * columns),
    )(table, tokens, weight, *messages, *halves, *coded)


def shrink_kernel(ks, rank, at, layout, table, kept_ref, *refs):
    buffers, o_ref = refs[1 if at else 0 : -1], refs[-1]
    if at:
        o_ref[:at] = refs[0][...]
    views = views_of(buffers, stages_of_all(ks), layout, rank)
    for i, k in enumerate(ks):
        shrink_into(o_ref, at + i, table, k, lambda j, k=k: kept_ref[k - 1, j], views, rank)


def shrink_call(ks, table, kept, before, buffers, layout, rank):
    width = kept.shape[3]
    at = sum(b.shape[0] for b in before)
    return pl.pallas_call(
        functools.partial(shrink_kernel, ks, rank, at, layout),
        in_specs=[SMEM] + [VMEM] * (1 + len(before) + len(buffers)),
        out_specs=VMEM,
        out_shape=jax.ShapeDtypeStruct((at + len(ks), SEGMENT_ROWS, MOST * rank), jnp.float32),
        compiler_params=params(4),
        cost_estimate=cost(
            len(ks) * MOST * 2 * SEGMENT_ROWS * width * 256, len(ks) * 4 * SEGMENT_ROWS * width
        ),
    )(table, kept, *before, *buffers)


def fetch_up(up, at, table, k, j, views, rank):
    columns = up.shape[2]
    _, _, within = segment_of(table, k, j)
    for stage, ref, first, whose, i in views:
        if stage not in stages_of(k):
            continue

        @pl.when((whose == table[k * ENTRIES]) & (within == i))
        def _(ref=ref, first=first):
            factor = ref[first : first + rank, ref.shape[1] - columns :]
            up[at, :rank, :] = factor
            up[at, rank:, :] = factor


def up_product(share, j, factor, rank):
    lane = lax.broadcasted_iota(jnp.int32, share.shape, 1)
    other = pltpu.roll(share, rank, 1)
    both = jnp.where((lane < rank) == (j == 0), share, other)
    high = both.astype(jnp.bfloat16).astype(jnp.float32)
    terms = jnp.where(lane < rank, high, both - high).astype(jnp.bfloat16)
    return jnp.dot(terms, factor, preferred_element_type=jnp.float32)


LATE = 2


def early_kernel(n_adapter, n_tensor, rank, layout, n_buffers, table, *refs):
    first = n_adapter - LATE
    upper_ref, lower_ref, refs = refs[0], refs[1], refs[2:]
    shrinks, refs = refs[: -4 - n_buffers], refs[-4 - n_buffers :]
    buffers, (o_ref, rest_ref, up, sums) = refs[:-4], refs[-4:]
    views = views_of(buffers, range(first), layout, rank)
    for k in range(first):
        for j in range(MOST):
            fetch_up(up, k * MOST + j, table, k, j, views, rank)
    shares = []
    for call in range(len(shrinks) // n_tensor):
        share = shrinks[call * n_tensor][...]
        for i in range(1, n_tensor):
            share = share + shrinks[call * n_tensor + i][...]
        shares += [share[i] for i in range(share.shape[0])]
    for k in range(n_adapter):
        for j in range(MOST):
            start, used, _ = segment_of(table, k, j)
            upper_rows = upper_ref.shape[0]

            @pl.when(start < upper_rows)
            def _(start=start):
                at = pl.multiple_of(jnp.minimum(start, upper_rows - SEGMENT_ROWS), SEGMENT_ROWS)
                sums[...] = upper_ref[pl.ds(at, SEGMENT_ROWS), :]

            @pl.when(start >= upper_rows)
            def _(start=start):
                at = pl.multiple_of(jnp.maximum(start - upper_rows, 0), SEGMENT_ROWS)
                sums[...] = lower_ref[pl.ds(at, SEGMENT_ROWS), :]

            value = sums[...]
            if k >= first:
                rest_ref[k - first, j] = value
                continue
            lora = up_product(shares[k], j, up[k * MOST + j], rank)

            @pl.when(used)
            def _(start=start, value=value, lora=lora):
                o_ref[pl.ds(start, SEGMENT_ROWS), :] = (value + adapter_scale * lora).astype(
                    jnp.bfloat16
                )


def early(n_adapter, n_tensor, table, upper, lower, shrinks, buffers, layout, rank):
    rows, columns = upper.shape[0] + lower.shape[0], upper.shape[1]
    return pl.pallas_call(
        functools.partial(early_kernel, n_adapter, n_tensor, rank, layout, len(buffers)),
        in_specs=[SMEM] + [VMEM] * (2 + len(shrinks) + len(buffers)),
        out_specs=[VMEM, VMEM],
        out_shape=[
            jax.ShapeDtypeStruct((rows, columns), jnp.bfloat16),
            jax.ShapeDtypeStruct((LATE, MOST, SEGMENT_ROWS, columns), jnp.float32),
        ],
        scratch_shapes=[
            pltpu.VMEM(((n_adapter - LATE) * MOST, 2 * rank, columns), jnp.bfloat16),
            pltpu.VMEM((SEGMENT_ROWS, columns), jnp.float32),
        ],
        compiler_params=params(16),
        cost_estimate=cost(6 * rows * rank * columns, (4 * n_tensor + 2) * rows * columns),
    )(table, upper, lower, *shrinks, *buffers)


def late_kernel(ks, n_tensor, rank, layout, table, *refs):
    rest_ref, shrinks, refs = refs[0], refs[1 : 1 + n_tensor], refs[1 + n_tensor :]
    buffers, (_, o_ref, up, out, sems) = refs[:-5], refs[-5:]
    views = views_of(buffers, stages_of_all(ks), layout, rank)
    stores = []
    for i, k in enumerate(ks):
        share = shrinks[0][i]
        for r in shrinks[1:]:
            share = share + r[i]
        for j in range(MOST):
            fetch_up(up, i * MOST + j, table, k, j, views, rank)
            start, used, _ = segment_of(table, k, j)
            lora = up_product(share, j, up[i * MOST + j], rank)
            out[i, j] = (rest_ref[i, j] + adapter_scale * lora).astype(jnp.bfloat16)
            store = pltpu.make_async_copy(
                out.at[i, j], o_ref.at[pl.ds(start, SEGMENT_ROWS), :], sems.at[i, j]
            )
            pl.when(used)(store.start)
            stores.append((used, store))
    for used, store in stores:
        pl.when(used)(store.wait)


def late(ks, n_tensor, table, rest, shrinks, buffers, value, layout, rank):
    rows, columns = value.shape
    return pl.pallas_call(
        functools.partial(late_kernel, ks, n_tensor, rank, layout),
        in_specs=[SMEM] + [VMEM] * (1 + len(shrinks) + len(buffers)) + [ANY],
        out_specs=ANY,
        out_shape=jax.ShapeDtypeStruct((rows, columns), jnp.bfloat16),
        scratch_shapes=[
            pltpu.VMEM((LATE * MOST, 2 * rank, columns), jnp.bfloat16),
            pltpu.VMEM((LATE, MOST, SEGMENT_ROWS, columns), jnp.bfloat16),
            pltpu.SemaphoreType.DMA((LATE, MOST)),
        ],
        input_output_aliases={2 + len(shrinks) + len(buffers): 0},
        compiler_params=params(8),
        cost_estimate=cost(
            6 * LATE * MOST * SEGMENT_ROWS * rank * columns,
            8 * LATE * MOST * SEGMENT_ROWS * columns,
        ),
    )(table, rest, *shrinks, *buffers, value)


def after(array, *others):
    return lax.optimization_barrier((array, *others))[0]


def on_device(
    tokens, value_weight, adapter_down_weight, adapter_up_weight, row_adapter_index, adapter_slot_of
):
    rows, width = tokens.shape
    per_device, _, rank = adapter_down_weight.shape
    n_adapter = lax.axis_size("adapter")
    n_tensor = lax.axis_size("tensor")
    columns = value_weight.shape[1] // n_tensor

    def swap_tensor(array, step):
        pairs = [(i, (i + step) % n_tensor) for i in range(n_tensor)]
        return lax.ppermute(array, "tensor", pairs)

    def along_line(array, stage):
        up = [(2 * i, 2 * (i + 1)) for i in range(stage - 1, n_adapter - 1)]
        down = [(2 * i + 1, 2 * (i - 1) + 1) for i in range(1, n_adapter - stage + 1)]
        return lax.ppermute(array, ("adapter", "dp"), up + down)

    def swap_cores(array):
        return lax.ppermute(array, "dp", [(0, 1), (1, 0)])

    down = jnp.swapaxes(adapter_down_weight, 1, 2).reshape(per_device * rank, width)
    up = adapter_up_weight.reshape(per_device * rank, value_weight.shape[1])
    tokens, value_weight, down, up = (
        pltpu.with_memory_space_constraint(a, pltpu.HBM) for a in (tokens, value_weight, down, up)
    )
    messages = message_call(down, up, columns, per_device)
    table = table_call(row_adapter_index, adapter_slot_of, n_adapter, per_device)
    last = n_adapter - 1
    buffers, shrinks = [list(messages)], []
    layout = [(per_device, 0), (per_device, 1)] + [(per_device, per_device)] * (last - 1)

    def buffers_of(stages):
        return [b for stage in stages for b in buffers[stage]]

    def shrink(ks, kept, before=()):
        mine = buffers_of(stages_of_all(ks))
        return shrink_call(ks, table, kept, list(before), mine, layout, rank)

    def add_shrink(mine):
        shrinks.extend([mine] + [swap_tensor(mine, step) for step in range(1, n_tensor)])

    others = range(1, n_tensor)

    def sent_for(step, chunks, rows):
        sizes = [number for _, number in chunks]
        return sent_call(rows, value_weight, step, n_tensor, columns, chunks[0][0], sizes)

    def send(parts, *ahead):
        return [swap_tensor(after(p, *ahead), step) for step, p in zip(others, parts)]

    held = [along_line(m, 1) for m in messages]
    part_a = [sent_for(step, CHUNKS[:1], tokens)[0] for step in others]
    sent = [send(part_a)]
    first = after(held[0], table, *part_a)
    rest_parts = [sent_for(step, CHUNKS[1:], after(tokens, first)) for step in others]
    parts = [[p[i] for p in rest_parts] for i in range(len(CHUNKS) - 1)]
    part_b = [p for group in parts for p in group]
    for stage in range(1, last):
        came = held
        if stage == 1:
            came = [first] + [after(h, *part_b) for h in held[1:]]
            sent.append(send(parts[0], *came, *sent[0]))
        if stage == 2:
            came = held[:1] + [after(h, upper) for h in held[1:]]
        held = [along_line(c, stage + 1) for c in came]
        if stage == 1:
            upper, kept = upper_call(
                after(table, held[0], *came), tokens, value_weight, columns, n_adapter
            )
        elif stage == 2:
            lower, before, joined = lower_call(
                after(table, *came), tokens, value_weight, messages, buffers[1], sent[0], columns
            )
            buffers[1] += [swap_cores(joined)]
            free = lower
            upper = add_call(1, 0, after(upper, held[0]), sent[1])
            lower = add_call(1, UPPER, after(lower, upper, *held[1:]), sent[1])
            before = shrink([1], after(kept, lower), [before])
        else:
            before = shrink([stage - 1], kept, [before])
        ahead = [free] if stage == 2 else []
        swapped = [swap_cores(after(c, *ahead)) for c in came] if stage > 1 else []
        buffers.append([*came, *swapped])
    add_shrink(before)
    value, remaining = early(
        n_adapter,
        n_tensor,
        table,
        upper,
        lower,
        shrinks,
        buffers_of(range(last - 1)),
        layout,
        rank,
    )
    buffers.append([*held, *[swap_cores(h) for h in held]])
    ks = (last - 1, last)
    add_shrink(shrink(ks, after(kept, *held)))
    return late(
        ks,
        n_tensor,
        table,
        remaining,
        shrinks[-n_tensor:],
        buffers_of(stages_of_all(ks)),
        value,
        layout,
        rank,
    )


def solution(mesh):
    return jax.shard_map(
        on_device,
        mesh=mesh,
        in_specs=(
            P(("groups", "adapter", "dp"), "tensor"),
            P("tensor", None),
            P(("groups", "adapter"), "tensor", None),
            P(("groups", "adapter"), None, None),
            P(("groups", "adapter", "dp")),
            P("groups"),
        ),
        out_specs=P(("groups", "adapter", "dp"), "tensor"),
        check_vma=False,
    )
```

```python
import functools

import jax
import jax.numpy as jnp
from jax import lax
from jax.experimental import pallas as pl
from jax.experimental.pallas import tpu as pltpu
from jax.sharding import PartitionSpec as P

SEGMENT_ROWS = 128
adapter_scale = 0.5
MOST = 2
BLOCK = 256
PIECES = 4
CHUNKS = ((6, 2), (0, 6))
UPPER = 3
ENTRIES = 8
MIDDLE = 1.5 * 2.0**23


def cost(flops, moved):
    return pl.CostEstimate(flops=int(flops), bytes_accessed=int(moved), transcendentals=0)


def params(mib):
    return pltpu.CompilerParams(vmem_limit_bytes=mib * 2**20)


ANY = pl.BlockSpec(memory_space=pl.ANY)
HBM = pl.BlockSpec(memory_space=pltpu.HBM)
SMEM = pl.BlockSpec(memory_space=pltpu.SMEM)
VMEM = pl.BlockSpec(memory_space=pltpu.VMEM)


def arrival_order(me, n_adapter):
    order = [me] + [jnp.int32(-1)] * (n_adapter - 1)
    count = jnp.int32(1)
    for distance in range(1, n_adapter):
        for other in (me - distance, me + distance):
            valid = (other >= 0) & (other < n_adapter)
            order = [jnp.where(valid & (count == k), other, o) for k, o in enumerate(order)]
            count = count + valid.astype(jnp.int32)
    return order


def views_of(refs, stages, layout, rank):
    me, core = lax.axis_index("adapter"), lax.axis_index("dp")
    refs, views = list(refs), []
    for stage in stages:
        came, swapped = layout[stage]
        toward = jnp.where(core == 0, -stage, stage)
        for i in range(came):
            views.append((stage, refs.pop(0), 0, me + toward if stage > 0 else me, i))
        for i in range(swapped):
            ref = refs.pop(0)
            for part in range(came // swapped):
                views.append((stage, ref, part * rank, me - toward, i + part))
    return views


def segment_of(table, k, j):
    seg = table[k * ENTRIES + 1 + 2 * j]
    start = pl.multiple_of(jnp.maximum(seg, 0) * SEGMENT_ROWS, SEGMENT_ROWS)
    return start, seg >= 0, table[k * ENTRIES + 2 + 2 * j]


def message_kernel(down_ref, up_ref, *refs):
    outs, sems = refs[:-1], refs[-1]
    rank = outs[0].shape[0]
    width = down_ref.shape[1]
    columns = outs[0].shape[1] - width
    start = pl.multiple_of(lax.axis_index("tensor") * columns, columns)
    copies = []
    for i, out in enumerate(outs):
        rows = pl.ds(i * rank, rank)
        copies += [
            pltpu.make_async_copy(down_ref.at[rows, :], out.at[:, pl.ds(0, width)], sems.at[0, i]),
            pltpu.make_async_copy(
                up_ref.at[rows, pl.ds(start, columns)], out.at[:, pl.ds(width, columns)], sems.at[1, i]
            ),
        ]
    for copy in copies:
        copy.start()
    for copy in copies:
        copy.wait()


def message_call(down, up, columns, per_device):
    rows, width = down.shape
    shape = jax.ShapeDtypeStruct((rows // per_device, width + columns), jnp.bfloat16)
    return pl.pallas_call(
        message_kernel,
        in_specs=[HBM, HBM],
        out_specs=[VMEM] * per_device,
        out_shape=[shape] * per_device,
        scratch_shapes=[pltpu.SemaphoreType.DMA((2, per_device))],
        compiler_params=params(8),
        cost_estimate=cost(0, 4 * rows * (width + columns)),
    )(down, up)


def table_kernel(n_adapter, per_device, ids, slots, table):
    seg_dev = ids.shape[0] // SEGMENT_ROWS
    used = [slots[ids[s * SEGMENT_ROWS]] for s in range(seg_dev)]
    for k, owner in enumerate(arrival_order(lax.axis_index("adapter"), n_adapter)):
        table[k * ENTRIES] = owner
        found, place = [jnp.int32(-1)] * MOST, [jnp.int32(0)] * MOST
        count = jnp.int32(0)
        for s, slot in enumerate(used):
            within = slot - owner * per_device
            hit = (within >= 0) & (within < per_device)
            for j in range(MOST):
                take = hit & (count == j)
                found[j] = jnp.where(take, s, found[j])
                place[j] = jnp.where(take, within, place[j])
            count = count + hit.astype(jnp.int32)
        for j in range(MOST):
            table[k * ENTRIES + 1 + 2 * j] = found[j]
            table[k * ENTRIES + 2 + 2 * j] = place[j]


def table_call(ids, slots, n_adapter, per_device):
    return pl.pallas_call(
        functools.partial(table_kernel, n_adapter, per_device),
        in_specs=[SMEM, SMEM],
        out_specs=SMEM,
        out_shape=jax.ShapeDtypeStruct((n_adapter * ENTRIES,), jnp.int32),
        cost_estimate=cost(0, 4 * ids.shape[0]),
    )(ids, slots)


def diagonal():
    shape = (SEGMENT_ROWS, SEGMENT_ROWS)
    return lax.broadcasted_iota(jnp.int32, shape, 0) == lax.broadcasted_iota(jnp.int32, shape, 1)


GROUP = SEGMENT_ROWS // 8
WORDS = 5 * GROUP


def coded_rows(segments):
    return segments * WORDS + 8


def encode(values, o_ref, unit, units):
    largest = jnp.maximum(jnp.max(jnp.abs(values), axis=1, keepdims=True), 2.0**-100)
    power = jnp.floor(jnp.log2(largest))
    whole = (values * jnp.exp2(18.0 - power) + MIDDLE).astype(jnp.int32) - int(MIDDLE)
    whole = jnp.clip(whole, -(2**19), 2**19 - 1)
    v = [whole[i * GROUP : (i + 1) * GROUP] for i in range(8)]
    over = [
        v[5] & 0xFFF,
        ((v[5] >> 12) & 0xFF) | ((v[6] & 0xF) << 8),
        (v[6] >> 4) & 0xFFF,
        ((v[6] >> 16) & 0xF) | ((v[7] & 0xFF) << 4),
        v[7] >> 8,
    ]
    for i in range(5):
        o_ref[unit * WORDS + i * GROUP : unit * WORDS + (i + 1) * GROUP, :] = (v[i] & 0xFFFFF) | (
            over[i] << 20
        )
    row = jnp.sum(jnp.where(diagonal(), power, 0.0), axis=0, keepdims=True)
    o_ref[units * WORDS + unit : units * WORDS + unit + 1, :SEGMENT_ROWS] = row.astype(jnp.int32)


def decode(ref, unit, units):
    w = [ref[unit * WORDS + i * GROUP : unit * WORDS + (i + 1) * GROUP, :] for i in range(5)]
    v = [(x << 12) >> 12 for x in w]
    v.append(((w[0] >> 20) & 0xFFF) | (((w[1] << 4) >> 24) << 12))
    v.append(((w[1] >> 28) & 0xF) | (((w[2] >> 20) & 0xFFF) << 4) | (((w[3] << 8) >> 28) << 16))
    v.append(((w[3] >> 24) & 0xFF) | ((w[4] >> 20) << 8))
    row = ref[units * WORDS + unit : units * WORDS + unit + 1, :SEGMENT_ROWS].astype(jnp.float32)
    power = jnp.sum(jnp.where(diagonal(), row, 0.0), axis=1, keepdims=True)
    return jnp.concatenate(v, axis=0).astype(jnp.float32) * jnp.exp2(power - 18.0)


def add_decoded(sums, chunk, refs, above):
    first, number = CHUNKS[chunk]
    for unit in range(number):
        at = first + unit - above
        if at < 0 or at >= sums.shape[0] // SEGMENT_ROWS:
            continue
        rows = pl.ds(at * SEGMENT_ROWS, SEGMENT_ROWS)
        value = sums[rows, :]
        for ref in refs:
            value = value + decode(ref, unit, number)
        sums[rows, :] = value


def load_base(first, segments, column, x_ref, w_ref, x, w, sems):
    width, columns = w.shape
    rows = segments * SEGMENT_ROWS
    start = pl.multiple_of(column * columns, columns)
    depth = width // PIECES
    blocks = [(r, min(BLOCK, rows - r)) for r in range(0, rows, BLOCK)]

    def x_copy(at, size, features, sem):
        return pltpu.make_async_copy(
            x_ref.at[pl.ds(first * SEGMENT_ROWS + at, size), features],
            x.at[pl.ds(at, size), features],
            sem,
        )

    work = []
    for i, (at, size) in enumerate(blocks):
        terms = []
        if i == 0:
            for p in range(PIECES):
                features = pl.ds(p * depth, depth)
                copies = (
                    pltpu.make_async_copy(
                        w_ref.at[features, pl.ds(start, columns)], w.at[features, :], sems.at[0, p]
                    ),
                    x_copy(0, size, features, sems.at[1, p]),
                )
                terms.append((copies, slice(p * depth, (p + 1) * depth)))
        else:
            terms.append(((x_copy(at, size, slice(None), sems.at[2, i]),), slice(None)))
        work.append((at, size, terms))
    for _, _, terms in work:
        for copies, _ in terms:
            for copy in copies:
                copy.start()
    return work


def block_product(x, w, at, size, terms):
    total = None
    for copies, features in terms:
        for copy in copies:
            copy.wait()
        term = jnp.dot(
            x[at : at + size, features], w[features, :], preferred_element_type=jnp.float32
        )
        total = term if total is None else total + term
    return total


def base_scratch(segments, width, columns):
    rows = segments * SEGMENT_ROWS
    return [
        pltpu.VMEM((rows, width), jnp.bfloat16),
        pltpu.VMEM((width, columns), jnp.bfloat16),
        pltpu.SemaphoreType.DMA((3, max(PIECES, rows // BLOCK + 1))),
    ]


def sent_kernel(first, sizes, step, n_tensor, x_ref, w_ref, *refs):
    outs, (x, w, sems) = refs[: len(sizes)], refs[len(sizes) :]
    column = lax.rem(lax.axis_index("tensor") + step, n_tensor)
    work = load_base(first, sum(sizes), column, x_ref, w_ref, x, w, sems)
    unit_of = [(out, unit) for out, size in enumerate(sizes) for unit in range(size)]
    for out, size in zip(outs, sizes):
        out[size * WORDS :, :] = jnp.zeros((8, w.shape[1]), jnp.int32)
    for at, size, terms in work:
        product = block_product(x, w, at, size, terms)
        for r in range(0, size, SEGMENT_ROWS):
            out, unit = unit_of[(at + r) // SEGMENT_ROWS]
            encode(product[r : r + SEGMENT_ROWS], outs[out], unit, sizes[out])


def sent_call(tokens, weight, step, n_tensor, columns, first, sizes):
    width = tokens.shape[1]
    rows = sum(sizes) * SEGMENT_ROWS
    return pl.pallas_call(
        functools.partial(sent_kernel, first, sizes, step, n_tensor),
        in_specs=[HBM, HBM],
        out_specs=[VMEM] * len(sizes),
        out_shape=[jax.ShapeDtypeStruct((coded_rows(n), columns), jnp.int32) for n in sizes],
        scratch_shapes=base_scratch(sum(sizes), width, columns),
        compiler_params=params(16),
        cost_estimate=cost(
            2 * rows * width * columns, 2 * rows * width + 2 * width * columns + 4 * rows * columns
        ),
    )(tokens, weight)


def add_kernel(chunk, above, sums_ref, *refs):
    coded_refs, o_ref = refs[:-1], refs[-1]
    o_ref[...] = sums_ref[...]
    add_decoded(o_ref, chunk, coded_refs, above)


def add_call(chunk, above, sums, coded):
    return pl.pallas_call(
        functools.partial(add_kernel, chunk, above),
        in_specs=[VMEM] * (1 + len(coded)),
        out_specs=VMEM,
        out_shape=jax.ShapeDtypeStruct(sums.shape, sums.dtype),
        compiler_params=params(8),
        cost_estimate=cost(40000 * sums.size, 12 * sums.size),
    )(sums, *coded)


def shrink_into(o_ref, at, table, k, rows_of, views, rank, pair):
    def one(j, carry):
        _, _, within = segment_of(table, k, j)
        for stage, ref, first, whose, i in views:
            if stage not in stages_of(k):
                continue

            @pl.when((whose == table[k * ENTRIES]) & (within == i))
            def _(ref=ref, first=first):
                rows = rows_of(j)
                pair[j] = lax.dot_general(
                    rows,
                    ref[first : first + rank, : rows.shape[1]],
                    (((1,), (1,)), ((), ())),
                    preferred_element_type=jnp.float32,
                )

        return carry

    lax.fori_loop(0, MOST, one, 0)
    for j in range(MOST):
        o_ref[at, :, j * rank : (j + 1) * rank] = pair[j]


def join_copies(halves, whole, sems):
    copies, rank = [], halves[0].shape[0]
    for i, half in enumerate(halves):
        copies.append(
            pltpu.make_async_copy(half, whole.at[pl.ds(i * rank, rank), :], sems.at[i])
        )
        copies[-1].start()
    return copies


def stages_of(k):
    return range((k + 1) // 2, k + 1)


def stages_of_all(ks):
    return range(stages_of(ks[0])[0], ks[-1] + 1)


def upper_kernel(n_adapter, table, x_ref, w_ref, o_ref, kept_ref, x, w, sems, kept_sems):
    work = load_base(0, x.shape[0] // SEGMENT_ROWS, lax.axis_index("tensor"), x_ref, w_ref, x, w, sems)
    keeps = []
    for k in range(1, n_adapter):
        for j in range(MOST):
            start, _, _ = segment_of(table, k, j)
            keeps.append(
                pltpu.make_async_copy(
                    x_ref.at[pl.ds(start, SEGMENT_ROWS), :],
                    kept_ref.at[k - 1, j],
                    kept_sems.at[k - 1, j],
                )
            )
            keeps[-1].start()
    for at, size, terms in work:
        o_ref[at : at + size, :] = block_product(x, w, at, size, terms)
    for copy in keeps:
        copy.wait()


def upper_call(table, tokens, weight, columns, n_adapter):
    rows, width = tokens.shape
    half = UPPER * SEGMENT_ROWS
    return pl.pallas_call(
        functools.partial(upper_kernel, n_adapter),
        in_specs=[SMEM, HBM, HBM],
        out_specs=[VMEM] * 2,
        out_shape=[
            jax.ShapeDtypeStruct((half, columns), jnp.float32),
            jax.ShapeDtypeStruct((n_adapter - 1, MOST, SEGMENT_ROWS, width), jnp.bfloat16),
        ],
        scratch_shapes=base_scratch(half // SEGMENT_ROWS, width, columns)
        + [pltpu.SemaphoreType.DMA((n_adapter - 1, MOST))],
        compiler_params=params(12),
        cost_estimate=cost(2 * half * width * columns, 2 * rows * width + 2 * width * columns),
    )(table, tokens, weight)


def lower_kernel(per_device, rank, table, x_ref, w_ref, *refs):
    messages, halves, refs = refs[:per_device], refs[per_device : 2 * per_device], refs[2 * per_device :]
    coded_refs, (o_ref, s_ref, whole_ref, x, w, sems, mine, mine_sems, join_sems, pair) = refs[:-10], refs[-10:]
    work = load_base(UPPER, x.shape[0] // SEGMENT_ROWS, lax.axis_index("tensor"), x_ref, w_ref, x, w, sems)
    joins = join_copies(halves, whole_ref, join_sems)
    loads = []
    for j in range(MOST):
        start, _, _ = segment_of(table, 0, j)
        loads.append(
            pltpu.make_async_copy(
                x_ref.at[pl.ds(start, SEGMENT_ROWS), :], mine.at[j], mine_sems.at[j]
            )
        )
        loads[-1].start()
    for at, size, terms in work:
        o_ref[at : at + size, :] = block_product(x, w, at, size, terms)
    add_decoded(o_ref, 0, coded_refs, UPPER)
    for copy in loads:
        copy.wait()
    views = views_of(messages, [0], [(per_device, 0)], rank)
    shrink_into(s_ref, 0, table, 0, lambda j: mine[j], views, rank, pair)
    for copy in joins:
        copy.wait()


def lower_call(table, tokens, weight, messages, halves, coded, columns):
    rows, width = tokens.shape
    half = rows - UPPER * SEGMENT_ROWS
    per_device, (rank, long) = len(messages), messages[0].shape
    return pl.pallas_call(
        functools.partial(lower_kernel, per_device, rank),
        in_specs=[SMEM, HBM, HBM] + [VMEM] * (2 * per_device + len(coded)),
        out_specs=[VMEM] * 3,
        out_shape=[
            jax.ShapeDtypeStruct((half, columns), jnp.float32),
            jax.ShapeDtypeStruct((1, SEGMENT_ROWS, MOST * rank), jnp.float32),
            jax.ShapeDtypeStruct((per_device * rank, long), jnp.bfloat16),
        ],
        scratch_shapes=base_scratch(half // SEGMENT_ROWS, width, columns)
        + [
            pltpu.VMEM((MOST, SEGMENT_ROWS, width), jnp.bfloat16),
            pltpu.SemaphoreType.DMA((MOST,)),
            pltpu.SemaphoreType.DMA((per_device,)),
            pltpu.VMEM((MOST, SEGMENT_ROWS, rank), jnp.float32),
        ],
        compiler_params=params(14),
        cost_estimate=cost(0 * half * width * columns, 4 * rows * columns),
    )(table, tokens, weight, *messages, *halves, *coded)


def shrink_kernel(ks, rank, at, layout, table, kept_ref, *refs):
    buffers, (o_ref, pair) = refs[1 if at else 0 : -2], refs[-2:]
    if at:
        o_ref[:at] = refs[0][...]
    views = views_of(buffers, stages_of_all(ks), layout, rank)
    for i, k in enumerate(ks):
        shrink_into(o_ref, at + i, table, k, lambda j, k=k: kept_ref[k - 1, j], views, rank, pair)


def shrink_call(ks, table, kept, before, buffers, layout, rank):
    width = kept.shape[3]
    at = sum(b.shape[0] for b in before)
    return pl.pallas_call(
        functools.partial(shrink_kernel, ks, rank, at, layout),
        in_specs=[SMEM] + [VMEM] * (1 + len(before) + len(buffers)),
        out_specs=VMEM,
        out_shape=jax.ShapeDtypeStruct((at + len(ks), SEGMENT_ROWS, MOST * rank), jnp.float32),
        scratch_shapes=[pltpu.VMEM((MOST, SEGMENT_ROWS, rank), jnp.float32)],
        compiler_params=params(4),
        cost_estimate=cost(
            len(ks) * MOST * 2 * SEGMENT_ROWS * width * 256, len(ks) * 4 * SEGMENT_ROWS * width
        ),
    )(table, kept, *before, *buffers)


def fetch_up(up, at, table, k, j, views, rank):
    columns = up.shape[2]
    _, _, within = segment_of(table, k, j)
    for stage, ref, first, whose, i in views:
        if stage not in stages_of(k):
            continue

        @pl.when((whose == table[k * ENTRIES]) & (within == i))
        def _(ref=ref, first=first):
            factor = ref[first : first + rank, ref.shape[1] - columns :]
            up[at, :rank, :] = factor
            up[at, rank:, :] = factor


def up_product(share, j, factor, rank):
    lane = lax.broadcasted_iota(jnp.int32, share.shape, 1)
    other = pltpu.roll(share, rank, 1)
    both = jnp.where((lane < rank) == (j == 0), share, other)
    high = both.astype(jnp.bfloat16).astype(jnp.float32)
    terms = jnp.where(lane < rank, high, both - high).astype(jnp.bfloat16)
    return jnp.dot(terms, factor, preferred_element_type=jnp.float32)


LATE = 2


def early_kernel(n_adapter, n_tensor, rank, layout, n_buffers, table, *refs):
    first = n_adapter - LATE
    upper_ref, lower_ref, refs = refs[0], refs[1], refs[2:]
    shrinks, refs = refs[: -4 - n_buffers], refs[-4 - n_buffers :]
    buffers, (o_ref, rest_ref, up, sums) = refs[:-4], refs[-4:]
    views = views_of(buffers, range(first), layout, rank)
    for k in range(first):
        for j in range(MOST):
            fetch_up(up, k * MOST + j, table, k, j, views, rank)
    shares = []
    for call in range(len(shrinks) // n_tensor):
        share = shrinks[call * n_tensor][...]
        for i in range(1, n_tensor):
            share = share + shrinks[call * n_tensor + i][...]
        shares += [share[i] for i in range(share.shape[0])]
    for k in range(n_adapter):
        for j in range(MOST):
            start, used, _ = segment_of(table, k, j)
            upper_rows = upper_ref.shape[0]

            @pl.when(start < upper_rows)
            def _(start=start):
                at = pl.multiple_of(jnp.minimum(start, upper_rows - SEGMENT_ROWS), SEGMENT_ROWS)
                sums[...] = upper_ref[pl.ds(at, SEGMENT_ROWS), :]

            @pl.when(start >= upper_rows)
            def _(start=start):
                at = pl.multiple_of(jnp.maximum(start - upper_rows, 0), SEGMENT_ROWS)
                sums[...] = lower_ref[pl.ds(at, SEGMENT_ROWS), :]

            value = sums[...]
            if k >= first:
                rest_ref[k - first, j] = value
                continue
            lora = up_product(shares[k], j, up[k * MOST + j], rank)

            @pl.when(used)
            def _(start=start, value=value, lora=lora):
                o_ref[pl.ds(start, SEGMENT_ROWS), :] = (value + adapter_scale * lora).astype(
                    jnp.bfloat16
                )


def early(n_adapter, n_tensor, table, upper, lower, shrinks, buffers, layout, rank):
    rows, columns = upper.shape[0] + lower.shape[0], upper.shape[1]
    return pl.pallas_call(
        functools.partial(early_kernel, n_adapter, n_tensor, rank, layout, len(buffers)),
        in_specs=[SMEM] + [VMEM] * (2 + len(shrinks) + len(buffers)),
        out_specs=[VMEM, VMEM],
        out_shape=[
            jax.ShapeDtypeStruct((rows, columns), jnp.bfloat16),
            jax.ShapeDtypeStruct((LATE, MOST, SEGMENT_ROWS, columns), jnp.float32),
        ],
        scratch_shapes=[
            pltpu.VMEM(((n_adapter - LATE) * MOST, 2 * rank, columns), jnp.bfloat16),
            pltpu.VMEM((SEGMENT_ROWS, columns), jnp.float32),
        ],
        compiler_params=params(16),
        cost_estimate=cost(6 * rows * rank * columns, (4 * n_tensor + 2) * rows * columns),
    )(table, upper, lower, *shrinks, *buffers)


def late_kernel(ks, n_tensor, rank, layout, table, *refs):
    rest_ref, shrinks, refs = refs[0], refs[1 : 1 + n_tensor], refs[1 + n_tensor :]
    buffers, (_, o_ref, up, out, sems) = refs[:-5], refs[-5:]
    views = views_of(buffers, stages_of_all(ks), layout, rank)
    stores = []
    for i, k in enumerate(ks):
        share = shrinks[0][i]
        for r in shrinks[1:]:
            share = share + r[i]
        for j in range(MOST):
            fetch_up(up, i * MOST + j, table, k, j, views, rank)
            start, used, _ = segment_of(table, k, j)
            lora = up_product(share, j, up[i * MOST + j], rank)
            out[i, j] = (rest_ref[i, j] + adapter_scale * lora).astype(jnp.bfloat16)
            store = pltpu.make_async_copy(
                out.at[i, j], o_ref.at[pl.ds(start, SEGMENT_ROWS), :], sems.at[i, j]
            )
            pl.when(used)(store.start)
            stores.append((used, store))
    for used, store in stores:
        pl.when(used)(store.wait)


def late(ks, n_tensor, table, rest, shrinks, buffers, value, layout, rank):
    rows, columns = value.shape
    return pl.pallas_call(
        functools.partial(late_kernel, ks, n_tensor, rank, layout),
        in_specs=[SMEM] + [VMEM] * (1 + len(shrinks) + len(buffers)) + [ANY],
        out_specs=ANY,
        out_shape=jax.ShapeDtypeStruct((rows, columns), jnp.bfloat16),
        scratch_shapes=[
            pltpu.VMEM((LATE * MOST, 2 * rank, columns), jnp.bfloat16),
            pltpu.VMEM((LATE, MOST, SEGMENT_ROWS, columns), jnp.bfloat16),
            pltpu.SemaphoreType.DMA((LATE, MOST)),
        ],
        input_output_aliases={2 + len(shrinks) + len(buffers): 0},
        compiler_params=params(8),
        cost_estimate=cost(
            6 * LATE * MOST * SEGMENT_ROWS * rank * columns,
            8 * LATE * MOST * SEGMENT_ROWS * columns,
        ),
    )(table, rest, *shrinks, *buffers, value)


def after(array, *others):
    return lax.optimization_barrier((array, *others))[0]


def on_device(
    tokens, value_weight, adapter_down_weight, adapter_up_weight, row_adapter_index, adapter_slot_of
):
    rows, width = tokens.shape
    per_device, _, rank = adapter_down_weight.shape
    n_adapter = lax.axis_size("adapter")
    n_tensor = lax.axis_size("tensor")
    columns = value_weight.shape[1] // n_tensor

    def swap_tensor(array, step):
        pairs = [(i, (i + step) % n_tensor) for i in range(n_tensor)]
        return lax.ppermute(array, "tensor", pairs)

    def along_line(array, stage):
        up = [(2 * i, 2 * (i + 1)) for i in range(stage - 1, n_adapter - 1)]
        down = [(2 * i + 1, 2 * (i - 1) + 1) for i in range(1, n_adapter - stage + 1)]
        return lax.ppermute(array, ("adapter", "dp"), up + down)

    def swap_cores(array):
        return lax.ppermute(array, "dp", [(0, 1), (1, 0)])

    down = jnp.swapaxes(adapter_down_weight, 1, 2).reshape(per_device * rank, width)
    up = adapter_up_weight.reshape(per_device * rank, value_weight.shape[1])
    tokens, value_weight, down, up = (
        pltpu.with_memory_space_constraint(a, pltpu.HBM) for a in (tokens, value_weight, down, up)
    )
    messages = message_call(down, up, columns, per_device)
    table = table_call(row_adapter_index, adapter_slot_of, n_adapter, per_device)
    last = n_adapter - 1
    buffers, shrinks = [list(messages)], []
    layout = [(per_device, 0), (per_device, 1)] + [(per_device, per_device)] * (last - 1)

    def buffers_of(stages):
        return [b for stage in stages for b in buffers[stage]]

    def shrink(ks, kept, before=()):
        mine = buffers_of(stages_of_all(ks))
        return shrink_call(ks, table, kept, list(before), mine, layout, rank)

    def add_shrink(mine):
        shrinks.extend([mine] + [swap_tensor(mine, step) for step in range(1, n_tensor)])

    others = range(1, n_tensor)

    def sent_for(step, chunks, rows):
        sizes = [number for _, number in chunks]
        return sent_call(rows, value_weight, step, n_tensor, columns, chunks[0][0], sizes)

    def send(parts, *ahead):
        return [swap_tensor(after(p, *ahead), step) for step, p in zip(others, parts)]

    held = [along_line(m, 1) for m in messages]
    part_a = [sent_for(step, CHUNKS[:1], tokens)[0] for step in others]
    sent = [send(part_a)]
    first = after(held[0], table, *part_a)
    rest_parts = [sent_for(step, CHUNKS[1:], after(tokens, first)) for step in others]
    parts = [[p[i] for p in rest_parts] for i in range(len(CHUNKS) - 1)]
    part_b = [p for group in parts for p in group]
    for stage in range(1, last):
        came = held
        if stage == 1:
            came = [first] + [after(h, *part_b) for h in held[1:]]
            sent.append(send(parts[0], *came, *sent[0]))
        if stage == 2:
            came = held[:1] + [after(h, upper) for h in held[1:]]
        held = [along_line(c, stage + 1) for c in came]
        if stage == 1:
            upper, kept = upper_call(
                after(table, held[0], *came), tokens, value_weight, columns, n_adapter
            )
        elif stage == 2:
            lower, before, joined = lower_call(
                after(table, *came), tokens, value_weight, messages, buffers[1], sent[0], columns
            )
            buffers[1] += [swap_cores(joined)]
            free = lower
            upper = add_call(1, 0, after(upper, held[0]), sent[1])
            lower = add_call(1, UPPER, after(lower, upper, *held[1:]), sent[1])
            before = shrink([1], after(kept, lower), [before])
        else:
            before = shrink([stage - 1], kept, [before])
        ahead = [free] if stage == 2 else []
        swapped = [swap_cores(after(c, *ahead)) for c in came] if stage > 1 else []
        buffers.append([*came, *swapped])
    add_shrink(before)
    value, remaining = early(
        n_adapter,
        n_tensor,
        table,
        upper,
        lower,
        shrinks,
        buffers_of(range(last - 1)),
        layout,
        rank,
    )
    buffers.append([*held, *[swap_cores(h) for h in held]])
    ks = (last - 1, last)
    add_shrink(shrink(ks, after(kept, *held)))
    return late(
        ks,
        n_tensor,
        table,
        remaining,
        shrinks[-n_tensor:],
        buffers_of(stages_of_all(ks)),
        value,
        layout,
        rank,
    )


def solution(mesh):
    return jax.shard_map(
        on_device,
        mesh=mesh,
        in_specs=(
            P(("groups", "adapter", "dp"), "tensor"),
            P("tensor", None),
            P(("groups", "adapter"), "tensor", None),
            P(("groups", "adapter"), None, None),
            P(("groups", "adapter", "dp")),
            P("groups"),
        ),
        out_specs=P(("groups", "adapter", "dp"), "tensor"),
        check_vma=False,
    )
```

```python
import functools

import jax
import jax.numpy as jnp
from jax import lax
from jax.experimental import pallas as pl
from jax.experimental.pallas import tpu as pltpu
from jax.sharding import PartitionSpec as P

SEGMENT_ROWS = 128
adapter_scale = 0.5
MOST = 2
BLOCK = 256
PIECES = 4
CHUNKS = ((6, 2), (0, 6))
UPPER = 3
ENTRIES = 8
MIDDLE = 1.5 * 2.0**23


def cost(flops, moved):
    return pl.CostEstimate(flops=int(flops), bytes_accessed=int(moved), transcendentals=0)


def params(mib):
    return pltpu.CompilerParams(vmem_limit_bytes=mib * 2**20)


ANY = pl.BlockSpec(memory_space=pl.ANY)
HBM = pl.BlockSpec(memory_space=pltpu.HBM)
SMEM = pl.BlockSpec(memory_space=pltpu.SMEM)
VMEM = pl.BlockSpec(memory_space=pltpu.VMEM)


def arrival_order(me, n_adapter):
    order = [me] + [jnp.int32(-1)] * (n_adapter - 1)
    count = jnp.int32(1)
    for distance in range(1, n_adapter):
        for other in (me - distance, me + distance):
            valid = (other >= 0) & (other < n_adapter)
            order = [jnp.where(valid & (count == k), other, o) for k, o in enumerate(order)]
            count = count + valid.astype(jnp.int32)
    return order


def views_of(refs, stages, layout, rank):
    me, core = lax.axis_index("adapter"), lax.axis_index("dp")
    refs, views = list(refs), []
    for stage in stages:
        came, swapped = layout[stage]
        toward = jnp.where(core == 0, -stage, stage)
        for i in range(came):
            views.append((stage, refs.pop(0), 0, me + toward if stage > 0 else me, i))
        for i in range(swapped):
            ref = refs.pop(0)
            for part in range(came // swapped):
                views.append((stage, ref, part * rank, me - toward, i + part))
    return views


def segment_of(table, k, j):
    seg = table[k * ENTRIES + 1 + 2 * j]
    start = pl.multiple_of(jnp.maximum(seg, 0) * SEGMENT_ROWS, SEGMENT_ROWS)
    return start, seg >= 0, table[k * ENTRIES + 2 + 2 * j]


def message_kernel(down_ref, up_ref, *refs):
    outs, sems = refs[:-1], refs[-1]
    rank = outs[0].shape[0]
    width = down_ref.shape[1]
    columns = outs[0].shape[1] - width
    start = pl.multiple_of(lax.axis_index("tensor") * columns, columns)
    copies = []
    for i, out in enumerate(outs):
        rows = pl.ds(i * rank, rank)
        copies += [
            pltpu.make_async_copy(down_ref.at[rows, :], out.at[:, pl.ds(0, width)], sems.at[0, i]),
            pltpu.make_async_copy(
                up_ref.at[rows, pl.ds(start, columns)], out.at[:, pl.ds(width, columns)], sems.at[1, i]
            ),
        ]
    for copy in copies:
        copy.start()
    for copy in copies:
        copy.wait()


def message_call(down, up, columns, per_device):
    rows, width = down.shape
    shape = jax.ShapeDtypeStruct((rows // per_device, width + columns), jnp.bfloat16)
    return pl.pallas_call(
        message_kernel,
        in_specs=[HBM, HBM],
        out_specs=[VMEM] * per_device,
        out_shape=[shape] * per_device,
        scratch_shapes=[pltpu.SemaphoreType.DMA((2, per_device))],
        compiler_params=params(8),
        cost_estimate=cost(0, 4 * rows * (width + columns)),
    )(down, up)


def table_kernel(n_adapter, per_device, ids, slots, table):
    seg_dev = ids.shape[0] // SEGMENT_ROWS
    used = [slots[ids[s * SEGMENT_ROWS]] for s in range(seg_dev)]
    for k, owner in enumerate(arrival_order(lax.axis_index("adapter"), n_adapter)):
        table[k * ENTRIES] = owner
        found, place = [jnp.int32(-1)] * MOST, [jnp.int32(0)] * MOST
        count = jnp.int32(0)
        for s, slot in enumerate(used):
            within = slot - owner * per_device
            hit = (within >= 0) & (within < per_device)
            for j in range(MOST):
                take = hit & (count == j)
                found[j] = jnp.where(take, s, found[j])
                place[j] = jnp.where(take, within, place[j])
            count = count + hit.astype(jnp.int32)
        for j in range(MOST):
            table[k * ENTRIES + 1 + 2 * j] = found[j]
            table[k * ENTRIES + 2 + 2 * j] = place[j]


def table_call(ids, slots, n_adapter, per_device):
    return pl.pallas_call(
        functools.partial(table_kernel, n_adapter, per_device),
        in_specs=[SMEM, SMEM],
        out_specs=SMEM,
        out_shape=jax.ShapeDtypeStruct((n_adapter * ENTRIES,), jnp.int32),
        cost_estimate=cost(0, 4 * ids.shape[0]),
    )(ids, slots)


def diagonal():
    shape = (SEGMENT_ROWS, SEGMENT_ROWS)
    return lax.broadcasted_iota(jnp.int32, shape, 0) == lax.broadcasted_iota(jnp.int32, shape, 1)


GROUP = SEGMENT_ROWS // 8
WORDS = 5 * GROUP


def coded_rows(segments):
    return segments * WORDS + 8


def encode(values, o_ref, unit, units):
    largest = jnp.maximum(jnp.max(jnp.abs(values), axis=1, keepdims=True), 2.0**-100)
    power = jnp.floor(jnp.log2(largest))
    whole = (values * jnp.exp2(18.0 - power) + MIDDLE).astype(jnp.int32) - int(MIDDLE)
    whole = jnp.clip(whole, -(2**19), 2**19 - 1)
    v = [whole[i * GROUP : (i + 1) * GROUP] for i in range(8)]
    over = [
        v[5] & 0xFFF,
        ((v[5] >> 12) & 0xFF) | ((v[6] & 0xF) << 8),
        (v[6] >> 4) & 0xFFF,
        ((v[6] >> 16) & 0xF) | ((v[7] & 0xFF) << 4),
        v[7] >> 8,
    ]
    for i in range(5):
        o_ref[unit * WORDS + i * GROUP : unit * WORDS + (i + 1) * GROUP, :] = (v[i] & 0xFFFFF) | (
            over[i] << 20
        )
    row = jnp.sum(jnp.where(diagonal(), power, 0.0), axis=0, keepdims=True)
    o_ref[units * WORDS + unit : units * WORDS + unit + 1, :SEGMENT_ROWS] = row.astype(jnp.int32)


def decode(ref, unit, units):
    w = [ref[unit * WORDS + i * GROUP : unit * WORDS + (i + 1) * GROUP, :] for i in range(5)]
    v = [(x << 12) >> 12 for x in w]
    v.append(((w[0] >> 20) & 0xFFF) | (((w[1] << 4) >> 24) << 12))
    v.append(((w[1] >> 28) & 0xF) | (((w[2] >> 20) & 0xFFF) << 4) | (((w[3] << 8) >> 28) << 16))
    v.append(((w[3] >> 24) & 0xFF) | ((w[4] >> 20) << 8))
    row = ref[units * WORDS + unit : units * WORDS + unit + 1, :SEGMENT_ROWS].astype(jnp.float32)
    power = jnp.sum(jnp.where(diagonal(), row, 0.0), axis=1, keepdims=True)
    return jnp.concatenate(v, axis=0).astype(jnp.float32) * jnp.exp2(power - 18.0)


def add_decoded(sums, chunk, refs, above):
    first, number = CHUNKS[chunk]
    for unit in range(number):
        at = first + unit - above
        if at < 0 or at >= sums.shape[0] // SEGMENT_ROWS:
            continue
        rows = pl.ds(at * SEGMENT_ROWS, SEGMENT_ROWS)
        value = sums[rows, :]
        for ref in refs:
            value = value + decode(ref, unit, number)
        sums[rows, :] = value


def load_base(first, segments, column, x_ref, w_ref, x, w, sems):
    width, columns = w.shape
    rows = segments * SEGMENT_ROWS
    start = pl.multiple_of(column * columns, columns)
    depth = width // PIECES
    blocks = [(r, min(BLOCK, rows - r)) for r in range(0, rows, BLOCK)]

    def x_copy(at, size, features, sem):
        return pltpu.make_async_copy(
            x_ref.at[pl.ds(first * SEGMENT_ROWS + at, size), features],
            x.at[pl.ds(at, size), features],
            sem,
        )

    work = []
    for i, (at, size) in enumerate(blocks):
        terms = []
        if i == 0:
            for p in range(PIECES):
                features = pl.ds(p * depth, depth)
                copies = (
                    pltpu.make_async_copy(
                        w_ref.at[features, pl.ds(start, columns)], w.at[features, :], sems.at[0, p]
                    ),
                    x_copy(0, size, features, sems.at[1, p]),
                )
                terms.append((copies, slice(p * depth, (p + 1) * depth)))
        else:
            terms.append(((x_copy(at, size, slice(None), sems.at[2, i]),), slice(None)))
        work.append((at, size, terms))
    for _, _, terms in work:
        for copies, _ in terms:
            for copy in copies:
                copy.start()
    return work


def block_product(x, w, at, size, terms):
    total = None
    for copies, features in terms:
        for copy in copies:
            copy.wait()
        term = jnp.dot(
            x[at : at + size, features], w[features, :], preferred_element_type=jnp.float32
        )
        total = term if total is None else total + term
    return total


def base_scratch(segments, width, columns):
    rows = segments * SEGMENT_ROWS
    return [
        pltpu.VMEM((rows, width), jnp.bfloat16),
        pltpu.VMEM((width, columns), jnp.bfloat16),
        pltpu.SemaphoreType.DMA((3, max(PIECES, rows // BLOCK + 1))),
    ]


def sent_kernel(first, sizes, step, n_tensor, x_ref, w_ref, *refs):
    outs, (x, w, sems) = refs[: len(sizes)], refs[len(sizes) :]
    column = lax.rem(lax.axis_index("tensor") + step, n_tensor)
    work = load_base(first, sum(sizes), column, x_ref, w_ref, x, w, sems)
    unit_of = [(out, unit) for out, size in enumerate(sizes) for unit in range(size)]
    for out, size in zip(outs, sizes):
        out[size * WORDS :, :] = jnp.zeros((8, w.shape[1]), jnp.int32)
    for at, size, terms in work:
        product = block_product(x, w, at, size, terms)
        for r in range(0, size, SEGMENT_ROWS):
            out, unit = unit_of[(at + r) // SEGMENT_ROWS]
            encode(product[r : r + SEGMENT_ROWS], outs[out], unit, sizes[out])


def sent_call(tokens, weight, step, n_tensor, columns, first, sizes):
    width = tokens.shape[1]
    rows = sum(sizes) * SEGMENT_ROWS
    return pl.pallas_call(
        functools.partial(sent_kernel, first, sizes, step, n_tensor),
        in_specs=[HBM, HBM],
        out_specs=[VMEM] * len(sizes),
        out_shape=[jax.ShapeDtypeStruct((coded_rows(n), columns), jnp.int32) for n in sizes],
        scratch_shapes=base_scratch(sum(sizes), width, columns),
        compiler_params=params(16),
        cost_estimate=cost(
            2 * rows * width * columns, 2 * rows * width + 2 * width * columns + 4 * rows * columns
        ),
    )(tokens, weight)


def add_kernel(chunk, above, sums_ref, *refs):
    coded_refs, o_ref = refs[:-1], refs[-1]
    o_ref[...] = sums_ref[...]
    add_decoded(o_ref, chunk, coded_refs, above)


def add_call(chunk, above, sums, coded):
    return pl.pallas_call(
        functools.partial(add_kernel, chunk, above),
        in_specs=[VMEM] * (1 + len(coded)),
        out_specs=VMEM,
        out_shape=jax.ShapeDtypeStruct(sums.shape, sums.dtype),
        compiler_params=params(8),
        cost_estimate=cost(40000 * sums.size, 12 * sums.size),
    )(sums, *coded)


def shrink_into(o_ref, at, table, k, rows_of, views, rank, pair):
    def one(j, carry):
        _, _, within = segment_of(table, k, j)
        for stage, ref, first, whose, i in views:
            if stage not in stages_of(k):
                continue

            @pl.when((whose == table[k * ENTRIES]) & (within == i))
            def _(ref=ref, first=first):
                rows = rows_of(j)
                pair[j] = lax.dot_general(
                    rows,
                    ref[first : first + rank, : rows.shape[1]],
                    (((1,), (1,)), ((), ())),
                    preferred_element_type=jnp.float32,
                )

        return carry

    lax.fori_loop(0, MOST, one, 0)
    for j in range(MOST):
        o_ref[at, :, j * rank : (j + 1) * rank] = pair[j]


def join_copies(halves, whole, sems):
    copies, rank = [], halves[0].shape[0]
    for i, half in enumerate(halves):
        copies.append(
            pltpu.make_async_copy(half, whole.at[pl.ds(i * rank, rank), :], sems.at[i])
        )
        copies[-1].start()
    return copies


def stages_of(k):
    return range((k + 1) // 2, k + 1)


def stages_of_all(ks):
    return range(stages_of(ks[0])[0], ks[-1] + 1)


def upper_kernel(n_adapter, table, x_ref, w_ref, o_ref, kept_ref, x, w, sems, kept_sems):
    work = load_base(0, x.shape[0] // SEGMENT_ROWS, lax.axis_index("tensor"), x_ref, w_ref, x, w, sems)
    keeps = []
    for k in range(1, n_adapter):
        for j in range(MOST):
            start, _, _ = segment_of(table, k, j)
            keeps.append(
                pltpu.make_async_copy(
                    x_ref.at[pl.ds(start, SEGMENT_ROWS), :],
                    kept_ref.at[k - 1, j],
                    kept_sems.at[k - 1, j],
                )
            )
            keeps[-1].start()
    for at, size, terms in work:
        o_ref[at : at + size, :] = block_product(x, w, at, size, terms)
    for copy in keeps:
        copy.wait()


def upper_call(table, tokens, weight, columns, n_adapter):
    rows, width = tokens.shape
    half = UPPER * SEGMENT_ROWS
    return pl.pallas_call(
        functools.partial(upper_kernel, n_adapter),
        in_specs=[SMEM, HBM, HBM],
        out_specs=[VMEM] * 2,
        out_shape=[
            jax.ShapeDtypeStruct((half, columns), jnp.float32),
            jax.ShapeDtypeStruct((n_adapter - 1, MOST, SEGMENT_ROWS, width), jnp.bfloat16),
        ],
        scratch_shapes=base_scratch(half // SEGMENT_ROWS, width, columns)
        + [pltpu.SemaphoreType.DMA((n_adapter - 1, MOST))],
        compiler_params=params(12),
        cost_estimate=cost(2 * half * width * columns, 2 * rows * width + 2 * width * columns),
    )(table, tokens, weight)


def lower_kernel(per_device, rank, table, x_ref, w_ref, *refs):
    messages, halves, refs = refs[:per_device], refs[per_device : 2 * per_device], refs[2 * per_device :]
    coded_refs, (o_ref, s_ref, whole_ref, x, w, sems, mine, mine_sems, join_sems, pair) = refs[:-10], refs[-10:]
    work = load_base(UPPER, x.shape[0] // SEGMENT_ROWS, lax.axis_index("tensor"), x_ref, w_ref, x, w, sems)
    joins = join_copies(halves, whole_ref, join_sems)
    loads = []
    for j in range(MOST):
        start, _, _ = segment_of(table, 0, j)
        loads.append(
            pltpu.make_async_copy(
                x_ref.at[pl.ds(start, SEGMENT_ROWS), :], mine.at[j], mine_sems.at[j]
            )
        )
        loads[-1].start()
    for at, size, terms in work:
        o_ref[at : at + size, :] = block_product(x, w, at, size, terms)
    add_decoded(o_ref, 0, coded_refs, UPPER)
    for copy in loads:
        copy.wait()
    views = views_of(messages, [0], [(per_device, 0)], rank)
    shrink_into(s_ref, 0, table, 0, lambda j: mine[j], views, rank, pair)
    for copy in joins:
        copy.wait()


def lower_call(table, tokens, weight, messages, halves, coded, columns):
    rows, width = tokens.shape
    half = rows - UPPER * SEGMENT_ROWS
    per_device, (rank, long) = len(messages), messages[0].shape
    return pl.pallas_call(
        functools.partial(lower_kernel, per_device, rank),
        in_specs=[SMEM, HBM, HBM] + [VMEM] * (2 * per_device + len(coded)),
        out_specs=[VMEM] * 3,
        out_shape=[
            jax.ShapeDtypeStruct((half, columns), jnp.float32),
            jax.ShapeDtypeStruct((1, SEGMENT_ROWS, MOST * rank), jnp.float32),
            jax.ShapeDtypeStruct((per_device * rank, long), jnp.bfloat16),
        ],
        scratch_shapes=base_scratch(half // SEGMENT_ROWS, width, columns)
        + [
            pltpu.VMEM((MOST, SEGMENT_ROWS, width), jnp.bfloat16),
            pltpu.SemaphoreType.DMA((MOST,)),
            pltpu.SemaphoreType.DMA((per_device,)),
            pltpu.VMEM((MOST, SEGMENT_ROWS, rank), jnp.float32),
        ],
        compiler_params=params(14),
        cost_estimate=cost(0 * half * width * columns, 4 * rows * columns),
    )(table, tokens, weight, *messages, *halves, *coded)


def shrink_kernel(ks, rank, at, layout, table, kept_ref, *refs):
    buffers, (o_ref, pair) = refs[1 if at else 0 : -2], refs[-2:]
    if at:
        o_ref[:at] = refs[0][...]
    views = views_of(buffers, stages_of_all(ks), layout, rank)
    for i, k in enumerate(ks):
        shrink_into(o_ref, at + i, table, k, lambda j, k=k: kept_ref[k - 1, j], views, rank, pair)


def shrink_call(ks, table, kept, before, buffers, layout, rank):
    width = kept.shape[3]
    at = sum(b.shape[0] for b in before)
    return pl.pallas_call(
        functools.partial(shrink_kernel, ks, rank, at, layout),
        in_specs=[SMEM] + [VMEM] * (1 + len(before) + len(buffers)),
        out_specs=VMEM,
        out_shape=jax.ShapeDtypeStruct((at + len(ks), SEGMENT_ROWS, MOST * rank), jnp.float32),
        scratch_shapes=[pltpu.VMEM((MOST, SEGMENT_ROWS, rank), jnp.float32)],
        compiler_params=params(4),
        cost_estimate=cost(
            len(ks) * MOST * 2 * SEGMENT_ROWS * width * 256, len(ks) * 4 * SEGMENT_ROWS * width
        ),
    )(table, kept, *before, *buffers)


def fetch_up(up, at, table, k, j, views, rank):
    columns = up.shape[2]
    _, _, within = segment_of(table, k, j)
    for stage, ref, first, whose, i in views:
        if stage not in stages_of(k):
            continue

        @pl.when((whose == table[k * ENTRIES]) & (within == i))
        def _(ref=ref, first=first):
            factor = ref[first : first + rank, ref.shape[1] - columns :]
            up[at, :rank, :] = factor
            up[at, rank:, :] = factor


def up_product(share, j, factor, rank):
    lane = lax.broadcasted_iota(jnp.int32, share.shape, 1)
    other = pltpu.roll(share, rank, 1)
    both = jnp.where((lane < rank) == (j == 0), share, other)
    high = both.astype(jnp.bfloat16).astype(jnp.float32)
    terms = jnp.where(lane < rank, high, both - high).astype(jnp.bfloat16)
    return jnp.dot(terms, factor, preferred_element_type=jnp.float32)


LATE = 2


def early_kernel(n_adapter, n_tensor, rank, layout, n_buffers, table, *refs):
    first = n_adapter - LATE
    upper_ref, lower_ref, refs = refs[0], refs[1], refs[2:]
    shrinks, refs = refs[: -7 - n_buffers], refs[-7 - n_buffers :]
    buffers, (o_ref, rest_ref, late_up, up, sums, out, sems) = refs[:-7], refs[-7:]
    views = views_of(buffers, range(n_adapter), layout, rank)
    stores = []
    for k in range(first):
        for j in range(MOST):
            fetch_up(up, k * MOST + j, table, k, j, views, rank)
    shares = []
    for call in range(len(shrinks) // n_tensor):
        share = shrinks[call * n_tensor][...]
        for i in range(1, n_tensor):
            share = share + shrinks[call * n_tensor + i][...]
        shares += [share[i] for i in range(share.shape[0])]
    for k in range(n_adapter):
        for j in range(MOST):
            start, used, _ = segment_of(table, k, j)
            upper_rows = upper_ref.shape[0]

            @pl.when(start < upper_rows)
            def _(start=start):
                at = pl.multiple_of(jnp.minimum(start, upper_rows - SEGMENT_ROWS), SEGMENT_ROWS)
                sums[...] = upper_ref[pl.ds(at, SEGMENT_ROWS), :]

            @pl.when(start >= upper_rows)
            def _(start=start):
                at = pl.multiple_of(jnp.maximum(start - upper_rows, 0), SEGMENT_ROWS)
                sums[...] = lower_ref[pl.ds(at, SEGMENT_ROWS), :]

            value = sums[...]
            if k >= first:
                rest_ref[k - first, j] = value
                fetch_up(late_up, (k - first) * MOST + j, table, k, j, views, rank)
                continue
            lora = up_product(shares[k], j, up[k * MOST + j], rank)
            out[k, j] = (value + adapter_scale * lora).astype(jnp.bfloat16)
            store = pltpu.make_async_copy(
                out.at[k, j], o_ref.at[pl.ds(start, SEGMENT_ROWS), :], sems.at[k, j]
            )
            pl.when(used)(store.start)
            stores.append((used, store))
    for used, store in stores:
        pl.when(used)(store.wait)


def early(n_adapter, n_tensor, table, upper, lower, shrinks, buffers, layout, rank):
    rows, columns = upper.shape[0] + lower.shape[0], upper.shape[1]
    return pl.pallas_call(
        functools.partial(early_kernel, n_adapter, n_tensor, rank, layout, len(buffers)),
        in_specs=[SMEM] + [VMEM] * (2 + len(shrinks) + len(buffers)),
        out_specs=[ANY, VMEM, VMEM],
        out_shape=[
            jax.ShapeDtypeStruct((rows, columns), jnp.bfloat16),
            jax.ShapeDtypeStruct((LATE, MOST, SEGMENT_ROWS, columns), jnp.float32),
            jax.ShapeDtypeStruct((LATE * MOST, 2 * rank, columns), jnp.bfloat16),
        ],
        scratch_shapes=[
            pltpu.VMEM(((n_adapter - LATE) * MOST, 2 * rank, columns), jnp.bfloat16),
            pltpu.VMEM((SEGMENT_ROWS, columns), jnp.float32),
            pltpu.VMEM((n_adapter - LATE, MOST, SEGMENT_ROWS, columns), jnp.bfloat16),
            pltpu.SemaphoreType.DMA((n_adapter - LATE, MOST)),
        ],
        compiler_params=params(16),
        cost_estimate=cost(6 * rows * rank * columns, (4 * n_tensor + 2) * rows * columns),
    )(table, upper, lower, *shrinks, *buffers)


def late_kernel(ks, n_tensor, rank, table, *refs):
    rest_ref, shrinks, refs = refs[0], refs[1 : 1 + n_tensor], refs[1 + n_tensor :]
    up, _, o_ref, out, sems = refs
    stores = []
    for i, k in enumerate(ks):
        share = shrinks[0][i]
        for r in shrinks[1:]:
            share = share + r[i]
        for j in range(MOST):
            start, used, _ = segment_of(table, k, j)
            lora = up_product(share, j, up[i * MOST + j], rank)
            out[i, j] = (rest_ref[i, j] + adapter_scale * lora).astype(jnp.bfloat16)
            store = pltpu.make_async_copy(
                out.at[i, j], o_ref.at[pl.ds(start, SEGMENT_ROWS), :], sems.at[i, j]
            )
            pl.when(used)(store.start)
            stores.append((used, store))
    for used, store in stores:
        pl.when(used)(store.wait)


def late(ks, n_tensor, table, rest, shrinks, up, value, rank):
    rows, columns = value.shape
    return pl.pallas_call(
        functools.partial(late_kernel, ks, n_tensor, rank),
        in_specs=[SMEM] + [VMEM] * (2 + len(shrinks)) + [ANY],
        out_specs=ANY,
        out_shape=jax.ShapeDtypeStruct((rows, columns), jnp.bfloat16),
        scratch_shapes=[
            pltpu.VMEM((LATE, MOST, SEGMENT_ROWS, columns), jnp.bfloat16),
            pltpu.SemaphoreType.DMA((LATE, MOST)),
        ],
        input_output_aliases={3 + len(shrinks): 0},
        compiler_params=params(8),
        cost_estimate=cost(
            6 * LATE * MOST * SEGMENT_ROWS * rank * columns,
            8 * LATE * MOST * SEGMENT_ROWS * columns,
        ),
    )(table, rest, *shrinks, up, value)


def after(array, *others):
    return lax.optimization_barrier((array, *others))[0]


def on_device(
    tokens, value_weight, adapter_down_weight, adapter_up_weight, row_adapter_index, adapter_slot_of
):
    rows, width = tokens.shape
    per_device, _, rank = adapter_down_weight.shape
    n_adapter = lax.axis_size("adapter")
    n_tensor = lax.axis_size("tensor")
    columns = value_weight.shape[1] // n_tensor

    def swap_tensor(array, step):
        pairs = [(i, (i + step) % n_tensor) for i in range(n_tensor)]
        return lax.ppermute(array, "tensor", pairs)

    def along_line(array, stage):
        up = [(2 * i, 2 * (i + 1)) for i in range(stage - 1, n_adapter - 1)]
        down = [(2 * i + 1, 2 * (i - 1) + 1) for i in range(1, n_adapter - stage + 1)]
        return lax.ppermute(array, ("adapter", "dp"), up + down)

    def swap_cores(array):
        return lax.ppermute(array, "dp", [(0, 1), (1, 0)])

    down = jnp.swapaxes(adapter_down_weight, 1, 2).reshape(per_device * rank, width)
    up = adapter_up_weight.reshape(per_device * rank, value_weight.shape[1])
    tokens, value_weight, down, up = (
        pltpu.with_memory_space_constraint(a, pltpu.HBM) for a in (tokens, value_weight, down, up)
    )
    messages = message_call(down, up, columns, per_device)
    table = table_call(row_adapter_index, adapter_slot_of, n_adapter, per_device)
    last = n_adapter - 1
    buffers, shrinks = [list(messages)], []
    layout = [(per_device, 0), (per_device, 1)] + [(per_device, per_device)] * (last - 1)

    def buffers_of(stages):
        return [b for stage in stages for b in buffers[stage]]

    def shrink(ks, kept, before=()):
        mine = buffers_of(stages_of_all(ks))
        return shrink_call(ks, table, kept, list(before), mine, layout, rank)

    def add_shrink(mine):
        shrinks.extend([mine] + [swap_tensor(mine, step) for step in range(1, n_tensor)])

    others = range(1, n_tensor)

    def sent_for(step, chunks, rows):
        sizes = [number for _, number in chunks]
        return sent_call(rows, value_weight, step, n_tensor, columns, chunks[0][0], sizes)

    def send(parts, *ahead):
        return [swap_tensor(after(p, *ahead), step) for step, p in zip(others, parts)]

    held = [along_line(m, 1) for m in messages]
    part_a = [sent_for(step, CHUNKS[:1], tokens)[0] for step in others]
    sent = [send(part_a)]
    first = after(held[0], table, *part_a)
    rest_parts = [sent_for(step, CHUNKS[1:], after(tokens, first)) for step in others]
    parts = [[p[i] for p in rest_parts] for i in range(len(CHUNKS) - 1)]
    part_b = [p for group in parts for p in group]
    for stage in range(1, last):
        came = held
        if stage == 1:
            came = [first] + [after(h, *part_b) for h in held[1:]]
            sent.append(send(parts[0], *came, *sent[0]))
        if stage == 2:
            came = held[:1] + [after(h, upper) for h in held[1:]]
        held = [along_line(c, stage + 1) for c in came]
        if stage == 1:
            upper, kept = upper_call(
                after(table, held[0], *came), tokens, value_weight, columns, n_adapter
            )
        elif stage == 2:
            lower, before, joined = lower_call(
                after(table, *came), tokens, value_weight, messages, buffers[1], sent[0], columns
            )
            buffers[1] += [swap_cores(joined)]
            free = lower
            upper = add_call(1, 0, after(upper, held[0]), sent[1])
            lower = add_call(1, UPPER, after(lower, upper, *held[1:]), sent[1])
            before = shrink([1], after(kept, lower), [before])
        else:
            before = shrink([stage - 1], kept, [before])
        ahead = [free] if stage == 2 else []
        swapped = [swap_cores(after(c, *ahead)) for c in came] if stage > 1 else []
        buffers.append([*came, *swapped])
    add_shrink(before)
    buffers.append([*held, *[swap_cores(h) for h in held]])
    value, remaining, factors = early(
        n_adapter,
        n_tensor,
        table,
        upper,
        lower,
        shrinks,
        buffers_of(range(n_adapter)),
        layout,
        rank,
    )
    ks = (last - 1, last)
    add_shrink(shrink(ks, after(kept, *held)))
    return late(
        ks,
        n_tensor,
        table,
        remaining,
        shrinks[-n_tensor:],
        factors,
        value,
        rank,
    )


def solution(mesh):
    return jax.shard_map(
        on_device,
        mesh=mesh,
        in_specs=(
            P(("groups", "adapter", "dp"), "tensor"),
            P("tensor", None),
            P(("groups", "adapter"), "tensor", None),
            P(("groups", "adapter"), None, None),
            P(("groups", "adapter", "dp")),
            P("groups"),
        ),
        out_specs=P(("groups", "adapter", "dp"), "tensor"),
        check_vma=False,
    )
```

```python
import functools

import jax
import jax.numpy as jnp
from jax import lax
from jax.experimental import pallas as pl
from jax.experimental.pallas import tpu as pltpu
from jax.sharding import PartitionSpec as P

SEGMENT_ROWS = 128
adapter_scale = 0.5
MOST = 2
BLOCK = 256
PIECES = 4
CHUNKS = ((6, 2), (0, 6))
UPPER = 3
ENTRIES = 8
MIDDLE = 1.5 * 2.0**23


def cost(flops, moved):
    return pl.CostEstimate(flops=int(flops), bytes_accessed=int(moved), transcendentals=0)


def params(mib):
    return pltpu.CompilerParams(vmem_limit_bytes=mib * 2**20)


ANY = pl.BlockSpec(memory_space=pl.ANY)
HBM = pl.BlockSpec(memory_space=pltpu.HBM)
SMEM = pl.BlockSpec(memory_space=pltpu.SMEM)
VMEM = pl.BlockSpec(memory_space=pltpu.VMEM)


def arrival_order(me, n_adapter):
    order = [me] + [jnp.int32(-1)] * (n_adapter - 1)
    count = jnp.int32(1)
    for distance in range(1, n_adapter):
        for other in (me - distance, me + distance):
            valid = (other >= 0) & (other < n_adapter)
            order = [jnp.where(valid & (count == k), other, o) for k, o in enumerate(order)]
            count = count + valid.astype(jnp.int32)
    return order


def views_of(refs, stages, layout, rank):
    me, core = lax.axis_index("adapter"), lax.axis_index("dp")
    refs, views = list(refs), []
    for stage in stages:
        came, swapped = layout[stage]
        toward = jnp.where(core == 0, -stage, stage)
        for i in range(came):
            views.append((stage, refs.pop(0), 0, me + toward if stage > 0 else me, i))
        for i in range(swapped):
            ref = refs.pop(0)
            for part in range(came // swapped):
                views.append((stage, ref, part * rank, me - toward, i + part))
    return views


def segment_of(table, k, j):
    seg = table[k * ENTRIES + 1 + 2 * j]
    start = pl.multiple_of(jnp.maximum(seg, 0) * SEGMENT_ROWS, SEGMENT_ROWS)
    return start, seg >= 0, table[k * ENTRIES + 2 + 2 * j]


def message_kernel(adapter, down_ref, up_ref, *refs):
    outs, sems = refs[:-1], refs[-1]
    rank = outs[0].shape[0]
    width = down_ref.shape[1]
    columns = outs[0].shape[1] - width
    start = pl.multiple_of(lax.axis_index("tensor") * columns, columns)
    copies = []
    for i, out in enumerate(outs):
        rows = pl.ds((adapter + i) * rank, rank)
        copies += [
            pltpu.make_async_copy(down_ref.at[rows, :], out.at[:, pl.ds(0, width)], sems.at[0, i]),
            pltpu.make_async_copy(
                up_ref.at[rows, pl.ds(start, columns)], out.at[:, pl.ds(width, columns)], sems.at[1, i]
            ),
        ]
    for copy in copies:
        copy.start()
    for copy in copies:
        copy.wait()


def message_call(down, up, columns, per_device, adapter):
    rows, width = down.shape
    shape = jax.ShapeDtypeStruct((rows // per_device, width + columns), jnp.bfloat16)
    return pl.pallas_call(
        functools.partial(message_kernel, adapter),
        in_specs=[HBM, HBM],
        out_specs=[VMEM],
        out_shape=[shape],
        scratch_shapes=[pltpu.SemaphoreType.DMA((2, 1))],
        compiler_params=params(8),
        cost_estimate=cost(0, 4 * rows * (width + columns)),
    )(down, up)[0]


def table_kernel(n_adapter, per_device, ids, slots, table):
    seg_dev = ids.shape[0] // SEGMENT_ROWS
    used = [slots[ids[s * SEGMENT_ROWS]] for s in range(seg_dev)]
    for k, owner in enumerate(arrival_order(lax.axis_index("adapter"), n_adapter)):
        table[k * ENTRIES] = owner
        found, place = [jnp.int32(-1)] * MOST, [jnp.int32(0)] * MOST
        count = jnp.int32(0)
        for s, slot in enumerate(used):
            within = slot - owner * per_device
            hit = (within >= 0) & (within < per_device)
            for j in range(MOST):
                take = hit & (count == j)
                found[j] = jnp.where(take, s, found[j])
                place[j] = jnp.where(take, within, place[j])
            count = count + hit.astype(jnp.int32)
        for j in range(MOST):
            table[k * ENTRIES + 1 + 2 * j] = found[j]
            table[k * ENTRIES + 2 + 2 * j] = place[j]


def table_call(ids, slots, n_adapter, per_device):
    return pl.pallas_call(
        functools.partial(table_kernel, n_adapter, per_device),
        in_specs=[SMEM, SMEM],
        out_specs=SMEM,
        out_shape=jax.ShapeDtypeStruct((n_adapter * ENTRIES,), jnp.int32),
        cost_estimate=cost(0, 4 * ids.shape[0]),
    )(ids, slots)


def diagonal():
    shape = (SEGMENT_ROWS, SEGMENT_ROWS)
    return lax.broadcasted_iota(jnp.int32, shape, 0) == lax.broadcasted_iota(jnp.int32, shape, 1)


GROUP = SEGMENT_ROWS // 8
WORDS = 5 * GROUP


def coded_rows(segments):
    return segments * WORDS + 8


def encode(values, o_ref, unit, units):
    largest = jnp.maximum(jnp.max(jnp.abs(values), axis=1, keepdims=True), 2.0**-100)
    power = jnp.floor(jnp.log2(largest))
    whole = (values * jnp.exp2(18.0 - power) + MIDDLE).astype(jnp.int32) - int(MIDDLE)
    whole = jnp.clip(whole, -(2**19), 2**19 - 1)
    v = [whole[i * GROUP : (i + 1) * GROUP] for i in range(8)]
    over = [
        v[5] & 0xFFF,
        ((v[5] >> 12) & 0xFF) | ((v[6] & 0xF) << 8),
        (v[6] >> 4) & 0xFFF,
        ((v[6] >> 16) & 0xF) | ((v[7] & 0xFF) << 4),
        v[7] >> 8,
    ]
    for i in range(5):
        o_ref[unit * WORDS + i * GROUP : unit * WORDS + (i + 1) * GROUP, :] = (v[i] & 0xFFFFF) | (
            over[i] << 20
        )
    row = jnp.sum(jnp.where(diagonal(), power, 0.0), axis=0, keepdims=True)
    o_ref[units * WORDS + unit : units * WORDS + unit + 1, :SEGMENT_ROWS] = row.astype(jnp.int32)


def decode(ref, unit, units):
    w = [ref[unit * WORDS + i * GROUP : unit * WORDS + (i + 1) * GROUP, :] for i in range(5)]
    v = [(x << 12) >> 12 for x in w]
    v.append(((w[0] >> 20) & 0xFFF) | (((w[1] << 4) >> 24) << 12))
    v.append(((w[1] >> 28) & 0xF) | (((w[2] >> 20) & 0xFFF) << 4) | (((w[3] << 8) >> 28) << 16))
    v.append(((w[3] >> 24) & 0xFF) | ((w[4] >> 20) << 8))
    row = ref[units * WORDS + unit : units * WORDS + unit + 1, :SEGMENT_ROWS].astype(jnp.float32)
    power = jnp.sum(jnp.where(diagonal(), row, 0.0), axis=1, keepdims=True)
    return jnp.concatenate(v, axis=0).astype(jnp.float32) * jnp.exp2(power - 18.0)


def add_decoded(sums, chunk, refs, above):
    first, number = CHUNKS[chunk]
    for unit in range(number):
        at = first + unit - above
        if at < 0 or at >= sums.shape[0] // SEGMENT_ROWS:
            continue
        rows = pl.ds(at * SEGMENT_ROWS, SEGMENT_ROWS)
        value = sums[rows, :]
        for ref in refs:
            value = value + decode(ref, unit, number)
        sums[rows, :] = value


def load_base(first, segments, column, x_ref, w_ref, x, w, sems):
    width, columns = w.shape
    rows = segments * SEGMENT_ROWS
    start = pl.multiple_of(column * columns, columns)
    depth = width // PIECES
    blocks = [(r, min(BLOCK, rows - r)) for r in range(0, rows, BLOCK)]

    def x_copy(at, size, features, sem):
        return pltpu.make_async_copy(
            x_ref.at[pl.ds(first * SEGMENT_ROWS + at, size), features],
            x.at[pl.ds(at, size), features],
            sem,
        )

    work = []
    for i, (at, size) in enumerate(blocks):
        terms = []
        if i == 0:
            for p in range(PIECES):
                features = pl.ds(p * depth, depth)
                copies = (
                    pltpu.make_async_copy(
                        w_ref.at[features, pl.ds(start, columns)], w.at[features, :], sems.at[0, p]
                    ),
                    x_copy(0, size, features, sems.at[1, p]),
                )
                terms.append((copies, slice(p * depth, (p + 1) * depth)))
        else:
            terms.append(((x_copy(at, size, slice(None), sems.at[2, i]),), slice(None)))
        work.append((at, size, terms))
    for _, _, terms in work:
        for copies, _ in terms:
            for copy in copies:
                copy.start()
    return work


def block_product(x, w, at, size, terms):
    total = None
    for copies, features in terms:
        for copy in copies:
            copy.wait()
        term = jnp.dot(
            x[at : at + size, features], w[features, :], preferred_element_type=jnp.float32
        )
        total = term if total is None else total + term
    return total


def base_scratch(segments, width, columns):
    rows = segments * SEGMENT_ROWS
    return [
        pltpu.VMEM((rows, width), jnp.bfloat16),
        pltpu.VMEM((width, columns), jnp.bfloat16),
        pltpu.SemaphoreType.DMA((3, max(PIECES, rows // BLOCK + 1))),
    ]


def sent_kernel(first, sizes, step, n_tensor, x_ref, w_ref, *refs):
    outs, (x, w, sems) = refs[: len(sizes)], refs[len(sizes) :]
    column = lax.rem(lax.axis_index("tensor") + step, n_tensor)
    work = load_base(first, sum(sizes), column, x_ref, w_ref, x, w, sems)
    unit_of = [(out, unit) for out, size in enumerate(sizes) for unit in range(size)]
    for out, size in zip(outs, sizes):
        out[size * WORDS :, :] = jnp.zeros((8, w.shape[1]), jnp.int32)
    for at, size, terms in work:
        product = block_product(x, w, at, size, terms)
        for r in range(0, size, SEGMENT_ROWS):
            out, unit = unit_of[(at + r) // SEGMENT_ROWS]
            encode(product[r : r + SEGMENT_ROWS], outs[out], unit, sizes[out])


def sent_call(tokens, weight, step, n_tensor, columns, first, sizes):
    width = tokens.shape[1]
    rows = sum(sizes) * SEGMENT_ROWS
    return pl.pallas_call(
        functools.partial(sent_kernel, first, sizes, step, n_tensor),
        in_specs=[HBM, HBM],
        out_specs=[VMEM] * len(sizes),
        out_shape=[jax.ShapeDtypeStruct((coded_rows(n), columns), jnp.int32) for n in sizes],
        scratch_shapes=base_scratch(sum(sizes), width, columns),
        compiler_params=params(16),
        cost_estimate=cost(
            2 * rows * width * columns, 2 * rows * width + 2 * width * columns + 4 * rows * columns
        ),
    )(tokens, weight)


def add_kernel(chunk, above, sums_ref, *refs):
    coded_refs, o_ref = refs[:-1], refs[-1]
    o_ref[...] = sums_ref[...]
    add_decoded(o_ref, chunk, coded_refs, above)


def add_call(chunk, above, sums, coded):
    return pl.pallas_call(
        functools.partial(add_kernel, chunk, above),
        in_specs=[VMEM] * (1 + len(coded)),
        out_specs=VMEM,
        out_shape=jax.ShapeDtypeStruct(sums.shape, sums.dtype),
        compiler_params=params(8),
        cost_estimate=cost(40000 * sums.size, 12 * sums.size),
    )(sums, *coded)


def shrink_into(o_ref, at, table, k, rows_of, views, rank, pair):
    def one(j, carry):
        _, _, within = segment_of(table, k, j)
        for stage, ref, first, whose, i in views:
            if stage not in stages_of(k):
                continue

            @pl.when((whose == table[k * ENTRIES]) & (within == i))
            def _(ref=ref, first=first):
                rows = rows_of(j)
                pair[j] = lax.dot_general(
                    rows,
                    ref[first : first + rank, : rows.shape[1]],
                    (((1,), (1,)), ((), ())),
                    preferred_element_type=jnp.float32,
                )

        return carry

    lax.fori_loop(0, MOST, one, 0)
    for j in range(MOST):
        o_ref[at, :, j * rank : (j + 1) * rank] = pair[j]


def join_copies(halves, whole, sems):
    copies, rank = [], halves[0].shape[0]
    for i, half in enumerate(halves):
        copies.append(
            pltpu.make_async_copy(half, whole.at[pl.ds(i * rank, rank), :], sems.at[i])
        )
        copies[-1].start()
    return copies


def stages_of(k):
    return range((k + 1) // 2, k + 1)


def stages_of_all(ks):
    return range(stages_of(ks[0])[0], ks[-1] + 1)


def upper_kernel(n_adapter, table, x_ref, w_ref, o_ref, kept_ref, x, w, sems, kept_sems):
    work = load_base(0, x.shape[0] // SEGMENT_ROWS, lax.axis_index("tensor"), x_ref, w_ref, x, w, sems)
    keeps = []
    for k in range(1, n_adapter):
        for j in range(MOST):
            start, _, _ = segment_of(table, k, j)
            keeps.append(
                pltpu.make_async_copy(
                    x_ref.at[pl.ds(start, SEGMENT_ROWS), :],
                    kept_ref.at[k - 1, j],
                    kept_sems.at[k - 1, j],
                )
            )
            keeps[-1].start()
    for at, size, terms in work:
        o_ref[at : at + size, :] = block_product(x, w, at, size, terms)
    for copy in keeps:
        copy.wait()


def upper_call(table, tokens, weight, columns, n_adapter):
    rows, width = tokens.shape
    half = UPPER * SEGMENT_ROWS
    return pl.pallas_call(
        functools.partial(upper_kernel, n_adapter),
        in_specs=[SMEM, HBM, HBM],
        out_specs=[VMEM] * 2,
        out_shape=[
            jax.ShapeDtypeStruct((half, columns), jnp.float32),
            jax.ShapeDtypeStruct((n_adapter - 1, MOST, SEGMENT_ROWS, width), jnp.bfloat16),
        ],
        scratch_shapes=base_scratch(half // SEGMENT_ROWS, width, columns)
        + [pltpu.SemaphoreType.DMA((n_adapter - 1, MOST))],
        compiler_params=params(12),
        cost_estimate=cost(2 * half * width * columns, 2 * rows * width + 2 * width * columns),
    )(table, tokens, weight)


def lower_kernel(per_device, rank, table, x_ref, w_ref, *refs):
    messages, halves, refs = refs[:per_device], refs[per_device : 2 * per_device], refs[2 * per_device :]
    coded_refs, (o_ref, s_ref, whole_ref, x, w, sems, mine, mine_sems, join_sems, pair) = refs[:-10], refs[-10:]
    work = load_base(UPPER, x.shape[0] // SEGMENT_ROWS, lax.axis_index("tensor"), x_ref, w_ref, x, w, sems)
    joins = join_copies(halves, whole_ref, join_sems)
    loads = []
    for j in range(MOST):
        start, _, _ = segment_of(table, 0, j)
        loads.append(
            pltpu.make_async_copy(
                x_ref.at[pl.ds(start, SEGMENT_ROWS), :], mine.at[j], mine_sems.at[j]
            )
        )
        loads[-1].start()
    for at, size, terms in work:
        o_ref[at : at + size, :] = block_product(x, w, at, size, terms)
    add_decoded(o_ref, 0, coded_refs, UPPER)
    for copy in loads:
        copy.wait()
    views = views_of(messages, [0], [(per_device, 0)], rank)
    shrink_into(s_ref, 0, table, 0, lambda j: mine[j], views, rank, pair)
    for copy in joins:
        copy.wait()


def lower_call(table, tokens, weight, messages, halves, coded, columns):
    rows, width = tokens.shape
    half = rows - UPPER * SEGMENT_ROWS
    per_device, (rank, long) = len(messages), messages[0].shape
    return pl.pallas_call(
        functools.partial(lower_kernel, per_device, rank),
        in_specs=[SMEM, HBM, HBM] + [VMEM] * (2 * per_device + len(coded)),
        out_specs=[VMEM] * 3,
        out_shape=[
            jax.ShapeDtypeStruct((half, columns), jnp.float32),
            jax.ShapeDtypeStruct((1, SEGMENT_ROWS, MOST * rank), jnp.float32),
            jax.ShapeDtypeStruct((per_device * rank, long), jnp.bfloat16),
        ],
        scratch_shapes=base_scratch(half // SEGMENT_ROWS, width, columns)
        + [
            pltpu.VMEM((MOST, SEGMENT_ROWS, width), jnp.bfloat16),
            pltpu.SemaphoreType.DMA((MOST,)),
            pltpu.SemaphoreType.DMA((per_device,)),
            pltpu.VMEM((MOST, SEGMENT_ROWS, rank), jnp.float32),
        ],
        compiler_params=params(14),
        cost_estimate=cost(0 * half * width * columns, 4 * rows * columns),
    )(table, tokens, weight, *messages, *halves, *coded)


def shrink_kernel(ks, rank, at, layout, table, kept_ref, *refs):
    buffers, (o_ref, pair) = refs[1 if at else 0 : -2], refs[-2:]
    if at:
        o_ref[:at] = refs[0][...]
    views = views_of(buffers, stages_of_all(ks), layout, rank)
    for i, k in enumerate(ks):
        shrink_into(o_ref, at + i, table, k, lambda j, k=k: kept_ref[k - 1, j], views, rank, pair)


def shrink_call(ks, table, kept, before, buffers, layout, rank):
    width = kept.shape[3]
    at = sum(b.shape[0] for b in before)
    return pl.pallas_call(
        functools.partial(shrink_kernel, ks, rank, at, layout),
        in_specs=[SMEM] + [VMEM] * (1 + len(before) + len(buffers)),
        out_specs=VMEM,
        out_shape=jax.ShapeDtypeStruct((at + len(ks), SEGMENT_ROWS, MOST * rank), jnp.float32),
        scratch_shapes=[pltpu.VMEM((MOST, SEGMENT_ROWS, rank), jnp.float32)],
        compiler_params=params(4),
        cost_estimate=cost(
            len(ks) * MOST * 2 * SEGMENT_ROWS * width * 256, len(ks) * 4 * SEGMENT_ROWS * width
        ),
    )(table, kept, *before, *buffers)


def fetch_up(up, at, table, k, j, views, rank):
    columns = up.shape[2]
    _, _, within = segment_of(table, k, j)
    for stage, ref, first, whose, i in views:
        if stage not in stages_of(k):
            continue

        @pl.when((whose == table[k * ENTRIES]) & (within == i))
        def _(ref=ref, first=first):
            factor = ref[first : first + rank, ref.shape[1] - columns :]
            up[at, :rank, :] = factor
            up[at, rank:, :] = factor


def up_product(share, j, factor, rank):
    lane = lax.broadcasted_iota(jnp.int32, share.shape, 1)
    other = pltpu.roll(share, rank, 1)
    both = jnp.where((lane < rank) == (j == 0), share, other)
    high = both.astype(jnp.bfloat16).astype(jnp.float32)
    terms = jnp.where(lane < rank, high, both - high).astype(jnp.bfloat16)
    return jnp.dot(terms, factor, preferred_element_type=jnp.float32)


LATE = 2


def early_kernel(n_adapter, n_tensor, rank, layout, n_buffers, table, *refs):
    first = n_adapter - LATE
    upper_ref, lower_ref, refs = refs[0], refs[1], refs[2:]
    shrinks, refs = refs[: -7 - n_buffers], refs[-7 - n_buffers :]
    buffers, (o_ref, rest_ref, late_up, up, sums, out, sems) = refs[:-7], refs[-7:]
    views = views_of(buffers, range(n_adapter), layout, rank)
    stores = []
    for k in range(first):
        for j in range(MOST):
            fetch_up(up, k * MOST + j, table, k, j, views, rank)
    shares = []
    for call in range(len(shrinks) // n_tensor):
        share = shrinks[call * n_tensor][...]
        for i in range(1, n_tensor):
            share = share + shrinks[call * n_tensor + i][...]
        shares += [share[i] for i in range(share.shape[0])]
    for k in range(n_adapter):
        for j in range(MOST):
            start, used, _ = segment_of(table, k, j)
            upper_rows = upper_ref.shape[0]

            @pl.when(start < upper_rows)
            def _(start=start):
                at = pl.multiple_of(jnp.minimum(start, upper_rows - SEGMENT_ROWS), SEGMENT_ROWS)
                sums[...] = upper_ref[pl.ds(at, SEGMENT_ROWS), :]

            @pl.when(start >= upper_rows)
            def _(start=start):
                at = pl.multiple_of(jnp.maximum(start - upper_rows, 0), SEGMENT_ROWS)
                sums[...] = lower_ref[pl.ds(at, SEGMENT_ROWS), :]

            value = sums[...]
            if k >= first:
                rest_ref[k - first, j] = value
                fetch_up(late_up, (k - first) * MOST + j, table, k, j, views, rank)
                continue
            lora = up_product(shares[k], j, up[k * MOST + j], rank)
            out[k, j] = (value + adapter_scale * lora).astype(jnp.bfloat16)
            store = pltpu.make_async_copy(
                out.at[k, j], o_ref.at[pl.ds(start, SEGMENT_ROWS), :], sems.at[k, j]
            )
            pl.when(used)(store.start)
            stores.append((used, store))
    for used, store in stores:
        pl.when(used)(store.wait)


def early(n_adapter, n_tensor, table, upper, lower, shrinks, buffers, layout, rank):
    rows, columns = upper.shape[0] + lower.shape[0], upper.shape[1]
    return pl.pallas_call(
        functools.partial(early_kernel, n_adapter, n_tensor, rank, layout, len(buffers)),
        in_specs=[SMEM] + [VMEM] * (2 + len(shrinks) + len(buffers)),
        out_specs=[ANY, VMEM, VMEM],
        out_shape=[
            jax.ShapeDtypeStruct((rows, columns), jnp.bfloat16),
            jax.ShapeDtypeStruct((LATE, MOST, SEGMENT_ROWS, columns), jnp.float32),
            jax.ShapeDtypeStruct((LATE * MOST, 2 * rank, columns), jnp.bfloat16),
        ],
        scratch_shapes=[
            pltpu.VMEM(((n_adapter - LATE) * MOST, 2 * rank, columns), jnp.bfloat16),
            pltpu.VMEM((SEGMENT_ROWS, columns), jnp.float32),
            pltpu.VMEM((n_adapter - LATE, MOST, SEGMENT_ROWS, columns), jnp.bfloat16),
            pltpu.SemaphoreType.DMA((n_adapter - LATE, MOST)),
        ],
        compiler_params=params(16),
        cost_estimate=cost(6 * rows * rank * columns, (4 * n_tensor + 2) * rows * columns),
    )(table, upper, lower, *shrinks, *buffers)


def late_kernel(ks, n_tensor, rank, table, *refs):
    rest_ref, shrinks, refs = refs[0], refs[1 : 1 + n_tensor], refs[1 + n_tensor :]
    up, _, o_ref, out, sems = refs
    stores = []
    for i, k in enumerate(ks):
        share = shrinks[0][i]
        for r in shrinks[1:]:
            share = share + r[i]
        for j in range(MOST):
            start, used, _ = segment_of(table, k, j)
            lora = up_product(share, j, up[i * MOST + j], rank)
            out[i, j] = (rest_ref[i, j] + adapter_scale * lora).astype(jnp.bfloat16)
            store = pltpu.make_async_copy(
                out.at[i, j], o_ref.at[pl.ds(start, SEGMENT_ROWS), :], sems.at[i, j]
            )
            pl.when(used)(store.start)
            stores.append((used, store))
    for used, store in stores:
        pl.when(used)(store.wait)


def late(ks, n_tensor, table, rest, shrinks, up, value, rank):
    rows, columns = value.shape
    return pl.pallas_call(
        functools.partial(late_kernel, ks, n_tensor, rank),
        in_specs=[SMEM] + [VMEM] * (2 + len(shrinks)) + [ANY],
        out_specs=ANY,
        out_shape=jax.ShapeDtypeStruct((rows, columns), jnp.bfloat16),
        scratch_shapes=[
            pltpu.VMEM((LATE, MOST, SEGMENT_ROWS, columns), jnp.bfloat16),
            pltpu.SemaphoreType.DMA((LATE, MOST)),
        ],
        input_output_aliases={3 + len(shrinks): 0},
        compiler_params=params(8),
        cost_estimate=cost(
            6 * LATE * MOST * SEGMENT_ROWS * rank * columns,
            8 * LATE * MOST * SEGMENT_ROWS * columns,
        ),
    )(table, rest, *shrinks, up, value)


def after(array, *others):
    return lax.optimization_barrier((array, *others))[0]


def on_device(
    tokens, value_weight, adapter_down_weight, adapter_up_weight, row_adapter_index, adapter_slot_of
):
    rows, width = tokens.shape
    per_device, _, rank = adapter_down_weight.shape
    n_adapter = lax.axis_size("adapter")
    n_tensor = lax.axis_size("tensor")
    columns = value_weight.shape[1] // n_tensor

    def swap_tensor(array, step):
        pairs = [(i, (i + step) % n_tensor) for i in range(n_tensor)]
        return lax.ppermute(array, "tensor", pairs)

    def along_line(array, stage):
        up = [(2 * i, 2 * (i + 1)) for i in range(stage - 1, n_adapter - 1)]
        down = [(2 * i + 1, 2 * (i - 1) + 1) for i in range(1, n_adapter - stage + 1)]
        return lax.ppermute(array, ("adapter", "dp"), up + down)

    def swap_cores(array):
        return lax.ppermute(array, "dp", [(0, 1), (1, 0)])

    down = jnp.swapaxes(adapter_down_weight, 1, 2).reshape(per_device * rank, width)
    up = adapter_up_weight.reshape(per_device * rank, value_weight.shape[1])
    tokens, value_weight, down, up = (
        pltpu.with_memory_space_constraint(a, pltpu.HBM) for a in (tokens, value_weight, down, up)
    )
    messages = [message_call(down, up, columns, per_device, i) for i in range(per_device)]
    table = table_call(row_adapter_index, adapter_slot_of, n_adapter, per_device)
    last = n_adapter - 1
    buffers, shrinks = [list(messages)], []
    layout = [(per_device, 0), (per_device, 1)] + [(per_device, per_device)] * (last - 1)

    def buffers_of(stages):
        return [b for stage in stages for b in buffers[stage]]

    def shrink(ks, kept, before=()):
        mine = buffers_of(stages_of_all(ks))
        return shrink_call(ks, table, kept, list(before), mine, layout, rank)

    def add_shrink(mine):
        shrinks.extend([mine] + [swap_tensor(mine, step) for step in range(1, n_tensor)])

    others = range(1, n_tensor)

    def sent_for(step, chunks, rows):
        sizes = [number for _, number in chunks]
        return sent_call(rows, value_weight, step, n_tensor, columns, chunks[0][0], sizes)

    def send(parts, *ahead):
        return [swap_tensor(after(p, *ahead), step) for step, p in zip(others, parts)]

    held = [along_line(m, 1) for m in messages]
    part_a = [sent_for(step, CHUNKS[:1], tokens)[0] for step in others]
    sent = [send(part_a)]
    first = after(held[0], table, *part_a)
    rest_parts = [sent_for(step, CHUNKS[1:], after(tokens, first)) for step in others]
    parts = [[p[i] for p in rest_parts] for i in range(len(CHUNKS) - 1)]
    part_b = [p for group in parts for p in group]
    for stage in range(1, last):
        came = held
        if stage == 1:
            came = [first] + [after(h, *part_b) for h in held[1:]]
            sent.append(send(parts[0], *came, *sent[0]))
        if stage == 2:
            came = held[:1] + [after(h, upper) for h in held[1:]]
        held = [along_line(c, stage + 1) for c in came]
        if stage == 1:
            upper, kept = upper_call(
                after(table, held[0], *came), tokens, value_weight, columns, n_adapter
            )
        elif stage == 2:
            lower, before, joined = lower_call(
                after(table, *came), tokens, value_weight, messages, buffers[1], sent[0], columns
            )
            buffers[1] += [swap_cores(joined)]
            free = lower
            upper = add_call(1, 0, after(upper, held[0]), sent[1])
            lower = add_call(1, UPPER, after(lower, upper, *held[1:]), sent[1])
            before = shrink([1], after(kept, lower), [before])
        else:
            before = shrink([stage - 1], kept, [before])
        ahead = [free] if stage == 2 else []
        swapped = [swap_cores(after(c, *ahead)) for c in came] if stage > 1 else []
        buffers.append([*came, *swapped])
    add_shrink(before)
    buffers.append([*held, *[swap_cores(h) for h in held]])
    value, remaining, factors = early(
        n_adapter,
        n_tensor,
        table,
        upper,
        lower,
        shrinks,
        buffers_of(range(n_adapter)),
        layout,
        rank,
    )
    ks = (last - 1, last)
    add_shrink(shrink(ks, after(kept, *held)))
    return late(
        ks,
        n_tensor,
        table,
        remaining,
        shrinks[-n_tensor:],
        factors,
        value,
        rank,
    )


def solution(mesh):
    return jax.shard_map(
        on_device,
        mesh=mesh,
        in_specs=(
            P(("groups", "adapter", "dp"), "tensor"),
            P("tensor", None),
            P(("groups", "adapter"), "tensor", None),
            P(("groups", "adapter"), None, None),
            P(("groups", "adapter", "dp")),
            P("groups"),
        ),
        out_specs=P(("groups", "adapter", "dp"), "tensor"),
        check_vma=False,
    )
```

```python
import functools

import jax
import jax.numpy as jnp
from jax import lax
from jax.experimental import pallas as pl
from jax.experimental.pallas import tpu as pltpu
from jax.sharding import PartitionSpec as P

SEGMENT_ROWS = 128
adapter_scale = 0.5
MOST = 2
BLOCK = 512
PIECES = 4
CHUNKS = ((6, 2), (0, 6))
UPPER = 3
ENTRIES = 8
MIDDLE = 1.5 * 2.0**23


def cost(flops, moved):
    return pl.CostEstimate(flops=int(flops), bytes_accessed=int(moved), transcendentals=0)


def params(mib):
    return pltpu.CompilerParams(vmem_limit_bytes=mib * 2**20)


ANY = pl.BlockSpec(memory_space=pl.ANY)
HBM = pl.BlockSpec(memory_space=pltpu.HBM)
SMEM = pl.BlockSpec(memory_space=pltpu.SMEM)
VMEM = pl.BlockSpec(memory_space=pltpu.VMEM)


def arrival_order(me, n_adapter):
    order = [me] + [jnp.int32(-1)] * (n_adapter - 1)
    count = jnp.int32(1)
    for distance in range(1, n_adapter):
        for other in (me - distance, me + distance):
            valid = (other >= 0) & (other < n_adapter)
            order = [jnp.where(valid & (count == k), other, o) for k, o in enumerate(order)]
            count = count + valid.astype(jnp.int32)
    return order


def views_of(refs, stages, layout, rank):
    me, core = lax.axis_index("adapter"), lax.axis_index("dp")
    refs, views = list(refs), []
    for stage in stages:
        came, swapped = layout[stage]
        toward = jnp.where(core == 0, -stage, stage)
        for i in range(came):
            views.append((stage, refs.pop(0), 0, me + toward if stage > 0 else me, i))
        for i in range(swapped):
            ref = refs.pop(0)
            for part in range(came // swapped):
                views.append((stage, ref, part * rank, me - toward, i + part))
    return views


def segment_of(table, k, j):
    seg = table[k * ENTRIES + 1 + 2 * j]
    start = pl.multiple_of(jnp.maximum(seg, 0) * SEGMENT_ROWS, SEGMENT_ROWS)
    return start, seg >= 0, table[k * ENTRIES + 2 + 2 * j]


def message_kernel(adapter, down_ref, up_ref, *refs):
    outs, sems = refs[:-1], refs[-1]
    rank = outs[0].shape[0]
    width = down_ref.shape[1]
    columns = outs[0].shape[1] - width
    start = pl.multiple_of(lax.axis_index("tensor") * columns, columns)
    copies = []
    for i, out in enumerate(outs):
        rows = pl.ds((adapter + i) * rank, rank)
        copies += [
            pltpu.make_async_copy(down_ref.at[rows, :], out.at[:, pl.ds(0, width)], sems.at[0, i]),
            pltpu.make_async_copy(
                up_ref.at[rows, pl.ds(start, columns)], out.at[:, pl.ds(width, columns)], sems.at[1, i]
            ),
        ]
    for copy in copies:
        copy.start()
    for copy in copies:
        copy.wait()


def message_call(down, up, columns, per_device, adapter):
    rows, width = down.shape
    shape = jax.ShapeDtypeStruct((rows // per_device, width + columns), jnp.bfloat16)
    return pl.pallas_call(
        functools.partial(message_kernel, adapter),
        in_specs=[HBM, HBM],
        out_specs=[VMEM],
        out_shape=[shape],
        scratch_shapes=[pltpu.SemaphoreType.DMA((2, 1))],
        compiler_params=params(8),
        cost_estimate=cost(0, 4 * rows * (width + columns)),
    )(down, up)[0]


def table_kernel(n_adapter, per_device, ids, slots, table):
    seg_dev = ids.shape[0] // SEGMENT_ROWS
    used = [slots[ids[s * SEGMENT_ROWS]] for s in range(seg_dev)]
    for k, owner in enumerate(arrival_order(lax.axis_index("adapter"), n_adapter)):
        table[k * ENTRIES] = owner
        found, place = [jnp.int32(-1)] * MOST, [jnp.int32(0)] * MOST
        count = jnp.int32(0)
        for s, slot in enumerate(used):
            within = slot - owner * per_device
            hit = (within >= 0) & (within < per_device)
            for j in range(MOST):
                take = hit & (count == j)
                found[j] = jnp.where(take, s, found[j])
                place[j] = jnp.where(take, within, place[j])
            count = count + hit.astype(jnp.int32)
        for j in range(MOST):
            table[k * ENTRIES + 1 + 2 * j] = found[j]
            table[k * ENTRIES + 2 + 2 * j] = place[j]


def table_call(ids, slots, n_adapter, per_device):
    return pl.pallas_call(
        functools.partial(table_kernel, n_adapter, per_device),
        in_specs=[SMEM, SMEM],
        out_specs=SMEM,
        out_shape=jax.ShapeDtypeStruct((n_adapter * ENTRIES,), jnp.int32),
        cost_estimate=cost(0, 4 * ids.shape[0]),
    )(ids, slots)


def diagonal():
    shape = (SEGMENT_ROWS, SEGMENT_ROWS)
    return lax.broadcasted_iota(jnp.int32, shape, 0) == lax.broadcasted_iota(jnp.int32, shape, 1)


GROUP = SEGMENT_ROWS // 8
WORDS = 5 * GROUP


def coded_rows(segments):
    return segments * WORDS + 8


def encode(values, o_ref, unit, units):
    largest = jnp.maximum(jnp.max(jnp.abs(values), axis=1, keepdims=True), 2.0**-100)
    power = jnp.floor(jnp.log2(largest))
    whole = (values * jnp.exp2(18.0 - power) + MIDDLE).astype(jnp.int32) - int(MIDDLE)
    whole = jnp.clip(whole, -(2**19), 2**19 - 1)
    v = [whole[i * GROUP : (i + 1) * GROUP] for i in range(8)]
    over = [
        v[5] & 0xFFF,
        ((v[5] >> 12) & 0xFF) | ((v[6] & 0xF) << 8),
        (v[6] >> 4) & 0xFFF,
        ((v[6] >> 16) & 0xF) | ((v[7] & 0xFF) << 4),
        v[7] >> 8,
    ]
    for i in range(5):
        o_ref[unit * WORDS + i * GROUP : unit * WORDS + (i + 1) * GROUP, :] = (v[i] & 0xFFFFF) | (
            over[i] << 20
        )
    row = jnp.sum(jnp.where(diagonal(), power, 0.0), axis=0, keepdims=True)
    o_ref[units * WORDS + unit : units * WORDS + unit + 1, :SEGMENT_ROWS] = row.astype(jnp.int32)


def decode(ref, unit, units):
    w = [ref[unit * WORDS + i * GROUP : unit * WORDS + (i + 1) * GROUP, :] for i in range(5)]
    v = [(x << 12) >> 12 for x in w]
    v.append(((w[0] >> 20) & 0xFFF) | (((w[1] << 4) >> 24) << 12))
    v.append(((w[1] >> 28) & 0xF) | (((w[2] >> 20) & 0xFFF) << 4) | (((w[3] << 8) >> 28) << 16))
    v.append(((w[3] >> 24) & 0xFF) | ((w[4] >> 20) << 8))
    row = ref[units * WORDS + unit : units * WORDS + unit + 1, :SEGMENT_ROWS].astype(jnp.float32)
    power = jnp.sum(jnp.where(diagonal(), row, 0.0), axis=1, keepdims=True)
    return jnp.concatenate(v, axis=0).astype(jnp.float32) * jnp.exp2(power - 18.0)


def add_decoded(sums, chunk, refs, above):
    first, number = CHUNKS[chunk]
    for unit in range(number):
        at = first + unit - above
        if at < 0 or at >= sums.shape[0] // SEGMENT_ROWS:
            continue
        rows = pl.ds(at * SEGMENT_ROWS, SEGMENT_ROWS)
        value = sums[rows, :]
        for ref in refs:
            value = value + decode(ref, unit, number)
        sums[rows, :] = value


def load_base(first, segments, column, x_ref, w_ref, x, w, sems):
    width, columns = w.shape
    rows = segments * SEGMENT_ROWS
    start = pl.multiple_of(column * columns, columns)
    depth = width // PIECES
    blocks = [(r, min(BLOCK, rows - r)) for r in range(0, rows, BLOCK)]

    def x_copy(at, size, features, sem):
        return pltpu.make_async_copy(
            x_ref.at[pl.ds(first * SEGMENT_ROWS + at, size), features],
            x.at[pl.ds(at, size), features],
            sem,
        )

    work = []
    for i, (at, size) in enumerate(blocks):
        terms = []
        if i == 0:
            for p in range(PIECES):
                features = pl.ds(p * depth, depth)
                copies = (
                    pltpu.make_async_copy(
                        w_ref.at[features, pl.ds(start, columns)], w.at[features, :], sems.at[0, p]
                    ),
                    x_copy(0, size, features, sems.at[1, p]),
                )
                terms.append((copies, slice(p * depth, (p + 1) * depth)))
        else:
            terms.append(((x_copy(at, size, slice(None), sems.at[2, i]),), slice(None)))
        work.append((at, size, terms))
    for _, _, terms in work:
        for copies, _ in terms:
            for copy in copies:
                copy.start()
    return work


def block_product(x, w, at, size, terms):
    total = None
    for copies, features in terms:
        for copy in copies:
            copy.wait()
        term = jnp.dot(
            x[at : at + size, features], w[features, :], preferred_element_type=jnp.float32
        )
        total = term if total is None else total + term
    return total


def base_scratch(segments, width, columns):
    rows = segments * SEGMENT_ROWS
    return [
        pltpu.VMEM((rows, width), jnp.bfloat16),
        pltpu.VMEM((width, columns), jnp.bfloat16),
        pltpu.SemaphoreType.DMA((3, max(PIECES, rows // BLOCK + 1))),
    ]


def sent_kernel(first, sizes, step, n_tensor, x_ref, w_ref, *refs):
    outs, (x, w, sems) = refs[: len(sizes)], refs[len(sizes) :]
    column = lax.rem(lax.axis_index("tensor") + step, n_tensor)
    work = load_base(first, sum(sizes), column, x_ref, w_ref, x, w, sems)
    unit_of = [(out, unit) for out, size in enumerate(sizes) for unit in range(size)]
    for out, size in zip(outs, sizes):
        out[size * WORDS :, :] = jnp.zeros((8, w.shape[1]), jnp.int32)
    for at, size, terms in work:
        product = block_product(x, w, at, size, terms)
        for r in range(0, size, SEGMENT_ROWS):
            out, unit = unit_of[(at + r) // SEGMENT_ROWS]
            encode(product[r : r + SEGMENT_ROWS], outs[out], unit, sizes[out])


def sent_call(tokens, weight, step, n_tensor, columns, first, sizes):
    width = tokens.shape[1]
    rows = sum(sizes) * SEGMENT_ROWS
    return pl.pallas_call(
        functools.partial(sent_kernel, first, sizes, step, n_tensor),
        in_specs=[HBM, HBM],
        out_specs=[VMEM] * len(sizes),
        out_shape=[jax.ShapeDtypeStruct((coded_rows(n), columns), jnp.int32) for n in sizes],
        scratch_shapes=base_scratch(sum(sizes), width, columns),
        compiler_params=params(16),
        cost_estimate=cost(
            2 * rows * width * columns, 2 * rows * width + 2 * width * columns + 4 * rows * columns
        ),
    )(tokens, weight)


def add_kernel(chunk, above, sums_ref, *refs):
    coded_refs, o_ref = refs[:-1], refs[-1]
    o_ref[...] = sums_ref[...]
    add_decoded(o_ref, chunk, coded_refs, above)


def add_call(chunk, above, sums, coded):
    return pl.pallas_call(
        functools.partial(add_kernel, chunk, above),
        in_specs=[VMEM] * (1 + len(coded)),
        out_specs=VMEM,
        out_shape=jax.ShapeDtypeStruct(sums.shape, sums.dtype),
        compiler_params=params(8),
        cost_estimate=cost(40000 * sums.size, 12 * sums.size),
    )(sums, *coded)


def shrink_into(o_ref, at, table, k, rows_of, views, rank, pair):
    def one(j, carry):
        _, _, within = segment_of(table, k, j)
        for stage, ref, first, whose, i in views:
            if stage not in stages_of(k):
                continue

            @pl.when((whose == table[k * ENTRIES]) & (within == i))
            def _(ref=ref, first=first):
                rows = rows_of(j)
                pair[j] = lax.dot_general(
                    rows,
                    ref[first : first + rank, : rows.shape[1]],
                    (((1,), (1,)), ((), ())),
                    preferred_element_type=jnp.float32,
                )

        return carry

    lax.fori_loop(0, MOST, one, 0)
    for j in range(MOST):
        o_ref[at, :, j * rank : (j + 1) * rank] = pair[j]


def join_copies(halves, whole, sems):
    copies, rank = [], halves[0].shape[0]
    for i, half in enumerate(halves):
        copies.append(
            pltpu.make_async_copy(half, whole.at[pl.ds(i * rank, rank), :], sems.at[i])
        )
        copies[-1].start()
    return copies


def stages_of(k):
    return range((k + 1) // 2, k + 1)


def stages_of_all(ks):
    return range(stages_of(ks[0])[0], ks[-1] + 1)


def upper_kernel(n_adapter, table, x_ref, w_ref, o_ref, kept_ref, x, w, sems, kept_sems):
    work = load_base(0, x.shape[0] // SEGMENT_ROWS, lax.axis_index("tensor"), x_ref, w_ref, x, w, sems)
    keeps = []
    for k in range(1, n_adapter):
        for j in range(MOST):
            start, _, _ = segment_of(table, k, j)
            keeps.append(
                pltpu.make_async_copy(
                    x_ref.at[pl.ds(start, SEGMENT_ROWS), :],
                    kept_ref.at[k - 1, j],
                    kept_sems.at[k - 1, j],
                )
            )
            keeps[-1].start()
    for at, size, terms in work:
        o_ref[at : at + size, :] = block_product(x, w, at, size, terms)
    for copy in keeps:
        copy.wait()


def upper_call(table, tokens, weight, columns, n_adapter):
    rows, width = tokens.shape
    half = UPPER * SEGMENT_ROWS
    return pl.pallas_call(
        functools.partial(upper_kernel, n_adapter),
        in_specs=[SMEM, HBM, HBM],
        out_specs=[VMEM] * 2,
        out_shape=[
            jax.ShapeDtypeStruct((half, columns), jnp.float32),
            jax.ShapeDtypeStruct((n_adapter - 1, MOST, SEGMENT_ROWS, width), jnp.bfloat16),
        ],
        scratch_shapes=base_scratch(half // SEGMENT_ROWS, width, columns)
        + [pltpu.SemaphoreType.DMA((n_adapter - 1, MOST))],
        compiler_params=params(12),
        cost_estimate=cost(2 * half * width * columns, 2 * rows * width + 2 * width * columns),
    )(table, tokens, weight)


def lower_kernel(per_device, rank, table, x_ref, w_ref, *refs):
    messages, halves, refs = refs[:per_device], refs[per_device : 2 * per_device], refs[2 * per_device :]
    coded_refs, (o_ref, s_ref, whole_ref, x, w, sems, mine, mine_sems, join_sems, pair) = refs[:-10], refs[-10:]
    work = load_base(UPPER, x.shape[0] // SEGMENT_ROWS, lax.axis_index("tensor"), x_ref, w_ref, x, w, sems)
    joins = join_copies(halves, whole_ref, join_sems)
    loads = []
    for j in range(MOST):
        start, _, _ = segment_of(table, 0, j)
        loads.append(
            pltpu.make_async_copy(
                x_ref.at[pl.ds(start, SEGMENT_ROWS), :], mine.at[j], mine_sems.at[j]
            )
        )
        loads[-1].start()
    for at, size, terms in work:
        o_ref[at : at + size, :] = block_product(x, w, at, size, terms)
    add_decoded(o_ref, 0, coded_refs, UPPER)
    for copy in loads:
        copy.wait()
    views = views_of(messages, [0], [(per_device, 0)], rank)
    shrink_into(s_ref, 0, table, 0, lambda j: mine[j], views, rank, pair)
    for copy in joins:
        copy.wait()


def lower_call(table, tokens, weight, messages, halves, coded, columns):
    rows, width = tokens.shape
    half = rows - UPPER * SEGMENT_ROWS
    per_device, (rank, long) = len(messages), messages[0].shape
    return pl.pallas_call(
        functools.partial(lower_kernel, per_device, rank),
        in_specs=[SMEM, HBM, HBM] + [VMEM] * (2 * per_device + len(coded)),
        out_specs=[VMEM] * 3,
        out_shape=[
            jax.ShapeDtypeStruct((half, columns), jnp.float32),
            jax.ShapeDtypeStruct((1, SEGMENT_ROWS, MOST * rank), jnp.float32),
            jax.ShapeDtypeStruct((per_device * rank, long), jnp.bfloat16),
        ],
        scratch_shapes=base_scratch(half // SEGMENT_ROWS, width, columns)
        + [
            pltpu.VMEM((MOST, SEGMENT_ROWS, width), jnp.bfloat16),
            pltpu.SemaphoreType.DMA((MOST,)),
            pltpu.SemaphoreType.DMA((per_device,)),
            pltpu.VMEM((MOST, SEGMENT_ROWS, rank), jnp.float32),
        ],
        compiler_params=params(14),
        cost_estimate=cost(0 * half * width * columns, 4 * rows * columns),
    )(table, tokens, weight, *messages, *halves, *coded)


def shrink_kernel(ks, rank, at, layout, table, kept_ref, *refs):
    buffers, (o_ref, pair) = refs[1 if at else 0 : -2], refs[-2:]
    if at:
        o_ref[:at] = refs[0][...]
    views = views_of(buffers, stages_of_all(ks), layout, rank)
    for i, k in enumerate(ks):
        shrink_into(o_ref, at + i, table, k, lambda j, k=k: kept_ref[k - 1, j], views, rank, pair)


def shrink_call(ks, table, kept, before, buffers, layout, rank):
    width = kept.shape[3]
    at = sum(b.shape[0] for b in before)
    return pl.pallas_call(
        functools.partial(shrink_kernel, ks, rank, at, layout),
        in_specs=[SMEM] + [VMEM] * (1 + len(before) + len(buffers)),
        out_specs=VMEM,
        out_shape=jax.ShapeDtypeStruct((at + len(ks), SEGMENT_ROWS, MOST * rank), jnp.float32),
        scratch_shapes=[pltpu.VMEM((MOST, SEGMENT_ROWS, rank), jnp.float32)],
        compiler_params=params(4),
        cost_estimate=cost(
            len(ks) * MOST * 2 * SEGMENT_ROWS * width * 256, len(ks) * 4 * SEGMENT_ROWS * width
        ),
    )(table, kept, *before, *buffers)


def fetch_up(up, at, table, k, j, views, rank):
    columns = up.shape[2]
    _, _, within = segment_of(table, k, j)
    for stage, ref, first, whose, i in views:
        if stage not in stages_of(k):
            continue

        @pl.when((whose == table[k * ENTRIES]) & (within == i))
        def _(ref=ref, first=first):
            factor = ref[first : first + rank, ref.shape[1] - columns :]
            up[at, :rank, :] = factor
            up[at, rank:, :] = factor


def up_product(share, j, factor, rank):
    lane = lax.broadcasted_iota(jnp.int32, share.shape, 1)
    other = pltpu.roll(share, rank, 1)
    both = jnp.where((lane < rank) == (j == 0), share, other)
    high = both.astype(jnp.bfloat16).astype(jnp.float32)
    terms = jnp.where(lane < rank, high, both - high).astype(jnp.bfloat16)
    return jnp.dot(terms, factor, preferred_element_type=jnp.float32)


LATE = 2


def early_kernel(n_adapter, n_tensor, rank, layout, n_buffers, table, *refs):
    first = n_adapter - LATE
    upper_ref, lower_ref, refs = refs[0], refs[1], refs[2:]
    shrinks, refs = refs[: -7 - n_buffers], refs[-7 - n_buffers :]
    buffers, (o_ref, rest_ref, late_up, up, sums, out, sems) = refs[:-7], refs[-7:]
    views = views_of(buffers, range(n_adapter), layout, rank)
    stores = []
    for k in range(first):
        for j in range(MOST):
            fetch_up(up, k * MOST + j, table, k, j, views, rank)
    shares = []
    for call in range(len(shrinks) // n_tensor):
        share = shrinks[call * n_tensor][...]
        for i in range(1, n_tensor):
            share = share + shrinks[call * n_tensor + i][...]
        shares += [share[i] for i in range(share.shape[0])]
    for k in range(n_adapter):
        for j in range(MOST):
            start, used, _ = segment_of(table, k, j)
            upper_rows = upper_ref.shape[0]

            @pl.when(start < upper_rows)
            def _(start=start):
                at = pl.multiple_of(jnp.minimum(start, upper_rows - SEGMENT_ROWS), SEGMENT_ROWS)
                sums[...] = upper_ref[pl.ds(at, SEGMENT_ROWS), :]

            @pl.when(start >= upper_rows)
            def _(start=start):
                at = pl.multiple_of(jnp.maximum(start - upper_rows, 0), SEGMENT_ROWS)
                sums[...] = lower_ref[pl.ds(at, SEGMENT_ROWS), :]

            value = sums[...]
            if k >= first:
                rest_ref[k - first, j] = value
                fetch_up(late_up, (k - first) * MOST + j, table, k, j, views, rank)
                continue
            lora = up_product(shares[k], j, up[k * MOST + j], rank)
            out[k, j] = (value + adapter_scale * lora).astype(jnp.bfloat16)
            store = pltpu.make_async_copy(
                out.at[k, j], o_ref.at[pl.ds(start, SEGMENT_ROWS), :], sems.at[k, j]
            )
            pl.when(used)(store.start)
            stores.append((used, store))
    for used, store in stores:
        pl.when(used)(store.wait)


def early(n_adapter, n_tensor, table, upper, lower, shrinks, buffers, layout, rank):
    rows, columns = upper.shape[0] + lower.shape[0], upper.shape[1]
    return pl.pallas_call(
        functools.partial(early_kernel, n_adapter, n_tensor, rank, layout, len(buffers)),
        in_specs=[SMEM] + [VMEM] * (2 + len(shrinks) + len(buffers)),
        out_specs=[ANY, VMEM, VMEM],
        out_shape=[
            jax.ShapeDtypeStruct((rows, columns), jnp.bfloat16),
            jax.ShapeDtypeStruct((LATE, MOST, SEGMENT_ROWS, columns), jnp.float32),
            jax.ShapeDtypeStruct((LATE * MOST, 2 * rank, columns), jnp.bfloat16),
        ],
        scratch_shapes=[
            pltpu.VMEM(((n_adapter - LATE) * MOST, 2 * rank, columns), jnp.bfloat16),
            pltpu.VMEM((SEGMENT_ROWS, columns), jnp.float32),
            pltpu.VMEM((n_adapter - LATE, MOST, SEGMENT_ROWS, columns), jnp.bfloat16),
            pltpu.SemaphoreType.DMA((n_adapter - LATE, MOST)),
        ],
        compiler_params=params(16),
        cost_estimate=cost(6 * rows * rank * columns, (4 * n_tensor + 2) * rows * columns),
    )(table, upper, lower, *shrinks, *buffers)


def late_kernel(ks, n_tensor, rank, table, *refs):
    rest_ref, shrinks, refs = refs[0], refs[1 : 1 + n_tensor], refs[1 + n_tensor :]
    up, _, o_ref, out, sems = refs
    stores = []
    for i, k in enumerate(ks):
        share = shrinks[0][i]
        for r in shrinks[1:]:
            share = share + r[i]
        for j in range(MOST):
            start, used, _ = segment_of(table, k, j)
            lora = up_product(share, j, up[i * MOST + j], rank)
            out[i, j] = (rest_ref[i, j] + adapter_scale * lora).astype(jnp.bfloat16)
            store = pltpu.make_async_copy(
                out.at[i, j], o_ref.at[pl.ds(start, SEGMENT_ROWS), :], sems.at[i, j]
            )
            pl.when(used)(store.start)
            stores.append((used, store))
    for used, store in stores:
        pl.when(used)(store.wait)


def late(ks, n_tensor, table, rest, shrinks, up, value, rank):
    rows, columns = value.shape
    return pl.pallas_call(
        functools.partial(late_kernel, ks, n_tensor, rank),
        in_specs=[SMEM] + [VMEM] * (2 + len(shrinks)) + [ANY],
        out_specs=ANY,
        out_shape=jax.ShapeDtypeStruct((rows, columns), jnp.bfloat16),
        scratch_shapes=[
            pltpu.VMEM((LATE, MOST, SEGMENT_ROWS, columns), jnp.bfloat16),
            pltpu.SemaphoreType.DMA((LATE, MOST)),
        ],
        input_output_aliases={3 + len(shrinks): 0},
        compiler_params=params(8),
        cost_estimate=cost(
            6 * LATE * MOST * SEGMENT_ROWS * rank * columns,
            8 * LATE * MOST * SEGMENT_ROWS * columns,
        ),
    )(table, rest, *shrinks, up, value)


def after(array, *others):
    return lax.optimization_barrier((array, *others))[0]


def on_device(
    tokens, value_weight, adapter_down_weight, adapter_up_weight, row_adapter_index, adapter_slot_of
):
    rows, width = tokens.shape
    per_device, _, rank = adapter_down_weight.shape
    n_adapter = lax.axis_size("adapter")
    n_tensor = lax.axis_size("tensor")
    columns = value_weight.shape[1] // n_tensor

    def swap_tensor(array, step):
        pairs = [(i, (i + step) % n_tensor) for i in range(n_tensor)]
        return lax.ppermute(array, "tensor", pairs)

    def along_line(array, stage):
        up = [(2 * i, 2 * (i + 1)) for i in range(stage - 1, n_adapter - 1)]
        down = [(2 * i + 1, 2 * (i - 1) + 1) for i in range(1, n_adapter - stage + 1)]
        return lax.ppermute(array, ("adapter", "dp"), up + down)

    def swap_cores(array):
        return lax.ppermute(array, "dp", [(0, 1), (1, 0)])

    down = jnp.swapaxes(adapter_down_weight, 1, 2).reshape(per_device * rank, width)
    up = adapter_up_weight.reshape(per_device * rank, value_weight.shape[1])
    tokens, value_weight, down, up = (
        pltpu.with_memory_space_constraint(a, pltpu.HBM) for a in (tokens, value_weight, down, up)
    )
    messages = [message_call(down, up, columns, per_device, i) for i in range(per_device)]
    table = table_call(row_adapter_index, adapter_slot_of, n_adapter, per_device)
    last = n_adapter - 1
    buffers, shrinks = [list(messages)], []
    layout = [(per_device, 0), (per_device, 1)] + [(per_device, per_device)] * (last - 1)

    def buffers_of(stages):
        return [b for stage in stages for b in buffers[stage]]

    def shrink(ks, kept, before=()):
        mine = buffers_of(stages_of_all(ks))
        return shrink_call(ks, table, kept, list(before), mine, layout, rank)

    def add_shrink(mine):
        shrinks.extend([mine] + [swap_tensor(mine, step) for step in range(1, n_tensor)])

    others = range(1, n_tensor)

    def sent_for(step, chunks, rows):
        sizes = [number for _, number in chunks]
        return sent_call(rows, value_weight, step, n_tensor, columns, chunks[0][0], sizes)

    def send(parts, *ahead):
        return [swap_tensor(after(p, *ahead), step) for step, p in zip(others, parts)]

    held = [along_line(m, 1) for m in messages]
    part_a = [sent_for(step, CHUNKS[:1], tokens)[0] for step in others]
    sent = [send(part_a)]
    first = after(held[0], table, *part_a)
    rest_parts = [sent_for(step, CHUNKS[1:], after(tokens, first)) for step in others]
    parts = [[p[i] for p in rest_parts] for i in range(len(CHUNKS) - 1)]
    part_b = [p for group in parts for p in group]
    for stage in range(1, last):
        came = held
        if stage == 1:
            came = [first] + [after(h, *part_b) for h in held[1:]]
            sent.append(send(parts[0], *came, *sent[0]))
        if stage == 2:
            came = held[:1] + [after(h, upper) for h in held[1:]]
        held = [along_line(c, stage + 1) for c in came]
        if stage == 1:
            upper, kept = upper_call(
                after(table, held[0], *came), tokens, value_weight, columns, n_adapter
            )
        elif stage == 2:
            lower, before, joined = lower_call(
                after(table, *came), tokens, value_weight, messages, buffers[1], sent[0], columns
            )
            buffers[1] += [swap_cores(joined)]
            free = lower
            upper = add_call(1, 0, after(upper, held[0]), sent[1])
            lower = add_call(1, UPPER, after(lower, upper, *held[1:]), sent[1])
            before = shrink([1], after(kept, lower), [before])
        else:
            before = shrink([stage - 1], kept, [before])
        ahead = [free] if stage == 2 else []
        swapped = [swap_cores(after(c, *ahead)) for c in came] if stage > 1 else []
        buffers.append([*came, *swapped])
    add_shrink(before)
    buffers.append([*held, *[swap_cores(h) for h in held]])
    value, remaining, factors = early(
        n_adapter,
        n_tensor,
        table,
        upper,
        lower,
        shrinks,
        buffers_of(range(n_adapter)),
        layout,
        rank,
    )
    ks = (last - 1, last)
    add_shrink(shrink(ks, after(kept, *held)))
    return late(
        ks,
        n_tensor,
        table,
        remaining,
        shrinks[-n_tensor:],
        factors,
        value,
        rank,
    )


def solution(mesh):
    return jax.shard_map(
        on_device,
        mesh=mesh,
        in_specs=(
            P(("groups", "adapter", "dp"), "tensor"),
            P("tensor", None),
            P(("groups", "adapter"), "tensor", None),
            P(("groups", "adapter"), None, None),
            P(("groups", "adapter", "dp")),
            P("groups"),
        ),
        out_specs=P(("groups", "adapter", "dp"), "tensor"),
        check_vma=False,
    )
```
